32 devices in a mesh: azim: 8 (over z, x), axial: 4 (over y, core).
Axes of the slice: x: 2, y: 2, z: 4, core: 2. Of those that a mesh axis runs over, the one named last changes fastest.
Arguments:
- rhs: float32 [8, 48, 4, 128], P('azim', None, 'axial'), may hold values from -6 to 6
- coupling: float32 [8, 48, 4, 128], P('azim', None, 'axial'), may hold values from 0.2 to 0.5
- fwd_coupling: bfloat16 [8, 48, 48, 4, 128], P('azim', None, None, 'axial'), may hold values from -1 to 1
- bwd_coupling: bfloat16 [8, 48, 48, 4, 128], P('azim', None, None, 'axial'), may hold values from -1 to 1
- block_inverse: bfloat16 [8, 48, 48, 4, 128], P('azim', None, None, 'axial'), may hold values from -1 to 1
Outputs:
- correction: float32 [8, 48, 4, 128], P('azim', None, 'axial')
- remaining: float32 [8, 48, 4, 128], P('azim', None, 'axial')
The draws below stay inside these ranges and needn't reach their ends.
All inputs are finite; a program needn't handle non-finite values.
Results may differ from the reference program's by a relative error of at most 0.0003.
Values sent between devices are 32-bit elements; how exact they have to be, the bound alone decides.
No kernel may reach another device: no remote copies, remote signals or barrier semaphores. Data moves between devices by JAX's collectives and lax.ppermute only.
A program may use at most 128 MiB of HBM per device.

```python
import math
import jax
import jax.numpy as jnp
from jax import lax

B = 48
GAP_LAYERS = 128
ANGULAR_PANELS = 8
FLOW_POSITIONS = 4


def coupling_blocks(key, slow_share, orient):
    divided_seeds = jax.random.split(key, 8)
    half = B // 2
    picker = jax.random.uniform(divided_seeds[0], (1, half, FLOW_POSITIONS, GAP_LAYERS))
    speed = jax.random.uniform(divided_seeds[1], (1, half, FLOW_POSITIONS, GAP_LAYERS), minval=0.4, maxval=1.0)
    factor = jnp.exp(jax.random.uniform(divided_seeds[2], (ANGULAR_PANELS, half, FLOW_POSITIONS, GAP_LAYERS), minval=math.log(0.5), maxval=math.log(2.0)))
    slow_rate = jnp.minimum(jnp.exp(-speed * factor / ANGULAR_PANELS), 0.998)
    fast_rate = jax.random.uniform(divided_seeds[3], (ANGULAR_PANELS, half, FLOW_POSITIONS, GAP_LAYERS), minval=0.3, maxval=0.8)
    coupled_speed = jnp.where(picker < slow_share, slow_rate, fast_rate)
    packet_bundles = jax.random.uniform(divided_seeds[4], (ANGULAR_PANELS, 1, FLOW_POSITIONS, GAP_LAYERS)) < 2.0 / ANGULAR_PANELS
    coupled_speed = coupled_speed * jnp.where(packet_bundles, 0.75, 1.0)
    turning = jax.random.uniform(divided_seeds[5], (ANGULAR_PANELS, half, FLOW_POSITIONS, GAP_LAYERS), minval=0.3, maxval=0.8)
    turning = turning * jnp.where(jax.random.uniform(divided_seeds[6], (ANGULAR_PANELS, half, FLOW_POSITIONS, GAP_LAYERS)) < 0.5, 1.0, -1.0)
    rate_rows = jnp.repeat(coupled_speed, 2, axis=1)[:, :, None]
    cosine = jnp.repeat(jnp.cos(turning), 2, axis=1)[:, :, None]
    sine = jnp.repeat(jnp.sin(turning), 2, axis=1)[:, :, None]
    row_index = lax.broadcasted_iota(jnp.int32, (1, B, B, 1, 1), 1)
    column_index = lax.broadcasted_iota(jnp.int32, (1, B, B, 1, 1), 2)
    same_pair = row_index // 2 == column_index // 2
    on_diagonal = row_index == column_index
    upper_row = row_index % 2 == 0
    paired = jnp.where(on_diagonal, cosine, jnp.where(upper_row, -sine, sine)) * rate_rows
    structured = jnp.where(same_pair, paired, 0.0) * orient
    noise = jnp.clip(jax.random.normal(divided_seeds[7], (ANGULAR_PANELS, B, B, FLOW_POSITIONS, GAP_LAYERS)), -4.0, 4.0) * (0.02 / math.sqrt(B))
    return (structured + noise).astype(jnp.bfloat16)


def draw_fwd_coupling(key, part):
    share = 0.5
    return coupling_blocks(jax.random.fold_in(key, 11), share, 1.0)


def draw_bwd_coupling(key, part):
    share = 0.5
    return coupling_blocks(jax.random.fold_in(key, 12), share, -1.0)


def draw_block_inverse(key, part):
    divided_seeds = jax.random.split(jax.random.fold_in(key, 13), 2)
    diagonal = jnp.exp(jax.random.uniform(divided_seeds[0], (ANGULAR_PANELS, B, 1, FLOW_POSITIONS, GAP_LAYERS), minval=math.log(0.04), maxval=math.log(0.15)))
    noise = jnp.clip(jax.random.normal(divided_seeds[1], (ANGULAR_PANELS, B, B, FLOW_POSITIONS, GAP_LAYERS)), -4.0, 4.0) * (0.07 / math.sqrt(B))
    row_index = lax.broadcasted_iota(jnp.int32, (1, B, B, 1, 1), 1)
    column_index = lax.broadcasted_iota(jnp.int32, (1, B, B, 1, 1), 2)
    return jnp.where(row_index == column_index, diagonal, noise).astype(jnp.bfloat16)


def block_levels(own_key, extent, shards, low, top_value):
    factor_of = 1.0
    for axis_at, blocks in shards:
        heights = jax.random.uniform(jax.random.fold_in(jax.random.fold_in(own_key, 6), axis_at), (blocks,), jnp.float32, low / len(shards), top_value / len(shards))
        factor_of = factor_of * jnp.repeat(jnp.exp(heights), extent[axis_at] // blocks).reshape((-1,) + (1,) * (len(extent) - 1 - axis_at))
    return factor_of


def bell_draw(own_key, extent, scale, bound, pieces=(), held_as=jnp.bfloat16):
    level = block_levels(own_key, extent, pieces, -0.22, 0.18) if pieces else 1.0
    entries = jax.random.normal(own_key, extent, jnp.float32) * scale * level
    return jnp.minimum(jnp.maximum(entries, -bound), bound).astype(held_as)


def setup_inputs(seed: int = 0) -> dict:
    seeds = jax.random.split(jax.random.key(seed), 6)
    rhs = bell_draw(seeds[0], (ANGULAR_PANELS, B, FLOW_POSITIONS, GAP_LAYERS), 1.0, 6.0, ((0, 8), (2, 4)), jnp.float32)
    coupling = jnp.clip(0.2 + 0.3 * jax.random.uniform(seeds[1], (ANGULAR_PANELS, B, FLOW_POSITIONS, GAP_LAYERS), jnp.float32) ** block_levels(seeds[1], (ANGULAR_PANELS, B, FLOW_POSITIONS, GAP_LAYERS), ((0, 8), (2, 4)), -0.2, 0.2), 0.2, 0.5)
    fwd_coupling = draw_fwd_coupling(jax.random.fold_in(seeds[5], 71), 0)
    bwd_coupling = draw_bwd_coupling(jax.random.fold_in(seeds[5], 71), 0)
    block_inverse = draw_block_inverse(jax.random.fold_in(seeds[5], 71), 0)
    return dict(rhs=rhs, coupling=coupling, fwd_coupling=fwd_coupling, bwd_coupling=bwd_coupling, block_inverse=block_inverse)


def reference(rhs, coupling, fwd_coupling, bwd_coupling, block_inverse):
    line_count = FLOW_POSITIONS * GAP_LAYERS
    forward_blocks = fwd_coupling.reshape(ANGULAR_PANELS, B, B, line_count)
    backward_blocks = bwd_coupling.reshape(ANGULAR_PANELS, B, B, line_count)
    inverse_blocks = block_inverse.reshape(ANGULAR_PANELS, B, B, line_count)
    source = rhs.reshape(ANGULAR_PANELS, B, line_count)
    coupling_field = coupling.reshape(ANGULAR_PANELS, B, line_count)

    def sweep(blocks, consts, reverse):
        def advance(carried, inputs):
            one_block, const_term = inputs
            carried = const_term - jnp.einsum("abl,al->bl", one_block.astype(jnp.float32), carried,
                                              precision=lax.Precision.HIGHEST)
            return carried, carried

        start_state = jnp.zeros((B, line_count), jnp.float32)
        wrapped, _ = lax.scan(advance, start_state, (blocks, consts), reverse=reverse)
        _, outputs = lax.scan(advance, wrapped, (blocks, consts), reverse=reverse)
        return outputs

    def precondition(vector):
        consts = lax.map(lambda members: jnp.einsum("abl,al->bl", members[0].astype(jnp.float32), members[1],
                                                    precision=lax.Precision.HIGHEST), (inverse_blocks, vector))
        forward = sweep(forward_blocks, consts, False)
        return sweep(backward_blocks, forward, True)

    def neighbours(field):
        grid = field.reshape(ANGULAR_PANELS, B, FLOW_POSITIONS, GAP_LAYERS)
        padded = jnp.pad(grid, ((0, 0), (0, 0), (1, 1), (0, 0)))
        return (padded[:, :, :-2] + padded[:, :, 2:]).reshape(ANGULAR_PANELS, B, line_count)

    applied_once = precondition(source)
    middle = source - applied_once + coupling_field * neighbours(applied_once)
    second = precondition(middle)
    correction = applied_once + second
    remaining = middle - second + coupling_field * neighbours(second)
    return correction.reshape(ANGULAR_PANELS, B, FLOW_POSITIONS, GAP_LAYERS), remaining.reshape(ANGULAR_PANELS, B, FLOW_POSITIONS, GAP_LAYERS)
```

```python
import jax
import jax.numpy as jnp
from jax import lax
from jax.experimental import pallas as pl
from jax.experimental.pallas import tpu as pltpu
from jax.sharding import PartitionSpec as P

highest = lax.Precision.HIGHEST
f32 = jnp.float32
BOTH = ("azim", "axial")


def lane_index():
    return lax.broadcasted_iota(jnp.int32, (8, 128), 1)


def row_index():
    return lax.broadcasted_iota(jnp.int32, (8, 128), 0)


def turn_lanes(tile, steps):
    steps = steps % 128
    return pltpu.roll(tile, steps, 1) if steps else tile


def turn_rows(tile, steps):
    steps = steps % 8
    return pltpu.roll(tile, steps, 0) if steps else tile


def swap_quads(tiles):
    lanes = lane_index()
    tiles = list(tiles)
    for bit, width in ((1, 4), (2, 8)):
        low = (lanes // width) % 2 == 0
        for first in range(4):
            if first & bit:
                continue
            one, two = tiles[first], tiles[first | bit]
            tiles[first] = jnp.where(low, one, turn_lanes(two, width))
            tiles[first | bit] = jnp.where(low, turn_lanes(one, -width), two)
    return tiles


def swap_rows(tile):
    lanes, rows = lane_index() // 16, row_index()
    for bit in (1, 2, 4):
        row_bit, lane_bit = (rows // bit) % 2, (lanes // bit) % 2
        up = turn_rows(turn_lanes(tile, 16 * bit), -bit)
        down = turn_rows(turn_lanes(tile, -16 * bit), bit)
        tile = jnp.where(row_bit == lane_bit, tile, jnp.where(row_bit == 0, up, down))
    return tile


def put_slots(out_ref, tiles, rows, base):
    zero = jnp.zeros((8, 128), f32)
    for half in range(2):
        group = [tiles[4 * half + x] if 4 * half + x < 6 else zero for x in range(4)]
        for quad, tile in enumerate(swap_quads(group)):
            out_ref[pl.ds(rows * quad + base + half, 8, stride=4 * rows), :] = tile


def get_slots(in_ref, rows, base):
    tiles = []
    for half in range(2):
        group = [in_ref[pl.ds(rows * quad + base + half, 8, stride=4 * rows), :] for quad in range(4)]
        tiles += swap_quads(group)
    return tiles[:6]


def put_cell_vector(out_ref, vector_ref, rows, base):
    put_slots(out_ref, [swap_rows(vector_ref[8 * t : 8 * t + 8, :]) for t in range(6)], rows, base)


def inverse_matvec(inverse_ref, vector_ref, out_ref):
    def step(group, totals):
        for inner in range(8):
            a = 8 * group + inner
            row = vector_ref[pl.ds(a, 1), :]
            totals = totals + inverse_ref[a].astype(f32) * row
        return totals

    out_ref[...] = lax.fori_loop(0, 6, step, jnp.zeros((48, 128), f32))


def pack_blocks(block_ref, out_ref):
    def body(group, carry):
        ah_pair, bh_pair = group // 3, group % 3
        quads = lane_index() // 4
        items = [None] * 32
        for y in range(2):
            for p in range(8):
                wide = block_ref[16 * ah_pair + 8 * y + p, pl.ds(pl.multiple_of(16 * bh_pair, 16), 16), :]
                wide = wide.astype(f32)
                for h in range(2):
                    i = 4 * p + 2 * y + h
                    items[i] = turn_lanes(turn_rows(wide[8 * h : 8 * h + 8], -p), 4 * i)
        for bit in (1, 2, 4, 8, 16):
            keep = (quads // bit) % 2 == 0
            items = [jnp.where(keep, items[j], items[(j + bit) % 32]) for j in range(32)]
        for e in range(32):
            out_ref[e, pl.ds(pl.multiple_of(8 * group, 8), 8), :] = turn_lanes(items[-e % 32], -4 * e)
        return carry

    lax.fori_loop(0, 9, body, 0)


def unpack_blocks(in_ref, out_ref):
    def body(cell, carry):
        for group in range(9):
            parts = [in_ref[4 * cell + k, 8 * group : 8 * group + 8, :] for k in range(4)]
            for x, tile in enumerate(swap_quads(parts)):
                at = 8 * (4 * group + x)
                out_ref[cell, at : at + 8, :] = tile
        return carry

    lax.fori_loop(0, 8, body, 0)


def tile_at(ah, bh):
    return 4 * (3 * (ah // 2) + bh // 2) + 2 * (ah % 2) + bh % 2


def line_sweep(blocks_ref, const_ref, out_ref, reverse):
    order = list(range(8))
    if reverse:
        order = order[::-1]
    state = None
    for turn in range(2):
        for cell in order:
            consts = [jnp.broadcast_to(const_ref[t, cell : cell + 1, :], (8, 128)) for t in range(6)]
            if state is None:
                state = consts
                continue
            following = []
            for bh in range(6):
                total = None
                for ah in range(6):
                    at = 8 * tile_at(ah, bh)
                    term = blocks_ref[cell, at : at + 8, :] * state[ah]
                    total = term if total is None else total + term
                total = pltpu.roll(total, 0, 1, stride=16, stride_axis=0)
                for span in (4, 2, 1):
                    total = total + turn_rows(total, span)
                following.append(consts[bh] - total)
            state = following
            if turn == 1:
                for t in range(6):
                    out_ref[t, cell : cell + 1, :] = state[t][0:1]


def stations_sum(tile):
    station = (lane_index() // 4) % 4
    before = jnp.where(station > 0, turn_lanes(tile, 4), 0.0)
    after = jnp.where(station < 3, turn_lanes(tile, -4), 0.0)
    return before + after


def first_send_kernel(inverse_ref, rhs_ref, coupling_ref, out_ref, c_ref):
    inverse_matvec(inverse_ref, rhs_ref, c_ref)
    put_cell_vector(out_ref, c_ref, 8, 0)
    put_cell_vector(out_ref, rhs_ref, 8, 2)
    put_cell_vector(out_ref, coupling_ref, 8, 4)
    for quad in range(4):
        for last in (6, 7):
            out_ref[pl.ds(8 * quad + last, 8, stride=32), :] = jnp.zeros((8, 128), f32)


def first_forward_kernel(vectors_ref, slots_ref, y_ref, blocks_ref, c_ref):
    unpack_blocks(slots_ref, blocks_ref)
    for t, tile in enumerate(get_slots(vectors_ref, 8, 0)):
        c_ref[t] = tile
    line_sweep(blocks_ref, c_ref, y_ref, False)


def first_backward_kernel(vectors_ref, slots_ref, y_ref, out_ref, first_ref, middle_ref, coupling_ref, blocks_ref):
    unpack_blocks(slots_ref, blocks_ref)
    line_sweep(blocks_ref, y_ref, first_ref, True)
    rhs = get_slots(vectors_ref, 8, 2)
    coupling = get_slots(vectors_ref, 8, 4)
    middle = []
    for t in range(6):
        first = first_ref[t]
        middle.append(rhs[t] - first + coupling[t] * stations_sum(first))
        middle_ref[t] = middle[t]
        coupling_ref[t] = coupling[t]
    put_slots(out_ref, middle, 2, 0)


def second_send_kernel(inverse_ref, slots_ref, out_ref, v_ref, c_ref):
    for t, tile in enumerate(get_slots(slots_ref, 2, 0)):
        v_ref[8 * t : 8 * t + 8, :] = swap_rows(tile)
    inverse_matvec(inverse_ref, v_ref, c_ref)
    put_cell_vector(out_ref, c_ref, 2, 0)


def second_kernel(
    slots_ref, forward_ref, backward_ref, first_ref, middle_ref, coupling_ref, out_ref, c_ref, y_ref, second_ref
):
    for t, tile in enumerate(get_slots(slots_ref, 2, 0)):
        c_ref[t] = tile
    line_sweep(forward_ref, c_ref, y_ref, False)
    line_sweep(backward_ref, y_ref, second_ref, True)
    correction, remaining = [], []
    for t in range(6):
        second = second_ref[t]
        correction.append(first_ref[t] + second)
        remaining.append(middle_ref[t] - second + coupling_ref[t] * stations_sum(second))
    put_slots(out_ref, correction, 4, 0)
    put_slots(out_ref, remaining, 4, 2)


def last_kernel(slots_ref, correction_ref, remaining_ref):
    for out_ref, base in ((correction_ref, 0), (remaining_ref, 2)):
        for t, tile in enumerate(get_slots(slots_ref, 4, base)):
            out_ref[8 * t : 8 * t + 8, :] = swap_rows(tile)


def shaped(*sizes):
    return jax.ShapeDtypeStruct(sizes, f32)


def call(kernel, outs, scratch=()):
    return pl.pallas_call(
        kernel,
        out_shape=outs,
        scratch_shapes=[pltpu.VMEM(sizes, f32) for sizes in scratch],
        compiler_params=pltpu.CompilerParams(vmem_limit_bytes=40 * 1024 * 1024),
    )


def exchange(slots, rows):
    moved = lax.all_to_all(slots.reshape(32, rows, 128), BOTH, 0, 0, tiled=True)
    return moved.reshape(32 * rows, 128)


def line_plan(rhs, coupling, fwd_coupling, bwd_coupling, block_inverse):
    source, coupling_field = rhs.reshape(48, 128), coupling.reshape(48, 128)
    inverse_blocks = block_inverse.reshape(48, 48, 128)
    tiles = shaped(6, 8, 128)
    held = shaped(8, 288, 128)

    vectors = call(first_send_kernel, shaped(256, 128), [(48, 128)])(inverse_blocks, source, coupling_field)
    vectors = exchange(vectors, 8)
    forward_slots = call(pack_blocks, shaped(32, 72, 128))(fwd_coupling.reshape(48, 48, 128))
    forward_slots = lax.all_to_all(forward_slots, BOTH, 0, 0, tiled=True)
    backward_slots = call(pack_blocks, shaped(32, 72, 128))(bwd_coupling.reshape(48, 48, 128))
    backward_slots = lax.all_to_all(backward_slots, BOTH, 0, 0, tiled=True)
    y, forward = call(first_forward_kernel, (tiles, held), [(6, 8, 128)])(vectors, forward_slots)
    slots, first, middle, coupling_lines, backward = call(
        first_backward_kernel, (shaped(64, 128), tiles, tiles, tiles, held)
    )(vectors, backward_slots, y)
    slots = exchange(slots, 2)
    slots = call(second_send_kernel, shaped(64, 128), [(48, 128), (48, 128)])(inverse_blocks, slots)
    slots = exchange(slots, 2)
    slots = call(second_kernel, shaped(128, 128), [(6, 8, 128)] * 3)(
        slots, forward, backward, first, middle, coupling_lines
    )
    slots = exchange(slots, 4)
    correction, remaining = call(last_kernel, (shaped(48, 128), shaped(48, 128)))(slots)
    return correction.reshape(rhs.shape), remaining.reshape(rhs.shape)


def from_behind(value, axis, steps):
    count = lax.axis_size(axis)
    initial, last = (max(0, -steps), min(count, count - steps))
    return lax.ppermute(value, axis, [(source, source + steps) for source in range(initial, last)])


def from_root(shard, axis, root):
    mine = lax.axis_index(axis) == root
    return lax.psum(jnp.where(mine, shard, jnp.zeros_like(shard)), axis)


def extended(block, sides, width):
    for axis, dim in sides:
        count = lax.axis_size(axis)
        forward = [(i, i + 1) for i in range(count - 1)]
        backward = [(target, source) for source, target in forward]
        low = lax.ppermute(
            lax.slice_in_dim(block, block.shape[dim] - width, None, axis=dim), axis, forward
        )
        high = lax.ppermute(lax.slice_in_dim(block, 0, width, axis=dim), axis, backward)
        block = jnp.concatenate([low, block, high], axis=dim)
    return block


def cell_stride(one_block, carried, const_term):
    return const_term - jnp.einsum(
        "abl,al->bl", one_block.astype(jnp.float32), carried, precision=highest
    )


def compose_cells(blocks, sequence):
    running = None
    for position in sequence:
        one_block = blocks[position].astype(jnp.float32)
        running = -jnp.swapaxes(one_block, 0, 1)
    return running


def doubling_maps(local_map, reverse):
    size = lax.axis_size("azim")
    index = lax.axis_index("azim")
    levels = []
    current = local_map
    distance = 1
    while distance < size:
        if reverse:
            moved = from_behind(current, "azim", -distance)
            exists = index + distance < size
        else:
            moved = from_behind(current, "azim", distance)
            exists = index >= distance
        levels.append((current, distance))
        current = jnp.where(
            exists, jnp.einsum("bcl,cal->bal", current, moved, precision=highest), current
        )
        distance = distance * 2
    return (levels, current)


def doubling_entries(map_levels, local_offset, reverse):
    levels, final_map = map_levels
    size = lax.axis_size("azim")
    index = lax.axis_index("azim")
    running = local_offset
    for current, distance in levels:
        if reverse:
            moved = from_behind(running, "azim", -distance)
        else:
            moved = from_behind(running, "azim", distance)
        running = jnp.einsum("bcl,cl->bl", current, moved, precision=highest) + running
    if reverse:
        wrapped = from_root(running, "azim", 0)
    else:
        wrapped = from_root(running, "azim", size - 1)
    leaving = jnp.einsum("bcl,cl->bl", final_map, wrapped, precision=highest) + running
    if reverse:
        shifted = from_behind(leaving, "azim", -1)
        first_device = index == size - 1
    else:
        shifted = from_behind(leaving, "azim", 1)
        first_device = index == 0
    return jnp.where(first_device, wrapped, shifted)


def sweep(blocks, consts, map_levels, reverse):
    cell_count = blocks.shape[0]
    sequence = list(range(cell_count))
    if reverse:
        sequence = sequence[::-1]
    carried = jnp.zeros(consts.shape[1:], jnp.float32)
    for position in sequence:
        carried = cell_stride(blocks[position], carried, consts[position])
    local_offset = carried
    incoming_maps = doubling_entries(map_levels, local_offset, reverse)
    outputs = [None] * cell_count
    carried = incoming_maps
    for position in sequence:
        carried = cell_stride(blocks[position], carried, consts[position])
        outputs[position] = carried
    return jnp.stack(outputs)


def on_device(rhs, coupling, fwd_coupling, bwd_coupling, block_inverse):
    cell_count, block_width, _, position_total, radial_count = fwd_coupling.shape
    line_count = position_total * radial_count
    forward_blocks = fwd_coupling.reshape(cell_count, block_width, block_width, line_count)
    backward_blocks = bwd_coupling.reshape(cell_count, block_width, block_width, line_count)
    inverse_blocks = block_inverse.reshape(cell_count, block_width, block_width, line_count)
    source = rhs.reshape(cell_count, block_width, line_count)
    coupling_field = coupling.reshape(cell_count, block_width, line_count)
    forward_map = compose_cells(forward_blocks, list(range(cell_count)))
    backward_map = compose_cells(backward_blocks, list(range(cell_count))[::-1])
    forward_levels = None
    backward_levels = None
    forward_levels = doubling_maps(forward_map, False)
    backward_levels = doubling_maps(backward_map, True)

    def precondition(vector):
        consts = jnp.stack(
            [
                jnp.einsum(
                    "abl,al->bl",
                    inverse_blocks[0].astype(jnp.float32),
                    vector[0],
                    precision=highest,
                )
            ]
        )
        forward = sweep(forward_blocks, consts, forward_levels, False)
        return sweep(backward_blocks, forward, backward_levels, True)

    def stations_sum(field):
        grid = field.reshape(cell_count, block_width, position_total, radial_count)
        padded = extended(grid, (("axial", 2),), 1)
        return (padded[:, :, :-2] + padded[:, :, 2:]).reshape(cell_count, block_width, line_count)

    applied_once = precondition(source)
    middle = source - applied_once + coupling_field * stations_sum(applied_once)
    second = precondition(middle)
    correction = applied_once + second
    remaining = middle - second + coupling_field * stations_sum(second)
    return (correction.reshape(rhs.shape), remaining.reshape(rhs.shape))


def solution(mesh):
    cells, stations = mesh.shape["azim"], mesh.shape["axial"]

    def on_each(rhs, coupling, fwd_coupling, bwd_coupling, block_inverse):
        local = fwd_coupling.shape
        if (cells, stations) == (8, 4) and local == (1, 48, 48, 1, 128):
            return line_plan(rhs, coupling, fwd_coupling, bwd_coupling, block_inverse)
        return on_device(rhs, coupling, fwd_coupling, bwd_coupling, block_inverse)

    return jax.shard_map(
        on_each,
        mesh=mesh,
        in_specs=(
            P("azim", None, "axial", None),
            P("azim", None, "axial", None),
            P("azim", None, None, "axial", None),
            P("azim", None, None, "axial", None),
            P("azim", None, None, "axial", None),
        ),
        out_specs=(P("azim", None, "axial", None), P("azim", None, "axial", None)),
        check_vma=False,
    )
```

```python
import jax
import jax.numpy as jnp
from jax import lax
from jax.experimental import pallas as pl
from jax.experimental.pallas import tpu as pltpu
from jax.sharding import PartitionSpec as P

highest = lax.Precision.HIGHEST
f32 = jnp.float32
BOTH = ("azim", "axial")
VMEM_LIMIT = 40 * 1024 * 1024


def lane_index():
    return lax.broadcasted_iota(jnp.int32, (8, 128), 1)


def row_index():
    return lax.broadcasted_iota(jnp.int32, (8, 128), 0)


def turn_lanes(tile, steps):
    steps = steps % 128
    return pltpu.roll(tile, steps, 1) if steps else tile


def turn_rows(tile, steps):
    steps = steps % 8
    return pltpu.roll(tile, steps, 0) if steps else tile


def swap_quads(tiles):
    lanes = lane_index()
    tiles = list(tiles)
    for bit, width in ((1, 4), (2, 8)):
        low = (lanes // width) % 2 == 0
        for first in range(4):
            if first & bit:
                continue
            one, two = tiles[first], tiles[first | bit]
            tiles[first] = jnp.where(low, one, turn_lanes(two, width))
            tiles[first | bit] = jnp.where(low, turn_lanes(one, -width), two)
    return tiles


def swap_rows(tile):
    lanes, rows = lane_index() // 16, row_index()
    for bit in (1, 2, 4):
        row_bit, lane_bit = (rows // bit) % 2, (lanes // bit) % 2
        up = turn_rows(turn_lanes(tile, 16 * bit), -bit)
        down = turn_rows(turn_lanes(tile, -16 * bit), bit)
        tile = jnp.where(row_bit == lane_bit, tile, jnp.where(row_bit == 0, up, down))
    return tile


def put_slots(out_ref, tiles, rows, base):
    zero = jnp.zeros((8, 128), f32)
    for half in range(2):
        group = [tiles[4 * half + x] if 4 * half + x < 6 else zero for x in range(4)]
        for quad, tile in enumerate(swap_quads(group)):
            out_ref[pl.ds(rows * quad + base + half, 8, stride=4 * rows), :] = tile


def get_slots(in_ref, rows, base):
    tiles = []
    for half in range(2):
        group = [in_ref[pl.ds(rows * quad + base + half, 8, stride=4 * rows), :] for quad in range(4)]
        tiles += swap_quads(group)
    return tiles[:6]


def put_cell_vector(out_ref, vector_ref, rows, base):
    put_slots(out_ref, [swap_rows(vector_ref[8 * t : 8 * t + 8, :]) for t in range(6)], rows, base)


def inverse_matvec(inverse_ref, vector_ref, out_ref):
    def step(group, totals):
        for inner in range(8):
            a = 8 * group + inner
            row = vector_ref[pl.ds(a, 1), :]
            totals = totals + inverse_ref[a].astype(f32) * row
        return totals

    out_ref[...] = lax.fori_loop(0, 6, step, jnp.zeros((48, 128), f32))


def pack_blocks(block_ref, out_ref):
    quads = lane_index() // 4
    keeps = [(bit, (quads & bit) == 0) for bit in (1, 2, 4, 8, 16)]
    for group in range(9):
        ah_pair, bh_pair = group // 3, group % 3
        items = [None] * 32
        for y in range(2):
            for p in range(8):
                wide = block_ref[16 * ah_pair + 8 * y + p, 16 * bh_pair : 16 * bh_pair + 16, :].astype(f32)
                for h in range(2):
                    i = 4 * p + 2 * y + h
                    items[i] = turn_lanes(turn_rows(wide[8 * h : 8 * h + 8], -p), 4 * i)
        for bit, keep in keeps:
            items = [jnp.where(keep, items[j], items[(j + bit) % 32]) for j in range(32)]
        for e in range(32):
            out_ref[e, 8 * group : 8 * group + 8, :] = turn_lanes(items[-e % 32], -4 * e)


def unpack_cell(in_ref, out_ref, cell):
    for group in range(9):
        parts = [in_ref[4 * cell + k, 8 * group : 8 * group + 8, :] for k in range(4)]
        for x, tile in enumerate(swap_quads(parts)):
            at = 8 * (4 * group + x)
            out_ref[cell, at : at + 8, :] = tile


def tile_at(ah, bh):
    return 4 * (3 * (ah // 2) + bh // 2) + 2 * (ah % 2) + bh % 2


def line_sweep(blocks_ref, const_ref, out_ref, reverse, slots_ref=None):
    order = list(range(8))
    if reverse:
        order = order[::-1]
    state = None
    for turn in range(2):
        for cell in order:
            if turn == 0 and slots_ref is not None:
                unpack_cell(slots_ref, blocks_ref, cell)
            consts = [jnp.broadcast_to(const_ref[t, cell : cell + 1, :], (8, 128)) for t in range(6)]
            if state is None:
                state = consts
                continue
            following = []
            for bh in range(6):
                total = None
                for ah in range(6):
                    at = 8 * tile_at(ah, bh)
                    term = blocks_ref[cell, at : at + 8, :] * state[ah]
                    total = term if total is None else total + term
                total = pltpu.roll(total, 0, 1, stride=16, stride_axis=0)
                for span in (4, 2, 1):
                    total = total + turn_rows(total, span)
                following.append(consts[bh] - total)
            state = following
            if turn == 1:
                for t in range(6):
                    out_ref[t, cell : cell + 1, :] = state[t][0:1]


def stations_sum(tile):
    station = (lane_index() // 4) % 4
    before = jnp.where(station > 0, turn_lanes(tile, 4), 0.0)
    after = jnp.where(station < 3, turn_lanes(tile, -4), 0.0)
    return before + after


def first_send_kernel(
    forward_hbm, inverse_hbm, rhs_hbm, coupling_hbm, out_ref, f_ref, i_ref, rhs_ref, coupling_ref, c_ref, packed_ref, sems
):
    pairs = ((rhs_hbm, rhs_ref), (inverse_hbm, i_ref), (coupling_hbm, coupling_ref), (forward_hbm, f_ref))
    copies = [pltpu.make_async_copy(source, target, sems.at[n]) for n, (source, target) in enumerate(pairs)]
    for copy in copies:
        copy.start()
    for copy in copies[:3]:
        copy.wait()
    inverse_matvec(i_ref, rhs_ref, c_ref)
    for n, vector_ref in enumerate((c_ref, rhs_ref, coupling_ref)):
        put_cell_vector(packed_ref, vector_ref, 8, 2 * n)
    for quad in range(4):
        for last in (6, 7):
            packed_ref[pl.ds(8 * quad + last, 8, stride=32), :] = jnp.zeros((8, 128), f32)
    for e in range(32):
        out_ref[e, 72:80, :] = packed_ref[8 * e : 8 * e + 8, :]
    copies[3].wait()
    pack_blocks(f_ref, out_ref)


def first_forward_kernel(slots_ref, y_ref, blocks_ref, vectors_ref, packed_ref, c_ref):
    for e in range(32):
        packed_ref[8 * e : 8 * e + 8, :] = slots_ref[e, 72:80, :]
    for t, tile in enumerate(get_slots(packed_ref, 8, 0)):
        c_ref[t] = tile
    for n in range(2):
        for t, tile in enumerate(get_slots(packed_ref, 8, 2 + 2 * n)):
            vectors_ref[n, t] = tile
    line_sweep(blocks_ref, c_ref, y_ref, False, slots_ref)


def first_backward_kernel(slots_ref, y_ref, vectors_ref, out_ref, first_ref, middle_ref, blocks_ref):
    line_sweep(blocks_ref, y_ref, first_ref, True, slots_ref)
    middle = []
    for t in range(6):
        first = first_ref[t]
        middle.append(vectors_ref[0, t] - first + vectors_ref[1, t] * stations_sum(first))
        middle_ref[t] = middle[t]
    put_slots(out_ref, middle, 2, 0)


def second_send_kernel(inverse_ref, slots_ref, out_ref, v_ref, c_ref):
    for t, tile in enumerate(get_slots(slots_ref, 2, 0)):
        v_ref[8 * t : 8 * t + 8, :] = swap_rows(tile)
    inverse_matvec(inverse_ref, v_ref, c_ref)
    put_cell_vector(out_ref, c_ref, 2, 0)


def second_kernel(
    slots_ref, forward_ref, backward_ref, first_ref, middle_ref, vectors_ref, out_ref, c_ref, y_ref, second_ref
):
    for t, tile in enumerate(get_slots(slots_ref, 2, 0)):
        c_ref[t] = tile
    line_sweep(forward_ref, c_ref, y_ref, False)
    line_sweep(backward_ref, y_ref, second_ref, True)
    correction, remaining = [], []
    for t in range(6):
        second = second_ref[t]
        correction.append(first_ref[t] + second)
        remaining.append(middle_ref[t] - second + vectors_ref[1, t] * stations_sum(second))
    put_slots(out_ref, correction, 4, 0)
    put_slots(out_ref, remaining, 4, 2)


def last_kernel(slots_ref, correction_ref, remaining_ref):
    for out_ref, base in ((correction_ref, 0), (remaining_ref, 2)):
        for t, tile in enumerate(get_slots(slots_ref, 4, base)):
            out_ref[8 * t : 8 * t + 8, :] = swap_rows(tile)


def shaped(*sizes):
    return jax.ShapeDtypeStruct(sizes, f32)


def call(kernel, outs, scratch=()):
    return pl.pallas_call(
        kernel,
        out_shape=outs,
        scratch_shapes=[pltpu.VMEM(sizes, f32) for sizes in scratch],
        compiler_params=pltpu.CompilerParams(vmem_limit_bytes=VMEM_LIMIT),
    )


def exchange(slots, rows):
    moved = lax.all_to_all(slots.reshape(32, rows, 128), BOTH, 0, 0, tiled=True)
    return moved.reshape(32 * rows, 128)


def line_plan(rhs, coupling, fwd_coupling, bwd_coupling, block_inverse):
    source, coupling_field = rhs.reshape(48, 128), coupling.reshape(48, 128)
    forward_blocks = fwd_coupling.reshape(48, 48, 128)
    backward_blocks = bwd_coupling.reshape(48, 48, 128)
    inverse_blocks = block_inverse.reshape(48, 48, 128)
    tiles, vectors, held = shaped(6, 8, 128), shaped(2, 6, 8, 128), shaped(8, 288, 128)

    slots = pl.pallas_call(
        first_send_kernel,
        out_shape=shaped(32, 80, 128),
        in_specs=[pl.BlockSpec(memory_space=pltpu.HBM)] * 4,
        scratch_shapes=[
            pltpu.VMEM((48, 48, 128), jnp.bfloat16),
            pltpu.VMEM((48, 48, 128), jnp.bfloat16),
            pltpu.VMEM((48, 128), f32),
            pltpu.VMEM((48, 128), f32),
            pltpu.VMEM((48, 128), f32),
            pltpu.VMEM((256, 128), f32),
            pltpu.SemaphoreType.DMA((4,)),
        ],
        compiler_params=pltpu.CompilerParams(vmem_limit_bytes=VMEM_LIMIT),
    )(forward_blocks, inverse_blocks, source, coupling_field)
    slots = lax.all_to_all(slots, BOTH, 0, 0, tiled=True)
    backward_slots = call(pack_blocks, shaped(32, 72, 128))(backward_blocks)
    backward_slots = lax.all_to_all(backward_slots, BOTH, 0, 0, tiled=True)
    y, forward, vectors = call(first_forward_kernel, (tiles, held, vectors), [(256, 128), (6, 8, 128)])(slots)
    slots, first, middle, backward = call(first_backward_kernel, (shaped(64, 128), tiles, tiles, held))(
        backward_slots, y, vectors
    )
    slots = exchange(slots, 2)
    slots = call(second_send_kernel, shaped(64, 128), [(48, 128), (48, 128)])(inverse_blocks, slots)
    slots = exchange(slots, 2)
    slots = call(second_kernel, shaped(128, 128), [(6, 8, 128)] * 3)(slots, forward, backward, first, middle, vectors)
    slots = exchange(slots, 4)
    correction, remaining = call(last_kernel, (shaped(48, 128), shaped(48, 128)))(slots)
    return correction.reshape(rhs.shape), remaining.reshape(rhs.shape)


def from_behind(value, axis, steps):
    count = lax.axis_size(axis)
    initial, last = (max(0, -steps), min(count, count - steps))
    return lax.ppermute(value, axis, [(source, source + steps) for source in range(initial, last)])


def from_root(shard, axis, root):
    mine = lax.axis_index(axis) == root
    return lax.psum(jnp.where(mine, shard, jnp.zeros_like(shard)), axis)


def extended(block, sides, width):
    for axis, dim in sides:
        count = lax.axis_size(axis)
        forward = [(i, i + 1) for i in range(count - 1)]
        backward = [(target, source) for source, target in forward]
        low = lax.ppermute(
            lax.slice_in_dim(block, block.shape[dim] - width, None, axis=dim), axis, forward
        )
        high = lax.ppermute(lax.slice_in_dim(block, 0, width, axis=dim), axis, backward)
        block = jnp.concatenate([low, block, high], axis=dim)
    return block


def cell_stride(one_block, carried, const_term):
    return const_term - jnp.einsum(
        "abl,al->bl", one_block.astype(jnp.float32), carried, precision=highest
    )


def compose_cells(blocks, sequence):
    running = None
    for position in sequence:
        one_block = blocks[position].astype(jnp.float32)
        running = -jnp.swapaxes(one_block, 0, 1)
    return running


def doubling_maps(local_map, reverse):
    size = lax.axis_size("azim")
    index = lax.axis_index("azim")
    levels = []
    current = local_map
    distance = 1
    while distance < size:
        if reverse:
            moved = from_behind(current, "azim", -distance)
            exists = index + distance < size
        else:
            moved = from_behind(current, "azim", distance)
            exists = index >= distance
        levels.append((current, distance))
        current = jnp.where(
            exists, jnp.einsum("bcl,cal->bal", current, moved, precision=highest), current
        )
        distance = distance * 2
    return (levels, current)


def doubling_entries(map_levels, local_offset, reverse):
    levels, final_map = map_levels
    size = lax.axis_size("azim")
    index = lax.axis_index("azim")
    running = local_offset
    for current, distance in levels:
        if reverse:
            moved = from_behind(running, "azim", -distance)
        else:
            moved = from_behind(running, "azim", distance)
        running = jnp.einsum("bcl,cl->bl", current, moved, precision=highest) + running
    if reverse:
        wrapped = from_root(running, "azim", 0)
    else:
        wrapped = from_root(running, "azim", size - 1)
    leaving = jnp.einsum("bcl,cl->bl", final_map, wrapped, precision=highest) + running
    if reverse:
        shifted = from_behind(leaving, "azim", -1)
        first_device = index == size - 1
    else:
        shifted = from_behind(leaving, "azim", 1)
        first_device = index == 0
    return jnp.where(first_device, wrapped, shifted)


def sweep(blocks, consts, map_levels, reverse):
    cell_count = blocks.shape[0]
    sequence = list(range(cell_count))
    if reverse:
        sequence = sequence[::-1]
    carried = jnp.zeros(consts.shape[1:], jnp.float32)
    for position in sequence:
        carried = cell_stride(blocks[position], carried, consts[position])
    local_offset = carried
    incoming_maps = doubling_entries(map_levels, local_offset, reverse)
    outputs = [None] * cell_count
    carried = incoming_maps
    for position in sequence:
        carried = cell_stride(blocks[position], carried, consts[position])
        outputs[position] = carried
    return jnp.stack(outputs)


def on_device(rhs, coupling, fwd_coupling, bwd_coupling, block_inverse):
    cell_count, block_width, _, position_total, radial_count = fwd_coupling.shape
    line_count = position_total * radial_count
    forward_blocks = fwd_coupling.reshape(cell_count, block_width, block_width, line_count)
    backward_blocks = bwd_coupling.reshape(cell_count, block_width, block_width, line_count)
    inverse_blocks = block_inverse.reshape(cell_count, block_width, block_width, line_count)
    source = rhs.reshape(cell_count, block_width, line_count)
    coupling_field = coupling.reshape(cell_count, block_width, line_count)
    forward_map = compose_cells(forward_blocks, list(range(cell_count)))
    backward_map = compose_cells(backward_blocks, list(range(cell_count))[::-1])
    forward_levels = None
    backward_levels = None
    forward_levels = doubling_maps(forward_map, False)
    backward_levels = doubling_maps(backward_map, True)

    def precondition(vector):
        consts = jnp.stack(
            [
                jnp.einsum(
                    "abl,al->bl",
                    inverse_blocks[0].astype(jnp.float32),
                    vector[0],
                    precision=highest,
                )
            ]
        )
        forward = sweep(forward_blocks, consts, forward_levels, False)
        return sweep(backward_blocks, forward, backward_levels, True)

    def stations_sum(field):
        grid = field.reshape(cell_count, block_width, position_total, radial_count)
        padded = extended(grid, (("axial", 2),), 1)
        return (padded[:, :, :-2] + padded[:, :, 2:]).reshape(cell_count, block_width, line_count)

    applied_once = precondition(source)
    middle = source - applied_once + coupling_field * stations_sum(applied_once)
    second = precondition(middle)
    correction = applied_once + second
    remaining = middle - second + coupling_field * stations_sum(second)
    return (correction.reshape(rhs.shape), remaining.reshape(rhs.shape))


def solution(mesh):
    cells, stations = mesh.shape["azim"], mesh.shape["axial"]

    def on_each(rhs, coupling, fwd_coupling, bwd_coupling, block_inverse):
        local = fwd_coupling.shape
        if (cells, stations) == (8, 4) and local == (1, 48, 48, 1, 128):
            return line_plan(rhs, coupling, fwd_coupling, bwd_coupling, block_inverse)
        return on_device(rhs, coupling, fwd_coupling, bwd_coupling, block_inverse)

    return jax.shard_map(
        on_each,
        mesh=mesh,
        in_specs=(
            P("azim", None, "axial", None),
            P("azim", None, "axial", None),
            P("azim", None, None, "axial", None),
            P("azim", None, None, "axial", None),
            P("azim", None, None, "axial", None),
        ),
        out_specs=(P("azim", None, "axial", None), P("azim", None, "axial", None)),
        check_vma=False,
    )
```

```python
import jax
import jax.numpy as jnp
from jax import lax
from jax.experimental import pallas as pl
from jax.experimental.pallas import tpu as pltpu
from jax.sharding import PartitionSpec as P

highest = lax.Precision.HIGHEST
f32 = jnp.float32
BOTH = ("azim", "axial")
VMEM_LIMIT = 40 * 1024 * 1024


def lane_index():
    return lax.broadcasted_iota(jnp.int32, (8, 128), 1)


def row_index():
    return lax.broadcasted_iota(jnp.int32, (8, 128), 0)


def turn_lanes(tile, steps):
    steps = steps % 128
    return pltpu.roll(tile, steps, 1) if steps else tile


def turn_rows(tile, steps):
    steps = steps % 8
    return pltpu.roll(tile, steps, 0) if steps else tile


def swap_quads(tiles):
    lanes = lane_index()
    tiles = list(tiles)
    for bit, width in ((1, 4), (2, 8)):
        low = (lanes // width) % 2 == 0
        for first in range(4):
            if first & bit:
                continue
            one, two = tiles[first], tiles[first | bit]
            tiles[first] = jnp.where(low, one, turn_lanes(two, width))
            tiles[first | bit] = jnp.where(low, turn_lanes(one, -width), two)
    return tiles


def swap_rows(tile):
    lanes, rows = lane_index() // 16, row_index()
    for bit in (1, 2, 4):
        row_bit, lane_bit = (rows // bit) % 2, (lanes // bit) % 2
        up = turn_rows(turn_lanes(tile, 16 * bit), -bit)
        down = turn_rows(turn_lanes(tile, -16 * bit), bit)
        tile = jnp.where(row_bit == lane_bit, tile, jnp.where(row_bit == 0, up, down))
    return tile


def put_slots(out_ref, tiles, rows, base):
    zero = jnp.zeros((8, 128), f32)
    for half in range(2):
        group = [tiles[4 * half + x] if 4 * half + x < 6 else zero for x in range(4)]
        for quad, tile in enumerate(swap_quads(group)):
            out_ref[pl.ds(rows * quad + base + half, 8, stride=4 * rows), :] = tile


def get_slots(in_ref, rows, base):
    tiles = []
    for half in range(2):
        group = [in_ref[pl.ds(rows * quad + base + half, 8, stride=4 * rows), :] for quad in range(4)]
        tiles += swap_quads(group)
    return tiles[:6]


def put_cell_vector(out_ref, vector_ref, rows, base):
    put_slots(out_ref, [swap_rows(vector_ref[8 * t : 8 * t + 8, :]) for t in range(6)], rows, base)


def inverse_matvec(inverse_ref, vector_ref, out_ref):
    def step(group, totals):
        for inner in range(8):
            a = 8 * group + inner
            row = vector_ref[pl.ds(a, 1), :]
            totals = totals + inverse_ref[a].astype(f32) * row
        return totals

    out_ref[...] = lax.fori_loop(0, 6, step, jnp.zeros((48, 128), f32))


def pack_blocks(block_ref, out_ref, base, finish):
    quads = lane_index() // 4
    keeps = [(bit, (quads & bit) == 0) for bit in (1, 2, 4, 8, 16)]
    for group in range(9):
        ah_pair, bh_pair = group // 3, group % 3
        items = [None] * 32
        for y in range(2):
            for p in range(8):
                wide = block_ref[16 * ah_pair + 8 * y + p, 16 * bh_pair : 16 * bh_pair + 16, :].astype(f32)
                for h in range(2):
                    i = 4 * p + 2 * y + h
                    items[i] = turn_lanes(turn_rows(wide[8 * h : 8 * h + 8], -p), 4 * i)
        for bit, keep in keeps:
            items = [jnp.where(keep, items[j], items[(j + bit) % 32]) for j in range(32)]
        for e in range(32):
            out_ref[e, base + 8 * group : base + 8 * group + 8, :] = turn_lanes(items[-e % 32], -4 * e)
        finish(base + 8 * group)


def unpack_cell(in_ref, base, out_ref, cell):
    for group in range(9):
        at = base + 8 * group
        parts = [in_ref[4 * cell + k, at : at + 8, :] for k in range(4)]
        for x, tile in enumerate(swap_quads(parts)):
            at = 8 * (4 * group + x)
            out_ref[cell, at : at + 8, :] = tile


def tile_at(ah, bh):
    return 4 * (3 * (ah // 2) + bh // 2) + 2 * (ah % 2) + bh % 2


def line_sweep(blocks_ref, const_ref, out_ref, reverse, beside=None):
    order = list(range(8))
    if reverse:
        order = order[::-1]
    state = None
    for turn in range(2):
        for n, cell in enumerate(order):
            if beside is not None:
                beside(turn, n)
            consts = [jnp.broadcast_to(const_ref[t, cell : cell + 1, :], (8, 128)) for t in range(6)]
            if state is None:
                state = consts
                continue
            following = []
            for bh in range(6):
                total = None
                for ah in range(6):
                    at = 8 * tile_at(ah, bh)
                    term = blocks_ref[cell, at : at + 8, :] * state[ah]
                    total = term if total is None else total + term
                total = pltpu.roll(total, 0, 1, stride=16, stride_axis=0)
                for span in (4, 2, 1):
                    total = total + turn_rows(total, span)
                following.append(consts[bh] - total)
            state = following
            if turn == 1:
                for t in range(6):
                    out_ref[t, cell : cell + 1, :] = state[t][0:1]


def stations_sum(tile):
    station = (lane_index() // 4) % 4
    before = jnp.where(station > 0, turn_lanes(tile, 4), 0.0)
    after = jnp.where(station < 3, turn_lanes(tile, -4), 0.0)
    return before + after


def first_send_kernel(
    forward_hbm, backward_hbm, inverse_hbm, rhs_hbm, coupling_hbm, out_hbm,
    f_ref, b_ref, i_ref, rhs_ref, coupling_ref, c_ref, vectors_ref, packed_ref, sems, out_sems,
):
    pairs = (
        (rhs_hbm, rhs_ref), (inverse_hbm, i_ref), (coupling_hbm, coupling_ref), (forward_hbm, f_ref), (backward_hbm, b_ref)
    )
    copies = [pltpu.make_async_copy(source, target, sems.at[n]) for n, (source, target) in enumerate(pairs)]
    for copy in copies:
        copy.start()
    leaving = []

    def finish(row):
        there = (slice(None), slice(row, row + 8), slice(None))
        leaving.append(pltpu.make_async_copy(packed_ref.at[there], out_hbm.at[there], out_sems.at[row // 8]))
        leaving[-1].start()

    for copy in copies[:3]:
        copy.wait()
    inverse_matvec(i_ref, rhs_ref, c_ref)
    for n, vector_ref in enumerate((c_ref, rhs_ref, coupling_ref)):
        put_cell_vector(vectors_ref, vector_ref, 8, 2 * n)
    for quad in range(4):
        for last in (6, 7):
            vectors_ref[pl.ds(8 * quad + last, 8, stride=32), :] = jnp.zeros((8, 128), f32)
    for e in range(32):
        packed_ref[e, 144:152, :] = vectors_ref[8 * e : 8 * e + 8, :]
    finish(144)
    copies[3].wait()
    pack_blocks(f_ref, packed_ref, 0, finish)
    copies[4].wait()
    pack_blocks(b_ref, packed_ref, 72, finish)
    for copy in leaving:
        copy.wait()


def first_kernel(
    slots_ref, out_ref, forward_ref, backward_ref, first_ref, middle_ref, coupling_ref, packed_ref, c_ref, y_ref
):
    for e in range(32):
        packed_ref[8 * e : 8 * e + 8, :] = slots_ref[e, 144:152, :]
    for t, tile in enumerate(get_slots(packed_ref, 8, 0)):
        c_ref[t] = tile

    def unpack(turn, n):
        if turn == 0:
            unpack_cell(slots_ref, 0, forward_ref, n)
        else:
            unpack_cell(slots_ref, 72, backward_ref, n)

    line_sweep(forward_ref, c_ref, y_ref, False, unpack)
    line_sweep(backward_ref, y_ref, first_ref, True)
    rhs = get_slots(packed_ref, 8, 2)
    coupling = get_slots(packed_ref, 8, 4)
    middle = []
    for t in range(6):
        first = first_ref[t]
        middle.append(rhs[t] - first + coupling[t] * stations_sum(first))
        middle_ref[t] = middle[t]
        coupling_ref[t] = coupling[t]
    put_slots(out_ref, middle, 2, 0)


def second_send_kernel(inverse_ref, slots_ref, out_ref, v_ref, c_ref):
    for t, tile in enumerate(get_slots(slots_ref, 2, 0)):
        v_ref[8 * t : 8 * t + 8, :] = swap_rows(tile)
    inverse_matvec(inverse_ref, v_ref, c_ref)
    put_cell_vector(out_ref, c_ref, 2, 0)


def second_kernel(
    slots_ref, forward_ref, backward_ref, first_ref, middle_ref, coupling_ref, out_ref, c_ref, y_ref, second_ref
):
    for t, tile in enumerate(get_slots(slots_ref, 2, 0)):
        c_ref[t] = tile
    line_sweep(forward_ref, c_ref, y_ref, False)
    line_sweep(backward_ref, y_ref, second_ref, True)
    correction, remaining = [], []
    for t in range(6):
        second = second_ref[t]
        correction.append(first_ref[t] + second)
        remaining.append(middle_ref[t] - second + coupling_ref[t] * stations_sum(second))
    put_slots(out_ref, correction, 4, 0)
    put_slots(out_ref, remaining, 4, 2)


def last_kernel(slots_ref, correction_ref, remaining_ref):
    for out_ref, base in ((correction_ref, 0), (remaining_ref, 2)):
        for t, tile in enumerate(get_slots(slots_ref, 4, base)):
            out_ref[8 * t : 8 * t + 8, :] = swap_rows(tile)


def shaped(*sizes):
    return jax.ShapeDtypeStruct(sizes, f32)


def call(kernel, outs, scratch=()):
    return pl.pallas_call(
        kernel,
        out_shape=outs,
        scratch_shapes=[pltpu.VMEM(sizes, f32) for sizes in scratch],
        compiler_params=pltpu.CompilerParams(vmem_limit_bytes=VMEM_LIMIT),
    )


def exchange(slots, rows):
    moved = lax.all_to_all(slots.reshape(32, rows, 128), BOTH, 0, 0, tiled=True)
    return moved.reshape(32 * rows, 128)


def line_plan(rhs, coupling, fwd_coupling, bwd_coupling, block_inverse):
    source, coupling_field = rhs.reshape(48, 128), coupling.reshape(48, 128)
    forward_blocks = fwd_coupling.reshape(48, 48, 128)
    backward_blocks = bwd_coupling.reshape(48, 48, 128)
    inverse_blocks = block_inverse.reshape(48, 48, 128)
    tiles, held = shaped(6, 8, 128), shaped(8, 288, 128)
    blocks = pltpu.VMEM((48, 48, 128), jnp.bfloat16)
    vector = pltpu.VMEM((48, 128), f32)

    slots = pl.pallas_call(
        first_send_kernel,
        out_shape=shaped(32, 152, 128),
        in_specs=[pl.BlockSpec(memory_space=pltpu.HBM)] * 5,
        out_specs=pl.BlockSpec(memory_space=pltpu.HBM),
        scratch_shapes=[blocks, blocks, blocks, vector, vector, vector]
        + [
            pltpu.VMEM((256, 128), f32),
            pltpu.VMEM((32, 152, 128), f32),
            pltpu.SemaphoreType.DMA((5,)),
            pltpu.SemaphoreType.DMA((19,)),
        ],
        compiler_params=pltpu.CompilerParams(vmem_limit_bytes=VMEM_LIMIT),
    )(*[
        pltpu.with_memory_space_constraint(array, pltpu.HBM)
        for array in (forward_blocks, backward_blocks, inverse_blocks, source, coupling_field)
    ])
    slots = lax.all_to_all(slots, BOTH, 0, 0, tiled=True)
    slots, forward, backward, first, middle, coupling_lines = call(
        first_kernel, (shaped(64, 128), held, held, tiles, tiles, tiles), [(256, 128), (6, 8, 128), (6, 8, 128)]
    )(slots)
    slots = exchange(slots, 2)
    slots = call(second_send_kernel, shaped(64, 128), [(48, 128), (48, 128)])(inverse_blocks, slots)
    slots = exchange(slots, 2)
    slots = call(second_kernel, shaped(128, 128), [(6, 8, 128)] * 3)(
        slots, forward, backward, first, middle, coupling_lines
    )
    slots = exchange(slots, 4)
    correction, remaining = call(last_kernel, (shaped(48, 128), shaped(48, 128)))(slots)
    return correction.reshape(rhs.shape), remaining.reshape(rhs.shape)


def from_behind(value, axis, steps):
    count = lax.axis_size(axis)
    initial, last = (max(0, -steps), min(count, count - steps))
    return lax.ppermute(value, axis, [(source, source + steps) for source in range(initial, last)])


def from_root(shard, axis, root):
    mine = lax.axis_index(axis) == root
    return lax.psum(jnp.where(mine, shard, jnp.zeros_like(shard)), axis)


def extended(block, sides, width):
    for axis, dim in sides:
        count = lax.axis_size(axis)
        forward = [(i, i + 1) for i in range(count - 1)]
        backward = [(target, source) for source, target in forward]
        low = lax.ppermute(
            lax.slice_in_dim(block, block.shape[dim] - width, None, axis=dim), axis, forward
        )
        high = lax.ppermute(lax.slice_in_dim(block, 0, width, axis=dim), axis, backward)
        block = jnp.concatenate([low, block, high], axis=dim)
    return block


def cell_stride(one_block, carried, const_term):
    return const_term - jnp.einsum(
        "abl,al->bl", one_block.astype(jnp.float32), carried, precision=highest
    )


def compose_cells(blocks, sequence):
    running = None
    for position in sequence:
        one_block = blocks[position].astype(jnp.float32)
        running = -jnp.swapaxes(one_block, 0, 1)
    return running


def doubling_maps(local_map, reverse):
    size = lax.axis_size("azim")
    index = lax.axis_index("azim")
    levels = []
    current = local_map
    distance = 1
    while distance < size:
        if reverse:
            moved = from_behind(current, "azim", -distance)
            exists = index + distance < size
        else:
            moved = from_behind(current, "azim", distance)
            exists = index >= distance
        levels.append((current, distance))
        current = jnp.where(
            exists, jnp.einsum("bcl,cal->bal", current, moved, precision=highest), current
        )
        distance = distance * 2
    return (levels, current)


def doubling_entries(map_levels, local_offset, reverse):
    levels, final_map = map_levels
    size = lax.axis_size("azim")
    index = lax.axis_index("azim")
    running = local_offset
    for current, distance in levels:
        if reverse:
            moved = from_behind(running, "azim", -distance)
        else:
            moved = from_behind(running, "azim", distance)
        running = jnp.einsum("bcl,cl->bl", current, moved, precision=highest) + running
    if reverse:
        wrapped = from_root(running, "azim", 0)
    else:
        wrapped = from_root(running, "azim", size - 1)
    leaving = jnp.einsum("bcl,cl->bl", final_map, wrapped, precision=highest) + running
    if reverse:
        shifted = from_behind(leaving, "azim", -1)
        first_device = index == size - 1
    else:
        shifted = from_behind(leaving, "azim", 1)
        first_device = index == 0
    return jnp.where(first_device, wrapped, shifted)


def sweep(blocks, consts, map_levels, reverse):
    cell_count = blocks.shape[0]
    sequence = list(range(cell_count))
    if reverse:
        sequence = sequence[::-1]
    carried = jnp.zeros(consts.shape[1:], jnp.float32)
    for position in sequence:
        carried = cell_stride(blocks[position], carried, consts[position])
    local_offset = carried
    incoming_maps = doubling_entries(map_levels, local_offset, reverse)
    outputs = [None] * cell_count
    carried = incoming_maps
    for position in sequence:
        carried = cell_stride(blocks[position], carried, consts[position])
        outputs[position] = carried
    return jnp.stack(outputs)


def on_device(rhs, coupling, fwd_coupling, bwd_coupling, block_inverse):
    cell_count, block_width, _, position_total, radial_count = fwd_coupling.shape
    line_count = position_total * radial_count
    forward_blocks = fwd_coupling.reshape(cell_count, block_width, block_width, line_count)
    backward_blocks = bwd_coupling.reshape(cell_count, block_width, block_width, line_count)
    inverse_blocks = block_inverse.reshape(cell_count, block_width, block_width, line_count)
    source = rhs.reshape(cell_count, block_width, line_count)
    coupling_field = coupling.reshape(cell_count, block_width, line_count)
    forward_map = compose_cells(forward_blocks, list(range(cell_count)))
    backward_map = compose_cells(backward_blocks, list(range(cell_count))[::-1])
    forward_levels = None
    backward_levels = None
    forward_levels = doubling_maps(forward_map, False)
    backward_levels = doubling_maps(backward_map, True)

    def precondition(vector):
        consts = jnp.stack(
            [
                jnp.einsum(
                    "abl,al->bl",
                    inverse_blocks[0].astype(jnp.float32),
                    vector[0],
                    precision=highest,
                )
            ]
        )
        forward = sweep(forward_blocks, consts, forward_levels, False)
        return sweep(backward_blocks, forward, backward_levels, True)

    def stations_sum(field):
        grid = field.reshape(cell_count, block_width, position_total, radial_count)
        padded = extended(grid, (("axial", 2),), 1)
        return (padded[:, :, :-2] + padded[:, :, 2:]).reshape(cell_count, block_width, line_count)

    applied_once = precondition(source)
    middle = source - applied_once + coupling_field * stations_sum(applied_once)
    second = precondition(middle)
    correction = applied_once + second
    remaining = middle - second + coupling_field * stations_sum(second)
    return (correction.reshape(rhs.shape), remaining.reshape(rhs.shape))


def solution(mesh):
    cells, stations = mesh.shape["azim"], mesh.shape["axial"]

    def on_each(rhs, coupling, fwd_coupling, bwd_coupling, block_inverse):
        local = fwd_coupling.shape
        if (cells, stations) == (8, 4) and local == (1, 48, 48, 1, 128):
            return line_plan(rhs, coupling, fwd_coupling, bwd_coupling, block_inverse)
        return on_device(rhs, coupling, fwd_coupling, bwd_coupling, block_inverse)

    return jax.shard_map(
        on_each,
        mesh=mesh,
        in_specs=(
            P("azim", None, "axial", None),
            P("azim", None, "axial", None),
            P("azim", None, None, "axial", None),
            P("azim", None, None, "axial", None),
            P("azim", None, None, "axial", None),
        ),
        out_specs=(P("azim", None, "axial", None), P("azim", None, "axial", None)),
        check_vma=False,
    )
```

```python
import functools

import jax
import jax.numpy as jnp
from jax import lax
from jax.experimental import pallas as pl
from jax.experimental.pallas import tpu as pltpu
from jax.sharding import PartitionSpec as P

highest = lax.Precision.HIGHEST
f32 = jnp.float32
BOTH = ("azim", "axial")
VMEM_LIMIT = 40 * 1024 * 1024


def lane_index():
    return lax.broadcasted_iota(jnp.int32, (8, 128), 1)


def row_index():
    return lax.broadcasted_iota(jnp.int32, (8, 128), 0)


def turn_lanes(tile, steps):
    steps = steps % 128
    return pltpu.roll(tile, steps, 1) if steps else tile


def turn_rows(tile, steps):
    steps = steps % 8
    return pltpu.roll(tile, steps, 0) if steps else tile


def swap_quads(tiles):
    lanes = lane_index()
    tiles = list(tiles)
    for bit, width in ((1, 4), (2, 8)):
        low = (lanes // width) % 2 == 0
        for first in range(4):
            if first & bit:
                continue
            one, two = tiles[first], tiles[first | bit]
            tiles[first] = jnp.where(low, one, turn_lanes(two, width))
            tiles[first | bit] = jnp.where(low, turn_lanes(one, -width), two)
    return tiles


def swap_rows(tile):
    lanes, rows = lane_index() // 16, row_index()
    for bit in (1, 2, 4):
        row_bit, lane_bit = (rows // bit) % 2, (lanes // bit) % 2
        up = turn_rows(turn_lanes(tile, 16 * bit), -bit)
        down = turn_rows(turn_lanes(tile, -16 * bit), bit)
        tile = jnp.where(row_bit == lane_bit, tile, jnp.where(row_bit == 0, up, down))
    return tile


def put_slots(out_ref, tiles, rows, base):
    zero = jnp.zeros((8, 128), f32)
    for half in range(2):
        group = [tiles[4 * half + x] if 4 * half + x < 6 else zero for x in range(4)]
        for quad, tile in enumerate(swap_quads(group)):
            out_ref[pl.ds(rows * quad + base + half, 8, stride=4 * rows), :] = tile


def get_slots(in_ref, rows, base):
    tiles = []
    for half in range(2):
        group = [in_ref[pl.ds(rows * quad + base + half, 8, stride=4 * rows), :] for quad in range(4)]
        tiles += swap_quads(group)
    return tiles[:6]


def put_cell_vector(out_ref, vector_ref, rows, base):
    put_slots(out_ref, [swap_rows(vector_ref[8 * t : 8 * t + 8, :]) for t in range(6)], rows, base)


def inverse_matvec(inverse_ref, vector_ref, out_ref):
    def step(group, totals):
        for inner in range(8):
            a = 8 * group + inner
            row = vector_ref[pl.ds(a, 1), :]
            totals = totals + inverse_ref[a].astype(f32) * row
        return totals

    out_ref[...] = lax.fori_loop(0, 6, step, jnp.zeros((48, 128), f32))


def pack_blocks(block_ref, out_ref, base, finish):
    quads = lane_index() // 4
    keeps = [(bit, (quads & bit) == 0) for bit in (1, 2, 4, 8, 16)]
    for group in range(9):
        ah_pair, bh_pair = group // 3, group % 3
        items = [None] * 32
        for y in range(2):
            for p in range(8):
                wide = block_ref[16 * ah_pair + 8 * y + p, 16 * bh_pair : 16 * bh_pair + 16, :].astype(f32)
                for h in range(2):
                    i = 4 * p + 2 * y + h
                    items[i] = turn_lanes(turn_rows(wide[8 * h : 8 * h + 8], -p), 4 * i)
        for bit, keep in keeps:
            items = [jnp.where(keep, items[j], items[(j + bit) % 32]) for j in range(32)]
        for e in range(32):
            out_ref[e, base + 8 * group : base + 8 * group + 8, :] = turn_lanes(items[-e % 32], -4 * e)
        finish(base + 8 * group)


def unpack_cell(in_ref, base, out_ref, cell):
    for group in range(9):
        at = base + 8 * group
        parts = [in_ref[4 * cell + k, at : at + 8, :] for k in range(4)]
        for x, tile in enumerate(swap_quads(parts)):
            at = 8 * (4 * group + x)
            out_ref[cell, at : at + 8, :] = tile


def tile_at(ah, bh):
    return 4 * (3 * (ah // 2) + bh // 2) + 2 * (ah % 2) + bh % 2


def line_sweep(blocks_ref, const_ref, out_ref, reverse, beside=None):
    order = list(range(8))
    if reverse:
        order = order[::-1]
    state = None
    for turn in range(2):
        for n, cell in enumerate(order):
            if beside is not None:
                beside(turn, n)
            consts = [jnp.broadcast_to(const_ref[t, cell : cell + 1, :], (8, 128)) for t in range(6)]
            if state is None:
                state = consts
                continue
            products = line_product(blocks_ref, cell, state)
            state = [const - product for const, product in zip(consts, products)]
            if turn == 1:
                for t in range(6):
                    out_ref[t, cell : cell + 1, :] = state[t][0:1]


def stations_sum(tile):
    station = (lane_index() // 4) % 4
    before = jnp.where(station > 0, turn_lanes(tile, 4), 0.0)
    after = jnp.where(station < 3, turn_lanes(tile, -4), 0.0)
    return before + after


def first_send_kernel(
    forward_hbm, backward_hbm, inverse_hbm, rhs_hbm, coupling_hbm, out_hbm,
    f_ref, b_ref, i_ref, rhs_ref, coupling_ref, c_ref, vectors_ref, packed_ref, sems, out_sems,
):
    pairs = (
        (rhs_hbm, rhs_ref), (inverse_hbm, i_ref), (coupling_hbm, coupling_ref), (forward_hbm, f_ref), (backward_hbm, b_ref)
    )
    copies = [pltpu.make_async_copy(source, target, sems.at[n]) for n, (source, target) in enumerate(pairs)]
    for copy in copies:
        copy.start()
    leaving = []

    def finish(row):
        there = (slice(None), slice(row, row + 8), slice(None))
        leaving.append(pltpu.make_async_copy(packed_ref.at[there], out_hbm.at[there], out_sems.at[row // 8]))
        leaving[-1].start()

    for copy in copies[:3]:
        copy.wait()
    inverse_matvec(i_ref, rhs_ref, c_ref)
    for n, vector_ref in enumerate((c_ref, rhs_ref, coupling_ref)):
        put_cell_vector(vectors_ref, vector_ref, 8, 2 * n)
    for quad in range(4):
        for last in (6, 7):
            vectors_ref[pl.ds(8 * quad + last, 8, stride=32), :] = jnp.zeros((8, 128), f32)
    for e in range(32):
        packed_ref[e, 144:152, :] = vectors_ref[8 * e : 8 * e + 8, :]
    finish(144)
    copies[3].wait()
    pack_blocks(f_ref, packed_ref, 0, finish)
    copies[4].wait()
    pack_blocks(b_ref, packed_ref, 72, finish)
    for copy in leaving:
        copy.wait()


def first_kernel(
    slots_ref, own_ref, other_ref, forward_ref, backward_ref, first_ref, middle_ref, coupling_ref, packed_ref, c_ref, y_ref
):
    for e in range(32):
        packed_ref[8 * e : 8 * e + 8, :] = slots_ref[e, 144:152, :]
    for t, tile in enumerate(get_slots(packed_ref, 8, 0)):
        c_ref[t] = tile

    def unpack(turn, n):
        if turn == 0:
            unpack_cell(slots_ref, 0, forward_ref, n)
        else:
            unpack_cell(slots_ref, 72, backward_ref, n)

    line_sweep(forward_ref, c_ref, y_ref, False, unpack)
    line_sweep(backward_ref, y_ref, first_ref, True)
    rhs = get_slots(packed_ref, 8, 2)
    coupling = get_slots(packed_ref, 8, 4)
    half, _ = half_position()
    for t in range(6):
        first = first_ref[t]
        middle = rhs[t] - first + coupling[t] * stations_sum(first)
        turned = turn_rows(middle, 4)
        other_ref[t] = jnp.where(half == 0, turned, middle)
        own_ref[t] = jnp.where(half == 0, middle, turned)
        middle_ref[t] = middle
        coupling_ref[t] = coupling[t]


def half_position():
    cell = lax.axis_index("azim")
    return cell // 4, (cell % 4) * 4 + lax.axis_index("axial")


def inverse_send_kernel(inverse_hbm, *refs):
    outs, (i_ref, packed_ref, sem, sems) = refs[:16], refs[16:]
    fetch = pltpu.make_async_copy(inverse_hbm, i_ref, sem.at[0])
    fetch.start()
    fetch.wait()
    pack_blocks(i_ref, packed_ref, 0, lambda row: None)
    half, place = half_position()
    copies = []
    for d in range(16):
        target = place ^ d
        for n, source in enumerate((16 * half + target, 16 * (1 - half) + target)):
            copies.append(
                pltpu.make_async_copy(packed_ref.at[source], outs[d].at[pl.ds(72 * n, 72), :], sems.at[2 * d + n])
            )
            copies[-1].start()
    for copy in copies:
        copy.wait()


def inverse_get_kernel(*refs):
    ins, (out_ref, stage_ref, sems) = refs[:16], refs[16:]
    _, place = half_position()
    copies = []
    for d in range(16):
        copies.append(pltpu.make_async_copy(ins[d], stage_ref.at[place ^ d], sems.at[d]))
        copies[-1].start()
    for copy in copies:
        copy.wait()
    for lines in range(2):
        for cell in range(4):
            unpack_cell(stage_ref, 72 * lines, out_ref.at[lines], cell)


def line_product(blocks_ref, cell, state):
    products = []
    for bh in range(6):
        total = None
        for ah in range(6):
            at = 8 * tile_at(ah, bh)
            term = blocks_ref[cell, at : at + 8, :] * state[ah]
            total = term if total is None else total + term
        total = pltpu.roll(total, 0, 1, stride=16, stride_axis=0)
        for span in (4, 2, 1):
            total = total + turn_rows(total, span)
        products.append(total)
    return products


def half_inverse_kernel(lines, vector_ref, blocks_ref, out_ref):
    rows = row_index()
    totals = [jnp.zeros((8, 128), f32)] * 6
    for cell in range(4):
        state = [jnp.broadcast_to(vector_ref[t, cell : cell + 1, :], (8, 128)) for t in range(6)]
        for t, product in enumerate(line_product(blocks_ref.at[lines], cell, state)):
            totals[t] = jnp.where(rows == cell, product, totals[t])
    for t in range(6):
        out_ref[t] = totals[t]


def second_kernel(
    own_ref, other_ref, forward_ref, backward_ref, first_ref, middle_ref, coupling_ref, out_ref, c_ref, y_ref, second_ref
):
    half, _ = half_position()
    low = row_index() < 4
    for t in range(6):
        tile = jnp.where(low, own_ref[t], turn_rows(other_ref[t], 4))
        c_ref[t] = jnp.where(half == 0, tile, turn_rows(tile, 4))
    line_sweep(forward_ref, c_ref, y_ref, False)
    line_sweep(backward_ref, y_ref, second_ref, True)
    correction, remaining = [], []
    for t in range(6):
        second = second_ref[t]
        correction.append(first_ref[t] + second)
        remaining.append(middle_ref[t] - second + coupling_ref[t] * stations_sum(second))
    put_slots(out_ref, correction, 4, 0)
    put_slots(out_ref, remaining, 4, 2)


def last_kernel(slots_ref, correction_ref, remaining_ref):
    for out_ref, base in ((correction_ref, 0), (remaining_ref, 2)):
        for t, tile in enumerate(get_slots(slots_ref, 4, base)):
            out_ref[8 * t : 8 * t + 8, :] = swap_rows(tile)


def shaped(*sizes):
    return jax.ShapeDtypeStruct(sizes, f32)


def call(kernel, outs, scratch=()):
    return pl.pallas_call(
        kernel,
        out_shape=outs,
        scratch_shapes=[pltpu.VMEM(sizes, f32) for sizes in scratch],
        compiler_params=pltpu.CompilerParams(vmem_limit_bytes=VMEM_LIMIT),
    )


def exchange(slots, rows):
    moved = lax.all_to_all(slots.reshape(32, rows, 128), BOTH, 0, 0, tiled=True)
    return moved.reshape(32 * rows, 128)


def line_plan(rhs, coupling, fwd_coupling, bwd_coupling, block_inverse):
    source, coupling_field = rhs.reshape(48, 128), coupling.reshape(48, 128)
    forward_blocks = fwd_coupling.reshape(48, 48, 128)
    backward_blocks = bwd_coupling.reshape(48, 48, 128)
    inverse_blocks = block_inverse.reshape(48, 48, 128)
    tiles, held = shaped(6, 8, 128), shaped(8, 288, 128)
    blocks = pltpu.VMEM((48, 48, 128), jnp.bfloat16)
    vector = pltpu.VMEM((48, 128), f32)

    slots = pl.pallas_call(
        first_send_kernel,
        out_shape=shaped(32, 152, 128),
        in_specs=[pl.BlockSpec(memory_space=pltpu.HBM)] * 5,
        out_specs=pl.BlockSpec(memory_space=pltpu.HBM),
        scratch_shapes=[blocks, blocks, blocks, vector, vector, vector]
        + [
            pltpu.VMEM((256, 128), f32),
            pltpu.VMEM((32, 152, 128), f32),
            pltpu.SemaphoreType.DMA((5,)),
            pltpu.SemaphoreType.DMA((19,)),
        ],
        compiler_params=pltpu.CompilerParams(vmem_limit_bytes=VMEM_LIMIT),
    )(*[
        pltpu.with_memory_space_constraint(array, pltpu.HBM)
        for array in (forward_blocks, backward_blocks, inverse_blocks, source, coupling_field)
    ])
    slots, inverse_blocks = lax.optimization_barrier((slots, inverse_blocks))
    slots = lax.all_to_all(slots, BOTH, 0, 0, tiled=True)

    parts = pl.pallas_call(
        inverse_send_kernel,
        out_shape=[shaped(144, 128)] * 16,
        in_specs=[pl.BlockSpec(memory_space=pltpu.HBM)],
        out_specs=[pl.BlockSpec(memory_space=pltpu.HBM)] * 16,
        scratch_shapes=[
            blocks, pltpu.VMEM((32, 72, 128), f32), pltpu.SemaphoreType.DMA((1,)), pltpu.SemaphoreType.DMA((32,))
        ],
        compiler_params=pltpu.CompilerParams(vmem_limit_bytes=VMEM_LIMIT),
    )(pltpu.with_memory_space_constraint(inverse_blocks, pltpu.HBM))
    parts = [parts[0]] + [
        lax.ppermute(parts[d], BOTH, [(e, e ^ d) for e in range(32)]) for d in range(1, 16)
    ]
    inverse = pl.pallas_call(
        inverse_get_kernel,
        out_shape=shaped(2, 4, 288, 128),
        in_specs=[pl.BlockSpec(memory_space=pltpu.HBM)] * 16,
        scratch_shapes=[pltpu.VMEM((16, 144, 128), f32), pltpu.SemaphoreType.DMA((16,))],
        compiler_params=pltpu.CompilerParams(vmem_limit_bytes=VMEM_LIMIT),
    )(*parts)

    own, other, forward, backward, first, middle, coupling_lines = call(
        first_kernel, (tiles, tiles, held, held, tiles, tiles, tiles), [(256, 128), (6, 8, 128), (6, 8, 128)]
    )(slots)

    def with_partner(vector):
        return lax.ppermute(vector, BOTH, [(e, e ^ 16) for e in range(32)])

    other = with_partner(other)
    own = call(functools.partial(half_inverse_kernel, 0), tiles)(own, inverse)
    other = call(functools.partial(half_inverse_kernel, 1), tiles)(other, inverse)
    other = with_partner(other)
    slots = call(second_kernel, shaped(128, 128), [(6, 8, 128)] * 3)(
        own, other, forward, backward, first, middle, coupling_lines
    )
    slots = exchange(slots, 4)
    correction, remaining = call(last_kernel, (shaped(48, 128), shaped(48, 128)))(slots)
    return correction.reshape(rhs.shape), remaining.reshape(rhs.shape)


def from_behind(value, axis, steps):
    count = lax.axis_size(axis)
    initial, last = (max(0, -steps), min(count, count - steps))
    return lax.ppermute(value, axis, [(source, source + steps) for source in range(initial, last)])


def from_root(shard, axis, root):
    mine = lax.axis_index(axis) == root
    return lax.psum(jnp.where(mine, shard, jnp.zeros_like(shard)), axis)


def extended(block, sides, width):
    for axis, dim in sides:
        count = lax.axis_size(axis)
        forward = [(i, i + 1) for i in range(count - 1)]
        backward = [(target, source) for source, target in forward]
        low = lax.ppermute(
            lax.slice_in_dim(block, block.shape[dim] - width, None, axis=dim), axis, forward
        )
        high = lax.ppermute(lax.slice_in_dim(block, 0, width, axis=dim), axis, backward)
        block = jnp.concatenate([low, block, high], axis=dim)
    return block


def cell_stride(one_block, carried, const_term):
    return const_term - jnp.einsum(
        "abl,al->bl", one_block.astype(jnp.float32), carried, precision=highest
    )


def compose_cells(blocks, sequence):
    running = None
    for position in sequence:
        one_block = blocks[position].astype(jnp.float32)
        running = -jnp.swapaxes(one_block, 0, 1)
    return running


def doubling_maps(local_map, reverse):
    size = lax.axis_size("azim")
    index = lax.axis_index("azim")
    levels = []
    current = local_map
    distance = 1
    while distance < size:
        if reverse:
            moved = from_behind(current, "azim", -distance)
            exists = index + distance < size
        else:
            moved = from_behind(current, "azim", distance)
            exists = index >= distance
        levels.append((current, distance))
        current = jnp.where(
            exists, jnp.einsum("bcl,cal->bal", current, moved, precision=highest), current
        )
        distance = distance * 2
    return (levels, current)


def doubling_entries(map_levels, local_offset, reverse):
    levels, final_map = map_levels
    size = lax.axis_size("azim")
    index = lax.axis_index("azim")
    running = local_offset
    for current, distance in levels:
        if reverse:
            moved = from_behind(running, "azim", -distance)
        else:
            moved = from_behind(running, "azim", distance)
        running = jnp.einsum("bcl,cl->bl", current, moved, precision=highest) + running
    if reverse:
        wrapped = from_root(running, "azim", 0)
    else:
        wrapped = from_root(running, "azim", size - 1)
    leaving = jnp.einsum("bcl,cl->bl", final_map, wrapped, precision=highest) + running
    if reverse:
        shifted = from_behind(leaving, "azim", -1)
        first_device = index == size - 1
    else:
        shifted = from_behind(leaving, "azim", 1)
        first_device = index == 0
    return jnp.where(first_device, wrapped, shifted)


def sweep(blocks, consts, map_levels, reverse):
    cell_count = blocks.shape[0]
    sequence = list(range(cell_count))
    if reverse:
        sequence = sequence[::-1]
    carried = jnp.zeros(consts.shape[1:], jnp.float32)
    for position in sequence:
        carried = cell_stride(blocks[position], carried, consts[position])
    local_offset = carried
    incoming_maps = doubling_entries(map_levels, local_offset, reverse)
    outputs = [None] * cell_count
    carried = incoming_maps
    for position in sequence:
        carried = cell_stride(blocks[position], carried, consts[position])
        outputs[position] = carried
    return jnp.stack(outputs)


def on_device(rhs, coupling, fwd_coupling, bwd_coupling, block_inverse):
    cell_count, block_width, _, position_total, radial_count = fwd_coupling.shape
    line_count = position_total * radial_count
    forward_blocks = fwd_coupling.reshape(cell_count, block_width, block_width, line_count)
    backward_blocks = bwd_coupling.reshape(cell_count, block_width, block_width, line_count)
    inverse_blocks = block_inverse.reshape(cell_count, block_width, block_width, line_count)
    source = rhs.reshape(cell_count, block_width, line_count)
    coupling_field = coupling.reshape(cell_count, block_width, line_count)
    forward_map = compose_cells(forward_blocks, list(range(cell_count)))
    backward_map = compose_cells(backward_blocks, list(range(cell_count))[::-1])
    forward_levels = None
    backward_levels = None
    forward_levels = doubling_maps(forward_map, False)
    backward_levels = doubling_maps(backward_map, True)

    def precondition(vector):
        consts = jnp.stack(
            [
                jnp.einsum(
                    "abl,al->bl",
                    inverse_blocks[0].astype(jnp.float32),
                    vector[0],
                    precision=highest,
                )
            ]
        )
        forward = sweep(forward_blocks, consts, forward_levels, False)
        return sweep(backward_blocks, forward, backward_levels, True)

    def stations_sum(field):
        grid = field.reshape(cell_count, block_width, position_total, radial_count)
        padded = extended(grid, (("axial", 2),), 1)
        return (padded[:, :, :-2] + padded[:, :, 2:]).reshape(cell_count, block_width, line_count)

    applied_once = precondition(source)
    middle = source - applied_once + coupling_field * stations_sum(applied_once)
    second = precondition(middle)
    correction = applied_once + second
    remaining = middle - second + coupling_field * stations_sum(second)
    return (correction.reshape(rhs.shape), remaining.reshape(rhs.shape))


def solution(mesh):
    cells, stations = mesh.shape["azim"], mesh.shape["axial"]

    def on_each(rhs, coupling, fwd_coupling, bwd_coupling, block_inverse):
        local = fwd_coupling.shape
        if (cells, stations) == (8, 4) and local == (1, 48, 48, 1, 128):
            return line_plan(rhs, coupling, fwd_coupling, bwd_coupling, block_inverse)
        return on_device(rhs, coupling, fwd_coupling, bwd_coupling, block_inverse)

    return jax.shard_map(
        on_each,
        mesh=mesh,
        in_specs=(
            P("azim", None, "axial", None),
            P("azim", None, "axial", None),
            P("azim", None, None, "axial", None),
            P("azim", None, None, "axial", None),
            P("azim", None, None, "axial", None),
        ),
        out_specs=(P("azim", None, "axial", None), P("azim", None, "axial", None)),
        check_vma=False,
    )
```

```python
import functools

import jax
import jax.numpy as jnp
from jax import lax
from jax.experimental import pallas as pl
from jax.experimental.pallas import tpu as pltpu
from jax.sharding import PartitionSpec as P

highest = lax.Precision.HIGHEST
f32 = jnp.float32
BOTH = ("azim", "axial")
VMEM_LIMIT = 40 * 1024 * 1024


def lane_index():
    return lax.broadcasted_iota(jnp.int32, (8, 128), 1)


def row_index():
    return lax.broadcasted_iota(jnp.int32, (8, 128), 0)


def turn_lanes(tile, steps):
    steps = steps % 128
    return pltpu.roll(tile, steps, 1) if steps else tile


def turn_rows(tile, steps):
    steps = steps % 8
    return pltpu.roll(tile, steps, 0) if steps else tile


def swap_quads(tiles):
    lanes = lane_index()
    tiles = list(tiles)
    for bit, width in ((1, 4), (2, 8)):
        low = (lanes // width) % 2 == 0
        for first in range(4):
            if first & bit:
                continue
            one, two = tiles[first], tiles[first | bit]
            tiles[first] = jnp.where(low, one, turn_lanes(two, width))
            tiles[first | bit] = jnp.where(low, turn_lanes(one, -width), two)
    return tiles


def swap_rows(tile):
    lanes, rows = lane_index() // 16, row_index()
    for bit in (1, 2, 4):
        row_bit, lane_bit = (rows // bit) % 2, (lanes // bit) % 2
        up = turn_rows(turn_lanes(tile, 16 * bit), -bit)
        down = turn_rows(turn_lanes(tile, -16 * bit), bit)
        tile = jnp.where(row_bit == lane_bit, tile, jnp.where(row_bit == 0, up, down))
    return tile


def put_slots(out_ref, tiles, rows, base):
    zero = jnp.zeros((8, 128), f32)
    for half in range(2):
        group = [tiles[4 * half + x] if 4 * half + x < 6 else zero for x in range(4)]
        for quad, tile in enumerate(swap_quads(group)):
            out_ref[pl.ds(rows * quad + base + half, 8, stride=4 * rows), :] = tile


def get_slots(in_ref, rows, base):
    tiles = []
    for half in range(2):
        group = [in_ref[pl.ds(rows * quad + base + half, 8, stride=4 * rows), :] for quad in range(4)]
        tiles += swap_quads(group)
    return tiles[:6]


def put_cell_vector(out_ref, vector_ref, rows, base):
    put_slots(out_ref, [swap_rows(vector_ref[8 * t : 8 * t + 8, :]) for t in range(6)], rows, base)


def inverse_matvec(inverse_ref, vector_ref, out_ref):
    def step(group, totals):
        for inner in range(8):
            a = 8 * group + inner
            row = vector_ref[pl.ds(a, 1), :]
            totals = totals + inverse_ref[a].astype(f32) * row
        return totals

    out_ref[...] = lax.fori_loop(0, 6, step, jnp.zeros((48, 128), f32))


def pack_blocks(block_ref, out_ref, base, fetches, finish):
    quads = lane_index() // 4
    keeps = [(bit, (quads & bit) == 0) for bit in (1, 2, 4, 8, 16)]
    for group in range(9):
        ah_pair, bh_pair = group // 3, group % 3
        if bh_pair == 0:
            fetches[ah_pair].wait()
        items = [None] * 32
        for y in range(2):
            for p in range(8):
                wide = block_ref[16 * ah_pair + 8 * y + p, 16 * bh_pair : 16 * bh_pair + 16, :].astype(f32)
                for h in range(2):
                    i = 4 * p + 2 * y + h
                    items[i] = turn_lanes(turn_rows(wide[8 * h : 8 * h + 8], -p), 4 * i)
        for bit, keep in keeps:
            items = [jnp.where(keep, items[j], items[(j + bit) % 32]) for j in range(32)]
        for e in range(32):
            out_ref[e, base + 8 * group : base + 8 * group + 8, :] = turn_lanes(items[-e % 32], -4 * e)
        finish(base + 8 * group)


def fetch_thirds(block_hbm, block_ref, sems):
    copies = []
    for third in range(3):
        there = (slice(16 * third, 16 * third + 16), slice(None), slice(None))
        copies.append(pltpu.make_async_copy(block_hbm.at[there], block_ref.at[there], sems.at[third]))
    return copies


def unpack_cell(in_ref, base, out_ref, cell):
    for group in range(9):
        at = base + 8 * group
        parts = [in_ref[4 * cell + k, at : at + 8, :] for k in range(4)]
        for x, tile in enumerate(swap_quads(parts)):
            at = 8 * (4 * group + x)
            out_ref[cell, at : at + 8, :] = tile


def tile_at(ah, bh):
    return 4 * (3 * (ah // 2) + bh // 2) + 2 * (ah % 2) + bh % 2


def line_sweep(blocks_ref, const_ref, out_ref, reverse, beside=None):
    order = list(range(8))
    if reverse:
        order = order[::-1]
    state = None
    for turn in range(2):
        for n, cell in enumerate(order):
            if beside is not None:
                beside(turn, n)
            consts = [jnp.broadcast_to(const_ref[t, cell : cell + 1, :], (8, 128)) for t in range(6)]
            if state is None:
                state = consts
                continue
            products = line_product(blocks_ref, cell, state)
            state = [const - product for const, product in zip(consts, products)]
            if turn == 1:
                for t in range(6):
                    out_ref[t, cell : cell + 1, :] = state[t][0:1]


def stations_sum(tile):
    station = (lane_index() // 4) % 4
    before = jnp.where(station > 0, turn_lanes(tile, 4), 0.0)
    after = jnp.where(station < 3, turn_lanes(tile, -4), 0.0)
    return before + after


def first_send_kernel(
    forward_hbm, backward_hbm, inverse_hbm, rhs_hbm, coupling_hbm, out_hbm,
    f_ref, b_ref, i_ref, rhs_ref, coupling_ref, c_ref, vectors_ref, packed_ref, sems, out_sems,
):
    forward = fetch_thirds(forward_hbm, f_ref, sems.at[0])
    inverse = fetch_thirds(inverse_hbm, i_ref, sems.at[1])
    backward = fetch_thirds(backward_hbm, b_ref, sems.at[2])
    vectors = [
        pltpu.make_async_copy(source, target, sems.at[3, n])
        for n, (source, target) in enumerate(((rhs_hbm, rhs_ref), (coupling_hbm, coupling_ref)))
    ]
    for copy in forward + vectors + inverse + backward:
        copy.start()
    leaving = []

    def finish(row):
        there = (slice(None), slice(row, row + 8), slice(None))
        leaving.append(pltpu.make_async_copy(packed_ref.at[there], out_hbm.at[there], out_sems.at[row // 8]))
        leaving[-1].start()

    pack_blocks(f_ref, packed_ref, 0, forward, finish)
    for copy in vectors + inverse:
        copy.wait()
    inverse_matvec(i_ref, rhs_ref, c_ref)
    for n, vector_ref in enumerate((c_ref, rhs_ref, coupling_ref)):
        put_cell_vector(vectors_ref, vector_ref, 8, 2 * n)
    for quad in range(4):
        for last in (6, 7):
            vectors_ref[pl.ds(8 * quad + last, 8, stride=32), :] = jnp.zeros((8, 128), f32)
    for e in range(32):
        packed_ref[e, 144:152, :] = vectors_ref[8 * e : 8 * e + 8, :]
    finish(144)
    pack_blocks(b_ref, packed_ref, 72, backward, finish)
    for copy in leaving:
        copy.wait()


def first_kernel(
    slots_ref, own_ref, other_ref, forward_ref, backward_ref, first_ref, middle_ref, coupling_ref, packed_ref, c_ref, y_ref
):
    for e in range(32):
        packed_ref[8 * e : 8 * e + 8, :] = slots_ref[e, 144:152, :]
    for t, tile in enumerate(get_slots(packed_ref, 8, 0)):
        c_ref[t] = tile

    def unpack(turn, n):
        if turn == 0:
            unpack_cell(slots_ref, 0, forward_ref, n)
        else:
            unpack_cell(slots_ref, 72, backward_ref, n)

    line_sweep(forward_ref, c_ref, y_ref, False, unpack)
    line_sweep(backward_ref, y_ref, first_ref, True)
    rhs = get_slots(packed_ref, 8, 2)
    coupling = get_slots(packed_ref, 8, 4)
    half, _ = half_position()
    for t in range(6):
        first = first_ref[t]
        middle = rhs[t] - first + coupling[t] * stations_sum(first)
        turned = turn_rows(middle, 4)
        other_ref[t] = jnp.where(half == 0, turned, middle)
        own_ref[t] = jnp.where(half == 0, middle, turned)
        middle_ref[t] = middle
        coupling_ref[t] = coupling[t]


def half_position():
    cell = lax.axis_index("azim")
    return cell // 4, (cell % 4) * 4 + lax.axis_index("axial")


def inverse_send_kernel(inverse_hbm, *refs):
    outs, (i_ref, packed_ref, fetch_sems, sems) = refs[:16], refs[16:]
    fetches = fetch_thirds(inverse_hbm, i_ref, fetch_sems)
    for copy in fetches:
        copy.start()
    pack_blocks(i_ref, packed_ref, 0, fetches, lambda row: None)
    half, place = half_position()
    copies = []
    for d in range(16):
        target = place ^ d
        for n, source in enumerate((16 * half + target, 16 * (1 - half) + target)):
            copies.append(
                pltpu.make_async_copy(packed_ref.at[source], outs[d].at[pl.ds(72 * n, 72), :], sems.at[2 * d + n])
            )
            copies[-1].start()
    for copy in copies:
        copy.wait()


def inverse_get_kernel(*refs):
    ins, out_ref = refs[3::-1], refs[4]
    for lines in range(2):
        for group in range(9):
            at = 72 * lines + 8 * group
            for x, tile in enumerate(swap_quads([part[at : at + 8, :] for part in ins])):
                at = 8 * (4 * group + x)
                out_ref[lines, at : at + 8, :] = tile


def turn_stations(tile, number):
    lanes = lane_index()
    for bit, width in ((1, 4), (2, 8)):
        other = jnp.where((lanes & width) == 0, turn_lanes(tile, -width), turn_lanes(tile, width))
        tile = jnp.where((number & bit) == 0, tile, other)
    return tile


def line_product(blocks_ref, cell, state):
    products = []
    for bh in range(6):
        total = None
        for ah in range(6):
            at = 8 * tile_at(ah, bh)
            term = blocks_ref[cell, at : at + 8, :] * state[ah]
            total = term if total is None else total + term
        total = pltpu.roll(total, 0, 1, stride=16, stride_axis=0)
        for span in (4, 2, 1):
            total = total + turn_rows(total, span)
        products.append(total)
    return products


def half_inverse_kernel(lines, vector_ref, *refs):
    blocks, (out_ref, turned_ref) = refs[:4], refs[4:]
    _, place = half_position()
    cell, station = place // 4, place % 4
    for t in range(6):
        turned_ref[t] = turn_stations(vector_ref[t], station)
    rows = row_index()
    totals = [jnp.zeros((8, 128), f32)] * 6
    for n in range(4):
        state = [jnp.broadcast_to(turned_ref[t, pl.ds(cell ^ n, 1), :], (8, 128)) for t in range(6)]
        for t, product in enumerate(line_product(blocks[n], lines, state)):
            totals[t] = jnp.where(rows == (cell ^ n), product, totals[t])
    for t in range(6):
        out_ref[t] = turn_stations(totals[t], station)


def second_kernel(
    own_ref, other_ref, forward_ref, backward_ref, first_ref, middle_ref, coupling_ref, out_ref, c_ref, y_ref, second_ref
):
    half, _ = half_position()
    low = row_index() < 4
    for t in range(6):
        tile = jnp.where(low, own_ref[t], turn_rows(other_ref[t], 4))
        c_ref[t] = jnp.where(half == 0, tile, turn_rows(tile, 4))
    line_sweep(forward_ref, c_ref, y_ref, False)
    line_sweep(backward_ref, y_ref, second_ref, True)
    correction, remaining = [], []
    for t in range(6):
        second = second_ref[t]
        correction.append(first_ref[t] + second)
        remaining.append(middle_ref[t] - second + coupling_ref[t] * stations_sum(second))
    put_slots(out_ref, correction, 4, 0)
    put_slots(out_ref, remaining, 4, 2)


def last_kernel(slots_ref, correction_ref, remaining_ref):
    for out_ref, base in ((correction_ref, 0), (remaining_ref, 2)):
        for t, tile in enumerate(get_slots(slots_ref, 4, base)):
            out_ref[8 * t : 8 * t + 8, :] = swap_rows(tile)


def shaped(*sizes):
    return jax.ShapeDtypeStruct(sizes, f32)


def call(kernel, outs, scratch=()):
    return pl.pallas_call(
        kernel,
        out_shape=outs,
        scratch_shapes=[pltpu.VMEM(sizes, f32) for sizes in scratch],
        compiler_params=pltpu.CompilerParams(vmem_limit_bytes=VMEM_LIMIT),
    )


def exchange(slots, rows):
    moved = lax.all_to_all(slots.reshape(32, rows, 128), BOTH, 0, 0, tiled=True)
    return moved.reshape(32 * rows, 128)


def line_plan(rhs, coupling, fwd_coupling, bwd_coupling, block_inverse):
    source, coupling_field = rhs.reshape(48, 128), coupling.reshape(48, 128)
    forward_blocks = fwd_coupling.reshape(48, 48, 128)
    backward_blocks = bwd_coupling.reshape(48, 48, 128)
    inverse_blocks = block_inverse.reshape(48, 48, 128)
    tiles, held = shaped(6, 8, 128), shaped(8, 288, 128)
    blocks = pltpu.VMEM((48, 48, 128), jnp.bfloat16)
    vector = pltpu.VMEM((48, 128), f32)

    slots = pl.pallas_call(
        first_send_kernel,
        out_shape=pltpu.HBM((32, 152, 128), f32),
        in_specs=[pl.BlockSpec(memory_space=pltpu.HBM)] * 5,
        out_specs=pl.BlockSpec(memory_space=pltpu.HBM),
        scratch_shapes=[blocks, blocks, blocks, vector, vector, vector]
        + [
            pltpu.VMEM((256, 128), f32),
            pltpu.VMEM((32, 152, 128), f32),
            pltpu.SemaphoreType.DMA((4, 3)),
            pltpu.SemaphoreType.DMA((19,)),
        ],
        compiler_params=pltpu.CompilerParams(vmem_limit_bytes=VMEM_LIMIT),
    )(*[
        pltpu.with_memory_space_constraint(array, pltpu.HBM)
        for array in (forward_blocks, backward_blocks, inverse_blocks, source, coupling_field)
    ])
    slots, inverse_blocks = lax.optimization_barrier((slots, inverse_blocks))
    slots = lax.all_to_all(slots, BOTH, 0, 0, tiled=True)

    parts = pl.pallas_call(
        inverse_send_kernel,
        out_shape=[shaped(144, 128)] * 16,
        in_specs=[pl.BlockSpec(memory_space=pltpu.HBM)],
        out_specs=[pl.BlockSpec(memory_space=pltpu.HBM)] * 16,
        scratch_shapes=[
            blocks, pltpu.VMEM((32, 72, 128), f32), pltpu.SemaphoreType.DMA((3,)), pltpu.SemaphoreType.DMA((32,))
        ],
        compiler_params=pltpu.CompilerParams(vmem_limit_bytes=VMEM_LIMIT),
    )(pltpu.with_memory_space_constraint(inverse_blocks, pltpu.HBM))
    parts = [
        parts[d] if d == 0 else lax.ppermute(parts[d], BOTH, [(e, e ^ d) for e in range(32)]) for d in range(15, -1, -1)
    ][::-1]
    inverse = [call(inverse_get_kernel, shaped(2, 288, 128))(*parts[4 * n : 4 * n + 4][::-1]) for n in (3, 2, 1, 0)]
    *inverse, slots = lax.optimization_barrier((*inverse, slots))
    inverse = inverse[::-1]

    own, other, forward, backward, first, middle, coupling_lines = call(
        first_kernel, (tiles, tiles, held, held, tiles, tiles, tiles), [(256, 128), (6, 8, 128), (6, 8, 128)]
    )(slots)

    def with_partner(vector):
        return lax.ppermute(vector, BOTH, [(e, e ^ 16) for e in range(32)])

    other = with_partner(other)
    own = call(functools.partial(half_inverse_kernel, 0), tiles, [(6, 8, 128)])(own, *inverse)
    other = call(functools.partial(half_inverse_kernel, 1), tiles, [(6, 8, 128)])(other, *inverse)
    other = with_partner(other)
    slots = call(second_kernel, shaped(128, 128), [(6, 8, 128)] * 3)(
        own, other, forward, backward, first, middle, coupling_lines
    )
    slots = exchange(slots, 4)
    correction, remaining = call(last_kernel, (shaped(48, 128), shaped(48, 128)))(slots)
    return correction.reshape(rhs.shape), remaining.reshape(rhs.shape)


def from_behind(value, axis, steps):
    count = lax.axis_size(axis)
    initial, last = (max(0, -steps), min(count, count - steps))
    return lax.ppermute(value, axis, [(source, source + steps) for source in range(initial, last)])


def from_root(shard, axis, root):
    mine = lax.axis_index(axis) == root
    return lax.psum(jnp.where(mine, shard, jnp.zeros_like(shard)), axis)


def extended(block, sides, width):
    for axis, dim in sides:
        count = lax.axis_size(axis)
        forward = [(i, i + 1) for i in range(count - 1)]
        backward = [(target, source) for source, target in forward]
        low = lax.ppermute(
            lax.slice_in_dim(block, block.shape[dim] - width, None, axis=dim), axis, forward
        )
        high = lax.ppermute(lax.slice_in_dim(block, 0, width, axis=dim), axis, backward)
        block = jnp.concatenate([low, block, high], axis=dim)
    return block


def cell_stride(one_block, carried, const_term):
    return const_term - jnp.einsum(
        "abl,al->bl", one_block.astype(jnp.float32), carried, precision=highest
    )


def compose_cells(blocks, sequence):
    running = None
    for position in sequence:
        one_block = blocks[position].astype(jnp.float32)
        running = -jnp.swapaxes(one_block, 0, 1)
    return running


def doubling_maps(local_map, reverse):
    size = lax.axis_size("azim")
    index = lax.axis_index("azim")
    levels = []
    current = local_map
    distance = 1
    while distance < size:
        if reverse:
            moved = from_behind(current, "azim", -distance)
            exists = index + distance < size
        else:
            moved = from_behind(current, "azim", distance)
            exists = index >= distance
        levels.append((current, distance))
        current = jnp.where(
            exists, jnp.einsum("bcl,cal->bal", current, moved, precision=highest), current
        )
        distance = distance * 2
    return (levels, current)


def doubling_entries(map_levels, local_offset, reverse):
    levels, final_map = map_levels
    size = lax.axis_size("azim")
    index = lax.axis_index("azim")
    running = local_offset
    for current, distance in levels:
        if reverse:
            moved = from_behind(running, "azim", -distance)
        else:
            moved = from_behind(running, "azim", distance)
        running = jnp.einsum("bcl,cl->bl", current, moved, precision=highest) + running
    if reverse:
        wrapped = from_root(running, "azim", 0)
    else:
        wrapped = from_root(running, "azim", size - 1)
    leaving = jnp.einsum("bcl,cl->bl", final_map, wrapped, precision=highest) + running
    if reverse:
        shifted = from_behind(leaving, "azim", -1)
        first_device = index == size - 1
    else:
        shifted = from_behind(leaving, "azim", 1)
        first_device = index == 0
    return jnp.where(first_device, wrapped, shifted)


def sweep(blocks, consts, map_levels, reverse):
    cell_count = blocks.shape[0]
    sequence = list(range(cell_count))
    if reverse:
        sequence = sequence[::-1]
    carried = jnp.zeros(consts.shape[1:], jnp.float32)
    for position in sequence:
        carried = cell_stride(blocks[position], carried, consts[position])
    local_offset = carried
    incoming_maps = doubling_entries(map_levels, local_offset, reverse)
    outputs = [None] * cell_count
    carried = incoming_maps
    for position in sequence:
        carried = cell_stride(blocks[position], carried, consts[position])
        outputs[position] = carried
    return jnp.stack(outputs)


def on_device(rhs, coupling, fwd_coupling, bwd_coupling, block_inverse):
    cell_count, block_width, _, position_total, radial_count = fwd_coupling.shape
    line_count = position_total * radial_count
    forward_blocks = fwd_coupling.reshape(cell_count, block_width, block_width, line_count)
    backward_blocks = bwd_coupling.reshape(cell_count, block_width, block_width, line_count)
    inverse_blocks = block_inverse.reshape(cell_count, block_width, block_width, line_count)
    source = rhs.reshape(cell_count, block_width, line_count)
    coupling_field = coupling.reshape(cell_count, block_width, line_count)
    forward_map = compose_cells(forward_blocks, list(range(cell_count)))
    backward_map = compose_cells(backward_blocks, list(range(cell_count))[::-1])
    forward_levels = None
    backward_levels = None
    forward_levels = doubling_maps(forward_map, False)
    backward_levels = doubling_maps(backward_map, True)

    def precondition(vector):
        consts = jnp.stack(
            [
                jnp.einsum(
                    "abl,al->bl",
                    inverse_blocks[0].astype(jnp.float32),
                    vector[0],
                    precision=highest,
                )
            ]
        )
        forward = sweep(forward_blocks, consts, forward_levels, False)
        return sweep(backward_blocks, forward, backward_levels, True)

    def stations_sum(field):
        grid = field.reshape(cell_count, block_width, position_total, radial_count)
        padded = extended(grid, (("axial", 2),), 1)
        return (padded[:, :, :-2] + padded[:, :, 2:]).reshape(cell_count, block_width, line_count)

    applied_once = precondition(source)
    middle = source - applied_once + coupling_field * stations_sum(applied_once)
    second = precondition(middle)
    correction = applied_once + second
    remaining = middle - second + coupling_field * stations_sum(second)
    return (correction.reshape(rhs.shape), remaining.reshape(rhs.shape))


def solution(mesh):
    cells, stations = mesh.shape["azim"], mesh.shape["axial"]

    def on_each(rhs, coupling, fwd_coupling, bwd_coupling, block_inverse):
        local = fwd_coupling.shape
        if (cells, stations) == (8, 4) and local == (1, 48, 48, 1, 128):
            return line_plan(rhs, coupling, fwd_coupling, bwd_coupling, block_inverse)
        return on_device(rhs, coupling, fwd_coupling, bwd_coupling, block_inverse)

    return jax.shard_map(
        on_each,
        mesh=mesh,
        in_specs=(
            P("azim", None, "axial", None),
            P("azim", None, "axial", None),
            P("azim", None, None, "axial", None),
            P("azim", None, None, "axial", None),
            P("azim", None, None, "axial", None),
        ),
        out_specs=(P("azim", None, "axial", None), P("azim", None, "axial", None)),
        check_vma=False,
    )
```

```python
import functools

import jax
import jax.numpy as jnp
from jax import lax
from jax.experimental import pallas as pl
from jax.experimental.pallas import tpu as pltpu
from jax.sharding import PartitionSpec as P

highest = lax.Precision.HIGHEST
f32 = jnp.float32
BOTH = ("azim", "axial")
VMEM_LIMIT = 40 * 1024 * 1024


def lane_index():
    return lax.broadcasted_iota(jnp.int32, (8, 128), 1)


def row_index():
    return lax.broadcasted_iota(jnp.int32, (8, 128), 0)


def turn_lanes(tile, steps):
    steps = steps % 128
    return pltpu.roll(tile, steps, 1) if steps else tile


def turn_rows(tile, steps):
    steps = steps % 8
    return pltpu.roll(tile, steps, 0) if steps else tile


def swap_quads(tiles):
    lanes = lane_index()
    tiles = list(tiles)
    for bit, width in ((1, 4), (2, 8)):
        low = (lanes // width) % 2 == 0
        for first in range(4):
            if first & bit:
                continue
            one, two = tiles[first], tiles[first | bit]
            tiles[first] = jnp.where(low, one, turn_lanes(two, width))
            tiles[first | bit] = jnp.where(low, turn_lanes(one, -width), two)
    return tiles


def swap_rows(tile):
    lanes, rows = lane_index() // 16, row_index()
    for bit in (1, 2, 4):
        row_bit, lane_bit = (rows // bit) % 2, (lanes // bit) % 2
        up = turn_rows(turn_lanes(tile, 16 * bit), -bit)
        down = turn_rows(turn_lanes(tile, -16 * bit), bit)
        tile = jnp.where(row_bit == lane_bit, tile, jnp.where(row_bit == 0, up, down))
    return tile


def put_slots(out_ref, tiles, rows, base):
    zero = jnp.zeros((8, 128), f32)
    for half in range(2):
        group = [tiles[4 * half + x] if 4 * half + x < 6 else zero for x in range(4)]
        for quad, tile in enumerate(swap_quads(group)):
            out_ref[pl.ds(rows * quad + base + half, 8, stride=4 * rows), :] = tile


def get_slots(in_ref, rows, base):
    tiles = []
    for half in range(2):
        group = [in_ref[pl.ds(rows * quad + base + half, 8, stride=4 * rows), :] for quad in range(4)]
        tiles += swap_quads(group)
    return tiles[:6]


def put_cell_vector(out_ref, vector_ref, rows, base):
    put_slots(out_ref, [swap_rows(vector_ref[8 * t : 8 * t + 8, :]) for t in range(6)], rows, base)


def inverse_matvec(inverse_ref, vector_ref, out_ref):
    def step(group, totals):
        for inner in range(8):
            a = 8 * group + inner
            row = vector_ref[pl.ds(a, 1), :]
            totals = totals + inverse_ref[a].astype(f32) * row
        return totals

    out_ref[...] = lax.fori_loop(0, 6, step, jnp.zeros((48, 128), f32))


def pack_blocks(block_ref, out_ref, base, fetches, finish):
    quads = lane_index() // 4
    keeps = [(bit, (quads & bit) == 0) for bit in (1, 2, 4, 8, 16)]
    for group in range(9):
        ah_pair, bh_pair = group // 3, group % 3
        if bh_pair == 0:
            fetches[ah_pair].wait()
        items = [None] * 32
        for y in range(2):
            for p in range(8):
                wide = block_ref[16 * ah_pair + 8 * y + p, 16 * bh_pair : 16 * bh_pair + 16, :].astype(f32)
                for h in range(2):
                    i = 4 * p + 2 * y + h
                    items[i] = turn_lanes(turn_rows(wide[8 * h : 8 * h + 8], -p), 4 * i)
        for bit, keep in keeps:
            items = [jnp.where(keep, items[j], items[(j + bit) % 32]) for j in range(32)]
        for e in range(32):
            out_ref[e, base + 8 * group : base + 8 * group + 8, :] = turn_lanes(items[-e % 32], -4 * e)
        finish(base + 8 * group)


def fetch_thirds(block_hbm, block_ref, sems):
    copies = []
    for third in range(3):
        there = (slice(16 * third, 16 * third + 16), slice(None), slice(None))
        copies.append(pltpu.make_async_copy(block_hbm.at[there], block_ref.at[there], sems.at[third]))
    return copies


def unpack_cell(in_ref, base, out_ref, cell):
    for group in range(9):
        at = base + 8 * group
        parts = [in_ref[4 * cell + k, at : at + 8, :] for k in range(4)]
        for x, tile in enumerate(swap_quads(parts)):
            at = 8 * (4 * group + x)
            out_ref[cell, at : at + 8, :] = tile


def tile_at(ah, bh):
    return 4 * (3 * (ah // 2) + bh // 2) + 2 * (ah % 2) + bh % 2


def line_sweep(blocks_ref, const_ref, out_ref, reverse, beside=None):
    order = list(range(8))
    if reverse:
        order = order[::-1]
    state = None
    for turn in range(2):
        for n, cell in enumerate(order):
            if beside is not None:
                beside(turn, n)
            consts = [jnp.broadcast_to(const_ref[t, cell : cell + 1, :], (8, 128)) for t in range(6)]
            if state is None:
                state = consts
                continue
            products = line_product(blocks_ref, cell, state)
            state = [const - product for const, product in zip(consts, products)]
            if turn == 1:
                for t in range(6):
                    out_ref[t, cell : cell + 1, :] = state[t][0:1]


def stations_sum(tile):
    station = (lane_index() // 4) % 4
    before = jnp.where(station > 0, turn_lanes(tile, 4), 0.0)
    after = jnp.where(station < 3, turn_lanes(tile, -4), 0.0)
    return before + after


def first_send_kernel(
    forward_hbm, backward_hbm, inverse_hbm, rhs_hbm, coupling_hbm, out_hbm,
    f_ref, b_ref, i_ref, rhs_ref, coupling_ref, c_ref, vectors_ref, packed_ref, sems, out_sems,
):
    forward = fetch_thirds(forward_hbm, f_ref, sems.at[0])
    inverse = fetch_thirds(inverse_hbm, i_ref, sems.at[1])
    backward = fetch_thirds(backward_hbm, b_ref, sems.at[2])
    vectors = [
        pltpu.make_async_copy(source, target, sems.at[3, n])
        for n, (source, target) in enumerate(((rhs_hbm, rhs_ref), (coupling_hbm, coupling_ref)))
    ]
    for copy in forward + vectors + inverse + backward:
        copy.start()
    leaving = []

    def finish(row):
        there = (slice(None), slice(row, row + 8), slice(None))
        leaving.append(pltpu.make_async_copy(packed_ref.at[there], out_hbm.at[there], out_sems.at[row // 8]))
        leaving[-1].start()

    pack_blocks(f_ref, packed_ref, 0, forward, finish)
    for copy in vectors + inverse:
        copy.wait()
    inverse_matvec(i_ref, rhs_ref, c_ref)
    for n, vector_ref in enumerate((c_ref, rhs_ref, coupling_ref)):
        put_cell_vector(vectors_ref, vector_ref, 8, 2 * n)
    for quad in range(4):
        for last in (6, 7):
            vectors_ref[pl.ds(8 * quad + last, 8, stride=32), :] = jnp.zeros((8, 128), f32)
    for e in range(32):
        packed_ref[e, 144:152, :] = vectors_ref[8 * e : 8 * e + 8, :]
    finish(144)
    pack_blocks(b_ref, packed_ref, 72, backward, finish)
    for copy in leaving:
        copy.wait()


def first_kernel(slots_ref, *refs):
    cells, refs = refs[:4], refs[4:]
    forward_ref, backward_ref, first_ref, middle_ref, coupling_ref, packed_ref, c_ref, y_ref = refs
    for e in range(32):
        packed_ref[8 * e : 8 * e + 8, :] = slots_ref[e, 144:152, :]
    for t, tile in enumerate(get_slots(packed_ref, 8, 0)):
        c_ref[t] = tile

    def unpack(turn, n):
        if turn == 0:
            unpack_cell(slots_ref, 0, forward_ref, n)
        else:
            unpack_cell(slots_ref, 72, backward_ref, n)

    line_sweep(forward_ref, c_ref, y_ref, False, unpack)
    line_sweep(backward_ref, y_ref, first_ref, True)
    rhs = get_slots(packed_ref, 8, 2)
    coupling = get_slots(packed_ref, 8, 4)
    layer, _ = layer_position()
    for t in range(6):
        first = first_ref[t]
        middle_ref[t] = rhs[t] - first + coupling[t] * stations_sum(first)
        coupling_ref[t] = coupling[t]
    for w in range(4):
        for t in range(6):
            cells[w][2 * t : 2 * t + 2, :] = middle_ref[t, pl.ds(2 * (layer ^ w), 2), :]
        cells[w][12:16, :] = jnp.zeros((4, 128), f32)


def layer_position():
    cell = lax.axis_index("azim")
    return cell // 2, (cell % 2) * 4 + lax.axis_index("axial")


def inverse_send_kernel(inverse_hbm, *refs):
    outs, (i_ref, packed_ref, fetch_sems, sems) = refs[:8], refs[8:]
    fetches = fetch_thirds(inverse_hbm, i_ref, fetch_sems)
    for copy in fetches:
        copy.start()
    pack_blocks(i_ref, packed_ref, 0, fetches, lambda row: None)
    layer, place = layer_position()
    copies = []
    for d in range(8):
        for w in range(4):
            source = packed_ref.at[(layer ^ w) * 8 + (place ^ d)]
            copies.append(pltpu.make_async_copy(source, outs[d].at[pl.ds(72 * w, 72), :], sems.at[4 * d + w]))
            copies[-1].start()
    for copy in copies:
        copy.wait()


def inverse_get_kernel(*refs):
    ins, out_ref = refs[3::-1], refs[4]
    for w in range(4):
        for group in range(9):
            at = 72 * w + 8 * group
            for x, tile in enumerate(swap_quads([part[at : at + 8, :] for part in ins])):
                at = 8 * (4 * group + x)
                out_ref[w, at : at + 8, :] = tile


def turn_stations(tile, number):
    lanes = lane_index()
    for bit, width in ((1, 4), (2, 8)):
        other = jnp.where((lanes & width) == 0, turn_lanes(tile, -width), turn_lanes(tile, width))
        tile = jnp.where((number & bit) == 0, tile, other)
    return tile


def line_product(blocks_ref, cell, state):
    products = []
    for bh in range(6):
        total = None
        for ah in range(6):
            at = 8 * tile_at(ah, bh)
            term = blocks_ref[cell, at : at + 8, :] * state[ah]
            total = term if total is None else total + term
        total = pltpu.roll(total, 0, 1, stride=16, stride_axis=0)
        for span in (4, 2, 1):
            total = total + turn_rows(total, span)
        products.append(total)
    return products


def layer_inverse_kernel(ways, *refs):
    count = len(ways)
    vectors, blocks, outs, (turned_ref, c_ref) = refs[:count], refs[count : count + 2], refs[count + 2 : -2], refs[-2:]
    _, place = layer_position()
    cell, station = place // 4, place % 4
    c_ref[...] = jnp.zeros((16, 128), f32)
    for w, vector_ref, out_ref in zip(ways, vectors, outs):
        for at in (0, 8):
            turned_ref[at : at + 8, :] = turn_stations(vector_ref[at : at + 8, :], station)
        for n in range(2):
            state = [jnp.broadcast_to(turned_ref[pl.ds(2 * t + (cell ^ n), 1), :], (8, 128)) for t in range(6)]
            for t, product in enumerate(line_product(blocks[n], w, state)):
                c_ref[pl.ds(2 * t + (cell ^ n), 1), :] = product[0:1]
        for at in (0, 8):
            out_ref[at : at + 8, :] = turn_stations(c_ref[at : at + 8, :], station)


def second_kernel(*refs):
    cells, refs = refs[:4], refs[4:]
    forward_ref, backward_ref, first_ref, middle_ref, coupling_ref, out_ref, c_ref, y_ref, second_ref = refs
    layer, _ = layer_position()
    for w in range(4):
        for t in range(6):
            c_ref[t, pl.ds(2 * (layer ^ w), 2), :] = cells[w][2 * t : 2 * t + 2, :]
    line_sweep(forward_ref, c_ref, y_ref, False)
    line_sweep(backward_ref, y_ref, second_ref, True)
    correction, remaining = [], []
    for t in range(6):
        second = second_ref[t]
        correction.append(first_ref[t] + second)
        remaining.append(middle_ref[t] - second + coupling_ref[t] * stations_sum(second))
    put_slots(out_ref, correction, 4, 0)
    put_slots(out_ref, remaining, 4, 2)


def last_kernel(slots_ref, correction_ref, remaining_ref):
    for out_ref, base in ((correction_ref, 0), (remaining_ref, 2)):
        for t, tile in enumerate(get_slots(slots_ref, 4, base)):
            out_ref[8 * t : 8 * t + 8, :] = swap_rows(tile)


def shaped(*sizes):
    return jax.ShapeDtypeStruct(sizes, f32)


def call(kernel, outs, scratch=()):
    return pl.pallas_call(
        kernel,
        out_shape=outs,
        scratch_shapes=[pltpu.VMEM(sizes, f32) for sizes in scratch],
        compiler_params=pltpu.CompilerParams(vmem_limit_bytes=VMEM_LIMIT),
    )


def exchange(slots, rows):
    moved = lax.all_to_all(slots.reshape(32, rows, 128), BOTH, 0, 0, tiled=True)
    return moved.reshape(32 * rows, 128)


def line_plan(rhs, coupling, fwd_coupling, bwd_coupling, block_inverse):
    source, coupling_field = rhs.reshape(48, 128), coupling.reshape(48, 128)
    forward_blocks = fwd_coupling.reshape(48, 48, 128)
    backward_blocks = bwd_coupling.reshape(48, 48, 128)
    inverse_blocks = block_inverse.reshape(48, 48, 128)
    tiles, held = shaped(6, 8, 128), shaped(8, 288, 128)
    blocks = pltpu.VMEM((48, 48, 128), jnp.bfloat16)
    vector = pltpu.VMEM((48, 128), f32)

    slots = pl.pallas_call(
        first_send_kernel,
        out_shape=pltpu.HBM((32, 152, 128), f32),
        in_specs=[pl.BlockSpec(memory_space=pltpu.HBM)] * 5,
        out_specs=pl.BlockSpec(memory_space=pltpu.HBM),
        scratch_shapes=[blocks, blocks, blocks, vector, vector, vector]
        + [
            pltpu.VMEM((256, 128), f32),
            pltpu.VMEM((32, 152, 128), f32),
            pltpu.SemaphoreType.DMA((4, 3)),
            pltpu.SemaphoreType.DMA((19,)),
        ],
        compiler_params=pltpu.CompilerParams(vmem_limit_bytes=VMEM_LIMIT),
    )(*[
        pltpu.with_memory_space_constraint(array, pltpu.HBM)
        for array in (forward_blocks, backward_blocks, inverse_blocks, source, coupling_field)
    ])
    slots, inverse_blocks = lax.optimization_barrier((slots, inverse_blocks))
    slots = lax.all_to_all(slots, BOTH, 0, 0, tiled=True)

    parts = pl.pallas_call(
        inverse_send_kernel,
        out_shape=[shaped(288, 128)] * 8,
        in_specs=[pl.BlockSpec(memory_space=pltpu.HBM)],
        out_specs=[pl.BlockSpec(memory_space=pltpu.HBM)] * 8,
        scratch_shapes=[
            blocks, pltpu.VMEM((32, 72, 128), f32), pltpu.SemaphoreType.DMA((3,)), pltpu.SemaphoreType.DMA((32,))
        ],
        compiler_params=pltpu.CompilerParams(vmem_limit_bytes=VMEM_LIMIT),
    )(pltpu.with_memory_space_constraint(inverse_blocks, pltpu.HBM))

    def across(array, way):
        return lax.ppermute(array, BOTH, [(e, e ^ way) for e in range(32)]) if way else array

    parts = [across(parts[d], d) for d in range(7, -1, -1)]
    inverse = [call(inverse_get_kernel, shaped(4, 288, 128))(*parts[4 * n : 4 * n + 4]) for n in range(2)]
    *inverse, slots = lax.optimization_barrier((*inverse, slots))
    inverse = inverse[::-1]

    cells = shaped(16, 128)
    *middles, forward, backward, first, middle, coupling_lines = call(
        first_kernel, [cells] * 4 + [held, held, tiles, tiles, tiles], [(256, 128), (6, 8, 128), (6, 8, 128)]
    )(slots)
    turned = [(16, 128), (16, 128)]
    away = [across(middles[w], 8 * w) for w in (1, 2, 3)]
    own = call(functools.partial(layer_inverse_kernel, (0,)), [cells], turned)(middles[0], *inverse)
    away = call(functools.partial(layer_inverse_kernel, (1, 2, 3)), [cells] * 3, turned)(*away, *inverse)
    away = [across(away[w - 1], 8 * w) for w in (1, 2, 3)]
    slots = call(second_kernel, shaped(128, 128), [(6, 8, 128)] * 3)(
        *own, *away, forward, backward, first, middle, coupling_lines
    )
    slots = exchange(slots, 4)
    correction, remaining = call(last_kernel, (shaped(48, 128), shaped(48, 128)))(slots)
    return correction.reshape(rhs.shape), remaining.reshape(rhs.shape)


def from_behind(value, axis, steps):
    count = lax.axis_size(axis)
    initial, last = (max(0, -steps), min(count, count - steps))
    return lax.ppermute(value, axis, [(source, source + steps) for source in range(initial, last)])


def from_root(shard, axis, root):
    mine = lax.axis_index(axis) == root
    return lax.psum(jnp.where(mine, shard, jnp.zeros_like(shard)), axis)


def extended(block, sides, width):
    for axis, dim in sides:
        count = lax.axis_size(axis)
        forward = [(i, i + 1) for i in range(count - 1)]
        backward = [(target, source) for source, target in forward]
        low = lax.ppermute(
            lax.slice_in_dim(block, block.shape[dim] - width, None, axis=dim), axis, forward
        )
        high = lax.ppermute(lax.slice_in_dim(block, 0, width, axis=dim), axis, backward)
        block = jnp.concatenate([low, block, high], axis=dim)
    return block


def cell_stride(one_block, carried, const_term):
    return const_term - jnp.einsum(
        "abl,al->bl", one_block.astype(jnp.float32), carried, precision=highest
    )


def compose_cells(blocks, sequence):
    running = None
    for position in sequence:
        one_block = blocks[position].astype(jnp.float32)
        running = -jnp.swapaxes(one_block, 0, 1)
    return running


def doubling_maps(local_map, reverse):
    size = lax.axis_size("azim")
    index = lax.axis_index("azim")
    levels = []
    current = local_map
    distance = 1
    while distance < size:
        if reverse:
            moved = from_behind(current, "azim", -distance)
            exists = index + distance < size
        else:
            moved = from_behind(current, "azim", distance)
            exists = index >= distance
        levels.append((current, distance))
        current = jnp.where(
            exists, jnp.einsum("bcl,cal->bal", current, moved, precision=highest), current
        )
        distance = distance * 2
    return (levels, current)


def doubling_entries(map_levels, local_offset, reverse):
    levels, final_map = map_levels
    size = lax.axis_size("azim")
    index = lax.axis_index("azim")
    running = local_offset
    for current, distance in levels:
        if reverse:
            moved = from_behind(running, "azim", -distance)
        else:
            moved = from_behind(running, "azim", distance)
        running = jnp.einsum("bcl,cl->bl", current, moved, precision=highest) + running
    if reverse:
        wrapped = from_root(running, "azim", 0)
    else:
        wrapped = from_root(running, "azim", size - 1)
    leaving = jnp.einsum("bcl,cl->bl", final_map, wrapped, precision=highest) + running
    if reverse:
        shifted = from_behind(leaving, "azim", -1)
        first_device = index == size - 1
    else:
        shifted = from_behind(leaving, "azim", 1)
        first_device = index == 0
    return jnp.where(first_device, wrapped, shifted)


def sweep(blocks, consts, map_levels, reverse):
    cell_count = blocks.shape[0]
    sequence = list(range(cell_count))
    if reverse:
        sequence = sequence[::-1]
    carried = jnp.zeros(consts.shape[1:], jnp.float32)
    for position in sequence:
        carried = cell_stride(blocks[position], carried, consts[position])
    local_offset = carried
    incoming_maps = doubling_entries(map_levels, local_offset, reverse)
    outputs = [None] * cell_count
    carried = incoming_maps
    for position in sequence:
        carried = cell_stride(blocks[position], carried, consts[position])
        outputs[position] = carried
    return jnp.stack(outputs)


def on_device(rhs, coupling, fwd_coupling, bwd_coupling, block_inverse):
    cell_count, block_width, _, position_total, radial_count = fwd_coupling.shape
    line_count = position_total * radial_count
    forward_blocks = fwd_coupling.reshape(cell_count, block_width, block_width, line_count)
    backward_blocks = bwd_coupling.reshape(cell_count, block_width, block_width, line_count)
    inverse_blocks = block_inverse.reshape(cell_count, block_width, block_width, line_count)
    source = rhs.reshape(cell_count, block_width, line_count)
    coupling_field = coupling.reshape(cell_count, block_width, line_count)
    forward_map = compose_cells(forward_blocks, list(range(cell_count)))
    backward_map = compose_cells(backward_blocks, list(range(cell_count))[::-1])
    forward_levels = None
    backward_levels = None
    forward_levels = doubling_maps(forward_map, False)
    backward_levels = doubling_maps(backward_map, True)

    def precondition(vector):
        consts = jnp.stack(
            [
                jnp.einsum(
                    "abl,al->bl",
                    inverse_blocks[0].astype(jnp.float32),
                    vector[0],
                    precision=highest,
                )
            ]
        )
        forward = sweep(forward_blocks, consts, forward_levels, False)
        return sweep(backward_blocks, forward, backward_levels, True)

    def stations_sum(field):
        grid = field.reshape(cell_count, block_width, position_total, radial_count)
        padded = extended(grid, (("axial", 2),), 1)
        return (padded[:, :, :-2] + padded[:, :, 2:]).reshape(cell_count, block_width, line_count)

    applied_once = precondition(source)
    middle = source - applied_once + coupling_field * stations_sum(applied_once)
    second = precondition(middle)
    correction = applied_once + second
    remaining = middle - second + coupling_field * stations_sum(second)
    return (correction.reshape(rhs.shape), remaining.reshape(rhs.shape))


def solution(mesh):
    cells, stations = mesh.shape["azim"], mesh.shape["axial"]

    def on_each(rhs, coupling, fwd_coupling, bwd_coupling, block_inverse):
        local = fwd_coupling.shape
        if (cells, stations) == (8, 4) and local == (1, 48, 48, 1, 128):
            return line_plan(rhs, coupling, fwd_coupling, bwd_coupling, block_inverse)
        return on_device(rhs, coupling, fwd_coupling, bwd_coupling, block_inverse)

    return jax.shard_map(
        on_each,
        mesh=mesh,
        in_specs=(
            P("azim", None, "axial", None),
            P("azim", None, "axial", None),
            P("azim", None, None, "axial", None),
            P("azim", None, None, "axial", None),
            P("azim", None, None, "axial", None),
        ),
        out_specs=(P("azim", None, "axial", None), P("azim", None, "axial", None)),
        check_vma=False,
    )
```

```python
import functools

import jax
import jax.numpy as jnp
from jax import lax
from jax.experimental import pallas as pl
from jax.experimental.pallas import tpu as pltpu
from jax.sharding import PartitionSpec as P

highest = lax.Precision.HIGHEST
f32 = jnp.float32
BOTH = ("azim", "axial")
VMEM_LIMIT = 16 * 1024 * 1024


def lane_index():
    return lax.broadcasted_iota(jnp.int32, (8, 128), 1)


def row_index():
    return lax.broadcasted_iota(jnp.int32, (8, 128), 0)


def turn_lanes(tile, steps):
    steps = steps % 128
    return pltpu.roll(tile, steps, 1) if steps else tile


def turn_rows(tile, steps):
    steps = steps % 8
    return pltpu.roll(tile, steps, 0) if steps else tile


def swap_quads(tiles):
    lanes = lane_index()
    tiles = list(tiles)
    for bit, width in ((1, 4), (2, 8)):
        low = (lanes // width) % 2 == 0
        for first in range(4):
            if first & bit:
                continue
            one, two = tiles[first], tiles[first | bit]
            tiles[first] = jnp.where(low, one, turn_lanes(two, width))
            tiles[first | bit] = jnp.where(low, turn_lanes(one, -width), two)
    return tiles


def swap_rows(tile):
    lanes, rows = lane_index() // 16, row_index()
    for bit in (1, 2, 4):
        row_bit, lane_bit = (rows // bit) % 2, (lanes // bit) % 2
        up = turn_rows(turn_lanes(tile, 16 * bit), -bit)
        down = turn_rows(turn_lanes(tile, -16 * bit), bit)
        tile = jnp.where(row_bit == lane_bit, tile, jnp.where(row_bit == 0, up, down))
    return tile


def put_slots(out_ref, tiles, rows, base):
    zero = jnp.zeros((8, 128), f32)
    for half in range(2):
        group = [tiles[4 * half + x] if 4 * half + x < 6 else zero for x in range(4)]
        for quad, tile in enumerate(swap_quads(group)):
            out_ref[pl.ds(rows * quad + base + half, 8, stride=4 * rows), :] = tile


def get_slots(in_ref, rows, base):
    tiles = []
    for half in range(2):
        group = [in_ref[pl.ds(rows * quad + base + half, 8, stride=4 * rows), :] for quad in range(4)]
        tiles += swap_quads(group)
    return tiles[:6]


def put_cell_vector(out_ref, vector_ref, rows, base):
    put_slots(out_ref, [swap_rows(vector_ref[8 * t : 8 * t + 8, :]) for t in range(6)], rows, base)


def inverse_matvec(inverse_ref, vector_ref, out_ref):
    def step(group, totals):
        for inner in range(8):
            a = 8 * group + inner
            row = vector_ref[pl.ds(a, 1), :]
            totals = totals + inverse_ref[a].astype(f32) * row
        return totals

    out_ref[...] = lax.fori_loop(0, 6, step, jnp.zeros((48, 128), f32))


def pack_blocks(block_ref, out_ref, base, fetches, finish):
    quads = lane_index() // 4
    keeps = [(bit, (quads & bit) == 0) for bit in (1, 2, 4, 8, 16)]
    for group in range(9):
        ah_pair, bh_pair = group // 3, group % 3
        if bh_pair == 0:
            fetches[ah_pair].wait()
        items = [None] * 32
        for y in range(2):
            for p in range(8):
                wide = block_ref[16 * ah_pair + 8 * y + p, 16 * bh_pair : 16 * bh_pair + 16, :].astype(f32)
                for h in range(2):
                    i = 4 * p + 2 * y + h
                    items[i] = turn_lanes(turn_rows(wide[8 * h : 8 * h + 8], -p), 4 * i)
        for bit, keep in keeps:
            items = [jnp.where(keep, items[j], items[(j + bit) % 32]) for j in range(32)]
        for e in range(32):
            out_ref[e, base + 8 * group : base + 8 * group + 8, :] = turn_lanes(items[-e % 32], -4 * e)
        finish(base + 8 * group)


def fetch_thirds(block_hbm, block_ref, sems):
    copies = []
    for third in range(3):
        there = (slice(16 * third, 16 * third + 16), slice(None), slice(None))
        copies.append(pltpu.make_async_copy(block_hbm.at[there], block_ref.at[there], sems.at[third]))
    return copies


def unpack_cell(in_ref, base, out_ref, cell):
    for group in range(9):
        at = base + 8 * group
        parts = [in_ref[4 * cell + k, at : at + 8, :] for k in range(4)]
        for x, tile in enumerate(swap_quads(parts)):
            at = 8 * (4 * group + x)
            out_ref[cell, at : at + 8, :] = tile


def tile_at(ah, bh):
    return 4 * (3 * (ah // 2) + bh // 2) + 2 * (ah % 2) + bh % 2


def line_sweep(blocks_ref, const_ref, out_ref, reverse, beside=None):
    order = list(range(8))
    if reverse:
        order = order[::-1]
    state = None
    for turn in range(2):
        for n, cell in enumerate(order):
            if beside is not None:
                beside(turn, n)
            consts = [jnp.broadcast_to(const_ref[t, cell : cell + 1, :], (8, 128)) for t in range(6)]
            if state is None:
                state = consts
                continue
            products = line_product(blocks_ref, cell, state)
            state = [const - product for const, product in zip(consts, products)]
            if turn == 1:
                for t in range(6):
                    out_ref[t, cell : cell + 1, :] = state[t][0:1]


def stations_sum(tile):
    station = (lane_index() // 4) % 4
    before = jnp.where(station > 0, turn_lanes(tile, 4), 0.0)
    after = jnp.where(station < 3, turn_lanes(tile, -4), 0.0)
    return before + after


def first_send_kernel(
    forward_hbm, backward_hbm, inverse_hbm, rhs_hbm, coupling_hbm, out_hbm,
    f_ref, b_ref, i_ref, rhs_ref, coupling_ref, c_ref, vectors_ref, packed_ref, sems, out_sems,
):
    forward = fetch_thirds(forward_hbm, f_ref, sems.at[0])
    inverse = fetch_thirds(inverse_hbm, i_ref, sems.at[1])
    backward = fetch_thirds(backward_hbm, b_ref, sems.at[2])
    vectors = [
        pltpu.make_async_copy(source, target, sems.at[3, n])
        for n, (source, target) in enumerate(((rhs_hbm, rhs_ref), (coupling_hbm, coupling_ref)))
    ]
    for copy in forward + vectors + inverse + backward:
        copy.start()
    leaving = []

    def finish(row):
        there = (slice(None), slice(row, row + 8), slice(None))
        leaving.append(pltpu.make_async_copy(packed_ref.at[there], out_hbm.at[there], out_sems.at[row // 8]))
        leaving[-1].start()

    pack_blocks(f_ref, packed_ref, 0, forward, finish)
    for copy in vectors + inverse:
        copy.wait()
    inverse_matvec(i_ref, rhs_ref, c_ref)
    for n, vector_ref in enumerate((c_ref, rhs_ref, coupling_ref)):
        put_cell_vector(vectors_ref, vector_ref, 8, 2 * n)
    for quad in range(4):
        for last in (6, 7):
            vectors_ref[pl.ds(8 * quad + last, 8, stride=32), :] = jnp.zeros((8, 128), f32)
    for e in range(32):
        packed_ref[e, 144:152, :] = vectors_ref[8 * e : 8 * e + 8, :]
    finish(144)
    pack_blocks(b_ref, packed_ref, 72, backward, finish)
    for copy in leaving:
        copy.wait()


def first_kernel(slots_ref, *refs):
    own_ref, other_ref, forward_ref, backward_ref, first_ref, middle_ref, coupling_ref, packed_ref, c_ref, y_ref = refs[4:]
    for e in range(32):
        packed_ref[8 * e : 8 * e + 8, :] = slots_ref[e, 144:152, :]
    for t, tile in enumerate(get_slots(packed_ref, 8, 0)):
        c_ref[t] = tile

    def unpack(turn, n):
        if turn == 0:
            unpack_cell(slots_ref, 0, forward_ref, n)
        else:
            unpack_cell(slots_ref, 72, backward_ref, n)

    line_sweep(forward_ref, c_ref, y_ref, False, unpack)
    line_sweep(backward_ref, y_ref, first_ref, True)
    rhs = get_slots(packed_ref, 8, 2)
    coupling = get_slots(packed_ref, 8, 4)
    half, _ = half_position()
    for t in range(6):
        first = first_ref[t]
        middle = rhs[t] - first + coupling[t] * stations_sum(first)
        turned = turn_rows(middle, 4)
        other_ref[t] = jnp.where(half == 0, turned, middle)
        own_ref[t] = jnp.where(half == 0, middle, turned)
        middle_ref[t] = middle
        coupling_ref[t] = coupling[t]


def half_position():
    cell = lax.axis_index("azim")
    return cell // 4, (cell % 4) * 4 + lax.axis_index("axial")


def inverse_send_kernel(inverse_hbm, *refs):
    outs, (i_ref, packed_ref, fetch_sems, sems) = refs[:16], refs[16:]
    fetches = fetch_thirds(inverse_hbm, i_ref, fetch_sems)
    for copy in fetches:
        copy.start()
    pack_blocks(i_ref, packed_ref, 0, fetches, lambda row: None)
    half, place = half_position()
    copies = []
    for d in range(16):
        target = place ^ d
        for n, source in enumerate((16 * half + target, 16 * (1 - half) + target)):
            copies.append(
                pltpu.make_async_copy(packed_ref.at[source], outs[d].at[pl.ds(72 * n, 72), :], sems.at[2 * d + n])
            )
            copies[-1].start()
    for copy in copies:
        copy.wait()


def inverse_get_kernel(*refs):
    ins, out_ref = refs[:4], refs[4]
    for lines in range(2):
        for group in range(9):
            at = 72 * lines + 8 * group
            for x, tile in enumerate(swap_quads([part[at : at + 8, :] for part in ins])):
                at = 8 * (4 * group + x)
                out_ref[lines, at : at + 8, :] = tile


def turn_stations(tile, number):
    lanes = lane_index()
    for bit, width in ((1, 4), (2, 8)):
        other = jnp.where((lanes & width) == 0, turn_lanes(tile, -width), turn_lanes(tile, width))
        tile = jnp.where((number & bit) == 0, tile, other)
    return tile


def line_product(blocks_ref, cell, state):
    products = []
    for bh in range(6):
        total = None
        for ah in range(6):
            at = 8 * tile_at(ah, bh)
            term = blocks_ref[cell, at : at + 8, :] * state[ah]
            total = term if total is None else total + term
        total = pltpu.roll(total, 0, 1, stride=16, stride_axis=0)
        for span in (4, 2, 1):
            total = total + turn_rows(total, span)
        products.append(total)
    return products


def half_inverse_kernel(lines, vector_ref, *refs):
    blocks, (out_ref, turned_ref) = refs[:4], refs[4:]
    _, place = half_position()
    cell, station = place // 4, place % 4
    for t in range(6):
        turned_ref[t] = turn_stations(vector_ref[t], station)
    rows = row_index()
    totals = [jnp.zeros((8, 128), f32)] * 6
    for n in range(4):
        state = [jnp.broadcast_to(turned_ref[t, pl.ds(cell ^ n, 1), :], (8, 128)) for t in range(6)]
        for t, product in enumerate(line_product(blocks[n], lines, state)):
            totals[t] = jnp.where(rows == (cell ^ n), product, totals[t])
    for t in range(6):
        out_ref[t] = turn_stations(totals[t], station)


def second_kernel(
    own_ref, other_ref, forward_ref, backward_ref, first_ref, middle_ref, coupling_ref, out_ref, c_ref, y_ref, second_ref
):
    half, _ = half_position()
    low = row_index() < 4
    for t in range(6):
        tile = jnp.where(low, own_ref[t], turn_rows(other_ref[t], 4))
        c_ref[t] = jnp.where(half == 0, tile, turn_rows(tile, 4))
    line_sweep(forward_ref, c_ref, y_ref, False)
    line_sweep(backward_ref, y_ref, second_ref, True)
    correction, remaining = [], []
    for t in range(6):
        second = second_ref[t]
        correction.append(first_ref[t] + second)
        remaining.append(middle_ref[t] - second + coupling_ref[t] * stations_sum(second))
    put_slots(out_ref, correction, 4, 0)
    put_slots(out_ref, remaining, 4, 2)


def last_kernel(slots_ref, correction_ref, remaining_ref):
    for out_ref, base in ((correction_ref, 0), (remaining_ref, 2)):
        for t, tile in enumerate(get_slots(slots_ref, 4, base)):
            out_ref[8 * t : 8 * t + 8, :] = swap_rows(tile)


def shaped(*sizes):
    return jax.ShapeDtypeStruct(sizes, f32)


def call(kernel, outs, scratch=(), **specs):
    return pl.pallas_call(
        kernel,
        out_shape=outs,
        scratch_shapes=[pltpu.VMEM(sizes, f32) for sizes in scratch],
        compiler_params=pltpu.CompilerParams(vmem_limit_bytes=VMEM_LIMIT),
        **specs,
    )


def exchange(slots, rows):
    moved = lax.all_to_all(slots.reshape(32, rows, 128), BOTH, 0, 0, tiled=True)
    return moved.reshape(32 * rows, 128)


def line_plan(rhs, coupling, fwd_coupling, bwd_coupling, block_inverse):
    source, coupling_field = rhs.reshape(48, 128), coupling.reshape(48, 128)
    forward_blocks = fwd_coupling.reshape(48, 48, 128)
    backward_blocks = bwd_coupling.reshape(48, 48, 128)
    inverse_blocks = block_inverse.reshape(48, 48, 128)
    tiles, held = shaped(6, 8, 128), shaped(8, 288, 128)
    blocks = pltpu.VMEM((48, 48, 128), jnp.bfloat16)
    vector = pltpu.VMEM((48, 128), f32)

    slots = pl.pallas_call(
        first_send_kernel,
        out_shape=pltpu.HBM((32, 152, 128), f32),
        in_specs=[pl.BlockSpec(memory_space=pltpu.HBM)] * 5,
        out_specs=pl.BlockSpec(memory_space=pltpu.HBM),
        scratch_shapes=[blocks, blocks, blocks, vector, vector, vector]
        + [
            pltpu.VMEM((256, 128), f32),
            pltpu.VMEM((32, 152, 128), f32),
            pltpu.SemaphoreType.DMA((4, 3)),
            pltpu.SemaphoreType.DMA((19,)),
        ],
        compiler_params=pltpu.CompilerParams(vmem_limit_bytes=VMEM_LIMIT),
    )(*[
        pltpu.with_memory_space_constraint(array, pltpu.HBM)
        for array in (forward_blocks, backward_blocks, inverse_blocks, source, coupling_field)
    ])
    slots, inverse_blocks = lax.optimization_barrier((slots, inverse_blocks))
    slots = lax.all_to_all(slots, BOTH, 0, 0, tiled=True)

    parts = pl.pallas_call(
        inverse_send_kernel,
        out_shape=[shaped(144, 128)] * 16,
        in_specs=[pl.BlockSpec(memory_space=pltpu.HBM)],
        out_specs=[pl.BlockSpec(memory_space=pltpu.HBM)] * 16,
        scratch_shapes=[
            blocks, pltpu.VMEM((32, 72, 128), f32), pltpu.SemaphoreType.DMA((3,)), pltpu.SemaphoreType.DMA((32,))
        ],
        compiler_params=pltpu.CompilerParams(vmem_limit_bytes=VMEM_LIMIT),
    )(pltpu.with_memory_space_constraint(inverse_blocks, pltpu.HBM))
    parts = [parts[0]] + [lax.ppermute(parts[d], BOTH, [(e, e ^ d) for e in range(32)]) for d in range(1, 16)]
    inverse = [call(inverse_get_kernel, shaped(2, 288, 128))(*parts[4 * n : 4 * n + 4]) for n in range(4)]

    own, other, forward, backward, first, middle, coupling_lines = call(
        first_kernel,
        (tiles, tiles, held, held, tiles, tiles, tiles),
        [(256, 128), (6, 8, 128), (6, 8, 128)],
        in_specs=[pl.BlockSpec(memory_space=pltpu.VMEM)] + [pl.BlockSpec(memory_space=pl.ANY)] * 4,
    )(slots, *inverse)

    def with_partner(vector):
        return lax.ppermute(vector, BOTH, [(e, e ^ 16) for e in range(32)])

    other = with_partner(other)
    own = call(functools.partial(half_inverse_kernel, 0), tiles, [(6, 8, 128)])(own, *inverse)
    other = call(functools.partial(half_inverse_kernel, 1), tiles, [(6, 8, 128)])(other, *inverse)
    other = with_partner(other)
    slots = call(second_kernel, shaped(128, 128), [(6, 8, 128)] * 3)(
        own, other, forward, backward, first, middle, coupling_lines
    )
    slots = exchange(slots, 4)
    correction, remaining = call(last_kernel, (shaped(48, 128), shaped(48, 128)))(slots)
    return correction.reshape(rhs.shape), remaining.reshape(rhs.shape)


def from_behind(value, axis, steps):
    count = lax.axis_size(axis)
    initial, last = (max(0, -steps), min(count, count - steps))
    return lax.ppermute(value, axis, [(source, source + steps) for source in range(initial, last)])


def from_root(shard, axis, root):
    mine = lax.axis_index(axis) == root
    return lax.psum(jnp.where(mine, shard, jnp.zeros_like(shard)), axis)


def extended(block, sides, width):
    for axis, dim in sides:
        count = lax.axis_size(axis)
        forward = [(i, i + 1) for i in range(count - 1)]
        backward = [(target, source) for source, target in forward]
        low = lax.ppermute(
            lax.slice_in_dim(block, block.shape[dim] - width, None, axis=dim), axis, forward
        )
        high = lax.ppermute(lax.slice_in_dim(block, 0, width, axis=dim), axis, backward)
        block = jnp.concatenate([low, block, high], axis=dim)
    return block


def cell_stride(one_block, carried, const_term):
    return const_term - jnp.einsum(
        "abl,al->bl", one_block.astype(jnp.float32), carried, precision=highest
    )


def compose_cells(blocks, sequence):
    running = None
    for position in sequence:
        one_block = blocks[position].astype(jnp.float32)
        running = -jnp.swapaxes(one_block, 0, 1)
    return running


def doubling_maps(local_map, reverse):
    size = lax.axis_size("azim")
    index = lax.axis_index("azim")
    levels = []
    current = local_map
    distance = 1
    while distance < size:
        if reverse:
            moved = from_behind(current, "azim", -distance)
            exists = index + distance < size
        else:
            moved = from_behind(current, "azim", distance)
            exists = index >= distance
        levels.append((current, distance))
        current = jnp.where(
            exists, jnp.einsum("bcl,cal->bal", current, moved, precision=highest), current
        )
        distance = distance * 2
    return (levels, current)


def doubling_entries(map_levels, local_offset, reverse):
    levels, final_map = map_levels
    size = lax.axis_size("azim")
    index = lax.axis_index("azim")
    running = local_offset
    for current, distance in levels:
        if reverse:
            moved = from_behind(running, "azim", -distance)
        else:
            moved = from_behind(running, "azim", distance)
        running = jnp.einsum("bcl,cl->bl", current, moved, precision=highest) + running
    if reverse:
        wrapped = from_root(running, "azim", 0)
    else:
        wrapped = from_root(running, "azim", size - 1)
    leaving = jnp.einsum("bcl,cl->bl", final_map, wrapped, precision=highest) + running
    if reverse:
        shifted = from_behind(leaving, "azim", -1)
        first_device = index == size - 1
    else:
        shifted = from_behind(leaving, "azim", 1)
        first_device = index == 0
    return jnp.where(first_device, wrapped, shifted)


def sweep(blocks, consts, map_levels, reverse):
    cell_count = blocks.shape[0]
    sequence = list(range(cell_count))
    if reverse:
        sequence = sequence[::-1]
    carried = jnp.zeros(consts.shape[1:], jnp.float32)
    for position in sequence:
        carried = cell_stride(blocks[position], carried, consts[position])
    local_offset = carried
    incoming_maps = doubling_entries(map_levels, local_offset, reverse)
    outputs = [None] * cell_count
    carried = incoming_maps
    for position in sequence:
        carried = cell_stride(blocks[position], carried, consts[position])
        outputs[position] = carried
    return jnp.stack(outputs)


def on_device(rhs, coupling, fwd_coupling, bwd_coupling, block_inverse):
    cell_count, block_width, _, position_total, radial_count = fwd_coupling.shape
    line_count = position_total * radial_count
    forward_blocks = fwd_coupling.reshape(cell_count, block_width, block_width, line_count)
    backward_blocks = bwd_coupling.reshape(cell_count, block_width, block_width, line_count)
    inverse_blocks = block_inverse.reshape(cell_count, block_width, block_width, line_count)
    source = rhs.reshape(cell_count, block_width, line_count)
    coupling_field = coupling.reshape(cell_count, block_width, line_count)
    forward_map = compose_cells(forward_blocks, list(range(cell_count)))
    backward_map = compose_cells(backward_blocks, list(range(cell_count))[::-1])
    forward_levels = None
    backward_levels = None
    forward_levels = doubling_maps(forward_map, False)
    backward_levels = doubling_maps(backward_map, True)

    def precondition(vector):
        consts = jnp.stack(
            [
                jnp.einsum(
                    "abl,al->bl",
                    inverse_blocks[0].astype(jnp.float32),
                    vector[0],
                    precision=highest,
                )
            ]
        )
        forward = sweep(forward_blocks, consts, forward_levels, False)
        return sweep(backward_blocks, forward, backward_levels, True)

    def stations_sum(field):
        grid = field.reshape(cell_count, block_width, position_total, radial_count)
        padded = extended(grid, (("axial", 2),), 1)
        return (padded[:, :, :-2] + padded[:, :, 2:]).reshape(cell_count, block_width, line_count)

    applied_once = precondition(source)
    middle = source - applied_once + coupling_field * stations_sum(applied_once)
    second = precondition(middle)
    correction = applied_once + second
    remaining = middle - second + coupling_field * stations_sum(second)
    return (correction.reshape(rhs.shape), remaining.reshape(rhs.shape))


def solution(mesh):
    cells, stations = mesh.shape["azim"], mesh.shape["axial"]

    def on_each(rhs, coupling, fwd_coupling, bwd_coupling, block_inverse):
        local = fwd_coupling.shape
        if (cells, stations) == (8, 4) and local == (1, 48, 48, 1, 128):
            return line_plan(rhs, coupling, fwd_coupling, bwd_coupling, block_inverse)
        return on_device(rhs, coupling, fwd_coupling, bwd_coupling, block_inverse)

    return jax.shard_map(
        on_each,
        mesh=mesh,
        in_specs=(
            P("azim", None, "axial", None),
            P("azim", None, "axial", None),
            P("azim", None, None, "axial", None),
            P("azim", None, None, "axial", None),
            P("azim", None, None, "axial", None),
        ),
        out_specs=(P("azim", None, "axial", None), P("azim", None, "axial", None)),
        check_vma=False,
    )
```

```python
import functools

import jax
import jax.numpy as jnp
from jax import lax
from jax.experimental import pallas as pl
from jax.experimental.pallas import tpu as pltpu
from jax.sharding import PartitionSpec as P

highest = lax.Precision.HIGHEST
f32 = jnp.float32
BOTH = ("azim", "axial")
VMEM_LIMIT = 16 * 1024 * 1024


def lane_index():
    return lax.broadcasted_iota(jnp.int32, (8, 128), 1)


def row_index():
    return lax.broadcasted_iota(jnp.int32, (8, 128), 0)


def turn_lanes(tile, steps):
    steps = steps % 128
    return pltpu.roll(tile, steps, 1) if steps else tile


def turn_rows(tile, steps):
    steps = steps % 8
    return pltpu.roll(tile, steps, 0) if steps else tile


def swap_quads(tiles):
    lanes = lane_index()
    tiles = list(tiles)
    for bit, width in ((1, 4), (2, 8)):
        low = (lanes // width) % 2 == 0
        for first in range(4):
            if first & bit:
                continue
            one, two = tiles[first], tiles[first | bit]
            tiles[first] = jnp.where(low, one, turn_lanes(two, width))
            tiles[first | bit] = jnp.where(low, turn_lanes(one, -width), two)
    return tiles


def swap_rows(tile):
    lanes, rows = lane_index() // 16, row_index()
    for bit in (1, 2, 4):
        row_bit, lane_bit = (rows // bit) % 2, (lanes // bit) % 2
        up = turn_rows(turn_lanes(tile, 16 * bit), -bit)
        down = turn_rows(turn_lanes(tile, -16 * bit), bit)
        tile = jnp.where(row_bit == lane_bit, tile, jnp.where(row_bit == 0, up, down))
    return tile


def put_slots(out_ref, tiles, rows, base):
    zero = jnp.zeros((8, 128), f32)
    for half in range(2):
        group = [tiles[4 * half + x] if 4 * half + x < 6 else zero for x in range(4)]
        for quad, tile in enumerate(swap_quads(group)):
            out_ref[pl.ds(rows * quad + base + half, 8, stride=4 * rows), :] = tile


def get_slots(in_ref, rows, base):
    tiles = []
    for half in range(2):
        group = [in_ref[pl.ds(rows * quad + base + half, 8, stride=4 * rows), :] for quad in range(4)]
        tiles += swap_quads(group)
    return tiles[:6]


def put_cell_vector(out_ref, vector_ref, rows, base):
    put_slots(out_ref, [swap_rows(vector_ref[8 * t : 8 * t + 8, :]) for t in range(6)], rows, base)


def inverse_matvec(inverse_ref, vector_ref, out_ref):
    def step(group, totals):
        for inner in range(8):
            a = 8 * group + inner
            row = vector_ref[pl.ds(a, 1), :]
            totals = totals + inverse_ref[a].astype(f32) * row
        return totals

    out_ref[...] = lax.fori_loop(0, 6, step, jnp.zeros((48, 128), f32))


def pack_blocks(block_ref, out_ref, base, fetches, finish):
    quads = lane_index() // 4
    keeps = [(bit, (quads & bit) == 0) for bit in (1, 2, 4, 8, 16)]
    for group in range(9):
        ah_pair, bh_pair = group // 3, group % 3
        if bh_pair == 0:
            fetches[ah_pair].wait()
        items = [None] * 32
        for y in range(2):
            for p in range(8):
                wide = block_ref[16 * ah_pair + 8 * y + p, 16 * bh_pair : 16 * bh_pair + 16, :].astype(f32)
                for h in range(2):
                    i = 4 * p + 2 * y + h
                    items[i] = turn_lanes(turn_rows(wide[8 * h : 8 * h + 8], -p), 4 * i)
        for bit, keep in keeps:
            items = [jnp.where(keep, items[j], items[(j + bit) % 32]) for j in range(32)]
        for e in range(32):
            out_ref[e, base + 8 * group : base + 8 * group + 8, :] = turn_lanes(items[-e % 32], -4 * e)
        finish(base + 8 * group)


def fetch_thirds(block_hbm, block_ref, sems):
    copies = []
    for third in range(3):
        there = (slice(16 * third, 16 * third + 16), slice(None), slice(None))
        copies.append(pltpu.make_async_copy(block_hbm.at[there], block_ref.at[there], sems.at[third]))
    return copies


def unpack_cell(in_ref, base, out_ref, cell):
    for group in range(9):
        at = base + 8 * group
        parts = [in_ref[4 * cell + k, at : at + 8, :] for k in range(4)]
        for x, tile in enumerate(swap_quads(parts)):
            at = 8 * (4 * group + x)
            out_ref[cell, at : at + 8, :] = tile


def tile_at(ah, bh):
    return 4 * (3 * (ah // 2) + bh // 2) + 2 * (ah % 2) + bh % 2


def line_sweep(blocks_ref, const_ref, out_ref, reverse, beside=None):
    order = list(range(8))
    if reverse:
        order = order[::-1]
    state = None
    for turn in range(2):
        for n, cell in enumerate(order):
            if beside is not None:
                beside(turn, n)
            consts = [jnp.broadcast_to(const_ref[t, cell : cell + 1, :], (8, 128)) for t in range(6)]
            if state is None:
                state = consts
                continue
            products = line_product(blocks_ref, cell, state)
            state = [const - product for const, product in zip(consts, products)]
            if turn == 1:
                for t in range(6):
                    out_ref[t, cell : cell + 1, :] = state[t][0:1]


def stations_sum(tile):
    station = (lane_index() // 4) % 4
    before = jnp.where(station > 0, turn_lanes(tile, 4), 0.0)
    after = jnp.where(station < 3, turn_lanes(tile, -4), 0.0)
    return before + after


def first_send_kernel(
    forward_hbm, backward_hbm, inverse_hbm, rhs_hbm, coupling_hbm, out_hbm,
    f_ref, b_ref, i_ref, rhs_ref, coupling_ref, c_ref, vectors_ref, packed_ref, sems, out_sems,
):
    forward = fetch_thirds(forward_hbm, f_ref, sems.at[0])
    inverse = fetch_thirds(inverse_hbm, i_ref, sems.at[1])
    backward = fetch_thirds(backward_hbm, b_ref, sems.at[2])
    vectors = [
        pltpu.make_async_copy(source, target, sems.at[3, n])
        for n, (source, target) in enumerate(((rhs_hbm, rhs_ref), (coupling_hbm, coupling_ref)))
    ]
    for copy in forward + vectors + inverse + backward:
        copy.start()
    leaving = []

    def finish(row):
        there = (slice(None), slice(row, row + 8), slice(None))
        leaving.append(pltpu.make_async_copy(packed_ref.at[there], out_hbm.at[there], out_sems.at[row // 8]))
        leaving[-1].start()

    pack_blocks(f_ref, packed_ref, 0, forward, finish)
    for copy in vectors + inverse:
        copy.wait()
    inverse_matvec(i_ref, rhs_ref, c_ref)
    for n, vector_ref in enumerate((c_ref, rhs_ref, coupling_ref)):
        put_cell_vector(vectors_ref, vector_ref, 8, 2 * n)
    for quad in range(4):
        for last in (6, 7):
            vectors_ref[pl.ds(8 * quad + last, 8, stride=32), :] = jnp.zeros((8, 128), f32)
    for e in range(32):
        packed_ref[e, 144:152, :] = vectors_ref[8 * e : 8 * e + 8, :]
    finish(144)
    pack_blocks(b_ref, packed_ref, 72, backward, finish)
    for copy in leaving:
        copy.wait()


def first_kernel(slots_ref, *refs):
    own_ref, other_ref, forward_ref, backward_ref, first_ref, middle_ref, coupling_ref, packed_ref, c_ref, y_ref = refs
    for e in range(32):
        packed_ref[8 * e : 8 * e + 8, :] = slots_ref[e, 144:152, :]
    for t, tile in enumerate(get_slots(packed_ref, 8, 0)):
        c_ref[t] = tile

    def unpack(turn, n):
        if turn == 0:
            unpack_cell(slots_ref, 0, forward_ref, n)
        else:
            unpack_cell(slots_ref, 72, backward_ref, n)

    line_sweep(forward_ref, c_ref, y_ref, False, unpack)
    line_sweep(backward_ref, y_ref, first_ref, True)
    rhs = get_slots(packed_ref, 8, 2)
    coupling = get_slots(packed_ref, 8, 4)
    half, _ = half_position()
    for t in range(6):
        first = first_ref[t]
        middle = rhs[t] - first + coupling[t] * stations_sum(first)
        turned = turn_rows(middle, 4)
        other_ref[t] = jnp.where(half == 0, turned, middle)
        own_ref[t] = jnp.where(half == 0, middle, turned)
        middle_ref[t] = middle
        coupling_ref[t] = coupling[t]


def half_position():
    cell = lax.axis_index("azim")
    return cell // 4, (cell % 4) * 4 + lax.axis_index("axial")


def inverse_send_kernel(inverse_hbm, *refs):
    outs, (i_ref, packed_ref, fetch_sems, sems) = refs[:16], refs[16:]
    fetches = fetch_thirds(inverse_hbm, i_ref, fetch_sems)
    for copy in fetches:
        copy.start()
    pack_blocks(i_ref, packed_ref, 0, fetches, lambda row: None)
    half, place = half_position()
    copies = []
    for d in range(16):
        target = place ^ d
        for n, source in enumerate((16 * half + target, 16 * (1 - half) + target)):
            copies.append(
                pltpu.make_async_copy(packed_ref.at[source], outs[d].at[pl.ds(72 * n, 72), :], sems.at[2 * d + n])
            )
            copies[-1].start()
    for copy in copies:
        copy.wait()


def inverse_get_kernel(*refs):
    ins, out_ref = refs[:4], refs[4]
    for lines in range(2):
        for group in range(9):
            at = 72 * lines + 8 * group
            for x, tile in enumerate(swap_quads([part[at : at + 8, :] for part in ins])):
                at = 8 * (4 * group + x)
                out_ref[lines, at : at + 8, :] = tile


def turn_stations(tile, number):
    lanes = lane_index()
    for bit, width in ((1, 4), (2, 8)):
        other = jnp.where((lanes & width) == 0, turn_lanes(tile, -width), turn_lanes(tile, width))
        tile = jnp.where((number & bit) == 0, tile, other)
    return tile


def line_product(blocks_ref, cell, state):
    products = []
    for bh in range(6):
        total = None
        for ah in range(6):
            at = 8 * tile_at(ah, bh)
            term = blocks_ref[cell, at : at + 8, :] * state[ah]
            total = term if total is None else total + term
        total = pltpu.roll(total, 0, 1, stride=16, stride_axis=0)
        for span in (4, 2, 1):
            total = total + turn_rows(total, span)
        products.append(total)
    return products


def half_inverse_kernel(lines, vector_ref, *refs):
    blocks, (out_ref, turned_ref) = refs[:4], refs[4:]
    _, place = half_position()
    cell, station = place // 4, place % 4
    for t in range(6):
        turned_ref[t] = turn_stations(vector_ref[t], station)
    rows = row_index()
    totals = [jnp.zeros((8, 128), f32)] * 6
    for n in range(4):
        state = [jnp.broadcast_to(turned_ref[t, pl.ds(cell ^ n, 1), :], (8, 128)) for t in range(6)]
        for t, product in enumerate(line_product(blocks[n], lines, state)):
            totals[t] = jnp.where(rows == (cell ^ n), product, totals[t])
    for t in range(6):
        out_ref[t] = turn_stations(totals[t], station)


def second_kernel(
    own_ref, other_ref, forward_ref, backward_ref, first_ref, middle_ref, coupling_ref, out_ref, c_ref, y_ref, second_ref
):
    half, _ = half_position()
    low = row_index() < 4
    for t in range(6):
        tile = jnp.where(low, own_ref[t], turn_rows(other_ref[t], 4))
        c_ref[t] = jnp.where(half == 0, tile, turn_rows(tile, 4))
    line_sweep(forward_ref, c_ref, y_ref, False)
    line_sweep(backward_ref, y_ref, second_ref, True)
    correction, remaining = [], []
    for t in range(6):
        second = second_ref[t]
        correction.append(first_ref[t] + second)
        remaining.append(middle_ref[t] - second + coupling_ref[t] * stations_sum(second))
    put_slots(out_ref, correction, 4, 0)
    put_slots(out_ref, remaining, 4, 2)


def last_kernel(slots_ref, correction_ref, remaining_ref):
    for out_ref, base in ((correction_ref, 0), (remaining_ref, 2)):
        for t, tile in enumerate(get_slots(slots_ref, 4, base)):
            out_ref[8 * t : 8 * t + 8, :] = swap_rows(tile)


def shaped(*sizes):
    return jax.ShapeDtypeStruct(sizes, f32)


def call(kernel, outs, scratch=()):
    return pl.pallas_call(
        kernel,
        out_shape=outs,
        scratch_shapes=[pltpu.VMEM(sizes, f32) for sizes in scratch],
        compiler_params=pltpu.CompilerParams(vmem_limit_bytes=VMEM_LIMIT),
    )


def exchange(slots, rows):
    moved = lax.all_to_all(slots.reshape(32, rows, 128), BOTH, 0, 0, tiled=True)
    return moved.reshape(32 * rows, 128)


def line_plan(rhs, coupling, fwd_coupling, bwd_coupling, block_inverse):
    source, coupling_field = rhs.reshape(48, 128), coupling.reshape(48, 128)
    forward_blocks = fwd_coupling.reshape(48, 48, 128)
    backward_blocks = bwd_coupling.reshape(48, 48, 128)
    inverse_blocks = block_inverse.reshape(48, 48, 128)
    tiles, held = shaped(6, 8, 128), shaped(8, 288, 128)
    blocks = pltpu.VMEM((48, 48, 128), jnp.bfloat16)
    vector = pltpu.VMEM((48, 128), f32)

    slots = pl.pallas_call(
        first_send_kernel,
        out_shape=pltpu.HBM((32, 152, 128), f32),
        in_specs=[pl.BlockSpec(memory_space=pltpu.HBM)] * 5,
        out_specs=pl.BlockSpec(memory_space=pltpu.HBM),
        scratch_shapes=[blocks, blocks, blocks, vector, vector, vector]
        + [
            pltpu.VMEM((256, 128), f32),
            pltpu.VMEM((32, 152, 128), f32),
            pltpu.SemaphoreType.DMA((4, 3)),
            pltpu.SemaphoreType.DMA((19,)),
        ],
        compiler_params=pltpu.CompilerParams(vmem_limit_bytes=VMEM_LIMIT),
    )(*[
        pltpu.with_memory_space_constraint(array, pltpu.HBM)
        for array in (forward_blocks, backward_blocks, inverse_blocks, source, coupling_field)
    ])
    slots, inverse_blocks = lax.optimization_barrier((slots, inverse_blocks))
    slots = lax.all_to_all(slots, BOTH, 0, 0, tiled=True)

    parts = pl.pallas_call(
        inverse_send_kernel,
        out_shape=[shaped(144, 128)] * 16,
        in_specs=[pl.BlockSpec(memory_space=pltpu.HBM)],
        out_specs=[pl.BlockSpec(memory_space=pltpu.HBM)] * 16,
        scratch_shapes=[
            blocks, pltpu.VMEM((32, 72, 128), f32), pltpu.SemaphoreType.DMA((3,)), pltpu.SemaphoreType.DMA((32,))
        ],
        compiler_params=pltpu.CompilerParams(vmem_limit_bytes=VMEM_LIMIT),
    )(pltpu.with_memory_space_constraint(inverse_blocks, pltpu.HBM))
    parts = [parts[0]] + [lax.ppermute(parts[d], BOTH, [(e, e ^ d) for e in range(32)]) for d in range(1, 16)]
    inverse = [call(inverse_get_kernel, shaped(2, 288, 128))(*parts[4 * n : 4 * n + 4]) for n in range(4)]

    own, other, forward, backward, first, middle, coupling_lines = call(
        first_kernel, (tiles, tiles, held, held, tiles, tiles, tiles), [(256, 128), (6, 8, 128), (6, 8, 128)]
    )(slots)

    def with_partner(vector):
        return lax.ppermute(vector, BOTH, [(e, e ^ 16) for e in range(32)])

    other = with_partner(other)
    own = call(functools.partial(half_inverse_kernel, 0), tiles, [(6, 8, 128)])(own, *inverse)
    other = call(functools.partial(half_inverse_kernel, 1), tiles, [(6, 8, 128)])(other, *inverse)
    other = with_partner(other)
    slots = call(second_kernel, shaped(128, 128), [(6, 8, 128)] * 3)(
        own, other, forward, backward, first, middle, coupling_lines
    )
    slots = exchange(slots, 4)
    correction, remaining = call(last_kernel, (shaped(48, 128), shaped(48, 128)))(slots)
    return correction.reshape(rhs.shape), remaining.reshape(rhs.shape)


def from_behind(value, axis, steps):
    count = lax.axis_size(axis)
    initial, last = (max(0, -steps), min(count, count - steps))
    return lax.ppermute(value, axis, [(source, source + steps) for source in range(initial, last)])


def from_root(shard, axis, root):
    mine = lax.axis_index(axis) == root
    return lax.psum(jnp.where(mine, shard, jnp.zeros_like(shard)), axis)


def extended(block, sides, width):
    for axis, dim in sides:
        count = lax.axis_size(axis)
        forward = [(i, i + 1) for i in range(count - 1)]
        backward = [(target, source) for source, target in forward]
        low = lax.ppermute(
            lax.slice_in_dim(block, block.shape[dim] - width, None, axis=dim), axis, forward
        )
        high = lax.ppermute(lax.slice_in_dim(block, 0, width, axis=dim), axis, backward)
        block = jnp.concatenate([low, block, high], axis=dim)
    return block


def cell_stride(one_block, carried, const_term):
    return const_term - jnp.einsum(
        "abl,al->bl", one_block.astype(jnp.float32), carried, precision=highest
    )


def compose_cells(blocks, sequence):
    running = None
    for position in sequence:
        one_block = blocks[position].astype(jnp.float32)
        running = -jnp.swapaxes(one_block, 0, 1)
    return running


def doubling_maps(local_map, reverse):
    size = lax.axis_size("azim")
    index = lax.axis_index("azim")
    levels = []
    current = local_map
    distance = 1
    while distance < size:
        if reverse:
            moved = from_behind(current, "azim", -distance)
            exists = index + distance < size
        else:
            moved = from_behind(current, "azim", distance)
            exists = index >= distance
        levels.append((current, distance))
        current = jnp.where(
            exists, jnp.einsum("bcl,cal->bal", current, moved, precision=highest), current
        )
        distance = distance * 2
    return (levels, current)


def doubling_entries(map_levels, local_offset, reverse):
    levels, final_map = map_levels
    size = lax.axis_size("azim")
    index = lax.axis_index("azim")
    running = local_offset
    for current, distance in levels:
        if reverse:
            moved = from_behind(running, "azim", -distance)
        else:
            moved = from_behind(running, "azim", distance)
        running = jnp.einsum("bcl,cl->bl", current, moved, precision=highest) + running
    if reverse:
        wrapped = from_root(running, "azim", 0)
    else:
        wrapped = from_root(running, "azim", size - 1)
    leaving = jnp.einsum("bcl,cl->bl", final_map, wrapped, precision=highest) + running
    if reverse:
        shifted = from_behind(leaving, "azim", -1)
        first_device = index == size - 1
    else:
        shifted = from_behind(leaving, "azim", 1)
        first_device = index == 0
    return jnp.where(first_device, wrapped, shifted)


def sweep(blocks, consts, map_levels, reverse):
    cell_count = blocks.shape[0]
    sequence = list(range(cell_count))
    if reverse:
        sequence = sequence[::-1]
    carried = jnp.zeros(consts.shape[1:], jnp.float32)
    for position in sequence:
        carried = cell_stride(blocks[position], carried, consts[position])
    local_offset = carried
    incoming_maps = doubling_entries(map_levels, local_offset, reverse)
    outputs = [None] * cell_count
    carried = incoming_maps
    for position in sequence:
        carried = cell_stride(blocks[position], carried, consts[position])
        outputs[position] = carried
    return jnp.stack(outputs)


def on_device(rhs, coupling, fwd_coupling, bwd_coupling, block_inverse):
    cell_count, block_width, _, position_total, radial_count = fwd_coupling.shape
    line_count = position_total * radial_count
    forward_blocks = fwd_coupling.reshape(cell_count, block_width, block_width, line_count)
    backward_blocks = bwd_coupling.reshape(cell_count, block_width, block_width, line_count)
    inverse_blocks = block_inverse.reshape(cell_count, block_width, block_width, line_count)
    source = rhs.reshape(cell_count, block_width, line_count)
    coupling_field = coupling.reshape(cell_count, block_width, line_count)
    forward_map = compose_cells(forward_blocks, list(range(cell_count)))
    backward_map = compose_cells(backward_blocks, list(range(cell_count))[::-1])
    forward_levels = None
    backward_levels = None
    forward_levels = doubling_maps(forward_map, False)
    backward_levels = doubling_maps(backward_map, True)

    def precondition(vector):
        consts = jnp.stack(
            [
                jnp.einsum(
                    "abl,al->bl",
                    inverse_blocks[0].astype(jnp.float32),
                    vector[0],
                    precision=highest,
                )
            ]
        )
        forward = sweep(forward_blocks, consts, forward_levels, False)
        return sweep(backward_blocks, forward, backward_levels, True)

    def stations_sum(field):
        grid = field.reshape(cell_count, block_width, position_total, radial_count)
        padded = extended(grid, (("axial", 2),), 1)
        return (padded[:, :, :-2] + padded[:, :, 2:]).reshape(cell_count, block_width, line_count)

    applied_once = precondition(source)
    middle = source - applied_once + coupling_field * stations_sum(applied_once)
    second = precondition(middle)
    correction = applied_once + second
    remaining = middle - second + coupling_field * stations_sum(second)
    return (correction.reshape(rhs.shape), remaining.reshape(rhs.shape))


def solution(mesh):
    cells, stations = mesh.shape["azim"], mesh.shape["axial"]

    def on_each(rhs, coupling, fwd_coupling, bwd_coupling, block_inverse):
        local = fwd_coupling.shape
        if (cells, stations) == (8, 4) and local == (1, 48, 48, 1, 128):
            return line_plan(rhs, coupling, fwd_coupling, bwd_coupling, block_inverse)
        return on_device(rhs, coupling, fwd_coupling, bwd_coupling, block_inverse)

    return jax.shard_map(
        on_each,
        mesh=mesh,
        in_specs=(
            P("azim", None, "axial", None),
            P("azim", None, "axial", None),
            P("azim", None, None, "axial", None),
            P("azim", None, None, "axial", None),
            P("azim", None, None, "axial", None),
        ),
        out_specs=(P("azim", None, "axial", None), P("azim", None, "axial", None)),
        check_vma=False,
    )
```

```python
import functools

import jax
import jax.numpy as jnp
from jax import lax
from jax.experimental import pallas as pl
from jax.experimental.pallas import tpu as pltpu
from jax.sharding import PartitionSpec as P

highest = lax.Precision.HIGHEST
f32 = jnp.float32
BOTH = ("azim", "axial")
VMEM_LIMIT = 16 * 1024 * 1024


def lane_index():
    return lax.broadcasted_iota(jnp.int32, (8, 128), 1)


def row_index():
    return lax.broadcasted_iota(jnp.int32, (8, 128), 0)


def turn_lanes(tile, steps):
    steps = steps % 128
    return pltpu.roll(tile, steps, 1) if steps else tile


def turn_rows(tile, steps):
    steps = steps % 8
    return pltpu.roll(tile, steps, 0) if steps else tile


def swap_quads(tiles):
    lanes = lane_index()
    tiles = list(tiles)
    for bit, width in ((1, 4), (2, 8)):
        low = (lanes // width) % 2 == 0
        for first in range(4):
            if first & bit:
                continue
            one, two = tiles[first], tiles[first | bit]
            tiles[first] = jnp.where(low, one, turn_lanes(two, width))
            tiles[first | bit] = jnp.where(low, turn_lanes(one, -width), two)
    return tiles


def swap_rows(tile):
    lanes, rows = lane_index() // 16, row_index()
    for bit in (1, 2, 4):
        row_bit, lane_bit = (rows // bit) % 2, (lanes // bit) % 2
        up = turn_rows(turn_lanes(tile, 16 * bit), -bit)
        down = turn_rows(turn_lanes(tile, -16 * bit), bit)
        tile = jnp.where(row_bit == lane_bit, tile, jnp.where(row_bit == 0, up, down))
    return tile


def put_slots(out_ref, tiles, rows, base):
    zero = jnp.zeros((8, 128), f32)
    for half in range(2):
        group = [tiles[4 * half + x] if 4 * half + x < 6 else zero for x in range(4)]
        for quad, tile in enumerate(swap_quads(group)):
            out_ref[pl.ds(rows * quad + base + half, 8, stride=4 * rows), :] = tile


def get_slots(in_ref, rows, base):
    tiles = []
    for half in range(2):
        group = [in_ref[pl.ds(rows * quad + base + half, 8, stride=4 * rows), :] for quad in range(4)]
        tiles += swap_quads(group)
    return tiles[:6]


def put_cell_vector(out_ref, vector_ref, rows, base):
    put_slots(out_ref, [swap_rows(vector_ref[8 * t : 8 * t + 8, :]) for t in range(6)], rows, base)


def inverse_matvec(inverse_ref, vector_ref, out_ref):
    def step(group, totals):
        for inner in range(8):
            a = 8 * group + inner
            row = vector_ref[pl.ds(a, 1), :]
            totals = totals + inverse_ref[a].astype(f32) * row
        return totals

    out_ref[...] = lax.fori_loop(0, 6, step, jnp.zeros((48, 128), f32))


def pack_blocks(block_ref, out_ref, base, fetches, finish):
    quads = lane_index() // 4
    keeps = [(bit, (quads & bit) == 0) for bit in (1, 2, 4, 8, 16)]
    for group in range(9):
        ah_pair, bh_pair = group // 3, group % 3
        if bh_pair == 0:
            fetches[ah_pair].wait()
        items = [None] * 32
        for y in range(2):
            for p in range(8):
                wide = block_ref[16 * ah_pair + 8 * y + p, 16 * bh_pair : 16 * bh_pair + 16, :].astype(f32)
                for h in range(2):
                    i = 4 * p + 2 * y + h
                    items[i] = turn_lanes(turn_rows(wide[8 * h : 8 * h + 8], -p), 4 * i)
        for bit, keep in keeps:
            items = [jnp.where(keep, items[j], items[(j + bit) % 32]) for j in range(32)]
        for e in range(32):
            out_ref[e, base + 8 * group : base + 8 * group + 8, :] = turn_lanes(items[-e % 32], -4 * e)
        finish(base + 8 * group)


def fetch_thirds(block_hbm, block_ref, sems):
    copies = []
    for third in range(3):
        there = (slice(16 * third, 16 * third + 16), slice(None), slice(None))
        copies.append(pltpu.make_async_copy(block_hbm.at[there], block_ref.at[there], sems.at[third]))
    return copies


def unpack_cell(in_ref, base, out_ref, cell):
    for group in range(9):
        at = base + 8 * group
        parts = [in_ref[4 * cell + k, at : at + 8, :] for k in range(4)]
        for x, tile in enumerate(swap_quads(parts)):
            at = 8 * (4 * group + x)
            out_ref[cell, at : at + 8, :] = tile


def tile_at(ah, bh):
    return 4 * (3 * (ah // 2) + bh // 2) + 2 * (ah % 2) + bh % 2


def line_sweep(blocks_ref, const_ref, out_ref, reverse, beside=None):
    order = list(range(8))
    if reverse:
        order = order[::-1]
    state = None
    for turn in range(2):
        for n, cell in enumerate(order):
            if beside is not None:
                beside(turn, n)
            consts = [jnp.broadcast_to(const_ref[t, cell : cell + 1, :], (8, 128)) for t in range(6)]
            if state is None:
                state = consts
                continue
            products = line_product(blocks_ref, cell, state)
            state = [const - product for const, product in zip(consts, products)]
            if turn == 1:
                for t in range(6):
                    out_ref[t, cell : cell + 1, :] = state[t][0:1]


def stations_sum(tile):
    station = (lane_index() // 4) % 4
    before = jnp.where(station > 0, turn_lanes(tile, 4), 0.0)
    after = jnp.where(station < 3, turn_lanes(tile, -4), 0.0)
    return before + after


def first_send_kernel(
    forward_hbm, backward_hbm, inverse_hbm, rhs_hbm, coupling_hbm, out_hbm,
    f_ref, b_ref, i_ref, rhs_ref, coupling_ref, c_ref, vectors_ref, packed_ref, sems, out_sems,
):
    forward = fetch_thirds(forward_hbm, f_ref, sems.at[0])
    inverse = fetch_thirds(inverse_hbm, i_ref, sems.at[1])
    backward = fetch_thirds(backward_hbm, b_ref, sems.at[2])
    vectors = [
        pltpu.make_async_copy(source, target, sems.at[3, n])
        for n, (source, target) in enumerate(((rhs_hbm, rhs_ref), (coupling_hbm, coupling_ref)))
    ]
    for copy in forward + vectors + inverse + backward:
        copy.start()
    leaving = []

    def finish(row):
        there = (slice(None), slice(row, row + 8), slice(None))
        leaving.append(pltpu.make_async_copy(packed_ref.at[there], out_hbm.at[there], out_sems.at[row // 8]))
        leaving[-1].start()

    pack_blocks(f_ref, packed_ref, 0, forward, finish)
    for copy in vectors + inverse:
        copy.wait()
    inverse_matvec(i_ref, rhs_ref, c_ref)
    for n, vector_ref in enumerate((c_ref, rhs_ref, coupling_ref)):
        put_cell_vector(vectors_ref, vector_ref, 8, 2 * n)
    for quad in range(4):
        for last in (6, 7):
            vectors_ref[pl.ds(8 * quad + last, 8, stride=32), :] = jnp.zeros((8, 128), f32)
    for e in range(32):
        packed_ref[e, 144:152, :] = vectors_ref[8 * e : 8 * e + 8, :]
    finish(144)
    pack_blocks(b_ref, packed_ref, 72, backward, finish)
    for copy in leaving:
        copy.wait()


def first_kernel(slots_ref, *refs):
    own_ref, other_ref, forward_ref, backward_ref, first_ref, middle_ref, coupling_ref, packed_ref, c_ref, y_ref = refs
    for e in range(32):
        packed_ref[8 * e : 8 * e + 8, :] = slots_ref[e, 144:152, :]
    for t, tile in enumerate(get_slots(packed_ref, 8, 0)):
        c_ref[t] = tile

    def unpack(turn, n):
        if turn == 0:
            unpack_cell(slots_ref, 0, forward_ref, n)
        else:
            unpack_cell(slots_ref, 72, backward_ref, n)

    line_sweep(forward_ref, c_ref, y_ref, False, unpack)
    line_sweep(backward_ref, y_ref, first_ref, True)
    rhs = get_slots(packed_ref, 8, 2)
    coupling = get_slots(packed_ref, 8, 4)
    half, _ = half_position()
    for t in range(6):
        first = first_ref[t]
        middle = rhs[t] - first + coupling[t] * stations_sum(first)
        turned = turn_rows(middle, 4)
        other_ref[t] = jnp.where(half == 0, turned, middle)
        own_ref[t] = jnp.where(half == 0, middle, turned)
        middle_ref[t] = middle
        coupling_ref[t] = coupling[t]


def half_position():
    cell = lax.axis_index("azim")
    return cell // 4, (cell % 4) * 4 + lax.axis_index("axial")


def inverse_send_kernel(inverse_hbm, *refs):
    outs, (i_ref, packed_ref, fetch_sems, sems) = refs[1:17], refs[17:]
    fetches = fetch_thirds(inverse_hbm, i_ref, fetch_sems)
    for copy in fetches:
        copy.start()
    pack_blocks(i_ref, packed_ref, 0, fetches, lambda row: None)
    half, place = half_position()
    copies = []
    for d in range(16):
        target = place ^ d
        for n, source in enumerate((16 * half + target, 16 * (1 - half) + target)):
            copies.append(
                pltpu.make_async_copy(packed_ref.at[source], outs[d].at[pl.ds(72 * n, 72), :], sems.at[2 * d + n])
            )
            copies[-1].start()
    for copy in copies:
        copy.wait()


def inverse_get_kernel(*refs):
    ins, out_ref = refs[:4], refs[4]
    for lines in range(2):
        for group in range(9):
            at = 72 * lines + 8 * group
            for x, tile in enumerate(swap_quads([part[at : at + 8, :] for part in ins])):
                at = 8 * (4 * group + x)
                out_ref[lines, at : at + 8, :] = tile


def turn_stations(tile, number):
    lanes = lane_index()
    for bit, width in ((1, 4), (2, 8)):
        other = jnp.where((lanes & width) == 0, turn_lanes(tile, -width), turn_lanes(tile, width))
        tile = jnp.where((number & bit) == 0, tile, other)
    return tile


def line_product(blocks_ref, cell, state):
    products = []
    for bh in range(6):
        total = None
        for ah in range(6):
            at = 8 * tile_at(ah, bh)
            term = blocks_ref[cell, at : at + 8, :] * state[ah]
            total = term if total is None else total + term
        total = pltpu.roll(total, 0, 1, stride=16, stride_axis=0)
        for span in (4, 2, 1):
            total = total + turn_rows(total, span)
        products.append(total)
    return products


def half_inverse_kernel(lines, vector_ref, *refs):
    blocks, (out_ref, turned_ref) = refs[:4], refs[4:]
    _, place = half_position()
    cell, station = place // 4, place % 4
    for t in range(6):
        turned_ref[t] = turn_stations(vector_ref[t], station)
    rows = row_index()
    totals = [jnp.zeros((8, 128), f32)] * 6
    for n in range(4):
        state = [jnp.broadcast_to(turned_ref[t, pl.ds(cell ^ n, 1), :], (8, 128)) for t in range(6)]
        for t, product in enumerate(line_product(blocks[n], lines, state)):
            totals[t] = jnp.where(rows == (cell ^ n), product, totals[t])
    for t in range(6):
        out_ref[t] = turn_stations(totals[t], station)


def second_kernel(
    own_ref, other_ref, forward_ref, backward_ref, first_ref, middle_ref, coupling_ref, out_ref, c_ref, y_ref, second_ref
):
    half, _ = half_position()
    low = row_index() < 4
    for t in range(6):
        tile = jnp.where(low, own_ref[t], turn_rows(other_ref[t], 4))
        c_ref[t] = jnp.where(half == 0, tile, turn_rows(tile, 4))
    line_sweep(forward_ref, c_ref, y_ref, False)
    line_sweep(backward_ref, y_ref, second_ref, True)
    correction, remaining = [], []
    for t in range(6):
        second = second_ref[t]
        correction.append(first_ref[t] + second)
        remaining.append(middle_ref[t] - second + coupling_ref[t] * stations_sum(second))
    put_slots(out_ref, correction, 4, 0)
    put_slots(out_ref, remaining, 4, 2)


def last_kernel(slots_ref, correction_ref, remaining_ref):
    for out_ref, base in ((correction_ref, 0), (remaining_ref, 2)):
        for t, tile in enumerate(get_slots(slots_ref, 4, base)):
            out_ref[8 * t : 8 * t + 8, :] = swap_rows(tile)


def shaped(*sizes):
    return jax.ShapeDtypeStruct(sizes, f32)


def call(kernel, outs, scratch=()):
    return pl.pallas_call(
        kernel,
        out_shape=outs,
        scratch_shapes=[pltpu.VMEM(sizes, f32) for sizes in scratch],
        compiler_params=pltpu.CompilerParams(vmem_limit_bytes=VMEM_LIMIT),
    )


def exchange(slots, rows):
    moved = lax.all_to_all(slots.reshape(32, rows, 128), BOTH, 0, 0, tiled=True)
    return moved.reshape(32 * rows, 128)


def line_plan(rhs, coupling, fwd_coupling, bwd_coupling, block_inverse):
    source, coupling_field = rhs.reshape(48, 128), coupling.reshape(48, 128)
    forward_blocks = fwd_coupling.reshape(48, 48, 128)
    backward_blocks = bwd_coupling.reshape(48, 48, 128)
    inverse_blocks = block_inverse.reshape(48, 48, 128)
    tiles, held = shaped(6, 8, 128), shaped(8, 288, 128)
    blocks = pltpu.VMEM((48, 48, 128), jnp.bfloat16)
    vector = pltpu.VMEM((48, 128), f32)

    slots = pl.pallas_call(
        first_send_kernel,
        out_shape=pltpu.HBM((32, 152, 128), f32),
        in_specs=[pl.BlockSpec(memory_space=pltpu.HBM)] * 5,
        out_specs=pl.BlockSpec(memory_space=pltpu.HBM),
        scratch_shapes=[blocks, blocks, blocks, vector, vector, vector]
        + [
            pltpu.VMEM((256, 128), f32),
            pltpu.VMEM((32, 152, 128), f32),
            pltpu.SemaphoreType.DMA((4, 3)),
            pltpu.SemaphoreType.DMA((19,)),
        ],
        compiler_params=pltpu.CompilerParams(vmem_limit_bytes=VMEM_LIMIT),
    )(*[
        pltpu.with_memory_space_constraint(array, pltpu.HBM)
        for array in (forward_blocks, backward_blocks, inverse_blocks, source, coupling_field)
    ])
    slots, inverse_blocks = lax.optimization_barrier((slots, inverse_blocks))
    early = lax.ppermute(source[:8], BOTH, [(e, e ^ 16) for e in range(32)])
    slots = lax.all_to_all(slots, BOTH, 0, 0, tiled=True)

    parts = pl.pallas_call(
        inverse_send_kernel,
        out_shape=[shaped(144, 128)] * 16,
        in_specs=[pl.BlockSpec(memory_space=pltpu.HBM), pl.BlockSpec(memory_space=pl.ANY)],
        out_specs=[pl.BlockSpec(memory_space=pltpu.HBM)] * 16,
        scratch_shapes=[
            blocks, pltpu.VMEM((32, 72, 128), f32), pltpu.SemaphoreType.DMA((3,)), pltpu.SemaphoreType.DMA((32,))
        ],
        compiler_params=pltpu.CompilerParams(vmem_limit_bytes=VMEM_LIMIT),
    )(pltpu.with_memory_space_constraint(inverse_blocks, pltpu.HBM), early)
    parts = [parts[0]] + [lax.ppermute(parts[d], BOTH, [(e, e ^ d) for e in range(32)]) for d in range(1, 16)]
    inverse = [call(inverse_get_kernel, shaped(2, 288, 128))(*parts[4 * n : 4 * n + 4]) for n in range(4)]

    own, other, forward, backward, first, middle, coupling_lines = call(
        first_kernel, (tiles, tiles, held, held, tiles, tiles, tiles), [(256, 128), (6, 8, 128), (6, 8, 128)]
    )(slots)

    def with_partner(vector):
        return lax.ppermute(vector, BOTH, [(e, e ^ 16) for e in range(32)])

    other = with_partner(other)
    own = call(functools.partial(half_inverse_kernel, 0), tiles, [(6, 8, 128)])(own, *inverse)
    other = call(functools.partial(half_inverse_kernel, 1), tiles, [(6, 8, 128)])(other, *inverse)
    other = with_partner(other)
    slots = call(second_kernel, shaped(128, 128), [(6, 8, 128)] * 3)(
        own, other, forward, backward, first, middle, coupling_lines
    )
    slots = exchange(slots, 4)
    correction, remaining = call(last_kernel, (shaped(48, 128), shaped(48, 128)))(slots)
    return correction.reshape(rhs.shape), remaining.reshape(rhs.shape)


def from_behind(value, axis, steps):
    count = lax.axis_size(axis)
    initial, last = (max(0, -steps), min(count, count - steps))
    return lax.ppermute(value, axis, [(source, source + steps) for source in range(initial, last)])


def from_root(shard, axis, root):
    mine = lax.axis_index(axis) == root
    return lax.psum(jnp.where(mine, shard, jnp.zeros_like(shard)), axis)


def extended(block, sides, width):
    for axis, dim in sides:
        count = lax.axis_size(axis)
        forward = [(i, i + 1) for i in range(count - 1)]
        backward = [(target, source) for source, target in forward]
        low = lax.ppermute(
            lax.slice_in_dim(block, block.shape[dim] - width, None, axis=dim), axis, forward
        )
        high = lax.ppermute(lax.slice_in_dim(block, 0, width, axis=dim), axis, backward)
        block = jnp.concatenate([low, block, high], axis=dim)
    return block


def cell_stride(one_block, carried, const_term):
    return const_term - jnp.einsum(
        "abl,al->bl", one_block.astype(jnp.float32), carried, precision=highest
    )


def compose_cells(blocks, sequence):
    running = None
    for position in sequence:
        one_block = blocks[position].astype(jnp.float32)
        running = -jnp.swapaxes(one_block, 0, 1)
    return running


def doubling_maps(local_map, reverse):
    size = lax.axis_size("azim")
    index = lax.axis_index("azim")
    levels = []
    current = local_map
    distance = 1
    while distance < size:
        if reverse:
            moved = from_behind(current, "azim", -distance)
            exists = index + distance < size
        else:
            moved = from_behind(current, "azim", distance)
            exists = index >= distance
        levels.append((current, distance))
        current = jnp.where(
            exists, jnp.einsum("bcl,cal->bal", current, moved, precision=highest), current
        )
        distance = distance * 2
    return (levels, current)


def doubling_entries(map_levels, local_offset, reverse):
    levels, final_map = map_levels
    size = lax.axis_size("azim")
    index = lax.axis_index("azim")
    running = local_offset
    for current, distance in levels:
        if reverse:
            moved = from_behind(running, "azim", -distance)
        else:
            moved = from_behind(running, "azim", distance)
        running = jnp.einsum("bcl,cl->bl", current, moved, precision=highest) + running
    if reverse:
        wrapped = from_root(running, "azim", 0)
    else:
        wrapped = from_root(running, "azim", size - 1)
    leaving = jnp.einsum("bcl,cl->bl", final_map, wrapped, precision=highest) + running
    if reverse:
        shifted = from_behind(leaving, "azim", -1)
        first_device = index == size - 1
    else:
        shifted = from_behind(leaving, "azim", 1)
        first_device = index == 0
    return jnp.where(first_device, wrapped, shifted)


def sweep(blocks, consts, map_levels, reverse):
    cell_count = blocks.shape[0]
    sequence = list(range(cell_count))
    if reverse:
        sequence = sequence[::-1]
    carried = jnp.zeros(consts.shape[1:], jnp.float32)
    for position in sequence:
        carried = cell_stride(blocks[position], carried, consts[position])
    local_offset = carried
    incoming_maps = doubling_entries(map_levels, local_offset, reverse)
    outputs = [None] * cell_count
    carried = incoming_maps
    for position in sequence:
        carried = cell_stride(blocks[position], carried, consts[position])
        outputs[position] = carried
    return jnp.stack(outputs)


def on_device(rhs, coupling, fwd_coupling, bwd_coupling, block_inverse):
    cell_count, block_width, _, position_total, radial_count = fwd_coupling.shape
    line_count = position_total * radial_count
    forward_blocks = fwd_coupling.reshape(cell_count, block_width, block_width, line_count)
    backward_blocks = bwd_coupling.reshape(cell_count, block_width, block_width, line_count)
    inverse_blocks = block_inverse.reshape(cell_count, block_width, block_width, line_count)
    source = rhs.reshape(cell_count, block_width, line_count)
    coupling_field = coupling.reshape(cell_count, block_width, line_count)
    forward_map = compose_cells(forward_blocks, list(range(cell_count)))
    backward_map = compose_cells(backward_blocks, list(range(cell_count))[::-1])
    forward_levels = None
    backward_levels = None
    forward_levels = doubling_maps(forward_map, False)
    backward_levels = doubling_maps(backward_map, True)

    def precondition(vector):
        consts = jnp.stack(
            [
                jnp.einsum(
                    "abl,al->bl",
                    inverse_blocks[0].astype(jnp.float32),
                    vector[0],
                    precision=highest,
                )
            ]
        )
        forward = sweep(forward_blocks, consts, forward_levels, False)
        return sweep(backward_blocks, forward, backward_levels, True)

    def stations_sum(field):
        grid = field.reshape(cell_count, block_width, position_total, radial_count)
        padded = extended(grid, (("axial", 2),), 1)
        return (padded[:, :, :-2] + padded[:, :, 2:]).reshape(cell_count, block_width, line_count)

    applied_once = precondition(source)
    middle = source - applied_once + coupling_field * stations_sum(applied_once)
    second = precondition(middle)
    correction = applied_once + second
    remaining = middle - second + coupling_field * stations_sum(second)
    return (correction.reshape(rhs.shape), remaining.reshape(rhs.shape))


def solution(mesh):
    cells, stations = mesh.shape["azim"], mesh.shape["axial"]

    def on_each(rhs, coupling, fwd_coupling, bwd_coupling, block_inverse):
        local = fwd_coupling.shape
        if (cells, stations) == (8, 4) and local == (1, 48, 48, 1, 128):
            return line_plan(rhs, coupling, fwd_coupling, bwd_coupling, block_inverse)
        return on_device(rhs, coupling, fwd_coupling, bwd_coupling, block_inverse)

    return jax.shard_map(
        on_each,
        mesh=mesh,
        in_specs=(
            P("azim", None, "axial", None),
            P("azim", None, "axial", None),
            P("azim", None, None, "axial", None),
            P("azim", None, None, "axial", None),
            P("azim", None, None, "axial", None),
        ),
        out_specs=(P("azim", None, "axial", None), P("azim", None, "axial", None)),
        check_vma=False,
    )
```

```python
import functools

import jax
import jax.numpy as jnp
from jax import lax
from jax.experimental import pallas as pl
from jax.experimental.pallas import tpu as pltpu
from jax.sharding import PartitionSpec as P

highest = lax.Precision.HIGHEST
f32 = jnp.float32
BOTH = ("azim", "axial")
VMEM_LIMIT = 16 * 1024 * 1024


def lane_index():
    return lax.broadcasted_iota(jnp.int32, (8, 128), 1)


def row_index():
    return lax.broadcasted_iota(jnp.int32, (8, 128), 0)


def turn_lanes(tile, steps):
    steps = steps % 128
    return pltpu.roll(tile, steps, 1) if steps else tile


def turn_rows(tile, steps):
    steps = steps % 8
    return pltpu.roll(tile, steps, 0) if steps else tile


def swap_quads(tiles):
    lanes = lane_index()
    tiles = list(tiles)
    for bit, width in ((1, 4), (2, 8)):
        low = (lanes // width) % 2 == 0
        for first in range(4):
            if first & bit:
                continue
            one, two = tiles[first], tiles[first | bit]
            tiles[first] = jnp.where(low, one, turn_lanes(two, width))
            tiles[first | bit] = jnp.where(low, turn_lanes(one, -width), two)
    return tiles


def swap_rows(tile):
    lanes, rows = lane_index() // 16, row_index()
    for bit in (1, 2, 4):
        row_bit, lane_bit = (rows // bit) % 2, (lanes // bit) % 2
        up = turn_rows(turn_lanes(tile, 16 * bit), -bit)
        down = turn_rows(turn_lanes(tile, -16 * bit), bit)
        tile = jnp.where(row_bit == lane_bit, tile, jnp.where(row_bit == 0, up, down))
    return tile


def put_slots(out_ref, tiles, rows, base):
    zero = jnp.zeros((8, 128), f32)
    for half in range(2):
        group = [tiles[4 * half + x] if 4 * half + x < 6 else zero for x in range(4)]
        for quad, tile in enumerate(swap_quads(group)):
            out_ref[pl.ds(rows * quad + base + half, 8, stride=4 * rows), :] = tile


def get_slots(in_ref, rows, base):
    tiles = []
    for half in range(2):
        group = [in_ref[pl.ds(rows * quad + base + half, 8, stride=4 * rows), :] for quad in range(4)]
        tiles += swap_quads(group)
    return tiles[:6]


def put_cell_vector(out_ref, vector_ref, rows, base):
    put_slots(out_ref, [swap_rows(vector_ref[8 * t : 8 * t + 8, :]) for t in range(6)], rows, base)


def inverse_matvec(inverse_ref, vector_ref, out_ref):
    def step(group, totals):
        for inner in range(8):
            a = 8 * group + inner
            row = vector_ref[pl.ds(a, 1), :]
            totals = totals + inverse_ref[a].astype(f32) * row
        return totals

    out_ref[...] = lax.fori_loop(0, 6, step, jnp.zeros((48, 128), f32))


def pack_blocks(block_ref, out_ref, base, fetches, finish):
    quads = lane_index() // 4
    keeps = [(bit, (quads & bit) == 0) for bit in (1, 2, 4, 8, 16)]
    for group in range(9):
        ah_pair, bh_pair = group // 3, group % 3
        if bh_pair == 0:
            fetches[ah_pair].wait()
        items = [None] * 32
        for y in range(2):
            for p in range(8):
                wide = block_ref[16 * ah_pair + 8 * y + p, 16 * bh_pair : 16 * bh_pair + 16, :].astype(f32)
                for h in range(2):
                    i = 4 * p + 2 * y + h
                    items[i] = turn_lanes(turn_rows(wide[8 * h : 8 * h + 8], -p), 4 * i)
        for bit, keep in keeps:
            items = [jnp.where(keep, items[j], items[(j + bit) % 32]) for j in range(32)]
        for e in range(32):
            out_ref[e, base + 8 * group : base + 8 * group + 8, :] = turn_lanes(items[-e % 32], -4 * e)
        finish(base + 8 * group)


def fetch_thirds(block_hbm, block_ref, sems):
    copies = []
    for third in range(3):
        there = (slice(16 * third, 16 * third + 16), slice(None), slice(None))
        copies.append(pltpu.make_async_copy(block_hbm.at[there], block_ref.at[there], sems.at[third]))
    return copies


def unpack_cell(in_ref, base, out_ref, cell):
    for group in range(9):
        at = base + 8 * group
        parts = [in_ref[4 * cell + k, at : at + 8, :] for k in range(4)]
        for x, tile in enumerate(swap_quads(parts)):
            at = 8 * (4 * group + x)
            out_ref[cell, at : at + 8, :] = tile


def tile_at(ah, bh):
    return 4 * (3 * (ah // 2) + bh // 2) + 2 * (ah % 2) + bh % 2


def line_sweep(blocks_ref, const_ref, out_ref, reverse, beside=None):
    order = list(range(8))
    if reverse:
        order = order[::-1]
    state = None
    for turn in range(2):
        for n, cell in enumerate(order):
            if beside is not None:
                beside(turn, n)
            consts = [jnp.broadcast_to(const_ref[t, cell : cell + 1, :], (8, 128)) for t in range(6)]
            if state is None:
                state = consts
                continue
            products = line_product(blocks_ref, cell, state)
            state = [const - product for const, product in zip(consts, products)]
            if turn == 1:
                for t in range(6):
                    out_ref[t, cell : cell + 1, :] = state[t][0:1]


def stations_sum(tile):
    station = (lane_index() // 4) % 4
    before = jnp.where(station > 0, turn_lanes(tile, 4), 0.0)
    after = jnp.where(station < 3, turn_lanes(tile, -4), 0.0)
    return before + after


def first_send_kernel(
    forward_hbm, backward_hbm, inverse_hbm, rhs_hbm, coupling_hbm, out_hbm,
    f_ref, b_ref, i_ref, rhs_ref, coupling_ref, c_ref, vectors_ref, packed_ref, sems, out_sems,
):
    forward = fetch_thirds(forward_hbm, f_ref, sems.at[0])
    inverse = fetch_thirds(inverse_hbm, i_ref, sems.at[1])
    backward = fetch_thirds(backward_hbm, b_ref, sems.at[2])
    vectors = [
        pltpu.make_async_copy(source, target, sems.at[3, n])
        for n, (source, target) in enumerate(((rhs_hbm, rhs_ref), (coupling_hbm, coupling_ref)))
    ]
    for copy in forward + vectors + inverse + backward:
        copy.start()
    leaving = []

    def finish(row):
        there = (slice(None), slice(row, row + 8), slice(None))
        leaving.append(pltpu.make_async_copy(packed_ref.at[there], out_hbm.at[there], out_sems.at[row // 8]))
        leaving[-1].start()

    pack_blocks(f_ref, packed_ref, 0, forward, finish)
    for copy in vectors + inverse:
        copy.wait()
    inverse_matvec(i_ref, rhs_ref, c_ref)
    for n, vector_ref in enumerate((c_ref, rhs_ref, coupling_ref)):
        put_cell_vector(vectors_ref, vector_ref, 8, 2 * n)
    for quad in range(4):
        for last in (6, 7):
            vectors_ref[pl.ds(8 * quad + last, 8, stride=32), :] = jnp.zeros((8, 128), f32)
    for e in range(32):
        packed_ref[e, 144:152, :] = vectors_ref[8 * e : 8 * e + 8, :]
    finish(144)
    pack_blocks(b_ref, packed_ref, 72, backward, finish)
    for copy in leaving:
        copy.wait()


def first_kernel(slots_ref, *refs):
    own_ref, other_ref, forward_ref, backward_ref, first_ref, middle_ref, coupling_ref, packed_ref, c_ref, y_ref = refs
    for e in range(32):
        packed_ref[8 * e : 8 * e + 8, :] = slots_ref[e, 144:152, :]
    for t, tile in enumerate(get_slots(packed_ref, 8, 0)):
        c_ref[t] = tile

    def unpack(turn, n):
        if turn == 0:
            unpack_cell(slots_ref, 0, forward_ref, n)
        else:
            unpack_cell(slots_ref, 72, backward_ref, n)

    line_sweep(forward_ref, c_ref, y_ref, False, unpack)
    line_sweep(backward_ref, y_ref, first_ref, True)
    rhs = get_slots(packed_ref, 8, 2)
    coupling = get_slots(packed_ref, 8, 4)
    half, _ = half_position()
    low = row_index() < 4
    own, other = [], []
    for t in range(6):
        first = first_ref[t]
        middle = rhs[t] - first + coupling[t] * stations_sum(first)
        turned = turn_rows(middle, 4)
        other.append(jnp.where(half == 0, turned, middle))
        own.append(jnp.where(half == 0, middle, turned))
        middle_ref[t] = middle
        coupling_ref[t] = coupling[t]
    for u in range(3):
        other_ref[u] = jnp.where(low, other[2 * u], turn_rows(other[2 * u + 1], 4))
        own_ref[u] = jnp.where(low, own[2 * u], turn_rows(own[2 * u + 1], 4))


def half_position():
    cell = lax.axis_index("azim")
    return cell // 4, (cell % 4) * 4 + lax.axis_index("axial")


def inverse_send_kernel(inverse_hbm, *refs):
    outs, (i_ref, packed_ref, fetch_sems, sems) = refs[:16], refs[16:]
    fetches = fetch_thirds(inverse_hbm, i_ref, fetch_sems)
    for copy in fetches:
        copy.start()
    pack_blocks(i_ref, packed_ref, 0, fetches, lambda row: None)
    half, place = half_position()
    copies = []
    for d in range(16):
        target = place ^ d
        for n, source in enumerate((16 * half + target, 16 * (1 - half) + target)):
            copies.append(
                pltpu.make_async_copy(packed_ref.at[source], outs[d].at[pl.ds(72 * n, 72), :], sems.at[2 * d + n])
            )
            copies[-1].start()
    for copy in copies:
        copy.wait()


def inverse_get_kernel(*refs):
    ins, out_ref = refs[:16], refs[16]
    for n in range(4):
        for lines in range(2):
            for group in range(9):
                at = 72 * lines + 8 * group
                for x, tile in enumerate(swap_quads([part[at : at + 8, :] for part in ins[4 * n : 4 * n + 4]])):
                    at = 8 * (4 * group + x)
                    out_ref[n, lines, at : at + 8, :] = tile


def turn_stations(tile, number):
    lanes = lane_index()
    for bit, width in ((1, 4), (2, 8)):
        other = jnp.where((lanes & width) == 0, turn_lanes(tile, -width), turn_lanes(tile, width))
        tile = jnp.where((number & bit) == 0, tile, other)
    return tile


def line_product(blocks_ref, cell, state):
    products = []
    for bh in range(6):
        total = None
        for ah in range(6):
            at = 8 * tile_at(ah, bh)
            term = blocks_ref[cell, at : at + 8, :] * state[ah]
            total = term if total is None else total + term
        total = pltpu.roll(total, 0, 1, stride=16, stride_axis=0)
        for span in (4, 2, 1):
            total = total + turn_rows(total, span)
        products.append(total)
    return products


def half_inverse_kernel(lines, vector_ref, blocks_ref, out_ref, turned_ref):
    _, place = half_position()
    cell, station = place // 4, place % 4
    for u in range(3):
        turned_ref[u] = turn_stations(vector_ref[u], station)
    rows = row_index()
    totals = [jnp.zeros((8, 128), f32)] * 3
    for n in range(4):
        state = [
            jnp.broadcast_to(turned_ref[t // 2, pl.ds(4 * (t % 2) + (cell ^ n), 1), :], (8, 128)) for t in range(6)
        ]
        for t, product in enumerate(line_product(blocks_ref.at[n], lines, state)):
            totals[t // 2] = jnp.where(rows == 4 * (t % 2) + (cell ^ n), product, totals[t // 2])
    for u in range(3):
        out_ref[u] = turn_stations(totals[u], station)


def second_kernel(
    own_ref, other_ref, forward_ref, backward_ref, first_ref, middle_ref, coupling_ref, out_ref, c_ref, y_ref, second_ref
):
    half, _ = half_position()
    low = row_index() < 4
    for t in range(6):
        own, other = own_ref[t // 2], other_ref[t // 2]
        if t % 2:
            own = turn_rows(own, 4)
        else:
            other = turn_rows(other, 4)
        tile = jnp.where(low, own, other)
        c_ref[t] = jnp.where(half == 0, tile, turn_rows(tile, 4))
    line_sweep(forward_ref, c_ref, y_ref, False)
    line_sweep(backward_ref, y_ref, second_ref, True)
    correction, remaining = [], []
    for t in range(6):
        second = second_ref[t]
        correction.append(first_ref[t] + second)
        remaining.append(middle_ref[t] - second + coupling_ref[t] * stations_sum(second))
    put_slots(out_ref, correction, 4, 0)
    put_slots(out_ref, remaining, 4, 2)


def last_kernel(slots_ref, correction_ref, remaining_ref):
    for out_ref, base in ((correction_ref, 0), (remaining_ref, 2)):
        for t, tile in enumerate(get_slots(slots_ref, 4, base)):
            out_ref[8 * t : 8 * t + 8, :] = swap_rows(tile)


def shaped(*sizes):
    return jax.ShapeDtypeStruct(sizes, f32)


def call(kernel, outs, scratch=()):
    return pl.pallas_call(
        kernel,
        out_shape=outs,
        scratch_shapes=[pltpu.VMEM(sizes, f32) for sizes in scratch],
        compiler_params=pltpu.CompilerParams(vmem_limit_bytes=VMEM_LIMIT),
    )


def exchange(slots, rows):
    moved = lax.all_to_all(slots.reshape(32, rows, 128), BOTH, 0, 0, tiled=True)
    return moved.reshape(32 * rows, 128)


def line_plan(rhs, coupling, fwd_coupling, bwd_coupling, block_inverse):
    source, coupling_field = rhs.reshape(48, 128), coupling.reshape(48, 128)
    forward_blocks = fwd_coupling.reshape(48, 48, 128)
    backward_blocks = bwd_coupling.reshape(48, 48, 128)
    inverse_blocks = block_inverse.reshape(48, 48, 128)
    tiles, pairs, held = shaped(6, 8, 128), shaped(3, 8, 128), shaped(8, 288, 128)
    blocks = pltpu.VMEM((48, 48, 128), jnp.bfloat16)
    vector = pltpu.VMEM((48, 128), f32)

    slots = pl.pallas_call(
        first_send_kernel,
        out_shape=pltpu.HBM((32, 152, 128), f32),
        in_specs=[pl.BlockSpec(memory_space=pltpu.HBM)] * 5,
        out_specs=pl.BlockSpec(memory_space=pltpu.HBM),
        scratch_shapes=[blocks, blocks, blocks, vector, vector, vector]
        + [
            pltpu.VMEM((256, 128), f32),
            pltpu.VMEM((32, 152, 128), f32),
            pltpu.SemaphoreType.DMA((4, 3)),
            pltpu.SemaphoreType.DMA((19,)),
        ],
        compiler_params=pltpu.CompilerParams(vmem_limit_bytes=VMEM_LIMIT),
    )(*[
        pltpu.with_memory_space_constraint(array, pltpu.HBM)
        for array in (forward_blocks, backward_blocks, inverse_blocks, source, coupling_field)
    ])
    slots, inverse_blocks = lax.optimization_barrier((slots, inverse_blocks))
    slots = lax.all_to_all(slots, BOTH, 0, 0, tiled=True)

    parts = pl.pallas_call(
        inverse_send_kernel,
        out_shape=[shaped(144, 128)] * 16,
        in_specs=[pl.BlockSpec(memory_space=pltpu.HBM)],
        out_specs=[pl.BlockSpec(memory_space=pltpu.HBM)] * 16,
        scratch_shapes=[
            blocks, pltpu.VMEM((32, 72, 128), f32), pltpu.SemaphoreType.DMA((3,)), pltpu.SemaphoreType.DMA((32,))
        ],
        compiler_params=pltpu.CompilerParams(vmem_limit_bytes=VMEM_LIMIT),
    )(pltpu.with_memory_space_constraint(inverse_blocks, pltpu.HBM))
    parts = [parts[0]] + [lax.ppermute(parts[d], BOTH, [(e, e ^ d) for e in range(32)]) for d in range(1, 16)]
    inverse = call(inverse_get_kernel, shaped(4, 2, 288, 128))(*parts)

    own, other, forward, backward, first, middle, coupling_lines = call(
        first_kernel, (pairs, pairs, held, held, tiles, tiles, tiles), [(256, 128), (6, 8, 128), (6, 8, 128)]
    )(slots)

    def with_partner(vector):
        return lax.ppermute(vector, BOTH, [(e, e ^ 16) for e in range(32)])

    other = with_partner(other)
    own = call(functools.partial(half_inverse_kernel, 0), pairs, [(3, 8, 128)])(own, inverse)
    other = call(functools.partial(half_inverse_kernel, 1), pairs, [(3, 8, 128)])(other, inverse)
    other = with_partner(other)
    slots = call(second_kernel, shaped(128, 128), [(6, 8, 128)] * 3)(
        own, other, forward, backward, first, middle, coupling_lines
    )
    slots = exchange(slots, 4)
    correction, remaining = call(last_kernel, (shaped(48, 128), shaped(48, 128)))(slots)
    return correction.reshape(rhs.shape), remaining.reshape(rhs.shape)


def from_behind(value, axis, steps):
    count = lax.axis_size(axis)
    initial, last = (max(0, -steps), min(count, count - steps))
    return lax.ppermute(value, axis, [(source, source + steps) for source in range(initial, last)])


def from_root(shard, axis, root):
    mine = lax.axis_index(axis) == root
    return lax.psum(jnp.where(mine, shard, jnp.zeros_like(shard)), axis)


def extended(block, sides, width):
    for axis, dim in sides:
        count = lax.axis_size(axis)
        forward = [(i, i + 1) for i in range(count - 1)]
        backward = [(target, source) for source, target in forward]
        low = lax.ppermute(
            lax.slice_in_dim(block, block.shape[dim] - width, None, axis=dim), axis, forward
        )
        high = lax.ppermute(lax.slice_in_dim(block, 0, width, axis=dim), axis, backward)
        block = jnp.concatenate([low, block, high], axis=dim)
    return block


def cell_stride(one_block, carried, const_term):
    return const_term - jnp.einsum(
        "abl,al->bl", one_block.astype(jnp.float32), carried, precision=highest
    )


def compose_cells(blocks, sequence):
    running = None
    for position in sequence:
        one_block = blocks[position].astype(jnp.float32)
        running = -jnp.swapaxes(one_block, 0, 1)
    return running


def doubling_maps(local_map, reverse):
    size = lax.axis_size("azim")
    index = lax.axis_index("azim")
    levels = []
    current = local_map
    distance = 1
    while distance < size:
        if reverse:
            moved = from_behind(current, "azim", -distance)
            exists = index + distance < size
        else:
            moved = from_behind(current, "azim", distance)
            exists = index >= distance
        levels.append((current, distance))
        current = jnp.where(
            exists, jnp.einsum("bcl,cal->bal", current, moved, precision=highest), current
        )
        distance = distance * 2
    return (levels, current)


def doubling_entries(map_levels, local_offset, reverse):
    levels, final_map = map_levels
    size = lax.axis_size("azim")
    index = lax.axis_index("azim")
    running = local_offset
    for current, distance in levels:
        if reverse:
            moved = from_behind(running, "azim", -distance)
        else:
            moved = from_behind(running, "azim", distance)
        running = jnp.einsum("bcl,cl->bl", current, moved, precision=highest) + running
    if reverse:
        wrapped = from_root(running, "azim", 0)
    else:
        wrapped = from_root(running, "azim", size - 1)
    leaving = jnp.einsum("bcl,cl->bl", final_map, wrapped, precision=highest) + running
    if reverse:
        shifted = from_behind(leaving, "azim", -1)
        first_device = index == size - 1
    else:
        shifted = from_behind(leaving, "azim", 1)
        first_device = index == 0
    return jnp.where(first_device, wrapped, shifted)


def sweep(blocks, consts, map_levels, reverse):
    cell_count = blocks.shape[0]
    sequence = list(range(cell_count))
    if reverse:
        sequence = sequence[::-1]
    carried = jnp.zeros(consts.shape[1:], jnp.float32)
    for position in sequence:
        carried = cell_stride(blocks[position], carried, consts[position])
    local_offset = carried
    incoming_maps = doubling_entries(map_levels, local_offset, reverse)
    outputs = [None] * cell_count
    carried = incoming_maps
    for position in sequence:
        carried = cell_stride(blocks[position], carried, consts[position])
        outputs[position] = carried
    return jnp.stack(outputs)


def on_device(rhs, coupling, fwd_coupling, bwd_coupling, block_inverse):
    cell_count, block_width, _, position_total, radial_count = fwd_coupling.shape
    line_count = position_total * radial_count
    forward_blocks = fwd_coupling.reshape(cell_count, block_width, block_width, line_count)
    backward_blocks = bwd_coupling.reshape(cell_count, block_width, block_width, line_count)
    inverse_blocks = block_inverse.reshape(cell_count, block_width, block_width, line_count)
    source = rhs.reshape(cell_count, block_width, line_count)
    coupling_field = coupling.reshape(cell_count, block_width, line_count)
    forward_map = compose_cells(forward_blocks, list(range(cell_count)))
    backward_map = compose_cells(backward_blocks, list(range(cell_count))[::-1])
    forward_levels = None
    backward_levels = None
    forward_levels = doubling_maps(forward_map, False)
    backward_levels = doubling_maps(backward_map, True)

    def precondition(vector):
        consts = jnp.stack(
            [
                jnp.einsum(
                    "abl,al->bl",
                    inverse_blocks[0].astype(jnp.float32),
                    vector[0],
                    precision=highest,
                )
            ]
        )
        forward = sweep(forward_blocks, consts, forward_levels, False)
        return sweep(backward_blocks, forward, backward_levels, True)

    def stations_sum(field):
        grid = field.reshape(cell_count, block_width, position_total, radial_count)
        padded = extended(grid, (("axial", 2),), 1)
        return (padded[:, :, :-2] + padded[:, :, 2:]).reshape(cell_count, block_width, line_count)

    applied_once = precondition(source)
    middle = source - applied_once + coupling_field * stations_sum(applied_once)
    second = precondition(middle)
    correction = applied_once + second
    remaining = middle - second + coupling_field * stations_sum(second)
    return (correction.reshape(rhs.shape), remaining.reshape(rhs.shape))


def solution(mesh):
    cells, stations = mesh.shape["azim"], mesh.shape["axial"]

    def on_each(rhs, coupling, fwd_coupling, bwd_coupling, block_inverse):
        local = fwd_coupling.shape
        if (cells, stations) == (8, 4) and local == (1, 48, 48, 1, 128):
            return line_plan(rhs, coupling, fwd_coupling, bwd_coupling, block_inverse)
        return on_device(rhs, coupling, fwd_coupling, bwd_coupling, block_inverse)

    return jax.shard_map(
        on_each,
        mesh=mesh,
        in_specs=(
            P("azim", None, "axial", None),
            P("azim", None, "axial", None),
            P("azim", None, None, "axial", None),
            P("azim", None, None, "axial", None),
            P("azim", None, None, "axial", None),
        ),
        out_specs=(P("azim", None, "axial", None), P("azim", None, "axial", None)),
        check_vma=False,
    )
```

```python
import functools

import jax
import jax.numpy as jnp
from jax import lax
from jax.experimental import pallas as pl
from jax.experimental.pallas import tpu as pltpu
from jax.sharding import PartitionSpec as P

highest = lax.Precision.HIGHEST
f32 = jnp.float32
BOTH = ("azim", "axial")
VMEM_LIMIT = 16 * 1024 * 1024


def lane_index():
    return lax.broadcasted_iota(jnp.int32, (8, 128), 1)


def row_index():
    return lax.broadcasted_iota(jnp.int32, (8, 128), 0)


def turn_lanes(tile, steps):
    steps = steps % 128
    return pltpu.roll(tile, steps, 1) if steps else tile


def turn_rows(tile, steps):
    steps = steps % 8
    return pltpu.roll(tile, steps, 0) if steps else tile


def swap_quads(tiles):
    lanes = lane_index()
    tiles = list(tiles)
    for bit, width in ((1, 4), (2, 8)):
        low = (lanes // width) % 2 == 0
        for first in range(4):
            if first & bit:
                continue
            one, two = tiles[first], tiles[first | bit]
            tiles[first] = jnp.where(low, one, turn_lanes(two, width))
            tiles[first | bit] = jnp.where(low, turn_lanes(one, -width), two)
    return tiles


def swap_rows(tile):
    lanes, rows = lane_index() // 16, row_index()
    for bit in (1, 2, 4):
        row_bit, lane_bit = (rows // bit) % 2, (lanes // bit) % 2
        up = turn_rows(turn_lanes(tile, 16 * bit), -bit)
        down = turn_rows(turn_lanes(tile, -16 * bit), bit)
        tile = jnp.where(row_bit == lane_bit, tile, jnp.where(row_bit == 0, up, down))
    return tile


def put_slots(out_ref, tiles, rows, base):
    zero = jnp.zeros((8, 128), f32)
    for half in range(2):
        group = [tiles[4 * half + x] if 4 * half + x < 6 else zero for x in range(4)]
        for quad, tile in enumerate(swap_quads(group)):
            out_ref[pl.ds(rows * quad + base + half, 8, stride=4 * rows), :] = tile


def get_slots(in_ref, rows, base):
    tiles = []
    for half in range(2):
        group = [in_ref[pl.ds(rows * quad + base + half, 8, stride=4 * rows), :] for quad in range(4)]
        tiles += swap_quads(group)
    return tiles[:6]


def put_cell_vector(out_ref, vector_ref, rows, base):
    put_slots(out_ref, [swap_rows(vector_ref[8 * t : 8 * t + 8, :]) for t in range(6)], rows, base)


def inverse_matvec(inverse_ref, vector_ref, out_ref):
    totals = None
    for a in range(48):
        term = inverse_ref[a].astype(f32) * vector_ref[a : a + 1, :]
        totals = term if totals is None else totals + term
    out_ref[...] = totals


def pack_blocks(block_ref, out_ref, base, groups):
    quads = lane_index() // 4
    keeps = [(bit, (quads & bit) == 0) for bit in (1, 2, 4, 8, 16)]
    for group in groups:
        ah_pair, bh_pair = group // 3, group % 3
        items = [None] * 32
        for y in range(2):
            for p in range(8):
                wide = block_ref[16 * ah_pair + 8 * y + p, 16 * bh_pair : 16 * bh_pair + 16, :].astype(f32)
                for h in range(2):
                    i = 4 * p + 2 * y + h
                    items[i] = turn_lanes(turn_rows(wide[8 * h : 8 * h + 8], -p), 4 * i)
        for bit, keep in keeps:
            items = [jnp.where(keep, items[j], items[(j + bit) % 32]) for j in range(32)]
        for e in range(32):
            out_ref[e, base + 8 * group : base + 8 * group + 8, :] = turn_lanes(items[-e % 32], -4 * e)


def fetch_thirds(block_hbm, block_ref, sems):
    copies = []
    for third in range(3):
        there = (slice(16 * third, 16 * third + 16), slice(None), slice(None))
        copies.append(pltpu.make_async_copy(block_hbm.at[there], block_ref.at[there], sems.at[third]))
    return copies


def unpack_cell(in_ref, base, out_ref, cell):
    for group in range(9):
        at = base + 8 * group
        parts = [in_ref[4 * cell + k, at : at + 8, :] for k in range(4)]
        for x, tile in enumerate(swap_quads(parts)):
            at = 8 * (4 * group + x)
            out_ref[cell, at : at + 8, :] = tile


def tile_at(ah, bh):
    return 4 * (3 * (ah // 2) + bh // 2) + 2 * (ah % 2) + bh % 2


def line_sweep(blocks_ref, const_ref, out_ref, reverse, beside=None):
    order = list(range(8))
    if reverse:
        order = order[::-1]
    state = None
    for turn in range(2):
        for n, cell in enumerate(order):
            if beside is not None:
                beside(turn, n)
            consts = [jnp.broadcast_to(const_ref[t, cell : cell + 1, :], (8, 128)) for t in range(6)]
            if state is None:
                state = consts
                continue
            products = line_product(blocks_ref, cell, state)
            state = [const - product for const, product in zip(consts, products)]
            if turn == 1:
                for t in range(6):
                    out_ref[t, cell : cell + 1, :] = state[t][0:1]


def stations_sum(tile):
    station = (lane_index() // 4) % 4
    before = jnp.where(station > 0, turn_lanes(tile, 4), 0.0)
    after = jnp.where(station < 3, turn_lanes(tile, -4), 0.0)
    return before + after


def first_send_kernel(
    forward_hbm, backward_hbm, inverse_hbm, rhs_hbm, coupling_hbm, out_hbm,
    f_ref, b_ref, i_ref, rhs_ref, coupling_ref, c_ref, vectors_ref, packed_ref, sems, out_sems,
):
    forward = fetch_thirds(forward_hbm, f_ref, sems.at[0])
    inverse = fetch_thirds(inverse_hbm, i_ref, sems.at[1])
    backward = fetch_thirds(backward_hbm, b_ref, sems.at[2])
    vectors = [
        pltpu.make_async_copy(source, target, sems.at[3, n])
        for n, (source, target) in enumerate(((rhs_hbm, rhs_ref), (coupling_hbm, coupling_ref)))
    ]
    for copy in forward + vectors + inverse + backward:
        copy.start()
    leaving = []

    def leave(row, rows):
        there = (slice(None), slice(row, row + rows), slice(None))
        leaving.append(pltpu.make_async_copy(packed_ref.at[there], out_hbm.at[there], out_sems.at[len(leaving)]))
        leaving[-1].start()

    for third in range(3):
        forward[third].wait()
        if third == 2:
            for copy in vectors + inverse:
                copy.wait()
            inverse_matvec(i_ref, rhs_ref, c_ref)
            for n, vector_ref in enumerate((c_ref, rhs_ref, coupling_ref)):
                put_cell_vector(vectors_ref, vector_ref, 8, 2 * n)
            for e in range(32):
                packed_ref[e, 144:152, :] = vectors_ref[8 * e : 8 * e + 8, :]
        pack_blocks(f_ref, packed_ref, 0, range(3 * third, 3 * third + 3))
        leave(24 * third, 24)
    leave(144, 8)
    for third in range(3):
        backward[third].wait()
        pack_blocks(b_ref, packed_ref, 72, range(3 * third, 3 * third + 3))
        leave(72 + 24 * third, 24)
    for copy in leaving:
        copy.wait()


def first_kernel(slots_ref, *refs):
    own_ref, other_ref, forward_ref, backward_ref, first_ref, middle_ref, coupling_ref, packed_ref, c_ref, y_ref = refs
    for e in range(32):
        packed_ref[8 * e : 8 * e + 8, :] = slots_ref[e, 144:152, :]
    for t, tile in enumerate(get_slots(packed_ref, 8, 0)):
        c_ref[t] = tile

    def unpack(turn, n):
        if turn == 0:
            unpack_cell(slots_ref, 0, forward_ref, n)
        else:
            unpack_cell(slots_ref, 72, backward_ref, n)

    line_sweep(forward_ref, c_ref, y_ref, False, unpack)
    line_sweep(backward_ref, y_ref, first_ref, True)
    rhs = get_slots(packed_ref, 8, 2)
    coupling = get_slots(packed_ref, 8, 4)
    half, _ = half_position()
    low = row_index() < 4
    own, other = [], []
    for t in range(6):
        first = first_ref[t]
        middle = rhs[t] - first + coupling[t] * stations_sum(first)
        turned = turn_rows(middle, 4)
        other.append(jnp.where(half == 0, turned, middle))
        own.append(jnp.where(half == 0, middle, turned))
        middle_ref[t] = middle
        coupling_ref[t] = coupling[t]
    for u in range(3):
        other_ref[u] = jnp.where(low, other[2 * u], turn_rows(other[2 * u + 1], 4))
        own_ref[u] = jnp.where(low, own[2 * u], turn_rows(own[2 * u + 1], 4))


def half_position():
    cell = lax.axis_index("azim")
    return cell // 4, (cell % 4) * 4 + lax.axis_index("axial")


def inverse_send_kernel(inverse_hbm, *refs):
    outs, (i_ref, packed_ref, fetch_sems, sems) = refs[:16], refs[16:]
    fetches = fetch_thirds(inverse_hbm, i_ref, fetch_sems)
    for copy in fetches:
        copy.start()
    for third, copy in enumerate(fetches):
        copy.wait()
        pack_blocks(i_ref, packed_ref, 0, range(3 * third, 3 * third + 3))
    half, place = half_position()
    copies = []
    for d in range(16):
        target = place ^ d
        for n, source in enumerate((16 * half + target, 16 * (1 - half) + target)):
            copies.append(
                pltpu.make_async_copy(packed_ref.at[source], outs[d].at[pl.ds(72 * n, 72), :], sems.at[2 * d + n])
            )
            copies[-1].start()
    for copy in copies:
        copy.wait()


def inverse_get_kernel(*refs):
    ins, out_ref = refs[:4], refs[4]
    for lines in range(2):
        for group in range(9):
            at = 72 * lines + 8 * group
            for x, tile in enumerate(swap_quads([part[at : at + 8, :] for part in ins])):
                at = 8 * (4 * group + x)
                out_ref[lines, at : at + 8, :] = tile


def turn_stations(tile, number):
    lanes = lane_index()
    for bit, width in ((1, 4), (2, 8)):
        other = jnp.where((lanes & width) == 0, turn_lanes(tile, -width), turn_lanes(tile, width))
        tile = jnp.where((number & bit) == 0, tile, other)
    return tile


def line_product(blocks_ref, cell, state):
    products = []
    for bh in range(6):
        total = None
        for ah in range(6):
            at = 8 * tile_at(ah, bh)
            term = blocks_ref[cell, at : at + 8, :] * state[ah]
            total = term if total is None else total + term
        total = pltpu.roll(total, 0, 1, stride=16, stride_axis=0)
        for span in (4, 2, 1):
            total = total + turn_rows(total, span)
        products.append(total)
    return products


def half_inverse_kernel(lines, vector_ref, *refs):
    blocks, (out_ref, turned_ref) = refs[:4], refs[4:]
    _, place = half_position()
    cell, station = place // 4, place % 4
    for u in range(3):
        turned_ref[u] = turn_stations(vector_ref[u], station)
    rows = row_index()
    totals = [jnp.zeros((8, 128), f32)] * 3
    for n in range(4):
        state = [
            jnp.broadcast_to(turned_ref[t // 2, pl.ds(4 * (t % 2) + (cell ^ n), 1), :], (8, 128)) for t in range(6)
        ]
        for t, product in enumerate(line_product(blocks[n], lines, state)):
            totals[t // 2] = jnp.where(rows == 4 * (t % 2) + (cell ^ n), product, totals[t // 2])
    for u in range(3):
        out_ref[u] = turn_stations(totals[u], station)


def second_kernel(
    own_ref, other_ref, forward_ref, backward_ref, first_ref, middle_ref, coupling_ref, out_ref, c_ref, y_ref, second_ref
):
    half, _ = half_position()
    low = row_index() < 4
    for t in range(6):
        own, other = own_ref[t // 2], other_ref[t // 2]
        if t % 2:
            own = turn_rows(own, 4)
        else:
            other = turn_rows(other, 4)
        tile = jnp.where(low, own, other)
        c_ref[t] = jnp.where(half == 0, tile, turn_rows(tile, 4))
    line_sweep(forward_ref, c_ref, y_ref, False)
    line_sweep(backward_ref, y_ref, second_ref, True)
    correction, remaining = [], []
    for t in range(6):
        second = second_ref[t]
        correction.append(first_ref[t] + second)
        remaining.append(middle_ref[t] - second + coupling_ref[t] * stations_sum(second))
    put_slots(out_ref, correction, 4, 0)
    put_slots(out_ref, remaining, 4, 2)


def last_kernel(slots_ref, correction_ref, remaining_ref):
    for out_ref, base in ((correction_ref, 0), (remaining_ref, 2)):
        for t, tile in enumerate(get_slots(slots_ref, 4, base)):
            out_ref[8 * t : 8 * t + 8, :] = swap_rows(tile)


def shaped(*sizes):
    return jax.ShapeDtypeStruct(sizes, f32)


def call(kernel, outs, scratch=()):
    return pl.pallas_call(
        kernel,
        out_shape=outs,
        scratch_shapes=[pltpu.VMEM(sizes, f32) for sizes in scratch],
        compiler_params=pltpu.CompilerParams(vmem_limit_bytes=VMEM_LIMIT),
    )


def exchange(slots, rows):
    moved = lax.all_to_all(slots.reshape(32, rows, 128), BOTH, 0, 0, tiled=True)
    return moved.reshape(32 * rows, 128)


def line_plan(rhs, coupling, fwd_coupling, bwd_coupling, block_inverse):
    source, coupling_field = rhs.reshape(48, 128), coupling.reshape(48, 128)
    forward_blocks = fwd_coupling.reshape(48, 48, 128)
    backward_blocks = bwd_coupling.reshape(48, 48, 128)
    inverse_blocks = block_inverse.reshape(48, 48, 128)
    tiles, pairs, held = shaped(6, 8, 128), shaped(3, 8, 128), shaped(8, 288, 128)
    blocks = pltpu.VMEM((48, 48, 128), jnp.bfloat16)
    vector = pltpu.VMEM((48, 128), f32)

    slots = pl.pallas_call(
        first_send_kernel,
        out_shape=pltpu.HBM((32, 152, 128), f32),
        in_specs=[pl.BlockSpec(memory_space=pltpu.HBM)] * 5,
        out_specs=pl.BlockSpec(memory_space=pltpu.HBM),
        scratch_shapes=[blocks, blocks, blocks, vector, vector, vector]
        + [
            pltpu.VMEM((256, 128), f32),
            pltpu.VMEM((32, 152, 128), f32),
            pltpu.SemaphoreType.DMA((4, 3)),
            pltpu.SemaphoreType.DMA((7,)),
        ],
        compiler_params=pltpu.CompilerParams(vmem_limit_bytes=VMEM_LIMIT),
    )(*[
        pltpu.with_memory_space_constraint(array, pltpu.HBM)
        for array in (forward_blocks, backward_blocks, inverse_blocks, source, coupling_field)
    ])
    slots, inverse_blocks = lax.optimization_barrier((slots, inverse_blocks))
    slots = lax.all_to_all(slots, BOTH, 0, 0, tiled=True)

    parts = pl.pallas_call(
        inverse_send_kernel,
        out_shape=[shaped(144, 128)] * 16,
        in_specs=[pl.BlockSpec(memory_space=pltpu.HBM)],
        out_specs=[pl.BlockSpec(memory_space=pltpu.HBM)] * 16,
        scratch_shapes=[
            blocks, pltpu.VMEM((32, 72, 128), f32), pltpu.SemaphoreType.DMA((3,)), pltpu.SemaphoreType.DMA((32,))
        ],
        compiler_params=pltpu.CompilerParams(vmem_limit_bytes=VMEM_LIMIT),
    )(pltpu.with_memory_space_constraint(inverse_blocks, pltpu.HBM))
    parts = [parts[0]] + [lax.ppermute(parts[d], BOTH, [(e, e ^ d) for e in range(32)]) for d in range(1, 16)]
    inverse = [
        call(inverse_get_kernel, pltpu.VMEM((2, 288, 128), f32))(*parts[4 * n : 4 * n + 4]) for n in range(4)
    ]

    own, other, forward, backward, first, middle, coupling_lines = call(
        first_kernel, (pairs, pairs, held, held, tiles, tiles, tiles), [(256, 128), (6, 8, 128), (6, 8, 128)]
    )(slots)

    def with_partner(vector):
        return lax.ppermute(vector, BOTH, [(e, e ^ 16) for e in range(32)])

    other = with_partner(other)
    own = call(functools.partial(half_inverse_kernel, 0), pairs, [(3, 8, 128)])(own, *inverse)
    other = call(functools.partial(half_inverse_kernel, 1), pairs, [(3, 8, 128)])(other, *inverse)
    other = with_partner(other)
    slots = call(second_kernel, shaped(128, 128), [(6, 8, 128)] * 3)(
        own, other, forward, backward, first, middle, coupling_lines
    )
    slots = exchange(slots, 4)
    correction, remaining = call(last_kernel, (shaped(48, 128), shaped(48, 128)))(slots)
    return correction.reshape(rhs.shape), remaining.reshape(rhs.shape)


def from_behind(value, axis, steps):
    count = lax.axis_size(axis)
    initial, last = (max(0, -steps), min(count, count - steps))
    return lax.ppermute(value, axis, [(source, source + steps) for source in range(initial, last)])


def from_root(shard, axis, root):
    mine = lax.axis_index(axis) == root
    return lax.psum(jnp.where(mine, shard, jnp.zeros_like(shard)), axis)


def extended(block, sides, width):
    for axis, dim in sides:
        count = lax.axis_size(axis)
        forward = [(i, i + 1) for i in range(count - 1)]
        backward = [(target, source) for source, target in forward]
        low = lax.ppermute(
            lax.slice_in_dim(block, block.shape[dim] - width, None, axis=dim), axis, forward
        )
        high = lax.ppermute(lax.slice_in_dim(block, 0, width, axis=dim), axis, backward)
        block = jnp.concatenate([low, block, high], axis=dim)
    return block


def cell_stride(one_block, carried, const_term):
    return const_term - jnp.einsum(
        "abl,al->bl", one_block.astype(jnp.float32), carried, precision=highest
    )


def compose_cells(blocks, sequence):
    running = None
    for position in sequence:
        one_block = blocks[position].astype(jnp.float32)
        running = -jnp.swapaxes(one_block, 0, 1)
    return running


def doubling_maps(local_map, reverse):
    size = lax.axis_size("azim")
    index = lax.axis_index("azim")
    levels = []
    current = local_map
    distance = 1
    while distance < size:
        if reverse:
            moved = from_behind(current, "azim", -distance)
            exists = index + distance < size
        else:
            moved = from_behind(current, "azim", distance)
            exists = index >= distance
        levels.append((current, distance))
        current = jnp.where(
            exists, jnp.einsum("bcl,cal->bal", current, moved, precision=highest), current
        )
        distance = distance * 2
    return (levels, current)


def doubling_entries(map_levels, local_offset, reverse):
    levels, final_map = map_levels
    size = lax.axis_size("azim")
    index = lax.axis_index("azim")
    running = local_offset
    for current, distance in levels:
        if reverse:
            moved = from_behind(running, "azim", -distance)
        else:
            moved = from_behind(running, "azim", distance)
        running = jnp.einsum("bcl,cl->bl", current, moved, precision=highest) + running
    if reverse:
        wrapped = from_root(running, "azim", 0)
    else:
        wrapped = from_root(running, "azim", size - 1)
    leaving = jnp.einsum("bcl,cl->bl", final_map, wrapped, precision=highest) + running
    if reverse:
        shifted = from_behind(leaving, "azim", -1)
        first_device = index == size - 1
    else:
        shifted = from_behind(leaving, "azim", 1)
        first_device = index == 0
    return jnp.where(first_device, wrapped, shifted)


def sweep(blocks, consts, map_levels, reverse):
    cell_count = blocks.shape[0]
    sequence = list(range(cell_count))
    if reverse:
        sequence = sequence[::-1]
    carried = jnp.zeros(consts.shape[1:], jnp.float32)
    for position in sequence:
        carried = cell_stride(blocks[position], carried, consts[position])
    local_offset = carried
    incoming_maps = doubling_entries(map_levels, local_offset, reverse)
    outputs = [None] * cell_count
    carried = incoming_maps
    for position in sequence:
        carried = cell_stride(blocks[position], carried, consts[position])
        outputs[position] = carried
    return jnp.stack(outputs)


def on_device(rhs, coupling, fwd_coupling, bwd_coupling, block_inverse):
    cell_count, block_width, _, position_total, radial_count = fwd_coupling.shape
    line_count = position_total * radial_count
    forward_blocks = fwd_coupling.reshape(cell_count, block_width, block_width, line_count)
    backward_blocks = bwd_coupling.reshape(cell_count, block_width, block_width, line_count)
    inverse_blocks = block_inverse.reshape(cell_count, block_width, block_width, line_count)
    source = rhs.reshape(cell_count, block_width, line_count)
    coupling_field = coupling.reshape(cell_count, block_width, line_count)
    forward_map = compose_cells(forward_blocks, list(range(cell_count)))
    backward_map = compose_cells(backward_blocks, list(range(cell_count))[::-1])
    forward_levels = None
    backward_levels = None
    forward_levels = doubling_maps(forward_map, False)
    backward_levels = doubling_maps(backward_map, True)

    def precondition(vector):
        consts = jnp.stack(
            [
                jnp.einsum(
                    "abl,al->bl",
                    inverse_blocks[0].astype(jnp.float32),
                    vector[0],
                    precision=highest,
                )
            ]
        )
        forward = sweep(forward_blocks, consts, forward_levels, False)
        return sweep(backward_blocks, forward, backward_levels, True)

    def stations_sum(field):
        grid = field.reshape(cell_count, block_width, position_total, radial_count)
        padded = extended(grid, (("axial", 2),), 1)
        return (padded[:, :, :-2] + padded[:, :, 2:]).reshape(cell_count, block_width, line_count)

    applied_once = precondition(source)
    middle = source - applied_once + coupling_field * stations_sum(applied_once)
    second = precondition(middle)
    correction = applied_once + second
    remaining = middle - second + coupling_field * stations_sum(second)
    return (correction.reshape(rhs.shape), remaining.reshape(rhs.shape))


def solution(mesh):
    cells, stations = mesh.shape["azim"], mesh.shape["axial"]

    def on_each(rhs, coupling, fwd_coupling, bwd_coupling, block_inverse):
        local = fwd_coupling.shape
        if (cells, stations) == (8, 4) and local == (1, 48, 48, 1, 128):
            return line_plan(rhs, coupling, fwd_coupling, bwd_coupling, block_inverse)
        return on_device(rhs, coupling, fwd_coupling, bwd_coupling, block_inverse)

    return jax.shard_map(
        on_each,
        mesh=mesh,
        in_specs=(
            P("azim", None, "axial", None),
            P("azim", None, "axial", None),
            P("azim", None, None, "axial", None),
            P("azim", None, None, "axial", None),
            P("azim", None, None, "axial", None),
        ),
        out_specs=(P("azim", None, "axial", None), P("azim", None, "axial", None)),
        check_vma=False,
    )
```

```python
import functools

import jax
import jax.numpy as jnp
from jax import lax
from jax.experimental import pallas as pl
from jax.experimental.pallas import tpu as pltpu
from jax.sharding import PartitionSpec as P

highest = lax.Precision.HIGHEST
f32 = jnp.float32
BOTH = ("azim", "axial")
VMEM_LIMIT = 16 * 1024 * 1024


def lane_index():
    return lax.broadcasted_iota(jnp.int32, (8, 128), 1)


def row_index():
    return lax.broadcasted_iota(jnp.int32, (8, 128), 0)


def turn_lanes(tile, steps):
    steps = steps % 128
    return pltpu.roll(tile, steps, 1) if steps else tile


def turn_rows(tile, steps):
    steps = steps % 8
    return pltpu.roll(tile, steps, 0) if steps else tile


def line_lanes():
    return lane_index() + 16 - 4 * lax.axis_index("axial")


def to_line(tile):
    return pltpu.roll(tile, 4 * (4 * lax.axis_index("azim") + lax.axis_index("axial")), 1)


def from_line(tile):
    return pltpu.roll(tile, (128 - 4 * (4 * lax.axis_index("azim") + lax.axis_index("axial"))) % 128, 1)


def swap_quads(tiles, lanes=None):
    lanes = lane_index() if lanes is None else lanes
    tiles = list(tiles)
    for bit, width in ((1, 4), (2, 8)):
        low = (lanes // width) % 2 == 0
        for first in range(4):
            if first & bit:
                continue
            one, two = tiles[first], tiles[first | bit]
            tiles[first] = jnp.where(low, one, turn_lanes(two, width))
            tiles[first | bit] = jnp.where(low, turn_lanes(one, -width), two)
    return tiles


def swap_rows(tile):
    lanes, rows = lane_index() // 16, row_index()
    for bit in (1, 2, 4):
        row_bit, lane_bit = (rows // bit) % 2, (lanes // bit) % 2
        up = turn_rows(turn_lanes(tile, 16 * bit), -bit)
        down = turn_rows(turn_lanes(tile, -16 * bit), bit)
        tile = jnp.where(row_bit == lane_bit, tile, jnp.where(row_bit == 0, up, down))
    return tile


def put_slots(out_ref, tiles, rows, base):
    zero = jnp.zeros((8, 128), f32)
    for half in range(2):
        group = [tiles[4 * half + x] if 4 * half + x < 6 else zero for x in range(4)]
        for quad, tile in enumerate(swap_quads(group)):
            out_ref[pl.ds(rows * quad + base + half, 8, stride=4 * rows), :] = tile


def get_slots(in_ref, rows, base):
    tiles = []
    for half in range(2):
        group = [in_ref[pl.ds(rows * quad + base + half, 8, stride=4 * rows), :] for quad in range(4)]
        tiles += swap_quads(group)
    return tiles[:6]


def put_cell_vector(out_ref, vector_ref, rows, base):
    put_slots(out_ref, [swap_rows(vector_ref[8 * t : 8 * t + 8, :]) for t in range(6)], rows, base)


def inverse_matvec(inverse_ref, vector_ref, out_ref):
    totals = None
    for a in range(48):
        term = inverse_ref[a].astype(f32) * vector_ref[a : a + 1, :]
        totals = term if totals is None else totals + term
    out_ref[...] = totals


def pack_blocks(block_ref, out_ref, base, groups):
    quads = lane_index() // 4
    keeps = [(bit, (quads & bit) == 0) for bit in (1, 2, 4, 8, 16)]
    for group in groups:
        ah_pair, bh_pair = group // 3, group % 3
        items = [None] * 32
        for y in range(2):
            for p in range(8):
                wide = block_ref[16 * ah_pair + 8 * y + p, 16 * bh_pair : 16 * bh_pair + 16, :].astype(f32)
                for h in range(2):
                    i = 4 * p + 2 * y + h
                    items[i] = turn_lanes(turn_rows(wide[8 * h : 8 * h + 8], -p), 4 * i)
        for bit, keep in keeps:
            items = [jnp.where(keep, items[j], items[(j + bit) % 32]) for j in range(32)]
        for e in range(32):
            out_ref[e, base + 8 * group : base + 8 * group + 8, :] = items[-e % 32]


def fetch_thirds(block_hbm, block_ref, sems):
    copies = []
    for third in range(3):
        there = (slice(16 * third, 16 * third + 16), slice(None), slice(None))
        copies.append(pltpu.make_async_copy(block_hbm.at[there], block_ref.at[there], sems.at[third]))
    return copies


def unpack_cell(in_ref, base, out_ref, cell):
    for group in range(9):
        at = base + 8 * group
        parts = [in_ref[4 * cell + k, at : at + 8, :] for k in range(4)]
        for x, tile in enumerate(swap_quads(parts, line_lanes())):
            at = 8 * (4 * group + x)
            out_ref[cell, at : at + 8, :] = tile


def tile_at(ah, bh):
    return 4 * (3 * (ah // 2) + bh // 2) + 2 * (ah % 2) + bh % 2


def line_sweep(blocks_ref, const_ref, out_ref, reverse, beside=None):
    order = list(range(8))
    if reverse:
        order = order[::-1]
    state = None
    for turn in range(2):
        for n, cell in enumerate(order):
            if beside is not None:
                beside(turn, n)
            consts = [jnp.broadcast_to(const_ref[t, cell : cell + 1, :], (8, 128)) for t in range(6)]
            if state is None:
                state = consts
                continue
            products = line_product(blocks_ref, cell, state)
            state = [const - product for const, product in zip(consts, products)]
            if turn == 1:
                for t in range(6):
                    out_ref[t, cell : cell + 1, :] = state[t][0:1]


def stations_sum(tile):
    station = (line_lanes() // 4) % 4
    before = jnp.where(station > 0, turn_lanes(tile, 4), 0.0)
    after = jnp.where(station < 3, turn_lanes(tile, -4), 0.0)
    return before + after


def first_send_kernel(
    forward_hbm, backward_hbm, inverse_hbm, rhs_hbm, coupling_hbm, out_hbm,
    f_ref, b_ref, i_ref, rhs_ref, coupling_ref, c_ref, vectors_ref, packed_ref, sems, out_sems,
):
    forward = fetch_thirds(forward_hbm, f_ref, sems.at[0])
    inverse = fetch_thirds(inverse_hbm, i_ref, sems.at[1])
    backward = fetch_thirds(backward_hbm, b_ref, sems.at[2])
    vectors = [
        pltpu.make_async_copy(source, target, sems.at[3, n])
        for n, (source, target) in enumerate(((rhs_hbm, rhs_ref), (coupling_hbm, coupling_ref)))
    ]
    for copy in forward + vectors + inverse:
        copy.start()
    leaving = []

    def leave(row, rows):
        there = (slice(None), slice(row, row + rows), slice(None))
        leaving.append(pltpu.make_async_copy(packed_ref.at[there], out_hbm.at[there], out_sems.at[len(leaving)]))
        leaving[-1].start()

    for third in range(3):
        forward[third].wait()
        if third == 0:
            for copy in backward:
                copy.start()
        pack_blocks(f_ref, packed_ref, 0, range(3 * third, 3 * third + 3))
        leave(24 * third, 24)
    for copy in vectors + inverse:
        copy.wait()
    for third in range(3):
        backward[third].wait()
        if third == 0:
            inverse_matvec(i_ref, rhs_ref, c_ref)
            for n, vector_ref in enumerate((c_ref, rhs_ref, coupling_ref)):
                put_cell_vector(vectors_ref, vector_ref, 8, 2 * n)
            for e in range(32):
                packed_ref[e, 144:152, :] = vectors_ref[8 * e : 8 * e + 8, :]
        pack_blocks(b_ref, packed_ref, 72, range(3 * third, 3 * third + 3))
        if third == 0:
            leave(144, 8)
        leave(72 + 24 * third, 24)
    for copy in leaving:
        copy.wait()


def first_kernel(slots_ref, *refs):
    own_ref, other_ref, forward_ref, backward_ref, first_ref, middle_ref, coupling_ref, packed_ref, c_ref, y_ref = refs
    for e in range(32):
        packed_ref[8 * e : 8 * e + 8, :] = slots_ref[e, 144:152, :]
    for t, tile in enumerate(get_slots(packed_ref, 8, 0)):
        c_ref[t] = to_line(tile)

    def unpack(turn, n):
        if turn == 0:
            unpack_cell(slots_ref, 0, forward_ref, n)
        else:
            unpack_cell(slots_ref, 72, backward_ref, n)

    line_sweep(forward_ref, c_ref, y_ref, False, unpack)
    line_sweep(backward_ref, y_ref, first_ref, True)
    rhs = [to_line(tile) for tile in get_slots(packed_ref, 8, 2)]
    coupling = [to_line(tile) for tile in get_slots(packed_ref, 8, 4)]
    half, _ = half_position()
    low = row_index() < 4
    own, other = [], []
    for t in range(6):
        first = first_ref[t]
        middle = rhs[t] - first + coupling[t] * stations_sum(first)
        turned = turn_rows(middle, 4)
        other.append(jnp.where(half == 0, turned, middle))
        own.append(jnp.where(half == 0, middle, turned))
        middle_ref[t] = middle
        coupling_ref[t] = coupling[t]
    for u in range(3):
        other_ref[u] = jnp.where(low, other[2 * u], turn_rows(other[2 * u + 1], 4))
        own_ref[u] = jnp.where(low, own[2 * u], turn_rows(own[2 * u + 1], 4))


def half_position():
    cell = lax.axis_index("azim")
    return cell // 4, (cell % 4) * 4 + lax.axis_index("axial")


def inverse_send_kernel(inverse_hbm, *refs):
    outs, (i_ref, packed_ref, fetch_sems, sems) = refs[:16], refs[16:]
    fetches = fetch_thirds(inverse_hbm, i_ref, fetch_sems)
    for copy in fetches:
        copy.start()
    for third, copy in enumerate(fetches):
        copy.wait()
        pack_blocks(i_ref, packed_ref, 0, range(3 * third, 3 * third + 3))
    half, place = half_position()
    copies = []
    for d in range(16):
        target = place ^ d
        for n, source in enumerate((16 * half + target, 16 * (1 - half) + target)):
            copies.append(
                pltpu.make_async_copy(packed_ref.at[source], outs[d].at[pl.ds(72 * n, 72), :], sems.at[2 * d + n])
            )
            copies[-1].start()
    for copy in copies:
        copy.wait()


def inverse_get_kernel(*refs):
    ins, out_ref = refs[:4], refs[4]
    for lines in range(2):
        for group in range(9):
            at = 72 * lines + 8 * group
            for x, tile in enumerate(swap_quads([part[at : at + 8, :] for part in ins], line_lanes())):
                at = 8 * (4 * group + x)
                out_ref[lines, at : at + 8, :] = tile


def turn_stations(tile, number):
    lanes = line_lanes()
    for bit, width in ((1, 4), (2, 8)):
        other = jnp.where((lanes & width) == 0, turn_lanes(tile, -width), turn_lanes(tile, width))
        tile = jnp.where((number & bit) == 0, tile, other)
    return tile


def line_product(blocks_ref, cell, state):
    products = []
    for bh in range(6):
        total = None
        for ah in range(6):
            at = 8 * tile_at(ah, bh)
            term = blocks_ref[cell, at : at + 8, :] * state[ah]
            total = term if total is None else total + term
        total = pltpu.roll(total, 0, 1, stride=16, stride_axis=0)
        for span in (4, 2, 1):
            total = total + turn_rows(total, span)
        products.append(total)
    return products


def half_inverse_kernel(lines, vector_ref, *refs):
    blocks, (out_ref, turned_ref) = refs[:4], refs[4:]
    _, place = half_position()
    cell, station = place // 4, place % 4
    for u in range(3):
        turned_ref[u] = turn_stations(vector_ref[u], station)
    rows = row_index()
    totals = [jnp.zeros((8, 128), f32)] * 3
    for n in range(4):
        state = [
            jnp.broadcast_to(turned_ref[t // 2, pl.ds(4 * (t % 2) + (cell ^ n), 1), :], (8, 128)) for t in range(6)
        ]
        for t, product in enumerate(line_product(blocks[n], lines, state)):
            totals[t // 2] = jnp.where(rows == 4 * (t % 2) + (cell ^ n), product, totals[t // 2])
    for u in range(3):
        out_ref[u] = turn_stations(totals[u], station)


def second_kernel(
    own_ref, other_ref, forward_ref, backward_ref, first_ref, middle_ref, coupling_ref, out_ref, c_ref, y_ref, second_ref
):
    half, _ = half_position()
    low = row_index() < 4
    for t in range(6):
        own, other = own_ref[t // 2], other_ref[t // 2]
        if t % 2:
            own = turn_rows(own, 4)
        else:
            other = turn_rows(other, 4)
        tile = jnp.where(low, own, other)
        c_ref[t] = jnp.where(half == 0, tile, turn_rows(tile, 4))
    line_sweep(forward_ref, c_ref, y_ref, False)
    line_sweep(backward_ref, y_ref, second_ref, True)
    correction, remaining = [], []
    for t in range(6):
        second = second_ref[t]
        correction.append(from_line(first_ref[t] + second))
        remaining.append(from_line(middle_ref[t] - second + coupling_ref[t] * stations_sum(second)))
    put_slots(out_ref, correction, 4, 0)
    put_slots(out_ref, remaining, 4, 2)


def last_kernel(slots_ref, correction_ref, remaining_ref):
    for out_ref, base in ((correction_ref, 0), (remaining_ref, 2)):
        for t, tile in enumerate(get_slots(slots_ref, 4, base)):
            out_ref[8 * t : 8 * t + 8, :] = swap_rows(tile)


def shaped(*sizes):
    return jax.ShapeDtypeStruct(sizes, f32)


def call(kernel, outs, scratch=()):
    return pl.pallas_call(
        kernel,
        out_shape=outs,
        scratch_shapes=[pltpu.VMEM(sizes, f32) for sizes in scratch],
        compiler_params=pltpu.CompilerParams(vmem_limit_bytes=VMEM_LIMIT),
    )


def exchange(slots, rows):
    moved = lax.all_to_all(slots.reshape(32, rows, 128), BOTH, 0, 0, tiled=True)
    return moved.reshape(32 * rows, 128)


def line_plan(rhs, coupling, fwd_coupling, bwd_coupling, block_inverse):
    source, coupling_field = rhs.reshape(48, 128), coupling.reshape(48, 128)
    forward_blocks = fwd_coupling.reshape(48, 48, 128)
    backward_blocks = bwd_coupling.reshape(48, 48, 128)
    inverse_blocks = block_inverse.reshape(48, 48, 128)
    tiles, pairs, held = shaped(6, 8, 128), shaped(3, 8, 128), shaped(8, 288, 128)
    blocks = pltpu.VMEM((48, 48, 128), jnp.bfloat16)
    vector = pltpu.VMEM((48, 128), f32)

    slots = pl.pallas_call(
        first_send_kernel,
        out_shape=pltpu.HBM((32, 152, 128), f32),
        in_specs=[pl.BlockSpec(memory_space=pltpu.HBM)] * 5,
        out_specs=pl.BlockSpec(memory_space=pltpu.HBM),
        scratch_shapes=[blocks, blocks, blocks, vector, vector, vector]
        + [
            pltpu.VMEM((256, 128), f32),
            pltpu.VMEM((32, 152, 128), f32),
            pltpu.SemaphoreType.DMA((4, 3)),
            pltpu.SemaphoreType.DMA((7,)),
        ],
        compiler_params=pltpu.CompilerParams(vmem_limit_bytes=VMEM_LIMIT),
    )(*[
        pltpu.with_memory_space_constraint(array, pltpu.HBM)
        for array in (forward_blocks, backward_blocks, inverse_blocks, source, coupling_field)
    ])
    slots, inverse_blocks = lax.optimization_barrier((slots, inverse_blocks))
    slots = lax.all_to_all(slots, BOTH, 0, 0, tiled=True)

    parts = pl.pallas_call(
        inverse_send_kernel,
        out_shape=[shaped(144, 128)] * 16,
        in_specs=[pl.BlockSpec(memory_space=pltpu.HBM)],
        out_specs=[pl.BlockSpec(memory_space=pltpu.HBM)] * 16,
        scratch_shapes=[
            blocks, pltpu.VMEM((32, 72, 128), f32), pltpu.SemaphoreType.DMA((3,)), pltpu.SemaphoreType.DMA((32,))
        ],
        compiler_params=pltpu.CompilerParams(vmem_limit_bytes=VMEM_LIMIT),
    )(pltpu.with_memory_space_constraint(inverse_blocks, pltpu.HBM))
    parts = [parts[0]] + [lax.ppermute(parts[d], BOTH, [(e, e ^ d) for e in range(32)]) for d in range(1, 16)]
    inverse = [
        call(inverse_get_kernel, pltpu.VMEM((2, 288, 128), f32))(*parts[4 * n : 4 * n + 4]) for n in range(4)
    ]

    own, other, forward, backward, first, middle, coupling_lines = call(
        first_kernel, (pairs, pairs, held, held, tiles, tiles, tiles), [(256, 128), (6, 8, 128), (6, 8, 128)]
    )(slots)

    def with_partner(vector):
        return lax.ppermute(vector, BOTH, [(e, e ^ 16) for e in range(32)])

    other = with_partner(other)
    own = call(functools.partial(half_inverse_kernel, 0), pairs, [(3, 8, 128)])(own, *inverse)
    other = call(functools.partial(half_inverse_kernel, 1), pairs, [(3, 8, 128)])(other, *inverse)
    other = with_partner(other)
    slots = call(second_kernel, shaped(128, 128), [(6, 8, 128)] * 3)(
        own, other, forward, backward, first, middle, coupling_lines
    )
    slots = exchange(slots, 4)
    correction, remaining = call(last_kernel, (shaped(48, 128), shaped(48, 128)))(slots)
    return correction.reshape(rhs.shape), remaining.reshape(rhs.shape)


def from_behind(value, axis, steps):
    count = lax.axis_size(axis)
    initial, last = (max(0, -steps), min(count, count - steps))
    return lax.ppermute(value, axis, [(source, source + steps) for source in range(initial, last)])


def from_root(shard, axis, root):
    mine = lax.axis_index(axis) == root
    return lax.psum(jnp.where(mine, shard, jnp.zeros_like(shard)), axis)


def extended(block, sides, width):
    for axis, dim in sides:
        count = lax.axis_size(axis)
        forward = [(i, i + 1) for i in range(count - 1)]
        backward = [(target, source) for source, target in forward]
        low = lax.ppermute(
            lax.slice_in_dim(block, block.shape[dim] - width, None, axis=dim), axis, forward
        )
        high = lax.ppermute(lax.slice_in_dim(block, 0, width, axis=dim), axis, backward)
        block = jnp.concatenate([low, block, high], axis=dim)
    return block


def cell_stride(one_block, carried, const_term):
    return const_term - jnp.einsum(
        "abl,al->bl", one_block.astype(jnp.float32), carried, precision=highest
    )


def compose_cells(blocks, sequence):
    running = None
    for position in sequence:
        one_block = blocks[position].astype(jnp.float32)
        running = -jnp.swapaxes(one_block, 0, 1)
    return running


def doubling_maps(local_map, reverse):
    size = lax.axis_size("azim")
    index = lax.axis_index("azim")
    levels = []
    current = local_map
    distance = 1
    while distance < size:
        if reverse:
            moved = from_behind(current, "azim", -distance)
            exists = index + distance < size
        else:
            moved = from_behind(current, "azim", distance)
            exists = index >= distance
        levels.append((current, distance))
        current = jnp.where(
            exists, jnp.einsum("bcl,cal->bal", current, moved, precision=highest), current
        )
        distance = distance * 2
    return (levels, current)


def doubling_entries(map_levels, local_offset, reverse):
    levels, final_map = map_levels
    size = lax.axis_size("azim")
    index = lax.axis_index("azim")
    running = local_offset
    for current, distance in levels:
        if reverse:
            moved = from_behind(running, "azim", -distance)
        else:
            moved = from_behind(running, "azim", distance)
        running = jnp.einsum("bcl,cl->bl", current, moved, precision=highest) + running
    if reverse:
        wrapped = from_root(running, "azim", 0)
    else:
        wrapped = from_root(running, "azim", size - 1)
    leaving = jnp.einsum("bcl,cl->bl", final_map, wrapped, precision=highest) + running
    if reverse:
        shifted = from_behind(leaving, "azim", -1)
        first_device = index == size - 1
    else:
        shifted = from_behind(leaving, "azim", 1)
        first_device = index == 0
    return jnp.where(first_device, wrapped, shifted)


def sweep(blocks, consts, map_levels, reverse):
    cell_count = blocks.shape[0]
    sequence = list(range(cell_count))
    if reverse:
        sequence = sequence[::-1]
    carried = jnp.zeros(consts.shape[1:], jnp.float32)
    for position in sequence:
        carried = cell_stride(blocks[position], carried, consts[position])
    local_offset = carried
    incoming_maps = doubling_entries(map_levels, local_offset, reverse)
    outputs = [None] * cell_count
    carried = incoming_maps
    for position in sequence:
        carried = cell_stride(blocks[position], carried, consts[position])
        outputs[position] = carried
    return jnp.stack(outputs)


def on_device(rhs, coupling, fwd_coupling, bwd_coupling, block_inverse):
    cell_count, block_width, _, position_total, radial_count = fwd_coupling.shape
    line_count = position_total * radial_count
    forward_blocks = fwd_coupling.reshape(cell_count, block_width, block_width, line_count)
    backward_blocks = bwd_coupling.reshape(cell_count, block_width, block_width, line_count)
    inverse_blocks = block_inverse.reshape(cell_count, block_width, block_width, line_count)
    source = rhs.reshape(cell_count, block_width, line_count)
    coupling_field = coupling.reshape(cell_count, block_width, line_count)
    forward_map = compose_cells(forward_blocks, list(range(cell_count)))
    backward_map = compose_cells(backward_blocks, list(range(cell_count))[::-1])
    forward_levels = None
    backward_levels = None
    forward_levels = doubling_maps(forward_map, False)
    backward_levels = doubling_maps(backward_map, True)

    def precondition(vector):
        consts = jnp.stack(
            [
                jnp.einsum(
                    "abl,al->bl",
                    inverse_blocks[0].astype(jnp.float32),
                    vector[0],
                    precision=highest,
                )
            ]
        )
        forward = sweep(forward_blocks, consts, forward_levels, False)
        return sweep(backward_blocks, forward, backward_levels, True)

    def stations_sum(field):
        grid = field.reshape(cell_count, block_width, position_total, radial_count)
        padded = extended(grid, (("axial", 2),), 1)
        return (padded[:, :, :-2] + padded[:, :, 2:]).reshape(cell_count, block_width, line_count)

    applied_once = precondition(source)
    middle = source - applied_once + coupling_field * stations_sum(applied_once)
    second = precondition(middle)
    correction = applied_once + second
    remaining = middle - second + coupling_field * stations_sum(second)
    return (correction.reshape(rhs.shape), remaining.reshape(rhs.shape))


def solution(mesh):
    cells, stations = mesh.shape["azim"], mesh.shape["axial"]

    def on_each(rhs, coupling, fwd_coupling, bwd_coupling, block_inverse):
        local = fwd_coupling.shape
        if (cells, stations) == (8, 4) and local == (1, 48, 48, 1, 128):
            return line_plan(rhs, coupling, fwd_coupling, bwd_coupling, block_inverse)
        return on_device(rhs, coupling, fwd_coupling, bwd_coupling, block_inverse)

    return jax.shard_map(
        on_each,
        mesh=mesh,
        in_specs=(
            P("azim", None, "axial", None),
            P("azim", None, "axial", None),
            P("azim", None, None, "axial", None),
            P("azim", None, None, "axial", None),
            P("azim", None, None, "axial", None),
        ),
        out_specs=(P("azim", None, "axial", None), P("azim", None, "axial", None)),
        check_vma=False,
    )
```

```python
import functools

import jax
import jax.numpy as jnp
from jax import lax
from jax.experimental import pallas as pl
from jax.experimental.pallas import tpu as pltpu
from jax.sharding import PartitionSpec as P

highest = lax.Precision.HIGHEST
f32 = jnp.float32
BOTH = ("azim", "axial")
VMEM_LIMIT = 16 * 1024 * 1024


def lane_index():
    return lax.broadcasted_iota(jnp.int32, (8, 128), 1)


def row_index():
    return lax.broadcasted_iota(jnp.int32, (8, 128), 0)


def turn_lanes(tile, steps):
    steps = steps % 128
    return pltpu.roll(tile, steps, 1) if steps else tile


def turn_rows(tile, steps):
    steps = steps % 8
    return pltpu.roll(tile, steps, 0) if steps else tile


def line_lanes():
    return lane_index() + 16 - 4 * lax.axis_index("axial")


def to_line(tile):
    return pltpu.roll(tile, 4 * (4 * lax.axis_index("azim") + lax.axis_index("axial")), 1)


def from_line(tile):
    return pltpu.roll(tile, (128 - 4 * (4 * lax.axis_index("azim") + lax.axis_index("axial"))) % 128, 1)


def swap_quads(tiles, lanes=None):
    lanes = lane_index() if lanes is None else lanes
    tiles = list(tiles)
    for bit, width in ((1, 4), (2, 8)):
        low = (lanes // width) % 2 == 0
        for first in range(4):
            if first & bit:
                continue
            one, two = tiles[first], tiles[first | bit]
            tiles[first] = jnp.where(low, one, turn_lanes(two, width))
            tiles[first | bit] = jnp.where(low, turn_lanes(one, -width), two)
    return tiles


def swap_rows(tile):
    lanes, rows = lane_index() // 16, row_index()
    for bit in (1, 2, 4):
        row_bit, lane_bit = (rows // bit) % 2, (lanes // bit) % 2
        up = turn_rows(turn_lanes(tile, 16 * bit), -bit)
        down = turn_rows(turn_lanes(tile, -16 * bit), bit)
        tile = jnp.where(row_bit == lane_bit, tile, jnp.where(row_bit == 0, up, down))
    return tile


def put_slots(out_ref, tiles, rows, base):
    zero = jnp.zeros((8, 128), f32)
    for half in range(2):
        group = [tiles[4 * half + x] if 4 * half + x < 6 else zero for x in range(4)]
        for quad, tile in enumerate(swap_quads(group)):
            out_ref[pl.ds(rows * quad + base + half, 8, stride=4 * rows), :] = tile


def get_slots(in_ref, rows, base):
    tiles = []
    for half in range(2):
        group = [in_ref[pl.ds(rows * quad + base + half, 8, stride=4 * rows), :] for quad in range(4)]
        tiles += swap_quads(group)
    return tiles[:6]


def put_cell_vector(out_ref, vector_ref, rows, base):
    put_slots(out_ref, [swap_rows(vector_ref[8 * t : 8 * t + 8, :]) for t in range(6)], rows, base)


def inverse_matvec(inverse_ref, vector_ref, out_ref):
    totals = None
    for a in range(48):
        term = inverse_ref[a].astype(f32) * vector_ref[a : a + 1, :]
        totals = term if totals is None else totals + term
    out_ref[...] = totals


def pack_blocks(block_ref, out_ref, base, groups):
    station = lax.axis_index("axial")
    quads = lane_index() // 4
    keeps = [(bit, (quads & bit) == 0) for bit in (1, 2, 4, 8, 16)]
    for group in groups:
        ah_pair, bh_pair = group // 3, group % 3
        items = [None] * 32
        for y in range(2):
            for p in range(8):
                wide = block_ref[16 * ah_pair + 8 * y + p, 16 * bh_pair : 16 * bh_pair + 16, :].astype(f32)
                for h in range(2):
                    i = 4 * p + 2 * y + h
                    items[i] = pltpu.roll(turn_rows(wide[8 * h : 8 * h + 8], -p), (4 * i + 4 * station) % 128, 1)
        for bit, keep in keeps:
            items = [jnp.where(keep, items[j], items[(j + bit) % 32]) for j in range(32)]
        for j in range(32):
            out_ref[(64 - j - station) % 32, base + 8 * group : base + 8 * group + 8, :] = items[j]


def fetch_thirds(block_hbm, block_ref, sems):
    copies = []
    for third in range(3):
        there = (slice(16 * third, 16 * third + 16), slice(None), slice(None))
        copies.append(pltpu.make_async_copy(block_hbm.at[there], block_ref.at[there], sems.at[third]))
    return copies


def join_stations(parts):
    chunk = line_lanes() // 4
    for bit in (1, 2):
        keep = (chunk & bit) == 0
        parts = [jnp.where(keep, parts[j], parts[(j + bit) % 4]) for j in range(4)]
    return [turn_lanes(parts[-x % 4], -4 * x) for x in range(4)]


def unpack_cell(in_ref, base, out_ref, cell):
    for group in range(9):
        at = base + 8 * group
        parts = [in_ref[4 * cell + k, at : at + 8, :] for k in range(4)]
        for x, tile in enumerate(join_stations(parts)):
            at = 8 * (4 * group + x)
            out_ref[cell, at : at + 8, :] = tile


def tile_at(ah, bh):
    return 4 * (3 * (ah // 2) + bh // 2) + 2 * (ah % 2) + bh % 2


def line_sweep(blocks_ref, const_ref, out_ref, reverse, beside=None):
    order = list(range(8))
    if reverse:
        order = order[::-1]
    state = None
    for turn in range(2):
        for n, cell in enumerate(order):
            if beside is not None:
                beside(turn, n)
            consts = [jnp.broadcast_to(const_ref[t, cell : cell + 1, :], (8, 128)) for t in range(6)]
            if state is None:
                state = consts
                continue
            products = line_product(blocks_ref, cell, state)
            state = [const - product for const, product in zip(consts, products)]
            if turn == 1:
                for t in range(6):
                    out_ref[t, cell : cell + 1, :] = state[t][0:1]


def stations_sum(tile):
    station = (line_lanes() // 4) % 4
    before = jnp.where(station > 0, turn_lanes(tile, 4), 0.0)
    after = jnp.where(station < 3, turn_lanes(tile, -4), 0.0)
    return before + after


def first_send_kernel(
    forward_hbm, backward_hbm, inverse_hbm, rhs_hbm, coupling_hbm, out_hbm,
    f_ref, b_ref, i_ref, rhs_ref, coupling_ref, c_ref, vectors_ref, packed_ref, sems, out_sems,
):
    forward = fetch_thirds(forward_hbm, f_ref, sems.at[0])
    inverse = fetch_thirds(inverse_hbm, i_ref, sems.at[1])
    backward = fetch_thirds(backward_hbm, b_ref, sems.at[2])
    vectors = [
        pltpu.make_async_copy(source, target, sems.at[3, n])
        for n, (source, target) in enumerate(((rhs_hbm, rhs_ref), (coupling_hbm, coupling_ref)))
    ]
    for copy in forward + vectors + inverse:
        copy.start()
    leaving = []

    def leave(row, rows):
        there = (slice(None), slice(row, row + rows), slice(None))
        leaving.append(pltpu.make_async_copy(packed_ref.at[there], out_hbm.at[there], out_sems.at[len(leaving)]))
        leaving[-1].start()

    for third in range(3):
        forward[third].wait()
        if third == 0:
            for copy in backward:
                copy.start()
        pack_blocks(f_ref, packed_ref, 0, range(3 * third, 3 * third + 3))
        leave(24 * third, 24)
    for copy in vectors + inverse:
        copy.wait()
    for third in range(3):
        backward[third].wait()
        if third == 0:
            inverse_matvec(i_ref, rhs_ref, c_ref)
            for n, vector_ref in enumerate((c_ref, rhs_ref, coupling_ref)):
                put_cell_vector(vectors_ref, vector_ref, 8, 2 * n)
            for e in range(32):
                packed_ref[e, 144:152, :] = vectors_ref[8 * e : 8 * e + 8, :]
        pack_blocks(b_ref, packed_ref, 72, range(3 * third, 3 * third + 3))
        if third == 0:
            leave(144, 8)
        leave(72 + 24 * third, 24)
    for copy in leaving:
        copy.wait()


def first_kernel(slots_ref, *refs):
    own_ref, other_ref, forward_ref, backward_ref, first_ref, middle_ref, coupling_ref, packed_ref, c_ref, y_ref = refs
    for e in range(32):
        packed_ref[8 * e : 8 * e + 8, :] = slots_ref[e, 144:152, :]
    for t, tile in enumerate(get_slots(packed_ref, 8, 0)):
        c_ref[t] = to_line(tile)

    def unpack(turn, n):
        if turn == 0:
            unpack_cell(slots_ref, 0, forward_ref, n)
        else:
            unpack_cell(slots_ref, 72, backward_ref, n)

    line_sweep(forward_ref, c_ref, y_ref, False, unpack)
    line_sweep(backward_ref, y_ref, first_ref, True)
    rhs = [to_line(tile) for tile in get_slots(packed_ref, 8, 2)]
    coupling = [to_line(tile) for tile in get_slots(packed_ref, 8, 4)]
    half, _ = half_position()
    low = row_index() < 4
    own, other = [], []
    for t in range(6):
        first = first_ref[t]
        middle = rhs[t] - first + coupling[t] * stations_sum(first)
        turned = turn_rows(middle, 4)
        other.append(jnp.where(half == 0, turned, middle))
        own.append(jnp.where(half == 0, middle, turned))
        middle_ref[t] = middle
        coupling_ref[t] = coupling[t]
    for u in range(3):
        other_ref[u] = jnp.where(low, other[2 * u], turn_rows(other[2 * u + 1], 4))
        own_ref[u] = jnp.where(low, own[2 * u], turn_rows(own[2 * u + 1], 4))


def half_position():
    cell = lax.axis_index("azim")
    return cell // 4, (cell % 4) * 4 + lax.axis_index("axial")


def inverse_send_kernel(inverse_hbm, *refs):
    outs, (i_ref, packed_ref, fetch_sems, sems) = refs[:16], refs[16:]
    fetches = fetch_thirds(inverse_hbm, i_ref, fetch_sems)
    for copy in fetches:
        copy.start()
    for third, copy in enumerate(fetches):
        copy.wait()
        pack_blocks(i_ref, packed_ref, 0, range(3 * third, 3 * third + 3))
    half, place = half_position()
    copies = []
    for d in range(16):
        target = place ^ d
        for n, source in enumerate((16 * half + target, 16 * (1 - half) + target)):
            copies.append(
                pltpu.make_async_copy(packed_ref.at[source], outs[d].at[pl.ds(72 * n, 72), :], sems.at[2 * d + n])
            )
            copies[-1].start()
    for copy in copies:
        copy.wait()


def inverse_get_kernel(*refs):
    ins, out_ref = refs[:4], refs[4]
    station = lax.axis_index("axial")
    for lines in range(2):
        for group in range(9):
            at = 72 * lines + 8 * group
            parts = [part[at : at + 8, :] for part in ins]
            for bit in (1, 2):
                parts = [jnp.where((station & bit) == 0, parts[k], parts[k ^ bit]) for k in range(4)]
            for x, tile in enumerate(join_stations(parts)):
                at = 8 * (4 * group + x)
                out_ref[lines, at : at + 8, :] = tile


def line_product(blocks_ref, cell, state):
    products = []
    for bh in range(6):
        total = None
        for ah in range(6):
            at = 8 * tile_at(ah, bh)
            term = blocks_ref[cell, at : at + 8, :] * state[ah]
            total = term if total is None else total + term
        total = pltpu.roll(total, 0, 1, stride=16, stride_axis=0)
        for span in (4, 2, 1):
            total = total + turn_rows(total, span)
        products.append(total)
    return products


def half_inverse_kernel(lines, vector_ref, *refs):
    blocks, out_ref = refs[:4], refs[4]
    _, place = half_position()
    cell = place // 4
    rows = row_index()
    totals = [jnp.zeros((8, 128), f32)] * 3
    for n in range(4):
        state = [
            jnp.broadcast_to(vector_ref[t // 2, pl.ds(4 * (t % 2) + (cell ^ n), 1), :], (8, 128)) for t in range(6)
        ]
        for t, product in enumerate(line_product(blocks[n], lines, state)):
            totals[t // 2] = jnp.where(rows == 4 * (t % 2) + (cell ^ n), product, totals[t // 2])
    for u in range(3):
        out_ref[u] = totals[u]


def second_kernel(
    own_ref, other_ref, forward_ref, backward_ref, first_ref, middle_ref, coupling_ref, out_ref, c_ref, y_ref, second_ref
):
    half, _ = half_position()
    low = row_index() < 4
    for t in range(6):
        own, other = own_ref[t // 2], other_ref[t // 2]
        if t % 2:
            own = turn_rows(own, 4)
        else:
            other = turn_rows(other, 4)
        tile = jnp.where(low, own, other)
        c_ref[t] = jnp.where(half == 0, tile, turn_rows(tile, 4))
    line_sweep(forward_ref, c_ref, y_ref, False)
    line_sweep(backward_ref, y_ref, second_ref, True)
    correction, remaining = [], []
    for t in range(6):
        second = second_ref[t]
        correction.append(from_line(first_ref[t] + second))
        remaining.append(from_line(middle_ref[t] - second + coupling_ref[t] * stations_sum(second)))
    put_slots(out_ref, correction, 4, 0)
    put_slots(out_ref, remaining, 4, 2)


def last_kernel(slots_ref, correction_ref, remaining_ref):
    for out_ref, base in ((correction_ref, 0), (remaining_ref, 2)):
        for t, tile in enumerate(get_slots(slots_ref, 4, base)):
            out_ref[8 * t : 8 * t + 8, :] = swap_rows(tile)


def shaped(*sizes):
    return jax.ShapeDtypeStruct(sizes, f32)


def call(kernel, outs, scratch=()):
    return pl.pallas_call(
        kernel,
        out_shape=outs,
        scratch_shapes=[pltpu.VMEM(sizes, f32) for sizes in scratch],
        compiler_params=pltpu.CompilerParams(vmem_limit_bytes=VMEM_LIMIT),
    )


def exchange(slots, rows):
    moved = lax.all_to_all(slots.reshape(32, rows, 128), BOTH, 0, 0, tiled=True)
    return moved.reshape(32 * rows, 128)


def line_plan(rhs, coupling, fwd_coupling, bwd_coupling, block_inverse):
    source, coupling_field = rhs.reshape(48, 128), coupling.reshape(48, 128)
    forward_blocks = fwd_coupling.reshape(48, 48, 128)
    backward_blocks = bwd_coupling.reshape(48, 48, 128)
    inverse_blocks = block_inverse.reshape(48, 48, 128)
    tiles, pairs, held = shaped(6, 8, 128), shaped(3, 8, 128), shaped(8, 288, 128)
    blocks = pltpu.VMEM((48, 48, 128), jnp.bfloat16)
    vector = pltpu.VMEM((48, 128), f32)

    slots = pl.pallas_call(
        first_send_kernel,
        out_shape=pltpu.HBM((32, 152, 128), f32),
        in_specs=[pl.BlockSpec(memory_space=pltpu.HBM)] * 5,
        out_specs=pl.BlockSpec(memory_space=pltpu.HBM),
        scratch_shapes=[blocks, blocks, blocks, vector, vector, vector]
        + [
            pltpu.VMEM((256, 128), f32),
            pltpu.VMEM((32, 152, 128), f32),
            pltpu.SemaphoreType.DMA((4, 3)),
            pltpu.SemaphoreType.DMA((7,)),
        ],
        compiler_params=pltpu.CompilerParams(vmem_limit_bytes=VMEM_LIMIT),
    )(*[
        pltpu.with_memory_space_constraint(array, pltpu.HBM)
        for array in (forward_blocks, backward_blocks, inverse_blocks, source, coupling_field)
    ])
    slots, inverse_blocks = lax.optimization_barrier((slots, inverse_blocks))
    slots = lax.all_to_all(slots, BOTH, 0, 0, tiled=True)

    parts = pl.pallas_call(
        inverse_send_kernel,
        out_shape=[shaped(144, 128)] * 16,
        in_specs=[pl.BlockSpec(memory_space=pltpu.HBM)],
        out_specs=[pl.BlockSpec(memory_space=pltpu.HBM)] * 16,
        scratch_shapes=[
            blocks, pltpu.VMEM((32, 72, 128), f32), pltpu.SemaphoreType.DMA((3,)), pltpu.SemaphoreType.DMA((32,))
        ],
        compiler_params=pltpu.CompilerParams(vmem_limit_bytes=VMEM_LIMIT),
    )(pltpu.with_memory_space_constraint(inverse_blocks, pltpu.HBM))
    parts = [parts[0]] + [lax.ppermute(parts[d], BOTH, [(e, e ^ d) for e in range(32)]) for d in range(1, 16)]
    inverse = [
        call(inverse_get_kernel, pltpu.VMEM((2, 288, 128), f32))(*parts[4 * n : 4 * n + 4]) for n in range(4)
    ]

    own, other, forward, backward, first, middle, coupling_lines = call(
        first_kernel, (pairs, pairs, held, held, tiles, tiles, tiles), [(256, 128), (6, 8, 128), (6, 8, 128)]
    )(slots)

    def with_partner(vector):
        return lax.ppermute(vector, BOTH, [(e, e ^ 16) for e in range(32)])

    other = with_partner(other)
    own = call(functools.partial(half_inverse_kernel, 0), pairs)(own, *inverse)
    other = call(functools.partial(half_inverse_kernel, 1), pairs)(other, *inverse)
    other = with_partner(other)
    slots = call(second_kernel, shaped(128, 128), [(6, 8, 128)] * 3)(
        own, other, forward, backward, first, middle, coupling_lines
    )
    slots = exchange(slots, 4)
    correction, remaining = call(last_kernel, (shaped(48, 128), shaped(48, 128)))(slots)
    return correction.reshape(rhs.shape), remaining.reshape(rhs.shape)


def from_behind(value, axis, steps):
    count = lax.axis_size(axis)
    initial, last = (max(0, -steps), min(count, count - steps))
    return lax.ppermute(value, axis, [(source, source + steps) for source in range(initial, last)])


def from_root(shard, axis, root):
    mine = lax.axis_index(axis) == root
    return lax.psum(jnp.where(mine, shard, jnp.zeros_like(shard)), axis)


def extended(block, sides, width):
    for axis, dim in sides:
        count = lax.axis_size(axis)
        forward = [(i, i + 1) for i in range(count - 1)]
        backward = [(target, source) for source, target in forward]
        low = lax.ppermute(
            lax.slice_in_dim(block, block.shape[dim] - width, None, axis=dim), axis, forward
        )
        high = lax.ppermute(lax.slice_in_dim(block, 0, width, axis=dim), axis, backward)
        block = jnp.concatenate([low, block, high], axis=dim)
    return block


def cell_stride(one_block, carried, const_term):
    return const_term - jnp.einsum(
        "abl,al->bl", one_block.astype(jnp.float32), carried, precision=highest
    )


def compose_cells(blocks, sequence):
    running = None
    for position in sequence:
        one_block = blocks[position].astype(jnp.float32)
        running = -jnp.swapaxes(one_block, 0, 1)
    return running


def doubling_maps(local_map, reverse):
    size = lax.axis_size("azim")
    index = lax.axis_index("azim")
    levels = []
    current = local_map
    distance = 1
    while distance < size:
        if reverse:
            moved = from_behind(current, "azim", -distance)
            exists = index + distance < size
        else:
            moved = from_behind(current, "azim", distance)
            exists = index >= distance
        levels.append((current, distance))
        current = jnp.where(
            exists, jnp.einsum("bcl,cal->bal", current, moved, precision=highest), current
        )
        distance = distance * 2
    return (levels, current)


def doubling_entries(map_levels, local_offset, reverse):
    levels, final_map = map_levels
    size = lax.axis_size("azim")
    index = lax.axis_index("azim")
    running = local_offset
    for current, distance in levels:
        if reverse:
            moved = from_behind(running, "azim", -distance)
        else:
            moved = from_behind(running, "azim", distance)
        running = jnp.einsum("bcl,cl->bl", current, moved, precision=highest) + running
    if reverse:
        wrapped = from_root(running, "azim", 0)
    else:
        wrapped = from_root(running, "azim", size - 1)
    leaving = jnp.einsum("bcl,cl->bl", final_map, wrapped, precision=highest) + running
    if reverse:
        shifted = from_behind(leaving, "azim", -1)
        first_device = index == size - 1
    else:
        shifted = from_behind(leaving, "azim", 1)
        first_device = index == 0
    return jnp.where(first_device, wrapped, shifted)


def sweep(blocks, consts, map_levels, reverse):
    cell_count = blocks.shape[0]
    sequence = list(range(cell_count))
    if reverse:
        sequence = sequence[::-1]
    carried = jnp.zeros(consts.shape[1:], jnp.float32)
    for position in sequence:
        carried = cell_stride(blocks[position], carried, consts[position])
    local_offset = carried
    incoming_maps = doubling_entries(map_levels, local_offset, reverse)
    outputs = [None] * cell_count
    carried = incoming_maps
    for position in sequence:
        carried = cell_stride(blocks[position], carried, consts[position])
        outputs[position] = carried
    return jnp.stack(outputs)


def on_device(rhs, coupling, fwd_coupling, bwd_coupling, block_inverse):
    cell_count, block_width, _, position_total, radial_count = fwd_coupling.shape
    line_count = position_total * radial_count
    forward_blocks = fwd_coupling.reshape(cell_count, block_width, block_width, line_count)
    backward_blocks = bwd_coupling.reshape(cell_count, block_width, block_width, line_count)
    inverse_blocks = block_inverse.reshape(cell_count, block_width, block_width, line_count)
    source = rhs.reshape(cell_count, block_width, line_count)
    coupling_field = coupling.reshape(cell_count, block_width, line_count)
    forward_map = compose_cells(forward_blocks, list(range(cell_count)))
    backward_map = compose_cells(backward_blocks, list(range(cell_count))[::-1])
    forward_levels = None
    backward_levels = None
    forward_levels = doubling_maps(forward_map, False)
    backward_levels = doubling_maps(backward_map, True)

    def precondition(vector):
        consts = jnp.stack(
            [
                jnp.einsum(
                    "abl,al->bl",
                    inverse_blocks[0].astype(jnp.float32),
                    vector[0],
                    precision=highest,
                )
            ]
        )
        forward = sweep(forward_blocks, consts, forward_levels, False)
        return sweep(backward_blocks, forward, backward_levels, True)

    def stations_sum(field):
        grid = field.reshape(cell_count, block_width, position_total, radial_count)
        padded = extended(grid, (("axial", 2),), 1)
        return (padded[:, :, :-2] + padded[:, :, 2:]).reshape(cell_count, block_width, line_count)

    applied_once = precondition(source)
    middle = source - applied_once + coupling_field * stations_sum(applied_once)
    second = precondition(middle)
    correction = applied_once + second
    remaining = middle - second + coupling_field * stations_sum(second)
    return (correction.reshape(rhs.shape), remaining.reshape(rhs.shape))


def solution(mesh):
    cells, stations = mesh.shape["azim"], mesh.shape["axial"]

    def on_each(rhs, coupling, fwd_coupling, bwd_coupling, block_inverse):
        local = fwd_coupling.shape
        if (cells, stations) == (8, 4) and local == (1, 48, 48, 1, 128):
            return line_plan(rhs, coupling, fwd_coupling, bwd_coupling, block_inverse)
        return on_device(rhs, coupling, fwd_coupling, bwd_coupling, block_inverse)

    return jax.shard_map(
        on_each,
        mesh=mesh,
        in_specs=(
            P("azim", None, "axial", None),
            P("azim", None, "axial", None),
            P("azim", None, None, "axial", None),
            P("azim", None, None, "axial", None),
            P("azim", None, None, "axial", None),
        ),
        out_specs=(P("azim", None, "axial", None), P("azim", None, "axial", None)),
        check_vma=False,
    )
```

```python
import functools

import jax
import jax.numpy as jnp
from jax import lax
from jax.experimental import pallas as pl
from jax.experimental.pallas import tpu as pltpu
from jax.sharding import PartitionSpec as P

highest = lax.Precision.HIGHEST
f32 = jnp.float32
BOTH = ("azim", "axial")
VMEM_LIMIT = 16 * 1024 * 1024


def lane_index():
    return lax.broadcasted_iota(jnp.int32, (8, 128), 1)


def row_index():
    return lax.broadcasted_iota(jnp.int32, (8, 128), 0)


def turn_lanes(tile, steps):
    steps = steps % 128
    return pltpu.roll(tile, steps, 1) if steps else tile


def turn_rows(tile, steps):
    steps = steps % 8
    return pltpu.roll(tile, steps, 0) if steps else tile


def line_lanes():
    return lane_index() + 16 - 4 * lax.axis_index("axial")


def to_line(tile):
    return pltpu.roll(tile, 4 * (4 * lax.axis_index("azim") + lax.axis_index("axial")), 1)


def from_line(tile):
    return pltpu.roll(tile, (128 - 4 * (4 * lax.axis_index("azim") + lax.axis_index("axial"))) % 128, 1)


def swap_quads(tiles, lanes=None):
    lanes = lane_index() if lanes is None else lanes
    tiles = list(tiles)
    for bit, width in ((1, 4), (2, 8)):
        low = (lanes // width) % 2 == 0
        for first in range(4):
            if first & bit:
                continue
            one, two = tiles[first], tiles[first | bit]
            tiles[first] = jnp.where(low, one, turn_lanes(two, width))
            tiles[first | bit] = jnp.where(low, turn_lanes(one, -width), two)
    return tiles


def swap_rows(tile):
    lanes, rows = lane_index() // 16, row_index()
    for bit in (1, 2, 4):
        row_bit, lane_bit = (rows // bit) % 2, (lanes // bit) % 2
        up = turn_rows(turn_lanes(tile, 16 * bit), -bit)
        down = turn_rows(turn_lanes(tile, -16 * bit), bit)
        tile = jnp.where(row_bit == lane_bit, tile, jnp.where(row_bit == 0, up, down))
    return tile


def put_slots(out_ref, tiles, rows, base):
    zero = jnp.zeros((8, 128), f32)
    for half in range(2):
        group = [tiles[4 * half + x] if 4 * half + x < 6 else zero for x in range(4)]
        for quad, tile in enumerate(swap_quads(group)):
            out_ref[pl.ds(rows * quad + base + half, 8, stride=4 * rows), :] = tile


def get_slots(in_ref, rows, base):
    tiles = []
    for half in range(2):
        group = [in_ref[pl.ds(rows * quad + base + half, 8, stride=4 * rows), :] for quad in range(4)]
        tiles += swap_quads(group)
    return tiles[:6]


def put_cell_vector(out_ref, vector_ref, rows, base):
    put_slots(out_ref, [swap_rows(vector_ref[8 * t : 8 * t + 8, :]) for t in range(6)], rows, base)


def inverse_matvec(inverse_ref, vector_ref, out_ref):
    totals = None
    for a in range(48):
        term = inverse_ref[a].astype(f32) * vector_ref[a : a + 1, :]
        totals = term if totals is None else totals + term
    out_ref[...] = totals


def pack_blocks(block_ref, out_ref, base, groups):
    station = lax.axis_index("axial")
    quads = lane_index() // 4
    keeps = [(bit, (quads & bit) == 0) for bit in (1, 2, 4, 8, 16)]
    for group in groups:
        ah_pair, bh_pair = group // 3, group % 3
        items = [None] * 32
        for y in range(2):
            for p in range(8):
                wide = block_ref[16 * ah_pair + 8 * y + p, 16 * bh_pair : 16 * bh_pair + 16, :].astype(f32)
                for h in range(2):
                    i = 4 * p + 2 * y + h
                    items[i] = pltpu.roll(turn_rows(wide[8 * h : 8 * h + 8], -p), (4 * i + 4 * station) % 128, 1)
        for bit, keep in keeps:
            items = [jnp.where(keep, items[j], items[(j + bit) % 32]) for j in range(32)]
        for slot in range(35):
            out_ref[slot, base + 8 * group : base + 8 * group + 8, :] = items[-slot % 32]


def fetch_thirds(block_hbm, block_ref, sems):
    copies = []
    for third in range(3):
        there = (slice(16 * third, 16 * third + 16), slice(None), slice(None))
        copies.append(pltpu.make_async_copy(block_hbm.at[there], block_ref.at[there], sems.at[third]))
    return copies


def join_stations(parts):
    chunk = line_lanes() // 4
    for bit in (1, 2):
        keep = (chunk & bit) == 0
        parts = [jnp.where(keep, parts[j], parts[(j + bit) % 4]) for j in range(4)]
    return [turn_lanes(parts[-x % 4], -4 * x) for x in range(4)]


def unpack_cell(in_ref, base, out_ref, cell):
    for group in range(9):
        at = base + 8 * group
        parts = [in_ref[4 * cell + k, at : at + 8, :] for k in range(4)]
        for x, tile in enumerate(join_stations(parts)):
            at = 8 * (4 * group + x)
            out_ref[cell, at : at + 8, :] = tile


def tile_at(ah, bh):
    return 4 * (3 * (ah // 2) + bh // 2) + 2 * (ah % 2) + bh % 2


def line_sweep(blocks_ref, const_ref, out_ref, reverse, beside=None):
    order = list(range(8))
    if reverse:
        order = order[::-1]
    state = None
    for turn in range(2):
        for n, cell in enumerate(order):
            if beside is not None:
                beside(turn, n)
            consts = [jnp.broadcast_to(const_ref[t, cell : cell + 1, :], (8, 128)) for t in range(6)]
            if state is None:
                state = consts
                continue
            state = line_step(blocks_ref, cell, state, consts)
            if turn == 1:
                for t in range(6):
                    out_ref[t, cell : cell + 1, :] = state[t][0:1]


def stations_sum(tile):
    station = (line_lanes() // 4) % 4
    before = jnp.where(station > 0, turn_lanes(tile, 4), 0.0)
    after = jnp.where(station < 3, turn_lanes(tile, -4), 0.0)
    return before + after


def first_send_kernel(
    forward_hbm, backward_hbm, inverse_hbm, rhs_hbm, coupling_hbm, out_hbm,
    f_ref, b_ref, i_ref, rhs_ref, coupling_ref, c_ref, vectors_ref, packed_ref, sems, out_sems,
):
    forward = fetch_thirds(forward_hbm, f_ref, sems.at[0])
    inverse = fetch_thirds(inverse_hbm, i_ref, sems.at[1])
    backward = fetch_thirds(backward_hbm, b_ref, sems.at[2])
    vectors = [
        pltpu.make_async_copy(source, target, sems.at[3, n])
        for n, (source, target) in enumerate(((rhs_hbm, rhs_ref), (coupling_hbm, coupling_ref)))
    ]
    for copy in forward + vectors + inverse:
        copy.start()
    leaving = []

    def leave(row, rows, first):
        source = packed_ref.at[pl.ds(first, 32), pl.ds(row, rows), :]
        target = out_hbm.at[:, pl.ds(row, rows), :]
        leaving.append(pltpu.make_async_copy(source, target, out_sems.at[len(leaving)]))
        leaving[-1].start()

    station = lax.axis_index("axial")

    for third in range(3):
        forward[third].wait()
        if third == 0:
            for copy in backward:
                copy.start()
        pack_blocks(f_ref, packed_ref, 0, range(3 * third, 3 * third + 3))
        leave(24 * third, 24, station)
    for copy in vectors + inverse:
        copy.wait()
    for third in range(3):
        backward[third].wait()
        if third == 0:
            inverse_matvec(i_ref, rhs_ref, c_ref)
            for n, vector_ref in enumerate((c_ref, rhs_ref, coupling_ref)):
                put_cell_vector(vectors_ref, vector_ref, 8, 2 * n)
            for e in range(32):
                packed_ref[e, 144:152, :] = vectors_ref[8 * e : 8 * e + 8, :]
        pack_blocks(b_ref, packed_ref, 72, range(3 * third, 3 * third + 3))
        if third == 0:
            leave(144, 8, 0)
        leave(72 + 24 * third, 24, station)
    for copy in leaving:
        copy.wait()


def first_kernel(slots_ref, *refs):
    own_ref, other_ref, forward_ref, backward_ref, first_ref, middle_ref, coupling_ref, packed_ref, c_ref, y_ref = refs
    for e in range(32):
        packed_ref[8 * e : 8 * e + 8, :] = slots_ref[e, 144:152, :]
    for t, tile in enumerate(get_slots(packed_ref, 8, 0)):
        c_ref[t] = to_line(tile)

    def unpack(turn, n):
        if turn == 0:
            unpack_cell(slots_ref, 0, forward_ref, n)
        else:
            unpack_cell(slots_ref, 72, backward_ref, n)

    line_sweep(forward_ref, c_ref, y_ref, False, unpack)
    line_sweep(backward_ref, y_ref, first_ref, True)
    rhs = [to_line(tile) for tile in get_slots(packed_ref, 8, 2)]
    coupling = [to_line(tile) for tile in get_slots(packed_ref, 8, 4)]
    half, _ = half_position()
    low = row_index() < 4
    own, other = [], []
    for t in range(6):
        first = first_ref[t]
        middle = rhs[t] - first + coupling[t] * stations_sum(first)
        turned = turn_rows(middle, 4)
        other.append(jnp.where(half == 0, turned, middle))
        own.append(jnp.where(half == 0, middle, turned))
        middle_ref[t] = middle
        coupling_ref[t] = coupling[t]
    for u in range(3):
        other_ref[u] = jnp.where(low, other[2 * u], turn_rows(other[2 * u + 1], 4))
        own_ref[u] = jnp.where(low, own[2 * u], turn_rows(own[2 * u + 1], 4))


def half_position():
    cell = lax.axis_index("azim")
    return cell // 4, (cell % 4) * 4 + lax.axis_index("axial")


def inverse_send_kernel(inverse_hbm, *refs):
    outs, (i_ref, packed_ref, fetch_sems, sems) = refs[:16], refs[16:]
    fetches = fetch_thirds(inverse_hbm, i_ref, fetch_sems)
    for copy in fetches:
        copy.start()
    for third, copy in enumerate(fetches):
        copy.wait()
        pack_blocks(i_ref, packed_ref, 0, range(3 * third, 3 * third + 3))
    half, place = half_position()
    station = place % 4
    copies = []
    for d in range(16):
        target = place ^ d
        for n, source in enumerate((16 * half + target, 16 * (1 - half) + target)):
            copies.append(
                pltpu.make_async_copy(packed_ref.at[source + station], outs[d].at[pl.ds(72 * n, 72), :], sems.at[2 * d + n])
            )
            copies[-1].start()
    for copy in copies:
        copy.wait()


def inverse_get_kernel(*refs):
    ins, out_ref = refs[:4], refs[4]
    station = lax.axis_index("axial")
    for lines in range(2):
        for group in range(9):
            at = 72 * lines + 8 * group
            parts = [part[at : at + 8, :] for part in ins]
            for bit in (1, 2):
                parts = [jnp.where((station & bit) == 0, parts[k], parts[k ^ bit]) for k in range(4)]
            for x, tile in enumerate(join_stations(parts)):
                at = 8 * (4 * group + x)
                out_ref[lines, at : at + 8, :] = tile


def line_step(blocks_ref, cell, state, consts):
    following = []
    for bh in range(6):
        terms = []
        for ah in range(6):
            at = 8 * tile_at(ah, bh)
            terms.append(blocks_ref[cell, at : at + 8, :] * state[ah])
        total = (terms[0] + terms[1]) + (terms[2] + terms[3]) + (terms[4] + terms[5])
        total = pltpu.roll(total, 0, 1, stride=16, stride_axis=0)
        for span in (4, 2):
            total = total + turn_rows(total, span)
        following.append((consts[bh] - total) - turn_rows(total, 1))
    return following


def half_inverse_kernel(lines, vector_ref, *refs):
    blocks, out_ref = refs[:4], refs[4]
    _, place = half_position()
    cell = place // 4
    rows = row_index()
    zero = jnp.zeros((8, 128), f32)
    totals = [zero] * 3
    for n in range(4):
        state = [
            jnp.broadcast_to(vector_ref[t // 2, pl.ds(4 * (t % 2) + (cell ^ n), 1), :], (8, 128)) for t in range(6)
        ]
        for t, product in enumerate(line_step(blocks[n], lines, state, [zero] * 6)):
            totals[t // 2] = jnp.where(rows == 4 * (t % 2) + (cell ^ n), product, totals[t // 2])
    for u in range(3):
        out_ref[u] = -totals[u]


def second_kernel(
    own_ref, other_ref, forward_ref, backward_ref, first_ref, middle_ref, coupling_ref, out_ref, c_ref, y_ref, second_ref
):
    half, _ = half_position()
    low = row_index() < 4
    for t in range(6):
        own, other = own_ref[t // 2], other_ref[t // 2]
        if t % 2:
            own = turn_rows(own, 4)
        else:
            other = turn_rows(other, 4)
        tile = jnp.where(low, own, other)
        c_ref[t] = jnp.where(half == 0, tile, turn_rows(tile, 4))
    line_sweep(forward_ref, c_ref, y_ref, False)
    line_sweep(backward_ref, y_ref, second_ref, True)
    correction, remaining = [], []
    for t in range(6):
        second = second_ref[t]
        correction.append(from_line(first_ref[t] + second))
        remaining.append(from_line(middle_ref[t] - second + coupling_ref[t] * stations_sum(second)))
    put_slots(out_ref, correction, 4, 0)
    put_slots(out_ref, remaining, 4, 2)


def last_kernel(slots_ref, correction_ref, remaining_ref):
    for out_ref, base in ((correction_ref, 0), (remaining_ref, 2)):
        for t, tile in enumerate(get_slots(slots_ref, 4, base)):
            out_ref[8 * t : 8 * t + 8, :] = swap_rows(tile)


def shaped(*sizes):
    return jax.ShapeDtypeStruct(sizes, f32)


def call(kernel, outs, scratch=()):
    return pl.pallas_call(
        kernel,
        out_shape=outs,
        scratch_shapes=[pltpu.VMEM(sizes, f32) for sizes in scratch],
        compiler_params=pltpu.CompilerParams(vmem_limit_bytes=VMEM_LIMIT),
    )


def exchange(slots, rows):
    moved = lax.all_to_all(slots.reshape(32, rows, 128), BOTH, 0, 0, tiled=True)
    return moved.reshape(32 * rows, 128)


def line_plan(rhs, coupling, fwd_coupling, bwd_coupling, block_inverse):
    source, coupling_field = rhs.reshape(48, 128), coupling.reshape(48, 128)
    forward_blocks = fwd_coupling.reshape(48, 48, 128)
    backward_blocks = bwd_coupling.reshape(48, 48, 128)
    inverse_blocks = block_inverse.reshape(48, 48, 128)
    tiles, pairs, held = shaped(6, 8, 128), shaped(3, 8, 128), shaped(8, 288, 128)
    blocks = pltpu.VMEM((48, 48, 128), jnp.bfloat16)
    vector = pltpu.VMEM((48, 128), f32)

    slots = pl.pallas_call(
        first_send_kernel,
        out_shape=pltpu.HBM((32, 152, 128), f32),
        in_specs=[pl.BlockSpec(memory_space=pltpu.HBM)] * 5,
        out_specs=pl.BlockSpec(memory_space=pltpu.HBM),
        scratch_shapes=[blocks, blocks, blocks, vector, vector, vector]
        + [
            pltpu.VMEM((256, 128), f32),
            pltpu.VMEM((35, 152, 128), f32),
            pltpu.SemaphoreType.DMA((4, 3)),
            pltpu.SemaphoreType.DMA((7,)),
        ],
        compiler_params=pltpu.CompilerParams(vmem_limit_bytes=VMEM_LIMIT),
    )(*[
        pltpu.with_memory_space_constraint(array, pltpu.HBM)
        for array in (forward_blocks, backward_blocks, inverse_blocks, source, coupling_field)
    ])
    slots, inverse_blocks = lax.optimization_barrier((slots, inverse_blocks))
    slots = lax.all_to_all(slots, BOTH, 0, 0, tiled=True)

    parts = pl.pallas_call(
        inverse_send_kernel,
        out_shape=[shaped(144, 128)] * 16,
        in_specs=[pl.BlockSpec(memory_space=pltpu.HBM)],
        out_specs=[pl.BlockSpec(memory_space=pltpu.HBM)] * 16,
        scratch_shapes=[
            blocks, pltpu.VMEM((35, 72, 128), f32), pltpu.SemaphoreType.DMA((3,)), pltpu.SemaphoreType.DMA((32,))
        ],
        compiler_params=pltpu.CompilerParams(vmem_limit_bytes=VMEM_LIMIT),
    )(pltpu.with_memory_space_constraint(inverse_blocks, pltpu.HBM))
    parts = [parts[0]] + [lax.ppermute(parts[d], BOTH, [(e, e ^ d) for e in range(32)]) for d in range(1, 16)]
    inverse = [
        call(inverse_get_kernel, pltpu.VMEM((2, 288, 128), f32))(*parts[4 * n : 4 * n + 4]) for n in range(4)
    ]

    own, other, forward, backward, first, middle, coupling_lines = call(
        first_kernel, (pairs, pairs, held, held, tiles, tiles, tiles), [(256, 128), (6, 8, 128), (6, 8, 128)]
    )(slots)

    def with_partner(vector):
        return lax.ppermute(vector, BOTH, [(e, e ^ 16) for e in range(32)])

    other = with_partner(other)
    own = call(functools.partial(half_inverse_kernel, 0), pairs)(own, *inverse)
    other = call(functools.partial(half_inverse_kernel, 1), pairs)(other, *inverse)
    other = with_partner(other)
    slots = call(second_kernel, shaped(128, 128), [(6, 8, 128)] * 3)(
        own, other, forward, backward, first, middle, coupling_lines
    )
    slots = exchange(slots, 4)
    correction, remaining = call(last_kernel, (shaped(48, 128), shaped(48, 128)))(slots)
    return correction.reshape(rhs.shape), remaining.reshape(rhs.shape)


def from_behind(value, axis, steps):
    count = lax.axis_size(axis)
    initial, last = (max(0, -steps), min(count, count - steps))
    return lax.ppermute(value, axis, [(source, source + steps) for source in range(initial, last)])


def from_root(shard, axis, root):
    mine = lax.axis_index(axis) == root
    return lax.psum(jnp.where(mine, shard, jnp.zeros_like(shard)), axis)


def extended(block, sides, width):
    for axis, dim in sides:
        count = lax.axis_size(axis)
        forward = [(i, i + 1) for i in range(count - 1)]
        backward = [(target, source) for source, target in forward]
        low = lax.ppermute(
            lax.slice_in_dim(block, block.shape[dim] - width, None, axis=dim), axis, forward
        )
        high = lax.ppermute(lax.slice_in_dim(block, 0, width, axis=dim), axis, backward)
        block = jnp.concatenate([low, block, high], axis=dim)
    return block


def cell_stride(one_block, carried, const_term):
    return const_term - jnp.einsum(
        "abl,al->bl", one_block.astype(jnp.float32), carried, precision=highest
    )


def compose_cells(blocks, sequence):
    running = None
    for position in sequence:
        one_block = blocks[position].astype(jnp.float32)
        running = -jnp.swapaxes(one_block, 0, 1)
    return running


def doubling_maps(local_map, reverse):
    size = lax.axis_size("azim")
    index = lax.axis_index("azim")
    levels = []
    current = local_map
    distance = 1
    while distance < size:
        if reverse:
            moved = from_behind(current, "azim", -distance)
            exists = index + distance < size
        else:
            moved = from_behind(current, "azim", distance)
            exists = index >= distance
        levels.append((current, distance))
        current = jnp.where(
            exists, jnp.einsum("bcl,cal->bal", current, moved, precision=highest), current
        )
        distance = distance * 2
    return (levels, current)


def doubling_entries(map_levels, local_offset, reverse):
    levels, final_map = map_levels
    size = lax.axis_size("azim")
    index = lax.axis_index("azim")
    running = local_offset
    for current, distance in levels:
        if reverse:
            moved = from_behind(running, "azim", -distance)
        else:
            moved = from_behind(running, "azim", distance)
        running = jnp.einsum("bcl,cl->bl", current, moved, precision=highest) + running
    if reverse:
        wrapped = from_root(running, "azim", 0)
    else:
        wrapped = from_root(running, "azim", size - 1)
    leaving = jnp.einsum("bcl,cl->bl", final_map, wrapped, precision=highest) + running
    if reverse:
        shifted = from_behind(leaving, "azim", -1)
        first_device = index == size - 1
    else:
        shifted = from_behind(leaving, "azim", 1)
        first_device = index == 0
    return jnp.where(first_device, wrapped, shifted)


def sweep(blocks, consts, map_levels, reverse):
    cell_count = blocks.shape[0]
    sequence = list(range(cell_count))
    if reverse:
        sequence = sequence[::-1]
    carried = jnp.zeros(consts.shape[1:], jnp.float32)
    for position in sequence:
        carried = cell_stride(blocks[position], carried, consts[position])
    local_offset = carried
    incoming_maps = doubling_entries(map_levels, local_offset, reverse)
    outputs = [None] * cell_count
    carried = incoming_maps
    for position in sequence:
        carried = cell_stride(blocks[position], carried, consts[position])
        outputs[position] = carried
    return jnp.stack(outputs)


def on_device(rhs, coupling, fwd_coupling, bwd_coupling, block_inverse):
    cell_count, block_width, _, position_total, radial_count = fwd_coupling.shape
    line_count = position_total * radial_count
    forward_blocks = fwd_coupling.reshape(cell_count, block_width, block_width, line_count)
    backward_blocks = bwd_coupling.reshape(cell_count, block_width, block_width, line_count)
    inverse_blocks = block_inverse.reshape(cell_count, block_width, block_width, line_count)
    source = rhs.reshape(cell_count, block_width, line_count)
    coupling_field = coupling.reshape(cell_count, block_width, line_count)
    forward_map = compose_cells(forward_blocks, list(range(cell_count)))
    backward_map = compose_cells(backward_blocks, list(range(cell_count))[::-1])
    forward_levels = None
    backward_levels = None
    forward_levels = doubling_maps(forward_map, False)
    backward_levels = doubling_maps(backward_map, True)

    def precondition(vector):
        consts = jnp.stack(
            [
                jnp.einsum(
                    "abl,al->bl",
                    inverse_blocks[0].astype(jnp.float32),
                    vector[0],
                    precision=highest,
                )
            ]
        )
        forward = sweep(forward_blocks, consts, forward_levels, False)
        return sweep(backward_blocks, forward, backward_levels, True)

    def stations_sum(field):
        grid = field.reshape(cell_count, block_width, position_total, radial_count)
        padded = extended(grid, (("axial", 2),), 1)
        return (padded[:, :, :-2] + padded[:, :, 2:]).reshape(cell_count, block_width, line_count)

    applied_once = precondition(source)
    middle = source - applied_once + coupling_field * stations_sum(applied_once)
    second = precondition(middle)
    correction = applied_once + second
    remaining = middle - second + coupling_field * stations_sum(second)
    return (correction.reshape(rhs.shape), remaining.reshape(rhs.shape))


def solution(mesh):
    cells, stations = mesh.shape["azim"], mesh.shape["axial"]

    def on_each(rhs, coupling, fwd_coupling, bwd_coupling, block_inverse):
        local = fwd_coupling.shape
        if (cells, stations) == (8, 4) and local == (1, 48, 48, 1, 128):
            return line_plan(rhs, coupling, fwd_coupling, bwd_coupling, block_inverse)
        return on_device(rhs, coupling, fwd_coupling, bwd_coupling, block_inverse)

    return jax.shard_map(
        on_each,
        mesh=mesh,
        in_specs=(
            P("azim", None, "axial", None),
            P("azim", None, "axial", None),
            P("azim", None, None, "axial", None),
            P("azim", None, None, "axial", None),
            P("azim", None, None, "axial", None),
        ),
        out_specs=(P("azim", None, "axial", None), P("azim", None, "axial", None)),
        check_vma=False,
    )
```

```python
import functools

import jax
import jax.numpy as jnp
from jax import lax
from jax.experimental import pallas as pl
from jax.experimental.pallas import tpu as pltpu
from jax.sharding import PartitionSpec as P

highest = lax.Precision.HIGHEST
f32 = jnp.float32
BOTH = ("azim", "axial")
VMEM_LIMIT = 16 * 1024 * 1024


def lane_index():
    return lax.broadcasted_iota(jnp.int32, (8, 128), 1)


def row_index():
    return lax.broadcasted_iota(jnp.int32, (8, 128), 0)


def turn_lanes(tile, steps):
    steps = steps % 128
    return pltpu.roll(tile, steps, 1) if steps else tile


def turn_rows(tile, steps):
    steps = steps % 8
    return pltpu.roll(tile, steps, 0) if steps else tile


def line_lanes():
    return lane_index() + 16 - 4 * lax.axis_index("axial")


def to_line(tile):
    return pltpu.roll(tile, 4 * (4 * lax.axis_index("azim") + lax.axis_index("axial")), 1)


def from_line(tile):
    return pltpu.roll(tile, (128 - 4 * (4 * lax.axis_index("azim") + lax.axis_index("axial"))) % 128, 1)


def swap_quads(tiles, lanes=None):
    lanes = lane_index() if lanes is None else lanes
    tiles = list(tiles)
    for bit, width in ((1, 4), (2, 8)):
        low = (lanes // width) % 2 == 0
        for first in range(4):
            if first & bit:
                continue
            one, two = tiles[first], tiles[first | bit]
            tiles[first] = jnp.where(low, one, turn_lanes(two, width))
            tiles[first | bit] = jnp.where(low, turn_lanes(one, -width), two)
    return tiles


def swap_rows(tile):
    lanes, rows = lane_index() // 16, row_index()
    for bit in (1, 2, 4):
        row_bit, lane_bit = (rows // bit) % 2, (lanes // bit) % 2
        up = turn_rows(turn_lanes(tile, 16 * bit), -bit)
        down = turn_rows(turn_lanes(tile, -16 * bit), bit)
        tile = jnp.where(row_bit == lane_bit, tile, jnp.where(row_bit == 0, up, down))
    return tile


def put_slots(out_ref, tiles, rows, base):
    zero = jnp.zeros((8, 128), f32)
    for half in range(2):
        group = [tiles[4 * half + x] if 4 * half + x < 6 else zero for x in range(4)]
        for quad, tile in enumerate(swap_quads(group)):
            out_ref[pl.ds(rows * quad + base + half, 8, stride=4 * rows), :] = tile


def get_slots(in_ref, rows, base):
    tiles = []
    for half in range(2):
        group = [in_ref[pl.ds(rows * quad + base + half, 8, stride=4 * rows), :] for quad in range(4)]
        tiles += swap_quads(group)
    return tiles[:6]


def put_cell_vector(out_ref, vector_ref, rows, base):
    put_slots(out_ref, [swap_rows(vector_ref[8 * t : 8 * t + 8, :]) for t in range(6)], rows, base)


def inverse_matvec(inverse_ref, vector_ref, out_ref):
    totals = None
    for a in range(48):
        term = inverse_ref[a].astype(f32) * vector_ref[a : a + 1, :]
        totals = term if totals is None else totals + term
    out_ref[...] = totals


def pack_blocks(block_ref, out_ref, base, groups):
    station = lax.axis_index("axial")
    quads = lane_index() // 4
    keeps = [(bit, (quads & bit) == 0) for bit in (1, 2, 4, 8, 16)]
    for group in groups:
        ah_pair, bh_pair = group // 3, group % 3
        items = [None] * 32
        for y in range(2):
            for p in range(8):
                wide = block_ref[16 * ah_pair + 8 * y + p, 16 * bh_pair : 16 * bh_pair + 16, :].astype(f32)
                for h in range(2):
                    i = 4 * p + 2 * y + h
                    items[i] = pltpu.roll(turn_rows(wide[8 * h : 8 * h + 8], -p), (4 * i + 4 * station) % 128, 1)
        for bit, keep in keeps:
            items = [jnp.where(keep, items[j], items[(j + bit) % 32]) for j in range(32)]
        for slot in range(35):
            out_ref[slot, base + 8 * group : base + 8 * group + 8, :] = items[-slot % 32]


def fetch_thirds(block_hbm, block_ref, sems):
    copies = []
    for third in range(3):
        there = (slice(16 * third, 16 * third + 16), slice(None), slice(None))
        copies.append(pltpu.make_async_copy(block_hbm.at[there], block_ref.at[there], sems.at[third]))
    return copies


def join_stations(parts):
    chunk = line_lanes() // 4
    for bit in (1, 2):
        keep = (chunk & bit) == 0
        parts = [jnp.where(keep, parts[j], parts[(j + bit) % 4]) for j in range(4)]
    return [turn_lanes(parts[-x % 4], -4 * x) for x in range(4)]


def unpack_cell(in_ref, base, out_ref, cell):
    for group in range(9):
        at = base + 8 * group
        parts = [in_ref[4 * cell + k, at : at + 8, :] for k in range(4)]
        for x, tile in enumerate(join_stations(parts)):
            at = 8 * (4 * group + x)
            out_ref[cell, at : at + 8, :] = tile


def tile_at(ah, bh):
    return 4 * (3 * (ah // 2) + bh // 2) + 2 * (ah % 2) + bh % 2


def line_sweep(blocks_ref, const_ref, out_ref, reverse, rows_ref, beside=None):
    order = list(range(8))
    if reverse:
        order = order[::-1]
    state = None
    for turn in range(2):
        for n, cell in enumerate(order):
            if beside is not None:
                beside(turn, n)
            consts = [jnp.broadcast_to(const_ref[t, cell : cell + 1, :], (8, 128)) for t in range(6)]
            if state is None:
                state = consts
                continue
            state = line_step(blocks_ref, cell, state, consts, rows_ref, 48 * (n % 2))
            if turn == 1:
                for t in range(6):
                    out_ref[t, cell : cell + 1, :] = state[t][0:1]


def stations_sum(tile):
    station = (line_lanes() // 4) % 4
    before = jnp.where(station > 0, turn_lanes(tile, 4), 0.0)
    after = jnp.where(station < 3, turn_lanes(tile, -4), 0.0)
    return before + after


def first_send_kernel(
    forward_hbm, backward_hbm, inverse_hbm, rhs_hbm, coupling_hbm, out_hbm,
    f_ref, b_ref, i_ref, rhs_ref, coupling_ref, c_ref, vectors_ref, packed_ref, sems, out_sems,
):
    forward = fetch_thirds(forward_hbm, f_ref, sems.at[0])
    inverse = fetch_thirds(inverse_hbm, i_ref, sems.at[1])
    backward = fetch_thirds(backward_hbm, b_ref, sems.at[2])
    vectors = [
        pltpu.make_async_copy(source, target, sems.at[3, n])
        for n, (source, target) in enumerate(((rhs_hbm, rhs_ref), (coupling_hbm, coupling_ref)))
    ]
    for copy in forward + vectors + inverse:
        copy.start()
    leaving = []

    def leave(row, rows, first):
        source = packed_ref.at[pl.ds(first, 32), pl.ds(row, rows), :]
        target = out_hbm.at[:, pl.ds(row, rows), :]
        leaving.append(pltpu.make_async_copy(source, target, out_sems.at[len(leaving)]))
        leaving[-1].start()

    station = lax.axis_index("axial")

    for third in range(3):
        forward[third].wait()
        if third == 0:
            for copy in backward:
                copy.start()
        pack_blocks(f_ref, packed_ref, 0, range(3 * third, 3 * third + 3))
        leave(24 * third, 24, station)
    for copy in vectors + inverse:
        copy.wait()
    for third in range(3):
        backward[third].wait()
        if third == 0:
            inverse_matvec(i_ref, rhs_ref, c_ref)
            for n, vector_ref in enumerate((c_ref, rhs_ref, coupling_ref)):
                put_cell_vector(vectors_ref, vector_ref, 8, 2 * n)
            for e in range(32):
                packed_ref[e, 144:152, :] = vectors_ref[8 * e : 8 * e + 8, :]
        pack_blocks(b_ref, packed_ref, 72, range(3 * third, 3 * third + 3))
        if third == 0:
            leave(144, 8, 0)
        leave(72 + 24 * third, 24, station)
    for copy in leaving:
        copy.wait()


def first_kernel(slots_ref, *refs):
    own_ref, other_ref, forward_ref, backward_ref, first_ref, middle_ref, coupling_ref, packed_ref, c_ref, y_ref, rows_ref = refs
    for e in range(32):
        packed_ref[8 * e : 8 * e + 8, :] = slots_ref[e, 144:152, :]
    for t, tile in enumerate(get_slots(packed_ref, 8, 0)):
        c_ref[t] = to_line(tile)

    def unpack(turn, n):
        if turn == 0:
            unpack_cell(slots_ref, 0, forward_ref, n)
        else:
            unpack_cell(slots_ref, 72, backward_ref, n)

    line_sweep(forward_ref, c_ref, y_ref, False, rows_ref, unpack)
    line_sweep(backward_ref, y_ref, first_ref, True, rows_ref)
    rhs = [to_line(tile) for tile in get_slots(packed_ref, 8, 2)]
    coupling = [to_line(tile) for tile in get_slots(packed_ref, 8, 4)]
    half, _ = half_position()
    low = row_index() < 4
    own, other = [], []
    for t in range(6):
        first = first_ref[t]
        middle = rhs[t] - first + coupling[t] * stations_sum(first)
        turned = turn_rows(middle, 4)
        other.append(jnp.where(half == 0, turned, middle))
        own.append(jnp.where(half == 0, middle, turned))
        middle_ref[t] = middle
        coupling_ref[t] = coupling[t]
    for u in range(3):
        other_ref[u] = jnp.where(low, other[2 * u], turn_rows(other[2 * u + 1], 4))
        own_ref[u] = jnp.where(low, own[2 * u], turn_rows(own[2 * u + 1], 4))


def half_position():
    cell = lax.axis_index("azim")
    return cell // 4, (cell % 4) * 4 + lax.axis_index("axial")


def inverse_send_kernel(inverse_hbm, *refs):
    outs, (i_ref, packed_ref, fetch_sems, sems) = refs[:16], refs[16:]
    fetches = fetch_thirds(inverse_hbm, i_ref, fetch_sems)
    for copy in fetches:
        copy.start()
    for third, copy in enumerate(fetches):
        copy.wait()
        pack_blocks(i_ref, packed_ref, 0, range(3 * third, 3 * third + 3))
    half, place = half_position()
    station = place % 4
    copies = []
    for d in range(16):
        target = place ^ d
        for n, source in enumerate((16 * half + target, 16 * (1 - half) + target)):
            copies.append(
                pltpu.make_async_copy(packed_ref.at[source + station], outs[d].at[pl.ds(72 * n, 72), :], sems.at[2 * d + n])
            )
            copies[-1].start()
    for copy in copies:
        copy.wait()


def inverse_get_kernel(*refs):
    ins, out_ref = refs[:4], refs[4]
    station = lax.axis_index("axial")
    for lines in range(2):
        for group in range(9):
            at = 72 * lines + 8 * group
            parts = [part[at : at + 8, :] for part in ins]
            for bit in (1, 2):
                parts = [jnp.where((station & bit) == 0, parts[k], parts[k ^ bit]) for k in range(4)]
            for x, tile in enumerate(join_stations(parts)):
                at = 8 * (4 * group + x)
                out_ref[lines, at : at + 8, :] = tile


def line_step(blocks_ref, cell, state, consts, rows_ref, base):
    following = []
    for bh in range(6):
        terms = []
        for ah in range(6):
            at = 8 * tile_at(ah, bh)
            terms.append(blocks_ref[cell, at : at + 8, :] * state[ah])
        total = (terms[0] + terms[1]) + (terms[2] + terms[3]) + (terms[4] + terms[5])
        at = base + 8 * bh
        rows_ref[at : at + 8, :] = pltpu.roll(total, 0, 1, stride=16, stride_axis=0)
        rows = [rows_ref[pl.ds(at + s, 8, stride=0), :] for s in range(8)]
        low, high = (rows[0] + rows[1]) + (rows[2] + rows[3]), (rows[4] + rows[5]) + (rows[6] + rows[7])
        following.append((consts[bh] - low) - high)
    return following


def half_inverse_kernel(lines, vector_ref, *refs):
    blocks, (out_ref, rows_ref) = refs[:4], refs[4:]
    _, place = half_position()
    cell = place // 4
    rows = row_index()
    zero = jnp.zeros((8, 128), f32)
    totals = [zero] * 3
    for n in range(4):
        state = [
            jnp.broadcast_to(vector_ref[t // 2, pl.ds(4 * (t % 2) + (cell ^ n), 1), :], (8, 128)) for t in range(6)
        ]
        for t, product in enumerate(line_step(blocks[n], lines, state, [zero] * 6, rows_ref, 48 * n)):
            totals[t // 2] = jnp.where(rows == 4 * (t % 2) + (cell ^ n), product, totals[t // 2])
    for u in range(3):
        out_ref[u] = -totals[u]


def second_kernel(
    own_ref, other_ref, forward_ref, backward_ref, first_ref, middle_ref, coupling_ref, out_ref, c_ref, y_ref, second_ref,
    rows_ref,
):
    half, _ = half_position()
    low = row_index() < 4
    for t in range(6):
        own, other = own_ref[t // 2], other_ref[t // 2]
        if t % 2:
            own = turn_rows(own, 4)
        else:
            other = turn_rows(other, 4)
        tile = jnp.where(low, own, other)
        c_ref[t] = jnp.where(half == 0, tile, turn_rows(tile, 4))
    line_sweep(forward_ref, c_ref, y_ref, False, rows_ref)
    line_sweep(backward_ref, y_ref, second_ref, True, rows_ref)
    correction, remaining = [], []
    for t in range(6):
        second = second_ref[t]
        correction.append(from_line(first_ref[t] + second))
        remaining.append(from_line(middle_ref[t] - second + coupling_ref[t] * stations_sum(second)))
    put_slots(out_ref, correction, 4, 0)
    put_slots(out_ref, remaining, 4, 2)


def last_kernel(slots_ref, correction_ref, remaining_ref):
    for out_ref, base in ((correction_ref, 0), (remaining_ref, 2)):
        for t, tile in enumerate(get_slots(slots_ref, 4, base)):
            out_ref[8 * t : 8 * t + 8, :] = swap_rows(tile)


def shaped(*sizes):
    return jax.ShapeDtypeStruct(sizes, f32)


def call(kernel, outs, scratch=()):
    return pl.pallas_call(
        kernel,
        out_shape=outs,
        scratch_shapes=[pltpu.VMEM(sizes, f32) for sizes in scratch],
        compiler_params=pltpu.CompilerParams(vmem_limit_bytes=VMEM_LIMIT),
    )


def exchange(slots, rows):
    moved = lax.all_to_all(slots.reshape(32, rows, 128), BOTH, 0, 0, tiled=True)
    return moved.reshape(32 * rows, 128)


def line_plan(rhs, coupling, fwd_coupling, bwd_coupling, block_inverse):
    source, coupling_field = rhs.reshape(48, 128), coupling.reshape(48, 128)
    forward_blocks = fwd_coupling.reshape(48, 48, 128)
    backward_blocks = bwd_coupling.reshape(48, 48, 128)
    inverse_blocks = block_inverse.reshape(48, 48, 128)
    tiles, pairs, held = shaped(6, 8, 128), shaped(3, 8, 128), shaped(8, 288, 128)
    blocks = pltpu.VMEM((48, 48, 128), jnp.bfloat16)
    vector = pltpu.VMEM((48, 128), f32)

    slots = pl.pallas_call(
        first_send_kernel,
        out_shape=pltpu.HBM((32, 152, 128), f32),
        in_specs=[pl.BlockSpec(memory_space=pltpu.HBM)] * 5,
        out_specs=pl.BlockSpec(memory_space=pltpu.HBM),
        scratch_shapes=[blocks, blocks, blocks, vector, vector, vector]
        + [
            pltpu.VMEM((256, 128), f32),
            pltpu.VMEM((35, 152, 128), f32),
            pltpu.SemaphoreType.DMA((4, 3)),
            pltpu.SemaphoreType.DMA((7,)),
        ],
        compiler_params=pltpu.CompilerParams(vmem_limit_bytes=VMEM_LIMIT),
    )(*[
        pltpu.with_memory_space_constraint(array, pltpu.HBM)
        for array in (forward_blocks, backward_blocks, inverse_blocks, source, coupling_field)
    ])
    slots, inverse_blocks = lax.optimization_barrier((slots, inverse_blocks))
    slots = lax.all_to_all(slots, BOTH, 0, 0, tiled=True)

    parts = pl.pallas_call(
        inverse_send_kernel,
        out_shape=[shaped(144, 128)] * 16,
        in_specs=[pl.BlockSpec(memory_space=pltpu.HBM)],
        out_specs=[pl.BlockSpec(memory_space=pltpu.HBM)] * 16,
        scratch_shapes=[
            blocks, pltpu.VMEM((35, 72, 128), f32), pltpu.SemaphoreType.DMA((3,)), pltpu.SemaphoreType.DMA((32,))
        ],
        compiler_params=pltpu.CompilerParams(vmem_limit_bytes=VMEM_LIMIT),
    )(pltpu.with_memory_space_constraint(inverse_blocks, pltpu.HBM))
    parts = [parts[0]] + [lax.ppermute(parts[d], BOTH, [(e, e ^ d) for e in range(32)]) for d in range(1, 16)]
    inverse = [
        call(inverse_get_kernel, pltpu.VMEM((2, 288, 128), f32))(*parts[4 * n : 4 * n + 4]) for n in range(4)
    ]

    own, other, forward, backward, first, middle, coupling_lines = call(
        first_kernel, (pairs, pairs, held, held, tiles, tiles, tiles), [(256, 128), (6, 8, 128), (6, 8, 128), (96, 128)]
    )(slots)

    def with_partner(vector):
        return lax.ppermute(vector, BOTH, [(e, e ^ 16) for e in range(32)])

    other = with_partner(other)
    own = call(functools.partial(half_inverse_kernel, 0), pairs, [(192, 128)])(own, *inverse)
    other = call(functools.partial(half_inverse_kernel, 1), pairs, [(192, 128)])(other, *inverse)
    other = with_partner(other)
    slots = call(second_kernel, shaped(128, 128), [(6, 8, 128)] * 3 + [(96, 128)])(
        own, other, forward, backward, first, middle, coupling_lines
    )
    slots = exchange(slots, 4)
    correction, remaining = call(last_kernel, (shaped(48, 128), shaped(48, 128)))(slots)
    return correction.reshape(rhs.shape), remaining.reshape(rhs.shape)


def from_behind(value, axis, steps):
    count = lax.axis_size(axis)
    initial, last = (max(0, -steps), min(count, count - steps))
    return lax.ppermute(value, axis, [(source, source + steps) for source in range(initial, last)])


def from_root(shard, axis, root):
    mine = lax.axis_index(axis) == root
    return lax.psum(jnp.where(mine, shard, jnp.zeros_like(shard)), axis)


def extended(block, sides, width):
    for axis, dim in sides:
        count = lax.axis_size(axis)
        forward = [(i, i + 1) for i in range(count - 1)]
        backward = [(target, source) for source, target in forward]
        low = lax.ppermute(
            lax.slice_in_dim(block, block.shape[dim] - width, None, axis=dim), axis, forward
        )
        high = lax.ppermute(lax.slice_in_dim(block, 0, width, axis=dim), axis, backward)
        block = jnp.concatenate([low, block, high], axis=dim)
    return block


def cell_stride(one_block, carried, const_term):
    return const_term - jnp.einsum(
        "abl,al->bl", one_block.astype(jnp.float32), carried, precision=highest
    )


def compose_cells(blocks, sequence):
    running = None
    for position in sequence:
        one_block = blocks[position].astype(jnp.float32)
        running = -jnp.swapaxes(one_block, 0, 1)
    return running


def doubling_maps(local_map, reverse):
    size = lax.axis_size("azim")
    index = lax.axis_index("azim")
    levels = []
    current = local_map
    distance = 1
    while distance < size:
        if reverse:
            moved = from_behind(current, "azim", -distance)
            exists = index + distance < size
        else:
            moved = from_behind(current, "azim", distance)
            exists = index >= distance
        levels.append((current, distance))
        current = jnp.where(
            exists, jnp.einsum("bcl,cal->bal", current, moved, precision=highest), current
        )
        distance = distance * 2
    return (levels, current)


def doubling_entries(map_levels, local_offset, reverse):
    levels, final_map = map_levels
    size = lax.axis_size("azim")
    index = lax.axis_index("azim")
    running = local_offset
    for current, distance in levels:
        if reverse:
            moved = from_behind(running, "azim", -distance)
        else:
            moved = from_behind(running, "azim", distance)
        running = jnp.einsum("bcl,cl->bl", current, moved, precision=highest) + running
    if reverse:
        wrapped = from_root(running, "azim", 0)
    else:
        wrapped = from_root(running, "azim", size - 1)
    leaving = jnp.einsum("bcl,cl->bl", final_map, wrapped, precision=highest) + running
    if reverse:
        shifted = from_behind(leaving, "azim", -1)
        first_device = index == size - 1
    else:
        shifted = from_behind(leaving, "azim", 1)
        first_device = index == 0
    return jnp.where(first_device, wrapped, shifted)


def sweep(blocks, consts, map_levels, reverse):
    cell_count = blocks.shape[0]
    sequence = list(range(cell_count))
    if reverse:
        sequence = sequence[::-1]
    carried = jnp.zeros(consts.shape[1:], jnp.float32)
    for position in sequence:
        carried = cell_stride(blocks[position], carried, consts[position])
    local_offset = carried
    incoming_maps = doubling_entries(map_levels, local_offset, reverse)
    outputs = [None] * cell_count
    carried = incoming_maps
    for position in sequence:
        carried = cell_stride(blocks[position], carried, consts[position])
        outputs[position] = carried
    return jnp.stack(outputs)


def on_device(rhs, coupling, fwd_coupling, bwd_coupling, block_inverse):
    cell_count, block_width, _, position_total, radial_count = fwd_coupling.shape
    line_count = position_total * radial_count
    forward_blocks = fwd_coupling.reshape(cell_count, block_width, block_width, line_count)
    backward_blocks = bwd_coupling.reshape(cell_count, block_width, block_width, line_count)
    inverse_blocks = block_inverse.reshape(cell_count, block_width, block_width, line_count)
    source = rhs.reshape(cell_count, block_width, line_count)
    coupling_field = coupling.reshape(cell_count, block_width, line_count)
    forward_map = compose_cells(forward_blocks, list(range(cell_count)))
    backward_map = compose_cells(backward_blocks, list(range(cell_count))[::-1])
    forward_levels = None
    backward_levels = None
    forward_levels = doubling_maps(forward_map, False)
    backward_levels = doubling_maps(backward_map, True)

    def precondition(vector):
        consts = jnp.stack(
            [
                jnp.einsum(
                    "abl,al->bl",
                    inverse_blocks[0].astype(jnp.float32),
                    vector[0],
                    precision=highest,
                )
            ]
        )
        forward = sweep(forward_blocks, consts, forward_levels, False)
        return sweep(backward_blocks, forward, backward_levels, True)

    def stations_sum(field):
        grid = field.reshape(cell_count, block_width, position_total, radial_count)
        padded = extended(grid, (("axial", 2),), 1)
        return (padded[:, :, :-2] + padded[:, :, 2:]).reshape(cell_count, block_width, line_count)

    applied_once = precondition(source)
    middle = source - applied_once + coupling_field * stations_sum(applied_once)
    second = precondition(middle)
    correction = applied_once + second
    remaining = middle - second + coupling_field * stations_sum(second)
    return (correction.reshape(rhs.shape), remaining.reshape(rhs.shape))


def solution(mesh):
    cells, stations = mesh.shape["azim"], mesh.shape["axial"]

    def on_each(rhs, coupling, fwd_coupling, bwd_coupling, block_inverse):
        local = fwd_coupling.shape
        if (cells, stations) == (8, 4) and local == (1, 48, 48, 1, 128):
            return line_plan(rhs, coupling, fwd_coupling, bwd_coupling, block_inverse)
        return on_device(rhs, coupling, fwd_coupling, bwd_coupling, block_inverse)

    return jax.shard_map(
        on_each,
        mesh=mesh,
        in_specs=(
            P("azim", None, "axial", None),
            P("azim", None, "axial", None),
            P("azim", None, None, "axial", None),
            P("azim", None, None, "axial", None),
            P("azim", None, None, "axial", None),
        ),
        out_specs=(P("azim", None, "axial", None), P("azim", None, "axial", None)),
        check_vma=False,
    )
```

```python
import functools

import jax
import jax.numpy as jnp
from jax import lax
from jax.experimental import pallas as pl
from jax.experimental.pallas import tpu as pltpu
from jax.sharding import PartitionSpec as P

highest = lax.Precision.HIGHEST
f32 = jnp.float32
BOTH = ("azim", "axial")
VMEM_LIMIT = 16 * 1024 * 1024


def lane_index():
    return lax.broadcasted_iota(jnp.int32, (8, 128), 1)


def row_index():
    return lax.broadcasted_iota(jnp.int32, (8, 128), 0)


def turn_lanes(tile, steps):
    steps = steps % 128
    return pltpu.roll(tile, steps, 1) if steps else tile


def turn_rows(tile, steps):
    steps = steps % 8
    return pltpu.roll(tile, steps, 0) if steps else tile


def line_lanes():
    return lane_index() + 16 - 4 * lax.axis_index("axial")


def to_line(tile):
    return pltpu.roll(tile, 4 * (4 * lax.axis_index("azim") + lax.axis_index("axial")), 1)


def from_line(tile):
    return pltpu.roll(tile, (128 - 4 * (4 * lax.axis_index("azim") + lax.axis_index("axial"))) % 128, 1)


def swap_quads(tiles, lanes=None):
    lanes = lane_index() if lanes is None else lanes
    tiles = list(tiles)
    for bit, width in ((1, 4), (2, 8)):
        low = (lanes // width) % 2 == 0
        for first in range(4):
            if first & bit:
                continue
            one, two = tiles[first], tiles[first | bit]
            tiles[first] = jnp.where(low, one, turn_lanes(two, width))
            tiles[first | bit] = jnp.where(low, turn_lanes(one, -width), two)
    return tiles


def swap_rows(tile):
    lanes, rows = lane_index() // 16, row_index()
    for bit in (1, 2, 4):
        row_bit, lane_bit = (rows // bit) % 2, (lanes // bit) % 2
        up = turn_rows(turn_lanes(tile, 16 * bit), -bit)
        down = turn_rows(turn_lanes(tile, -16 * bit), bit)
        tile = jnp.where(row_bit == lane_bit, tile, jnp.where(row_bit == 0, up, down))
    return tile


def put_slots(out_ref, tiles, rows, base):
    zero = jnp.zeros((8, 128), f32)
    for half in range(2):
        group = [tiles[4 * half + x] if 4 * half + x < 6 else zero for x in range(4)]
        for quad, tile in enumerate(swap_quads(group)):
            out_ref[pl.ds(rows * quad + base + half, 8, stride=4 * rows), :] = tile


def get_slots(in_ref, rows, base):
    tiles = []
    for half in range(2):
        group = [in_ref[pl.ds(rows * quad + base + half, 8, stride=4 * rows), :] for quad in range(4)]
        tiles += swap_quads(group)
    return tiles[:6]


def put_cell_vector(out_ref, vector_ref, rows, base):
    put_slots(out_ref, [swap_rows(vector_ref[8 * t : 8 * t + 8, :]) for t in range(6)], rows, base)


def inverse_matvec(inverse_ref, vector_ref, out_ref):
    totals = None
    for a in range(48):
        term = inverse_ref[a].astype(f32) * vector_ref[a : a + 1, :]
        totals = term if totals is None else totals + term
    out_ref[...] = totals


def pack_group(group, tile_of, out_ref, base):
    station = lax.axis_index("axial")
    quads = lane_index() // 4
    ah_pair, bh_pair = group // 3, group % 3
    items = []
    for i in range(32):
        p, y, h = i // 4, i // 2 % 2, i % 2
        items.append(pltpu.roll(tile_of(2 * ah_pair + y, 2 * bh_pair + h, p), (4 * i + 4 * station) % 128, 1))
    for bit in (1, 2, 4, 8, 16):
        keep = (quads & bit) == 0
        items = [jnp.where(keep, items[j], items[(j + bit) % 32]) for j in range(32)]
    for slot in range(35):
        out_ref[slot, base + 8 * group : base + 8 * group + 8, :] = items[-slot % 32]


def pack_third(third, kind, block_ref, wide_ref, out_ref, base):
    for n in range(16):
        a = 16 * third + n
        wide_ref[48 * a : 48 * a + 48, :] = block_ref[a].astype(f32)

    def tile_of(ah, bh, p):
        if kind == "even":
            return wide_ref[pl.ds(48 * 8 * ah + 8 * bh + p, 8, stride=48), :]
        at = 48 * (8 * ah + p) + 8 * bh
        tile = wide_ref[at : at + 8, :]
        return turn_rows(tile, -p) if kind == "skewed" else tile

    for group in range(3 * third, 3 * third + 3):
        pack_group(group, tile_of, out_ref, base)


def pack_by_parity(third, block_ref, wide_ref, out_ref, base):
    odd = lax.axis_index("azim") % 2

    @pl.when(odd == 0)
    def _():
        pack_third(third, "even", block_ref, wide_ref, out_ref, base)

    @pl.when(odd == 1)
    def _():
        pack_third(third, "odd", block_ref, wide_ref, out_ref, base)


def fetch_thirds(block_hbm, block_ref, sems):
    copies = []
    for third in range(3):
        there = (slice(16 * third, 16 * third + 16), slice(None), slice(None))
        copies.append(pltpu.make_async_copy(block_hbm.at[there], block_ref.at[there], sems.at[third]))
    return copies


def join_stations(parts):
    chunk = line_lanes() // 4
    for bit in (1, 2):
        keep = (chunk & bit) == 0
        parts = [jnp.where(keep, parts[j], parts[(j + bit) % 4]) for j in range(4)]
    return [turn_lanes(parts[-x % 4], -4 * x) for x in range(4)]


def unpack_cell(in_ref, base, out_ref, cell):
    for group in range(9):
        at = base + 8 * group
        parts = [in_ref[4 * cell + k, at : at + 8, :] for k in range(4)]
        for x, tile in enumerate(join_stations(parts)):
            at = 8 * (4 * group + x)
            out_ref[cell, at : at + 8, :] = tile


def tile_at(ah, bh):
    return 4 * (3 * (ah // 2) + bh // 2) + 2 * (ah % 2) + bh % 2


def diagonal(tile):
    turned = 4 * (4 * lax.axis_index("azim") + lax.axis_index("axial"))
    groups = (lane_index() + 128 - turned) % 128 // 16
    return jnp.where(groups == row_index(), tile, 0.0)


def over_groups(tile):
    for span in (64, 32, 16):
        tile = tile + turn_lanes(tile, span)
    return tile


def over_rows(tile):
    for span in (4, 2, 1):
        tile = tile + turn_rows(tile, span)
    return tile


def repeat_row(ref, t, cell):
    return jnp.broadcast_to(ref[t, cell : cell + 1, :], (8, 128))


def line_sweep(blocks_ref, const_of, keep, reverse, beside=None):
    order = list(range(8))
    if reverse:
        order = order[::-1]
    state = None
    for turn in range(2):
        for n, cell in enumerate(order):
            if beside is not None:
                beside(turn, n)
            consts = const_of(cell)
            if state is None:
                state = consts
                continue
            following = []
            for bh in range(6):
                terms = []
                for ah in range(6):
                    at = 8 * tile_at(ah, bh)
                    terms.append(blocks_ref[cell, at : at + 8, :] * state[ah])
                total = (terms[0] + terms[1]) + (terms[2] + terms[3]) + (terms[4] + terms[5])
                following.append(consts[bh] - (over_groups(total) if cell % 2 else over_rows(total)))
            state = following
            if turn == 1:
                keep(cell, state)


def both_sweeps(c_ref, forward_ref, backward_ref, y_ref, rows_ref, out_ref, beside=None):
    for cell in range(1, 8, 2):
        for t in range(6):
            rows_ref[cell // 2, t] = over_groups(diagonal(repeat_row(c_ref, t, cell)))

    def forward_const(cell):
        return [rows_ref[cell // 2, t] if cell % 2 else repeat_row(c_ref, t, cell) for t in range(6)]

    def forward_keep(cell, state):
        for t in range(6):
            y_ref[cell, t] = state[t]

    def backward_const(cell):
        return [y_ref[cell, t] for t in range(6)]

    def backward_keep(cell, state):
        for t in range(6):
            tile = over_rows(diagonal(state[t])) if cell % 2 else state[t]
            out_ref[t, cell : cell + 1, :] = tile[0:1]

    line_sweep(forward_ref, forward_const, forward_keep, False, beside)
    line_sweep(backward_ref, backward_const, backward_keep, True)


def stations_sum(tile):
    station = (line_lanes() // 4) % 4
    before = jnp.where(station > 0, turn_lanes(tile, 4), 0.0)
    after = jnp.where(station < 3, turn_lanes(tile, -4), 0.0)
    return before + after


def first_send_kernel(
    forward_hbm, backward_hbm, inverse_hbm, rhs_hbm, coupling_hbm, out_hbm,
    f_ref, b_ref, i_ref, wide_ref, rhs_ref, coupling_ref, c_ref, vectors_ref, packed_ref, sems, out_sems,
):
    forward = fetch_thirds(forward_hbm, f_ref, sems.at[0])
    inverse = fetch_thirds(inverse_hbm, i_ref, sems.at[1])
    backward = fetch_thirds(backward_hbm, b_ref, sems.at[2])
    vectors = [
        pltpu.make_async_copy(source, target, sems.at[3, n])
        for n, (source, target) in enumerate(((rhs_hbm, rhs_ref), (coupling_hbm, coupling_ref)))
    ]
    for copy in forward + vectors + inverse:
        copy.start()
    leaving = []

    def leave(row, rows, first):
        source = packed_ref.at[pl.ds(first, 32), pl.ds(row, rows), :]
        target = out_hbm.at[:, pl.ds(row, rows), :]
        leaving.append(pltpu.make_async_copy(source, target, out_sems.at[len(leaving)]))
        leaving[-1].start()

    station = lax.axis_index("axial")

    for third in range(3):
        forward[third].wait()
        if third == 0:
            for copy in backward:
                copy.start()
        pack_by_parity(third, f_ref, wide_ref, packed_ref, 0)
        leave(24 * third, 24, station)
    for copy in vectors + inverse:
        copy.wait()
    for third in range(3):
        backward[third].wait()
        if third == 0:
            inverse_matvec(i_ref, rhs_ref, c_ref)
            for n, vector_ref in enumerate((c_ref, rhs_ref, coupling_ref)):
                put_cell_vector(vectors_ref, vector_ref, 8, 2 * n)
            for e in range(32):
                packed_ref[e, 144:152, :] = vectors_ref[8 * e : 8 * e + 8, :]
        pack_by_parity(third, b_ref, wide_ref, packed_ref, 72)
        if third == 0:
            leave(144, 8, 0)
        leave(72 + 24 * third, 24, station)
    for copy in leaving:
        copy.wait()


def first_kernel(slots_ref, *refs):
    own_ref, other_ref, forward_ref, backward_ref, first_ref, middle_ref, coupling_ref, packed_ref, c_ref, y_ref, rows_ref = refs
    for e in range(32):
        packed_ref[8 * e : 8 * e + 8, :] = slots_ref[e, 144:152, :]
    for t, tile in enumerate(get_slots(packed_ref, 8, 0)):
        c_ref[t] = to_line(tile)

    def unpack(turn, n):
        if turn == 0:
            unpack_cell(slots_ref, 0, forward_ref, n)
        else:
            unpack_cell(slots_ref, 72, backward_ref, n)

    both_sweeps(c_ref, forward_ref, backward_ref, y_ref, rows_ref, first_ref, unpack)
    rhs = [to_line(tile) for tile in get_slots(packed_ref, 8, 2)]
    coupling = [to_line(tile) for tile in get_slots(packed_ref, 8, 4)]
    half, _ = half_position()
    low = row_index() < 4
    own, other = [], []
    for t in range(6):
        first = first_ref[t]
        middle = rhs[t] - first + coupling[t] * stations_sum(first)
        turned = turn_rows(middle, 4)
        other.append(jnp.where(half == 0, turned, middle))
        own.append(jnp.where(half == 0, middle, turned))
        middle_ref[t] = middle
        coupling_ref[t] = coupling[t]
    for u in range(3):
        other_ref[u] = jnp.where(low, other[2 * u], turn_rows(other[2 * u + 1], 4))
        own_ref[u] = jnp.where(low, own[2 * u], turn_rows(own[2 * u + 1], 4))


def half_position():
    cell = lax.axis_index("azim")
    return cell // 4, (cell % 4) * 4 + lax.axis_index("axial")


def inverse_send_kernel(inverse_hbm, *refs):
    outs, (i_ref, wide_ref, packed_ref, fetch_sems, sems) = refs[:16], refs[16:]
    fetches = fetch_thirds(inverse_hbm, i_ref, fetch_sems)
    for copy in fetches:
        copy.start()
    for third, copy in enumerate(fetches):
        copy.wait()
        pack_third(third, "skewed", i_ref, wide_ref, packed_ref, 0)
    half, place = half_position()
    station = place % 4
    copies = []
    for d in range(16):
        target = place ^ d
        for n, source in enumerate((16 * half + target, 16 * (1 - half) + target)):
            copies.append(
                pltpu.make_async_copy(packed_ref.at[source + station], outs[d].at[pl.ds(72 * n, 72), :], sems.at[2 * d + n])
            )
            copies[-1].start()
    for copy in copies:
        copy.wait()


def inverse_get_kernel(*refs):
    ins, out_ref = refs[:4], refs[4]
    station = lax.axis_index("axial")
    for lines in range(2):
        for group in range(9):
            at = 72 * lines + 8 * group
            parts = [part[at : at + 8, :] for part in ins]
            for bit in (1, 2):
                parts = [jnp.where((station & bit) == 0, parts[k], parts[k ^ bit]) for k in range(4)]
            for x, tile in enumerate(join_stations(parts)):
                at = 8 * (4 * group + x)
                out_ref[lines, at : at + 8, :] = tile


def line_step(blocks_ref, cell, state, consts):
    following = []
    for bh in range(6):
        terms = []
        for ah in range(6):
            at = 8 * tile_at(ah, bh)
            terms.append(blocks_ref[cell, at : at + 8, :] * state[ah])
        total = (terms[0] + terms[1]) + (terms[2] + terms[3]) + (terms[4] + terms[5])
        total = pltpu.roll(total, 0, 1, stride=16, stride_axis=0)
        for span in (4, 2):
            total = total + turn_rows(total, span)
        following.append((consts[bh] - total) - turn_rows(total, 1))
    return following


def half_inverse_kernel(lines, vector_ref, *refs):
    blocks, out_ref = refs[:4], refs[4]
    _, place = half_position()
    cell = place // 4
    rows = row_index()
    zero = jnp.zeros((8, 128), f32)
    totals = [zero] * 3
    for n in range(4):
        state = [
            jnp.broadcast_to(vector_ref[t // 2, pl.ds(4 * (t % 2) + (cell ^ n), 1), :], (8, 128)) for t in range(6)
        ]
        for t, product in enumerate(line_step(blocks[n], lines, state, [zero] * 6)):
            totals[t // 2] = jnp.where(rows == 4 * (t % 2) + (cell ^ n), product, totals[t // 2])
    for u in range(3):
        out_ref[u] = -totals[u]


def second_kernel(
    own_ref, other_ref, forward_ref, backward_ref, first_ref, middle_ref, coupling_ref, out_ref, c_ref, y_ref, rows_ref,
    second_ref,
):
    half, _ = half_position()
    low = row_index() < 4
    for t in range(6):
        own, other = own_ref[t // 2], other_ref[t // 2]
        if t % 2:
            own = turn_rows(own, 4)
        else:
            other = turn_rows(other, 4)
        tile = jnp.where(low, own, other)
        c_ref[t] = jnp.where(half == 0, tile, turn_rows(tile, 4))
    both_sweeps(c_ref, forward_ref, backward_ref, y_ref, rows_ref, second_ref)
    correction, remaining = [], []
    for t in range(6):
        second = second_ref[t]
        correction.append(from_line(first_ref[t] + second))
        remaining.append(from_line(middle_ref[t] - second + coupling_ref[t] * stations_sum(second)))
    put_slots(out_ref, correction, 4, 0)
    put_slots(out_ref, remaining, 4, 2)


def last_kernel(slots_ref, correction_ref, remaining_ref):
    for out_ref, base in ((correction_ref, 0), (remaining_ref, 2)):
        for t, tile in enumerate(get_slots(slots_ref, 4, base)):
            out_ref[8 * t : 8 * t + 8, :] = swap_rows(tile)


def shaped(*sizes):
    return jax.ShapeDtypeStruct(sizes, f32)


def call(kernel, outs, scratch=()):
    return pl.pallas_call(
        kernel,
        out_shape=outs,
        scratch_shapes=[pltpu.VMEM(sizes, f32) for sizes in scratch],
        compiler_params=pltpu.CompilerParams(vmem_limit_bytes=VMEM_LIMIT),
    )


def exchange(slots, rows):
    moved = lax.all_to_all(slots.reshape(32, rows, 128), BOTH, 0, 0, tiled=True)
    return moved.reshape(32 * rows, 128)


def line_plan(rhs, coupling, fwd_coupling, bwd_coupling, block_inverse):
    source, coupling_field = rhs.reshape(48, 128), coupling.reshape(48, 128)
    forward_blocks = fwd_coupling.reshape(48, 48, 128)
    backward_blocks = bwd_coupling.reshape(48, 48, 128)
    inverse_blocks = block_inverse.reshape(48, 48, 128)
    tiles, pairs, held = shaped(6, 8, 128), shaped(3, 8, 128), shaped(8, 288, 128)
    blocks = pltpu.VMEM((48, 48, 128), jnp.bfloat16)
    vector, wide = pltpu.VMEM((48, 128), f32), pltpu.VMEM((2304, 128), f32)

    slots = pl.pallas_call(
        first_send_kernel,
        out_shape=pltpu.HBM((32, 152, 128), f32),
        in_specs=[pl.BlockSpec(memory_space=pltpu.HBM)] * 5,
        out_specs=pl.BlockSpec(memory_space=pltpu.HBM),
        scratch_shapes=[blocks, blocks, blocks, wide, vector, vector, vector]
        + [
            pltpu.VMEM((256, 128), f32),
            pltpu.VMEM((35, 152, 128), f32),
            pltpu.SemaphoreType.DMA((4, 3)),
            pltpu.SemaphoreType.DMA((7,)),
        ],
        compiler_params=pltpu.CompilerParams(vmem_limit_bytes=VMEM_LIMIT),
    )(*[
        pltpu.with_memory_space_constraint(array, pltpu.HBM)
        for array in (forward_blocks, backward_blocks, inverse_blocks, source, coupling_field)
    ])
    slots, inverse_blocks = lax.optimization_barrier((slots, inverse_blocks))
    slots = lax.all_to_all(slots, BOTH, 0, 0, tiled=True)

    parts = pl.pallas_call(
        inverse_send_kernel,
        out_shape=[shaped(144, 128)] * 16,
        in_specs=[pl.BlockSpec(memory_space=pltpu.HBM)],
        out_specs=[pl.BlockSpec(memory_space=pltpu.HBM)] * 16,
        scratch_shapes=[
            blocks, wide, pltpu.VMEM((35, 72, 128), f32), pltpu.SemaphoreType.DMA((3,)), pltpu.SemaphoreType.DMA((32,))
        ],
        compiler_params=pltpu.CompilerParams(vmem_limit_bytes=VMEM_LIMIT),
    )(pltpu.with_memory_space_constraint(inverse_blocks, pltpu.HBM))
    parts = [parts[0]] + [lax.ppermute(parts[d], BOTH, [(e, e ^ d) for e in range(32)]) for d in range(1, 16)]
    inverse = [
        call(inverse_get_kernel, pltpu.VMEM((2, 288, 128), f32))(*parts[4 * n : 4 * n + 4]) for n in range(4)
    ]

    own, other, forward, backward, first, middle, coupling_lines = call(
        first_kernel, (pairs, pairs, held, held, tiles, tiles, tiles), [(256, 128), (6, 8, 128), (8, 6, 8, 128), (4, 6, 8, 128)]
    )(slots)

    def with_partner(vector):
        return lax.ppermute(vector, BOTH, [(e, e ^ 16) for e in range(32)])

    other = with_partner(other)
    own = call(functools.partial(half_inverse_kernel, 0), pairs)(own, *inverse)
    other = call(functools.partial(half_inverse_kernel, 1), pairs)(other, *inverse)
    other = with_partner(other)
    slots = call(second_kernel, shaped(128, 128), [(6, 8, 128), (8, 6, 8, 128), (4, 6, 8, 128), (6, 8, 128)])(
        own, other, forward, backward, first, middle, coupling_lines
    )
    slots = exchange(slots, 4)
    correction, remaining = call(last_kernel, (shaped(48, 128), shaped(48, 128)))(slots)
    return correction.reshape(rhs.shape), remaining.reshape(rhs.shape)


def from_behind(value, axis, steps):
    count = lax.axis_size(axis)
    initial, last = (max(0, -steps), min(count, count - steps))
    return lax.ppermute(value, axis, [(source, source + steps) for source in range(initial, last)])


def from_root(shard, axis, root):
    mine = lax.axis_index(axis) == root
    return lax.psum(jnp.where(mine, shard, jnp.zeros_like(shard)), axis)


def extended(block, sides, width):
    for axis, dim in sides:
        count = lax.axis_size(axis)
        forward = [(i, i + 1) for i in range(count - 1)]
        backward = [(target, source) for source, target in forward]
        low = lax.ppermute(
            lax.slice_in_dim(block, block.shape[dim] - width, None, axis=dim), axis, forward
        )
        high = lax.ppermute(lax.slice_in_dim(block, 0, width, axis=dim), axis, backward)
        block = jnp.concatenate([low, block, high], axis=dim)
    return block


def cell_stride(one_block, carried, const_term):
    return const_term - jnp.einsum(
        "abl,al->bl", one_block.astype(jnp.float32), carried, precision=highest
    )


def compose_cells(blocks, sequence):
    running = None
    for position in sequence:
        one_block = blocks[position].astype(jnp.float32)
        running = -jnp.swapaxes(one_block, 0, 1)
    return running


def doubling_maps(local_map, reverse):
    size = lax.axis_size("azim")
    index = lax.axis_index("azim")
    levels = []
    current = local_map
    distance = 1
    while distance < size:
        if reverse:
            moved = from_behind(current, "azim", -distance)
            exists = index + distance < size
        else:
            moved = from_behind(current, "azim", distance)
            exists = index >= distance
        levels.append((current, distance))
        current = jnp.where(
            exists, jnp.einsum("bcl,cal->bal", current, moved, precision=highest), current
        )
        distance = distance * 2
    return (levels, current)


def doubling_entries(map_levels, local_offset, reverse):
    levels, final_map = map_levels
    size = lax.axis_size("azim")
    index = lax.axis_index("azim")
    running = local_offset
    for current, distance in levels:
        if reverse:
            moved = from_behind(running, "azim", -distance)
        else:
            moved = from_behind(running, "azim", distance)
        running = jnp.einsum("bcl,cl->bl", current, moved, precision=highest) + running
    if reverse:
        wrapped = from_root(running, "azim", 0)
    else:
        wrapped = from_root(running, "azim", size - 1)
    leaving = jnp.einsum("bcl,cl->bl", final_map, wrapped, precision=highest) + running
    if reverse:
        shifted = from_behind(leaving, "azim", -1)
        first_device = index == size - 1
    else:
        shifted = from_behind(leaving, "azim", 1)
        first_device = index == 0
    return jnp.where(first_device, wrapped, shifted)


def sweep(blocks, consts, map_levels, reverse):
    cell_count = blocks.shape[0]
    sequence = list(range(cell_count))
    if reverse:
        sequence = sequence[::-1]
    carried = jnp.zeros(consts.shape[1:], jnp.float32)
    for position in sequence:
        carried = cell_stride(blocks[position], carried, consts[position])
    local_offset = carried
    incoming_maps = doubling_entries(map_levels, local_offset, reverse)
    outputs = [None] * cell_count
    carried = incoming_maps
    for position in sequence:
        carried = cell_stride(blocks[position], carried, consts[position])
        outputs[position] = carried
    return jnp.stack(outputs)


def on_device(rhs, coupling, fwd_coupling, bwd_coupling, block_inverse):
    cell_count, block_width, _, position_total, radial_count = fwd_coupling.shape
    line_count = position_total * radial_count
    forward_blocks = fwd_coupling.reshape(cell_count, block_width, block_width, line_count)
    backward_blocks = bwd_coupling.reshape(cell_count, block_width, block_width, line_count)
    inverse_blocks = block_inverse.reshape(cell_count, block_width, block_width, line_count)
    source = rhs.reshape(cell_count, block_width, line_count)
    coupling_field = coupling.reshape(cell_count, block_width, line_count)
    forward_map = compose_cells(forward_blocks, list(range(cell_count)))
    backward_map = compose_cells(backward_blocks, list(range(cell_count))[::-1])
    forward_levels = None
    backward_levels = None
    forward_levels = doubling_maps(forward_map, False)
    backward_levels = doubling_maps(backward_map, True)

    def precondition(vector):
        consts = jnp.stack(
            [
                jnp.einsum(
                    "abl,al->bl",
                    inverse_blocks[0].astype(jnp.float32),
                    vector[0],
                    precision=highest,
                )
            ]
        )
        forward = sweep(forward_blocks, consts, forward_levels, False)
        return sweep(backward_blocks, forward, backward_levels, True)

    def stations_sum(field):
        grid = field.reshape(cell_count, block_width, position_total, radial_count)
        padded = extended(grid, (("axial", 2),), 1)
        return (padded[:, :, :-2] + padded[:, :, 2:]).reshape(cell_count, block_width, line_count)

    applied_once = precondition(source)
    middle = source - applied_once + coupling_field * stations_sum(applied_once)
    second = precondition(middle)
    correction = applied_once + second
    remaining = middle - second + coupling_field * stations_sum(second)
    return (correction.reshape(rhs.shape), remaining.reshape(rhs.shape))


def solution(mesh):
    cells, stations = mesh.shape["azim"], mesh.shape["axial"]

    def on_each(rhs, coupling, fwd_coupling, bwd_coupling, block_inverse):
        local = fwd_coupling.shape
        if (cells, stations) == (8, 4) and local == (1, 48, 48, 1, 128):
            return line_plan(rhs, coupling, fwd_coupling, bwd_coupling, block_inverse)
        return on_device(rhs, coupling, fwd_coupling, bwd_coupling, block_inverse)

    return jax.shard_map(
        on_each,
        mesh=mesh,
        in_specs=(
            P("azim", None, "axial", None),
            P("azim", None, "axial", None),
            P("azim", None, None, "axial", None),
            P("azim", None, None, "axial", None),
            P("azim", None, None, "axial", None),
        ),
        out_specs=(P("azim", None, "axial", None), P("azim", None, "axial", None)),
        check_vma=False,
    )
```

```python
import functools

import jax
import jax.numpy as jnp
from jax import lax
from jax.experimental import pallas as pl
from jax.experimental.pallas import tpu as pltpu
from jax.sharding import PartitionSpec as P

highest = lax.Precision.HIGHEST
f32 = jnp.float32
BOTH = ("azim", "axial")
VMEM_LIMIT = 16 * 1024 * 1024


def lane_index():
    return lax.broadcasted_iota(jnp.int32, (8, 128), 1)


def row_index():
    return lax.broadcasted_iota(jnp.int32, (8, 128), 0)


def turn_lanes(tile, steps):
    steps = steps % 128
    return pltpu.roll(tile, steps, 1) if steps else tile


def turn_rows(tile, steps):
    steps = steps % 8
    return pltpu.roll(tile, steps, 0) if steps else tile


def line_lanes():
    return lane_index() + 16 - 4 * lax.axis_index("axial")


def to_line(tile):
    return pltpu.roll(tile, 4 * (4 * lax.axis_index("azim") + lax.axis_index("axial")), 1)


def from_line(tile):
    return pltpu.roll(tile, (128 - 4 * (4 * lax.axis_index("azim") + lax.axis_index("axial"))) % 128, 1)


def swap_quads(tiles, lanes=None):
    lanes = lane_index() if lanes is None else lanes
    tiles = list(tiles)
    for bit, width in ((1, 4), (2, 8)):
        low = (lanes // width) % 2 == 0
        for first in range(4):
            if first & bit:
                continue
            one, two = tiles[first], tiles[first | bit]
            tiles[first] = jnp.where(low, one, turn_lanes(two, width))
            tiles[first | bit] = jnp.where(low, turn_lanes(one, -width), two)
    return tiles


def swap_rows(tile):
    lanes, rows = lane_index() // 16, row_index()
    for bit in (1, 2, 4):
        row_bit, lane_bit = (rows // bit) % 2, (lanes // bit) % 2
        up = turn_rows(turn_lanes(tile, 16 * bit), -bit)
        down = turn_rows(turn_lanes(tile, -16 * bit), bit)
        tile = jnp.where(row_bit == lane_bit, tile, jnp.where(row_bit == 0, up, down))
    return tile


def put_slots(out_ref, tiles, rows, base):
    zero = jnp.zeros((8, 128), f32)
    for half in range(2):
        group = [tiles[4 * half + x] if 4 * half + x < 6 else zero for x in range(4)]
        for quad, tile in enumerate(swap_quads(group)):
            out_ref[pl.ds(rows * quad + base + half, 8, stride=4 * rows), :] = tile


def get_slots(in_ref, rows, base):
    tiles = []
    for half in range(2):
        group = [in_ref[pl.ds(rows * quad + base + half, 8, stride=4 * rows), :] for quad in range(4)]
        tiles += swap_quads(group)
    return tiles[:6]


def put_cell_vector(out_ref, vector_ref, rows, base):
    put_slots(out_ref, [swap_rows(vector_ref[8 * t : 8 * t + 8, :]) for t in range(6)], rows, base)


def inverse_matvec(inverse_ref, vector_ref, out_ref):
    totals = None
    for a in range(48):
        term = inverse_ref[a].astype(f32) * vector_ref[a : a + 1, :]
        totals = term if totals is None else totals + term
    out_ref[...] = totals


COMBINATIONS = [(ah, pair) for ah in range(6) for pair in range(3)]
GROUPS_OF_THIRD = ((0, 1), (2, 3, 4, 5), (6, 7, 8))


def group_tiles(group):
    if group == 8:
        return [COMBINATIONS[16 + x // 2] + (x % 2,) for x in range(4)]
    return [COMBINATIONS[4 * (group // 2) + x] + (group % 2,) for x in range(4)]


TILE_AT = {
    (ah, 2 * pair + half): 4 * group + x
    for group in range(9)
    for x, (ah, pair, half) in enumerate(group_tiles(group))
}


def pack_blocks(block_ref, out_ref, base, third):
    station = lax.axis_index("axial")
    quads = lane_index() // 4
    keeps = [(bit, (quads & bit) == 0) for bit in (1, 2, 4, 8, 16)]
    turned = {}
    for group in GROUPS_OF_THIRD[third]:
        items = []
        for i in range(32):
            p = i // 4
            ah, pair, half = group_tiles(group)[i % 4]
            steps = (4 * i + 4 * station) % 128
            if (ah, pair, i) not in turned:
                tile = block_ref[8 * ah + p, 16 * pair : 16 * pair + 16, :]
                turned[ah, pair, i] = pltpu.roll(tile, steps, 1).astype(f32)
            items.append(turn_rows(turned[ah, pair, i][8 * half : 8 * half + 8], -p))
        for bit, keep in keeps:
            items = [jnp.where(keep, items[j], items[(j + bit) % 32]) for j in range(32)]
        for slot in range(35):
            out_ref[slot, base + 8 * group : base + 8 * group + 8, :] = items[-slot % 32]


def fetch_thirds(block_hbm, block_ref, sems):
    copies = []
    for third in range(3):
        there = (slice(16 * third, 16 * third + 16), slice(None), slice(None))
        copies.append(pltpu.make_async_copy(block_hbm.at[there], block_ref.at[there], sems.at[third]))
    return copies


def join_stations(parts):
    chunk = line_lanes() // 4
    for bit in (1, 2):
        keep = (chunk & bit) == 0
        parts = [jnp.where(keep, parts[j], parts[(j + bit) % 4]) for j in range(4)]
    return [turn_lanes(parts[-x % 4], -4 * x) for x in range(4)]


def unpack_cell(in_ref, base, out_ref, cell):
    for group in range(9):
        at = base + 8 * group
        parts = [in_ref[4 * cell + k, at : at + 8, :] for k in range(4)]
        for x, tile in enumerate(join_stations(parts)):
            at = 8 * (4 * group + x)
            out_ref[cell, at : at + 8, :] = tile


def line_sweep(blocks_ref, const_ref, out_ref, reverse, beside=None):
    order = list(range(8))
    if reverse:
        order = order[::-1]
    state = None
    for turn in range(2):
        for n, cell in enumerate(order):
            if beside is not None:
                beside(turn, n)
            consts = [jnp.broadcast_to(const_ref[t, cell : cell + 1, :], (8, 128)) for t in range(6)]
            if state is None:
                state = consts
                continue
            state = line_step(blocks_ref, cell, state, consts)
            if turn == 1:
                for t in range(6):
                    out_ref[t, cell : cell + 1, :] = state[t][0:1]


def stations_sum(tile):
    station = (line_lanes() // 4) % 4
    before = jnp.where(station > 0, turn_lanes(tile, 4), 0.0)
    after = jnp.where(station < 3, turn_lanes(tile, -4), 0.0)
    return before + after


def first_send_kernel(
    forward_hbm, backward_hbm, inverse_hbm, rhs_hbm, coupling_hbm, out_hbm,
    f_ref, b_ref, i_ref, rhs_ref, coupling_ref, c_ref, vectors_ref, packed_ref, sems, out_sems,
):
    forward = fetch_thirds(forward_hbm, f_ref, sems.at[0])
    inverse = fetch_thirds(inverse_hbm, i_ref, sems.at[1])
    backward = fetch_thirds(backward_hbm, b_ref, sems.at[2])
    vectors = [
        pltpu.make_async_copy(source, target, sems.at[3, n])
        for n, (source, target) in enumerate(((rhs_hbm, rhs_ref), (coupling_hbm, coupling_ref)))
    ]
    for copy in forward + vectors + inverse:
        copy.start()
    leaving = []

    def leave(row, rows, first):
        source = packed_ref.at[pl.ds(first, 32), pl.ds(row, rows), :]
        target = out_hbm.at[:, pl.ds(row, rows), :]
        leaving.append(pltpu.make_async_copy(source, target, out_sems.at[len(leaving)]))
        leaving[-1].start()

    station = lax.axis_index("axial")

    for third in range(3):
        forward[third].wait()
        if third == 0:
            for copy in backward:
                copy.start()
        pack_blocks(f_ref, packed_ref, 0, third)
        leave((0, 16, 48)[third], (16, 32, 24)[third], station)
    for copy in vectors + inverse:
        copy.wait()
    for third in range(3):
        backward[third].wait()
        if third == 0:
            inverse_matvec(i_ref, rhs_ref, c_ref)
            for n, vector_ref in enumerate((c_ref, rhs_ref, coupling_ref)):
                put_cell_vector(vectors_ref, vector_ref, 8, 2 * n)
            for e in range(32):
                packed_ref[e, 144:152, :] = vectors_ref[8 * e : 8 * e + 8, :]
        pack_blocks(b_ref, packed_ref, 72, third)
        if third == 0:
            leave(144, 8, 0)
        leave((72, 88, 120)[third], (16, 32, 24)[third], station)
    for copy in leaving:
        copy.wait()


def first_kernel(slots_ref, *refs):
    own_ref, other_ref, forward_ref, backward_ref, first_ref, middle_ref, coupling_ref, packed_ref, c_ref, y_ref = refs
    for e in range(32):
        packed_ref[8 * e : 8 * e + 8, :] = slots_ref[e, 144:152, :]
    for t, tile in enumerate(get_slots(packed_ref, 8, 0)):
        c_ref[t] = to_line(tile)

    def unpack(turn, n):
        if turn == 0:
            unpack_cell(slots_ref, 0, forward_ref, n)
        else:
            unpack_cell(slots_ref, 72, backward_ref, n)

    line_sweep(forward_ref, c_ref, y_ref, False, unpack)
    line_sweep(backward_ref, y_ref, first_ref, True)
    rhs = [to_line(tile) for tile in get_slots(packed_ref, 8, 2)]
    coupling = [to_line(tile) for tile in get_slots(packed_ref, 8, 4)]
    half, _ = half_position()
    low = row_index() < 4
    own, other = [], []
    for t in range(6):
        first = first_ref[t]
        middle = rhs[t] - first + coupling[t] * stations_sum(first)
        turned = turn_rows(middle, 4)
        other.append(jnp.where(half == 0, turned, middle))
        own.append(jnp.where(half == 0, middle, turned))
        middle_ref[t] = middle
        coupling_ref[t] = coupling[t]
    for u in range(3):
        other_ref[u] = jnp.where(low, other[2 * u], turn_rows(other[2 * u + 1], 4))
        own_ref[u] = jnp.where(low, own[2 * u], turn_rows(own[2 * u + 1], 4))


def half_position():
    cell = lax.axis_index("azim")
    return cell // 4, (cell % 4) * 4 + lax.axis_index("axial")


def inverse_send_kernel(inverse_hbm, *refs):
    outs, (i_ref, packed_ref, fetch_sems, sems) = refs[:16], refs[16:]
    fetches = fetch_thirds(inverse_hbm, i_ref, fetch_sems)
    for copy in fetches:
        copy.start()
    for third, copy in enumerate(fetches):
        copy.wait()
        pack_blocks(i_ref, packed_ref, 0, third)
    half, place = half_position()
    station = place % 4
    copies = []
    for d in range(16):
        target = place ^ d
        for n, source in enumerate((16 * half + target, 16 * (1 - half) + target)):
            copies.append(
                pltpu.make_async_copy(packed_ref.at[source + station], outs[d].at[pl.ds(72 * n, 72), :], sems.at[2 * d + n])
            )
            copies[-1].start()
    for copy in copies:
        copy.wait()


def inverse_get_kernel(*refs):
    ins, out_ref = refs[:4], refs[4]
    station = lax.axis_index("axial")
    for lines in range(2):
        for group in range(9):
            at = 72 * lines + 8 * group
            parts = [part[at : at + 8, :] for part in ins]
            for bit in (1, 2):
                parts = [jnp.where((station & bit) == 0, parts[k], parts[k ^ bit]) for k in range(4)]
            for x, tile in enumerate(join_stations(parts)):
                at = 8 * (4 * group + x)
                out_ref[lines, at : at + 8, :] = tile


def line_step(blocks_ref, cell, state, consts):
    following = []
    for bh in range(6):
        terms = []
        for ah in range(6):
            at = 8 * TILE_AT[ah, bh]
            terms.append(blocks_ref[cell, at : at + 8, :] * state[ah])
        total = (terms[0] + terms[1]) + (terms[2] + terms[3]) + (terms[4] + terms[5])
        total = pltpu.roll(total, 0, 1, stride=16, stride_axis=0)
        for span in (4, 2):
            total = total + turn_rows(total, span)
        following.append((consts[bh] - total) - turn_rows(total, 1))
    return following


def half_inverse_kernel(lines, vector_ref, *refs):
    blocks, out_ref = refs[:4], refs[4]
    _, place = half_position()
    cell = place // 4
    rows = row_index()
    zero = jnp.zeros((8, 128), f32)
    totals = [zero] * 3
    for n in range(4):
        state = [
            jnp.broadcast_to(vector_ref[t // 2, pl.ds(4 * (t % 2) + (cell ^ n), 1), :], (8, 128)) for t in range(6)
        ]
        for t, product in enumerate(line_step(blocks[n], lines, state, [zero] * 6)):
            totals[t // 2] = jnp.where(rows == 4 * (t % 2) + (cell ^ n), product, totals[t // 2])
    for u in range(3):
        out_ref[u] = -totals[u]


def second_kernel(
    own_ref, other_ref, forward_ref, backward_ref, first_ref, middle_ref, coupling_ref, out_ref, c_ref, y_ref, second_ref
):
    half, _ = half_position()
    low = row_index() < 4
    for t in range(6):
        own, other = own_ref[t // 2], other_ref[t // 2]
        if t % 2:
            own = turn_rows(own, 4)
        else:
            other = turn_rows(other, 4)
        tile = jnp.where(low, own, other)
        c_ref[t] = jnp.where(half == 0, tile, turn_rows(tile, 4))
    line_sweep(forward_ref, c_ref, y_ref, False)
    line_sweep(backward_ref, y_ref, second_ref, True)
    correction, remaining = [], []
    for t in range(6):
        second = second_ref[t]
        correction.append(from_line(first_ref[t] + second))
        remaining.append(from_line(middle_ref[t] - second + coupling_ref[t] * stations_sum(second)))
    put_slots(out_ref, correction, 4, 0)
    put_slots(out_ref, remaining, 4, 2)


def last_kernel(slots_ref, correction_ref, remaining_ref):
    for out_ref, base in ((correction_ref, 0), (remaining_ref, 2)):
        for t, tile in enumerate(get_slots(slots_ref, 4, base)):
            out_ref[8 * t : 8 * t + 8, :] = swap_rows(tile)


def shaped(*sizes):
    return jax.ShapeDtypeStruct(sizes, f32)


def call(kernel, outs, scratch=()):
    return pl.pallas_call(
        kernel,
        out_shape=outs,
        scratch_shapes=[pltpu.VMEM(sizes, f32) for sizes in scratch],
        compiler_params=pltpu.CompilerParams(vmem_limit_bytes=VMEM_LIMIT),
    )


def exchange(slots, rows):
    moved = lax.all_to_all(slots.reshape(32, rows, 128), BOTH, 0, 0, tiled=True)
    return moved.reshape(32 * rows, 128)


def line_plan(rhs, coupling, fwd_coupling, bwd_coupling, block_inverse):
    source, coupling_field = rhs.reshape(48, 128), coupling.reshape(48, 128)
    forward_blocks = fwd_coupling.reshape(48, 48, 128)
    backward_blocks = bwd_coupling.reshape(48, 48, 128)
    inverse_blocks = block_inverse.reshape(48, 48, 128)
    tiles, pairs, held = shaped(6, 8, 128), shaped(3, 8, 128), shaped(8, 288, 128)
    blocks = pltpu.VMEM((48, 48, 128), jnp.bfloat16)
    vector = pltpu.VMEM((48, 128), f32)

    slots = pl.pallas_call(
        first_send_kernel,
        out_shape=pltpu.HBM((32, 152, 128), f32),
        in_specs=[pl.BlockSpec(memory_space=pltpu.HBM)] * 5,
        out_specs=pl.BlockSpec(memory_space=pltpu.HBM),
        scratch_shapes=[blocks, blocks, blocks, vector, vector, vector]
        + [
            pltpu.VMEM((256, 128), f32),
            pltpu.VMEM((35, 152, 128), f32),
            pltpu.SemaphoreType.DMA((4, 3)),
            pltpu.SemaphoreType.DMA((7,)),
        ],
        compiler_params=pltpu.CompilerParams(vmem_limit_bytes=VMEM_LIMIT),
    )(*[
        pltpu.with_memory_space_constraint(array, pltpu.HBM)
        for array in (forward_blocks, backward_blocks, inverse_blocks, source, coupling_field)
    ])
    slots, inverse_blocks = lax.optimization_barrier((slots, inverse_blocks))
    slots = lax.all_to_all(slots, BOTH, 0, 0, tiled=True)

    parts = pl.pallas_call(
        inverse_send_kernel,
        out_shape=[shaped(144, 128)] * 16,
        in_specs=[pl.BlockSpec(memory_space=pltpu.HBM)],
        out_specs=[pl.BlockSpec(memory_space=pltpu.HBM)] * 16,
        scratch_shapes=[
            blocks, pltpu.VMEM((35, 72, 128), f32), pltpu.SemaphoreType.DMA((3,)), pltpu.SemaphoreType.DMA((32,))
        ],
        compiler_params=pltpu.CompilerParams(vmem_limit_bytes=VMEM_LIMIT),
    )(pltpu.with_memory_space_constraint(inverse_blocks, pltpu.HBM))
    parts = [parts[0]] + [lax.ppermute(parts[d], BOTH, [(e, e ^ d) for e in range(32)]) for d in range(1, 16)]
    inverse = [
        call(inverse_get_kernel, pltpu.VMEM((2, 288, 128), f32))(*parts[4 * n : 4 * n + 4]) for n in range(4)
    ]

    own, other, forward, backward, first, middle, coupling_lines = call(
        first_kernel, (pairs, pairs, held, held, tiles, tiles, tiles), [(256, 128), (6, 8, 128), (6, 8, 128)]
    )(slots)

    def with_partner(vector):
        return lax.ppermute(vector, BOTH, [(e, e ^ 16) for e in range(32)])

    other = with_partner(other)
    own = call(functools.partial(half_inverse_kernel, 0), pairs)(own, *inverse)
    other = call(functools.partial(half_inverse_kernel, 1), pairs)(other, *inverse)
    other = with_partner(other)
    slots = call(second_kernel, shaped(128, 128), [(6, 8, 128)] * 3)(
        own, other, forward, backward, first, middle, coupling_lines
    )
    slots = exchange(slots, 4)
    correction, remaining = call(last_kernel, (shaped(48, 128), shaped(48, 128)))(slots)
    return correction.reshape(rhs.shape), remaining.reshape(rhs.shape)


def from_behind(value, axis, steps):
    count = lax.axis_size(axis)
    initial, last = (max(0, -steps), min(count, count - steps))
    return lax.ppermute(value, axis, [(source, source + steps) for source in range(initial, last)])


def from_root(shard, axis, root):
    mine = lax.axis_index(axis) == root
    return lax.psum(jnp.where(mine, shard, jnp.zeros_like(shard)), axis)


def extended(block, sides, width):
    for axis, dim in sides:
        count = lax.axis_size(axis)
        forward = [(i, i + 1) for i in range(count - 1)]
        backward = [(target, source) for source, target in forward]
        low = lax.ppermute(
            lax.slice_in_dim(block, block.shape[dim] - width, None, axis=dim), axis, forward
        )
        high = lax.ppermute(lax.slice_in_dim(block, 0, width, axis=dim), axis, backward)
        block = jnp.concatenate([low, block, high], axis=dim)
    return block


def cell_stride(one_block, carried, const_term):
    return const_term - jnp.einsum(
        "abl,al->bl", one_block.astype(jnp.float32), carried, precision=highest
    )


def compose_cells(blocks, sequence):
    running = None
    for position in sequence:
        one_block = blocks[position].astype(jnp.float32)
        running = -jnp.swapaxes(one_block, 0, 1)
    return running


def doubling_maps(local_map, reverse):
    size = lax.axis_size("azim")
    index = lax.axis_index("azim")
    levels = []
    current = local_map
    distance = 1
    while distance < size:
        if reverse:
            moved = from_behind(current, "azim", -distance)
            exists = index + distance < size
        else:
            moved = from_behind(current, "azim", distance)
            exists = index >= distance
        levels.append((current, distance))
        current = jnp.where(
            exists, jnp.einsum("bcl,cal->bal", current, moved, precision=highest), current
        )
        distance = distance * 2
    return (levels, current)


def doubling_entries(map_levels, local_offset, reverse):
    levels, final_map = map_levels
    size = lax.axis_size("azim")
    index = lax.axis_index("azim")
    running = local_offset
    for current, distance in levels:
        if reverse:
            moved = from_behind(running, "azim", -distance)
        else:
            moved = from_behind(running, "azim", distance)
        running = jnp.einsum("bcl,cl->bl", current, moved, precision=highest) + running
    if reverse:
        wrapped = from_root(running, "azim", 0)
    else:
        wrapped = from_root(running, "azim", size - 1)
    leaving = jnp.einsum("bcl,cl->bl", final_map, wrapped, precision=highest) + running
    if reverse:
        shifted = from_behind(leaving, "azim", -1)
        first_device = index == size - 1
    else:
        shifted = from_behind(leaving, "azim", 1)
        first_device = index == 0
    return jnp.where(first_device, wrapped, shifted)


def sweep(blocks, consts, map_levels, reverse):
    cell_count = blocks.shape[0]
    sequence = list(range(cell_count))
    if reverse:
        sequence = sequence[::-1]
    carried = jnp.zeros(consts.shape[1:], jnp.float32)
    for position in sequence:
        carried = cell_stride(blocks[position], carried, consts[position])
    local_offset = carried
    incoming_maps = doubling_entries(map_levels, local_offset, reverse)
    outputs = [None] * cell_count
    carried = incoming_maps
    for position in sequence:
        carried = cell_stride(blocks[position], carried, consts[position])
        outputs[position] = carried
    return jnp.stack(outputs)


def on_device(rhs, coupling, fwd_coupling, bwd_coupling, block_inverse):
    cell_count, block_width, _, position_total, radial_count = fwd_coupling.shape
    line_count = position_total * radial_count
    forward_blocks = fwd_coupling.reshape(cell_count, block_width, block_width, line_count)
    backward_blocks = bwd_coupling.reshape(cell_count, block_width, block_width, line_count)
    inverse_blocks = block_inverse.reshape(cell_count, block_width, block_width, line_count)
    source = rhs.reshape(cell_count, block_width, line_count)
    coupling_field = coupling.reshape(cell_count, block_width, line_count)
    forward_map = compose_cells(forward_blocks, list(range(cell_count)))
    backward_map = compose_cells(backward_blocks, list(range(cell_count))[::-1])
    forward_levels = None
    backward_levels = None
    forward_levels = doubling_maps(forward_map, False)
    backward_levels = doubling_maps(backward_map, True)

    def precondition(vector):
        consts = jnp.stack(
            [
                jnp.einsum(
                    "abl,al->bl",
                    inverse_blocks[0].astype(jnp.float32),
                    vector[0],
                    precision=highest,
                )
            ]
        )
        forward = sweep(forward_blocks, consts, forward_levels, False)
        return sweep(backward_blocks, forward, backward_levels, True)

    def stations_sum(field):
        grid = field.reshape(cell_count, block_width, position_total, radial_count)
        padded = extended(grid, (("axial", 2),), 1)
        return (padded[:, :, :-2] + padded[:, :, 2:]).reshape(cell_count, block_width, line_count)

    applied_once = precondition(source)
    middle = source - applied_once + coupling_field * stations_sum(applied_once)
    second = precondition(middle)
    correction = applied_once + second
    remaining = middle - second + coupling_field * stations_sum(second)
    return (correction.reshape(rhs.shape), remaining.reshape(rhs.shape))


def solution(mesh):
    cells, stations = mesh.shape["azim"], mesh.shape["axial"]

    def on_each(rhs, coupling, fwd_coupling, bwd_coupling, block_inverse):
        local = fwd_coupling.shape
        if (cells, stations) == (8, 4) and local == (1, 48, 48, 1, 128):
            return line_plan(rhs, coupling, fwd_coupling, bwd_coupling, block_inverse)
        return on_device(rhs, coupling, fwd_coupling, bwd_coupling, block_inverse)

    return jax.shard_map(
        on_each,
        mesh=mesh,
        in_specs=(
            P("azim", None, "axial", None),
            P("azim", None, "axial", None),
            P("azim", None, None, "axial", None),
            P("azim", None, None, "axial", None),
            P("azim", None, None, "axial", None),
        ),
        out_specs=(P("azim", None, "axial", None), P("azim", None, "axial", None)),
        check_vma=False,
    )
```

```python
import functools

import jax
import jax.numpy as jnp
from jax import lax
from jax.experimental import pallas as pl
from jax.experimental.pallas import tpu as pltpu
from jax.sharding import PartitionSpec as P

highest = lax.Precision.HIGHEST
f32 = jnp.float32
BOTH = ("azim", "axial")
VMEM_LIMIT = 16 * 1024 * 1024


def lane_index():
    return lax.broadcasted_iota(jnp.int32, (8, 128), 1)


def row_index():
    return lax.broadcasted_iota(jnp.int32, (8, 128), 0)


def turn_lanes(tile, steps):
    steps = steps % 128
    return pltpu.roll(tile, steps, 1) if steps else tile


def turn_rows(tile, steps):
    steps = steps % 8
    return pltpu.roll(tile, steps, 0) if steps else tile


def line_lanes():
    return lane_index() + 16 - 4 * lax.axis_index("axial")


def to_line(tile):
    return pltpu.roll(tile, 4 * (4 * lax.axis_index("azim") + lax.axis_index("axial")), 1)


def from_line(tile):
    return pltpu.roll(tile, (128 - 4 * (4 * lax.axis_index("azim") + lax.axis_index("axial"))) % 128, 1)


def swap_quads(tiles, lanes=None):
    lanes = lane_index() if lanes is None else lanes
    tiles = list(tiles)
    for bit, width in ((1, 4), (2, 8)):
        low = (lanes // width) % 2 == 0
        for first in range(4):
            if first & bit:
                continue
            one, two = tiles[first], tiles[first | bit]
            tiles[first] = jnp.where(low, one, turn_lanes(two, width))
            tiles[first | bit] = jnp.where(low, turn_lanes(one, -width), two)
    return tiles


def swap_rows(tile):
    lanes, rows = lane_index() // 16, row_index()
    for bit in (1, 2, 4):
        row_bit, lane_bit = (rows // bit) % 2, (lanes // bit) % 2
        up = turn_rows(turn_lanes(tile, 16 * bit), -bit)
        down = turn_rows(turn_lanes(tile, -16 * bit), bit)
        tile = jnp.where(row_bit == lane_bit, tile, jnp.where(row_bit == 0, up, down))
    return tile


def put_slots(out_ref, tiles, rows, base):
    zero = jnp.zeros((8, 128), f32)
    for half in range(2):
        group = [tiles[4 * half + x] if 4 * half + x < 6 else zero for x in range(4)]
        for quad, tile in enumerate(swap_quads(group)):
            out_ref[pl.ds(rows * quad + base + half, 8, stride=4 * rows), :] = tile


def get_slots(in_ref, rows, base):
    tiles = []
    for half in range(2):
        group = [in_ref[pl.ds(rows * quad + base + half, 8, stride=4 * rows), :] for quad in range(4)]
        tiles += swap_quads(group)
    return tiles[:6]


def put_cell_vector(out_ref, vector_ref, rows, base):
    put_slots(out_ref, [swap_rows(vector_ref[8 * t : 8 * t + 8, :]) for t in range(6)], rows, base)


def inverse_matvec(inverse_ref, vector_ref, out_ref):
    totals = None
    for a in range(48):
        term = inverse_ref[a].astype(f32) * vector_ref[a : a + 1, :]
        totals = term if totals is None else totals + term
    out_ref[...] = totals


COMBINATIONS = [(ah, pair) for ah in range(6) for pair in range(3)]
GROUPS_OF_THIRD = ((0, 1), (2, 3, 4, 5), (6, 7, 8))


def group_tiles(group):
    if group == 8:
        return [COMBINATIONS[16 + x // 2] + (x % 2,) for x in range(4)]
    return [COMBINATIONS[4 * (group // 2) + x] + (group % 2,) for x in range(4)]


TILE_AT = {
    (ah, 2 * pair + half): 4 * group + x
    for group in range(9)
    for x, (ah, pair, half) in enumerate(group_tiles(group))
}


def pack_blocks(block_ref, out_ref, base, third):
    station = lax.axis_index("axial")
    quads = lane_index() // 4
    keeps = [(bit, (quads & bit) == 0) for bit in (1, 2, 4, 8, 16)]
    turned = {}
    for group in GROUPS_OF_THIRD[third]:
        items = []
        for i in range(32):
            p = i // 4
            ah, pair, half = group_tiles(group)[i % 4]
            steps = (4 * i + 4 * station) % 128
            if (ah, pair, i) not in turned:
                tile = block_ref[8 * ah + p, 16 * pair : 16 * pair + 16, :]
                turned[ah, pair, i] = pltpu.roll(tile, steps, 1).astype(f32)
            items.append(turn_rows(turned[ah, pair, i][8 * half : 8 * half + 8], -p))
        for bit, keep in keeps:
            items = [jnp.where(keep, items[j], items[(j + bit) % 32]) for j in range(32)]
        for slot in range(35):
            out_ref[slot, base + 8 * group : base + 8 * group + 8, :] = items[-slot % 32]


def fetch_thirds(block_hbm, block_ref, sems):
    copies = []
    for third in range(3):
        there = (slice(16 * third, 16 * third + 16), slice(None), slice(None))
        copies.append(pltpu.make_async_copy(block_hbm.at[there], block_ref.at[there], sems.at[third]))
    return copies


def join_stations(parts):
    chunk = line_lanes() // 4
    for bit in (1, 2):
        keep = (chunk & bit) == 0
        parts = [jnp.where(keep, parts[j], parts[(j + bit) % 4]) for j in range(4)]
    return [turn_lanes(parts[-x % 4], -4 * x) for x in range(4)]


def unpack_cell(in_ref, base, out_ref, cell):
    for group in range(9):
        at = base + 8 * group
        parts = [in_ref[4 * cell + k, at : at + 8, :] for k in range(4)]
        for x, tile in enumerate(join_stations(parts)):
            at = 8 * (4 * group + x)
            out_ref[cell, at : at + 8, :] = tile


def line_sweep(blocks_ref, const_ref, out_ref, reverse, beside=None):
    order = list(range(8))
    if reverse:
        order = order[::-1]
    state = None
    for turn in range(2):
        for n, cell in enumerate(order):
            if beside is not None:
                beside(turn, n)
            consts = [jnp.broadcast_to(const_ref[t, cell : cell + 1, :], (8, 128)) for t in range(6)]
            if state is None:
                state = consts
                continue
            state = line_step(blocks_ref, cell, state, consts)
            if turn == 1:
                for t in range(6):
                    out_ref[t, cell : cell + 1, :] = state[t][0:1]


def stations_sum(tile):
    station = (line_lanes() // 4) % 4
    before = jnp.where(station > 0, turn_lanes(tile, 4), 0.0)
    after = jnp.where(station < 3, turn_lanes(tile, -4), 0.0)
    return before + after


def first_send_kernel(
    forward_hbm, backward_hbm, inverse_hbm, rhs_hbm, coupling_hbm, out_hbm,
    f_ref, b_ref, i_ref, rhs_ref, coupling_ref, c_ref, vectors_ref, packed_ref, sems, out_sems,
):
    forward = fetch_thirds(forward_hbm, f_ref, sems.at[0])
    inverse = fetch_thirds(inverse_hbm, i_ref, sems.at[1])
    backward = fetch_thirds(backward_hbm, b_ref, sems.at[2])
    vectors = [
        pltpu.make_async_copy(source, target, sems.at[3, n])
        for n, (source, target) in enumerate(((rhs_hbm, rhs_ref), (coupling_hbm, coupling_ref)))
    ]
    for copy in forward + vectors + inverse:
        copy.start()
    leaving = []

    def leave(row, rows, first):
        for part in range(4):
            source = packed_ref.at[pl.ds(first + 8 * part, 8), pl.ds(row, rows), :]
            target = out_hbm.at[pl.ds(8 * part, 8), pl.ds(row, rows), :]
            leaving.append(pltpu.make_async_copy(source, target, out_sems.at[len(leaving)]))
            leaving[-1].start()

    station = lax.axis_index("axial")

    for third in range(3):
        forward[third].wait()
        if third == 0:
            for copy in backward:
                copy.start()
        pack_blocks(f_ref, packed_ref, 0, third)
        leave((0, 16, 48)[third], (16, 32, 24)[third], station)
    for copy in vectors + inverse:
        copy.wait()
    for third in range(3):
        backward[third].wait()
        if third == 0:
            inverse_matvec(i_ref, rhs_ref, c_ref)
            for n, vector_ref in enumerate((c_ref, rhs_ref, coupling_ref)):
                put_cell_vector(vectors_ref, vector_ref, 8, 2 * n)
            for e in range(32):
                packed_ref[e, 144:152, :] = vectors_ref[8 * e : 8 * e + 8, :]
        pack_blocks(b_ref, packed_ref, 72, third)
        if third == 0:
            leave(144, 8, 0)
        leave((72, 88, 120)[third], (16, 32, 24)[third], station)
    for copy in leaving:
        copy.wait()


def first_kernel(slots_ref, *refs):
    own_ref, other_ref, forward_ref, backward_ref, first_ref, middle_ref, coupling_ref, packed_ref, c_ref, y_ref = refs
    for e in range(32):
        packed_ref[8 * e : 8 * e + 8, :] = slots_ref[e, 144:152, :]
    for t, tile in enumerate(get_slots(packed_ref, 8, 0)):
        c_ref[t] = to_line(tile)

    def unpack(turn, n):
        if turn == 0:
            unpack_cell(slots_ref, 0, forward_ref, n)
        else:
            unpack_cell(slots_ref, 72, backward_ref, n)

    line_sweep(forward_ref, c_ref, y_ref, False, unpack)
    line_sweep(backward_ref, y_ref, first_ref, True)
    rhs = [to_line(tile) for tile in get_slots(packed_ref, 8, 2)]
    coupling = [to_line(tile) for tile in get_slots(packed_ref, 8, 4)]
    half, _ = half_position()
    low = row_index() < 4
    own, other = [], []
    for t in range(6):
        first = first_ref[t]
        middle = rhs[t] - first + coupling[t] * stations_sum(first)
        turned = turn_rows(middle, 4)
        other.append(jnp.where(half == 0, turned, middle))
        own.append(jnp.where(half == 0, middle, turned))
        middle_ref[t] = middle
        coupling_ref[t] = coupling[t]
    for u in range(3):
        other_ref[u] = jnp.where(low, other[2 * u], turn_rows(other[2 * u + 1], 4))
        own_ref[u] = jnp.where(low, own[2 * u], turn_rows(own[2 * u + 1], 4))


def half_position():
    cell = lax.axis_index("azim")
    return cell // 4, (cell % 4) * 4 + lax.axis_index("axial")


def inverse_send_kernel(inverse_hbm, *refs):
    outs, (i_ref, packed_ref, fetch_sems, sems) = refs[:16], refs[16:]
    fetches = fetch_thirds(inverse_hbm, i_ref, fetch_sems)
    for copy in fetches:
        copy.start()
    for third, copy in enumerate(fetches):
        copy.wait()
        pack_blocks(i_ref, packed_ref, 0, third)
    half, place = half_position()
    station = place % 4
    copies = []
    for d in range(16):
        target = place ^ d
        for n, source in enumerate((16 * half + target, 16 * (1 - half) + target)):
            copies.append(
                pltpu.make_async_copy(packed_ref.at[source + station], outs[d].at[pl.ds(72 * n, 72), :], sems.at[2 * d + n])
            )
            copies[-1].start()
    for copy in copies:
        copy.wait()


def inverse_get_kernel(*refs):
    ins, out_ref = refs[:4], refs[4]
    station = lax.axis_index("axial")
    for lines in range(2):
        for group in range(9):
            at = 72 * lines + 8 * group
            parts = [part[at : at + 8, :] for part in ins]
            for bit in (1, 2):
                parts = [jnp.where((station & bit) == 0, parts[k], parts[k ^ bit]) for k in range(4)]
            for x, tile in enumerate(join_stations(parts)):
                at = 8 * (4 * group + x)
                out_ref[lines, at : at + 8, :] = tile


def line_step(blocks_ref, cell, state, consts):
    following = []
    for bh in range(6):
        terms = []
        for ah in range(6):
            at = 8 * TILE_AT[ah, bh]
            terms.append(blocks_ref[cell, at : at + 8, :] * state[ah])
        total = (terms[0] + terms[1]) + (terms[2] + terms[3]) + (terms[4] + terms[5])
        total = pltpu.roll(total, 0, 1, stride=16, stride_axis=0)
        for span in (4, 2):
            total = total + turn_rows(total, span)
        following.append((consts[bh] - total) - turn_rows(total, 1))
    return following


def half_inverse_kernel(lines, vector_ref, *refs):
    blocks, out_ref = refs[:4], refs[4]
    _, place = half_position()
    cell = place // 4
    rows = row_index()
    zero = jnp.zeros((8, 128), f32)
    totals = [zero] * 3
    for n in range(4):
        state = [
            jnp.broadcast_to(vector_ref[t // 2, pl.ds(4 * (t % 2) + (cell ^ n), 1), :], (8, 128)) for t in range(6)
        ]
        for t, product in enumerate(line_step(blocks[n], lines, state, [zero] * 6)):
            totals[t // 2] = jnp.where(rows == 4 * (t % 2) + (cell ^ n), product, totals[t // 2])
    for u in range(3):
        out_ref[u] = -totals[u]


def second_kernel(
    own_ref, other_ref, forward_ref, backward_ref, first_ref, middle_ref, coupling_ref, out_ref, c_ref, y_ref, second_ref
):
    half, _ = half_position()
    low = row_index() < 4
    for t in range(6):
        own, other = own_ref[t // 2], other_ref[t // 2]
        if t % 2:
            own = turn_rows(own, 4)
        else:
            other = turn_rows(other, 4)
        tile = jnp.where(low, own, other)
        c_ref[t] = jnp.where(half == 0, tile, turn_rows(tile, 4))
    line_sweep(forward_ref, c_ref, y_ref, False)
    line_sweep(backward_ref, y_ref, second_ref, True)
    correction, remaining = [], []
    for t in range(6):
        second = second_ref[t]
        correction.append(from_line(first_ref[t] + second))
        remaining.append(from_line(middle_ref[t] - second + coupling_ref[t] * stations_sum(second)))
    put_slots(out_ref, correction, 4, 0)
    put_slots(out_ref, remaining, 4, 2)


def last_kernel(slots_ref, correction_ref, remaining_ref):
    for out_ref, base in ((correction_ref, 0), (remaining_ref, 2)):
        for t, tile in enumerate(get_slots(slots_ref, 4, base)):
            out_ref[8 * t : 8 * t + 8, :] = swap_rows(tile)


def shaped(*sizes):
    return jax.ShapeDtypeStruct(sizes, f32)


def call(kernel, outs, scratch=()):
    return pl.pallas_call(
        kernel,
        out_shape=outs,
        scratch_shapes=[pltpu.VMEM(sizes, f32) for sizes in scratch],
        compiler_params=pltpu.CompilerParams(vmem_limit_bytes=VMEM_LIMIT),
    )


def exchange(slots, rows):
    moved = lax.all_to_all(slots.reshape(32, rows, 128), BOTH, 0, 0, tiled=True)
    return moved.reshape(32 * rows, 128)


def line_plan(rhs, coupling, fwd_coupling, bwd_coupling, block_inverse):
    source, coupling_field = rhs.reshape(48, 128), coupling.reshape(48, 128)
    forward_blocks = fwd_coupling.reshape(48, 48, 128)
    backward_blocks = bwd_coupling.reshape(48, 48, 128)
    inverse_blocks = block_inverse.reshape(48, 48, 128)
    tiles, pairs, held = shaped(6, 8, 128), shaped(3, 8, 128), shaped(8, 288, 128)
    blocks = pltpu.VMEM((48, 48, 128), jnp.bfloat16)
    vector = pltpu.VMEM((48, 128), f32)

    slots = pl.pallas_call(
        first_send_kernel,
        out_shape=pltpu.HBM((32, 152, 128), f32),
        in_specs=[pl.BlockSpec(memory_space=pltpu.HBM)] * 5,
        out_specs=pl.BlockSpec(memory_space=pltpu.HBM),
        scratch_shapes=[blocks, blocks, blocks, vector, vector, vector]
        + [
            pltpu.VMEM((256, 128), f32),
            pltpu.VMEM((35, 152, 128), f32),
            pltpu.SemaphoreType.DMA((4, 3)),
            pltpu.SemaphoreType.DMA((28,)),
        ],
        compiler_params=pltpu.CompilerParams(vmem_limit_bytes=VMEM_LIMIT),
    )(*[
        pltpu.with_memory_space_constraint(array, pltpu.HBM)
        for array in (forward_blocks, backward_blocks, inverse_blocks, source, coupling_field)
    ])
    slots, inverse_blocks = lax.optimization_barrier((slots, inverse_blocks))
    slots = lax.all_to_all(slots, BOTH, 0, 0, tiled=True)

    parts = pl.pallas_call(
        inverse_send_kernel,
        out_shape=[shaped(144, 128)] * 16,
        in_specs=[pl.BlockSpec(memory_space=pltpu.HBM)],
        out_specs=[pl.BlockSpec(memory_space=pltpu.HBM)] * 16,
        scratch_shapes=[
            blocks, pltpu.VMEM((35, 72, 128), f32), pltpu.SemaphoreType.DMA((3,)), pltpu.SemaphoreType.DMA((32,))
        ],
        compiler_params=pltpu.CompilerParams(vmem_limit_bytes=VMEM_LIMIT),
    )(pltpu.with_memory_space_constraint(inverse_blocks, pltpu.HBM))
    parts = [parts[0]] + [lax.ppermute(parts[d], BOTH, [(e, e ^ d) for e in range(32)]) for d in range(1, 16)]
    inverse = [
        call(inverse_get_kernel, pltpu.VMEM((2, 288, 128), f32))(*parts[4 * n : 4 * n + 4]) for n in range(4)
    ]

    own, other, forward, backward, first, middle, coupling_lines = call(
        first_kernel, (pairs, pairs, held, held, tiles, tiles, tiles), [(256, 128), (6, 8, 128), (6, 8, 128)]
    )(slots)

    def with_partner(vector):
        return lax.ppermute(vector, BOTH, [(e, e ^ 16) for e in range(32)])

    other = with_partner(other)
    own = call(functools.partial(half_inverse_kernel, 0), pairs)(own, *inverse)
    other = call(functools.partial(half_inverse_kernel, 1), pairs)(other, *inverse)
    other = with_partner(other)
    slots = call(second_kernel, shaped(128, 128), [(6, 8, 128)] * 3)(
        own, other, forward, backward, first, middle, coupling_lines
    )
    slots = exchange(slots, 4)
    correction, remaining = call(last_kernel, (shaped(48, 128), shaped(48, 128)))(slots)
    return correction.reshape(rhs.shape), remaining.reshape(rhs.shape)


def from_behind(value, axis, steps):
    count = lax.axis_size(axis)
    initial, last = (max(0, -steps), min(count, count - steps))
    return lax.ppermute(value, axis, [(source, source + steps) for source in range(initial, last)])


def from_root(shard, axis, root):
    mine = lax.axis_index(axis) == root
    return lax.psum(jnp.where(mine, shard, jnp.zeros_like(shard)), axis)


def extended(block, sides, width):
    for axis, dim in sides:
        count = lax.axis_size(axis)
        forward = [(i, i + 1) for i in range(count - 1)]
        backward = [(target, source) for source, target in forward]
        low = lax.ppermute(
            lax.slice_in_dim(block, block.shape[dim] - width, None, axis=dim), axis, forward
        )
        high = lax.ppermute(lax.slice_in_dim(block, 0, width, axis=dim), axis, backward)
        block = jnp.concatenate([low, block, high], axis=dim)
    return block


def cell_stride(one_block, carried, const_term):
    return const_term - jnp.einsum(
        "abl,al->bl", one_block.astype(jnp.float32), carried, precision=highest
    )


def compose_cells(blocks, sequence):
    running = None
    for position in sequence:
        one_block = blocks[position].astype(jnp.float32)
        running = -jnp.swapaxes(one_block, 0, 1)
    return running


def doubling_maps(local_map, reverse):
    size = lax.axis_size("azim")
    index = lax.axis_index("azim")
    levels = []
    current = local_map
    distance = 1
    while distance < size:
        if reverse:
            moved = from_behind(current, "azim", -distance)
            exists = index + distance < size
        else:
            moved = from_behind(current, "azim", distance)
            exists = index >= distance
        levels.append((current, distance))
        current = jnp.where(
            exists, jnp.einsum("bcl,cal->bal", current, moved, precision=highest), current
        )
        distance = distance * 2
    return (levels, current)


def doubling_entries(map_levels, local_offset, reverse):
    levels, final_map = map_levels
    size = lax.axis_size("azim")
    index = lax.axis_index("azim")
    running = local_offset
    for current, distance in levels:
        if reverse:
            moved = from_behind(running, "azim", -distance)
        else:
            moved = from_behind(running, "azim", distance)
        running = jnp.einsum("bcl,cl->bl", current, moved, precision=highest) + running
    if reverse:
        wrapped = from_root(running, "azim", 0)
    else:
        wrapped = from_root(running, "azim", size - 1)
    leaving = jnp.einsum("bcl,cl->bl", final_map, wrapped, precision=highest) + running
    if reverse:
        shifted = from_behind(leaving, "azim", -1)
        first_device = index == size - 1
    else:
        shifted = from_behind(leaving, "azim", 1)
        first_device = index == 0
    return jnp.where(first_device, wrapped, shifted)


def sweep(blocks, consts, map_levels, reverse):
    cell_count = blocks.shape[0]
    sequence = list(range(cell_count))
    if reverse:
        sequence = sequence[::-1]
    carried = jnp.zeros(consts.shape[1:], jnp.float32)
    for position in sequence:
        carried = cell_stride(blocks[position], carried, consts[position])
    local_offset = carried
    incoming_maps = doubling_entries(map_levels, local_offset, reverse)
    outputs = [None] * cell_count
    carried = incoming_maps
    for position in sequence:
        carried = cell_stride(blocks[position], carried, consts[position])
        outputs[position] = carried
    return jnp.stack(outputs)


def on_device(rhs, coupling, fwd_coupling, bwd_coupling, block_inverse):
    cell_count, block_width, _, position_total, radial_count = fwd_coupling.shape
    line_count = position_total * radial_count
    forward_blocks = fwd_coupling.reshape(cell_count, block_width, block_width, line_count)
    backward_blocks = bwd_coupling.reshape(cell_count, block_width, block_width, line_count)
    inverse_blocks = block_inverse.reshape(cell_count, block_width, block_width, line_count)
    source = rhs.reshape(cell_count, block_width, line_count)
    coupling_field = coupling.reshape(cell_count, block_width, line_count)
    forward_map = compose_cells(forward_blocks, list(range(cell_count)))
    backward_map = compose_cells(backward_blocks, list(range(cell_count))[::-1])
    forward_levels = None
    backward_levels = None
    forward_levels = doubling_maps(forward_map, False)
    backward_levels = doubling_maps(backward_map, True)

    def precondition(vector):
        consts = jnp.stack(
            [
                jnp.einsum(
                    "abl,al->bl",
                    inverse_blocks[0].astype(jnp.float32),
                    vector[0],
                    precision=highest,
                )
            ]
        )
        forward = sweep(forward_blocks, consts, forward_levels, False)
        return sweep(backward_blocks, forward, backward_levels, True)

    def stations_sum(field):
        grid = field.reshape(cell_count, block_width, position_total, radial_count)
        padded = extended(grid, (("axial", 2),), 1)
        return (padded[:, :, :-2] + padded[:, :, 2:]).reshape(cell_count, block_width, line_count)

    applied_once = precondition(source)
    middle = source - applied_once + coupling_field * stations_sum(applied_once)
    second = precondition(middle)
    correction = applied_once + second
    remaining = middle - second + coupling_field * stations_sum(second)
    return (correction.reshape(rhs.shape), remaining.reshape(rhs.shape))


def solution(mesh):
    cells, stations = mesh.shape["azim"], mesh.shape["axial"]

    def on_each(rhs, coupling, fwd_coupling, bwd_coupling, block_inverse):
        local = fwd_coupling.shape
        if (cells, stations) == (8, 4) and local == (1, 48, 48, 1, 128):
            return line_plan(rhs, coupling, fwd_coupling, bwd_coupling, block_inverse)
        return on_device(rhs, coupling, fwd_coupling, bwd_coupling, block_inverse)

    return jax.shard_map(
        on_each,
        mesh=mesh,
        in_specs=(
            P("azim", None, "axial", None),
            P("azim", None, "axial", None),
            P("azim", None, None, "axial", None),
            P("azim", None, None, "axial", None),
            P("azim", None, None, "axial", None),
        ),
        out_specs=(P("azim", None, "axial", None), P("azim", None, "axial", None)),
        check_vma=False,
    )
```

```python
import functools

import jax
import jax.numpy as jnp
from jax import lax
from jax.experimental import pallas as pl
from jax.experimental.pallas import tpu as pltpu
from jax.sharding import PartitionSpec as P

highest = lax.Precision.HIGHEST
f32 = jnp.float32
BOTH = ("azim", "axial")
SLOTS = ("axial", "azim")
VMEM_LIMIT = 16 * 1024 * 1024


def lane_index():
    return lax.broadcasted_iota(jnp.int32, (8, 128), 1)


def row_index():
    return lax.broadcasted_iota(jnp.int32, (8, 128), 0)


def turn_lanes(tile, steps):
    steps = steps % 128
    return pltpu.roll(tile, steps, 1) if steps else tile


def turn_rows(tile, steps):
    steps = steps % 8
    return pltpu.roll(tile, steps, 0) if steps else tile


def line_lanes():
    return lane_index() + 16 - 4 * (lax.axis_index("azim") % 4)


def slot_number():
    return 8 * lax.axis_index("axial") + lax.axis_index("azim")


def to_line(tile):
    return pltpu.roll(tile, 4 * slot_number(), 1)


def from_line(tile):
    return pltpu.roll(tile, (128 - 4 * slot_number()) % 128, 1)


def swap_quads(tiles, lanes=None):
    lanes = lane_index() if lanes is None else lanes
    tiles = list(tiles)
    for bit, width in ((1, 4), (2, 8)):
        low = (lanes // width) % 2 == 0
        for first in range(4):
            if first & bit:
                continue
            one, two = tiles[first], tiles[first | bit]
            tiles[first] = jnp.where(low, one, turn_lanes(two, width))
            tiles[first | bit] = jnp.where(low, turn_lanes(one, -width), two)
    return tiles


def swap_rows(tile):
    lanes, rows = lane_index() // 16, row_index()
    for bit in (1, 2, 4):
        row_bit, lane_bit = (rows // bit) % 2, (lanes // bit) % 2
        up = turn_rows(turn_lanes(tile, 16 * bit), -bit)
        down = turn_rows(turn_lanes(tile, -16 * bit), bit)
        tile = jnp.where(row_bit == lane_bit, tile, jnp.where(row_bit == 0, up, down))
    return tile


def slot_rows(rows, quad, line_side):
    return (8 * rows * quad, rows) if line_side else (rows * quad, 4 * rows)


def put_slots(out_ref, tiles, rows, base, line_side=False):
    zero = jnp.zeros((8, 128), f32)
    for half in range(2):
        group = [tiles[4 * half + x] if 4 * half + x < 6 else zero for x in range(4)]
        for quad, tile in enumerate(swap_quads(group)):
            start, stride = slot_rows(rows, quad, line_side)
            out_ref[pl.ds(start + base + half, 8, stride=stride), :] = tile


def get_slots(in_ref, rows, base, line_side=False):
    tiles = []
    for half in range(2):
        group = []
        for quad in range(4):
            start, stride = slot_rows(rows, quad, line_side)
            group.append(in_ref[pl.ds(start + base + half, 8, stride=stride), :])
        tiles += swap_quads(group)
    return tiles[:6]


def put_cell_vector(out_ref, vector_ref, rows, base):
    put_slots(out_ref, [swap_rows(vector_ref[8 * t : 8 * t + 8, :]) for t in range(6)], rows, base)


def inverse_matvec(inverse_ref, vector_ref, out_ref):
    totals = None
    for a in range(48):
        term = inverse_ref[a].astype(f32) * vector_ref[a : a + 1, :]
        totals = term if totals is None else totals + term
    out_ref[...] = totals


COMBINATIONS = [(ah, pair) for ah in range(6) for pair in range(3)]
GROUPS_OF_THIRD = ((0, 1), (2, 3, 4, 5), (6, 7, 8))


def group_tiles(group):
    if group == 8:
        return [COMBINATIONS[16 + x // 2] + (x % 2,) for x in range(4)]
    return [COMBINATIONS[4 * (group // 2) + x] + (group % 2,) for x in range(4)]


TILE_AT = {
    (ah, 2 * pair + half): 4 * group + x
    for group in range(9)
    for x, (ah, pair, half) in enumerate(group_tiles(group))
}


def pack_blocks(block_ref, out_ref, base, third):
    station = lax.axis_index("axial")
    quads = lane_index() // 4
    keeps = [(bit, (quads & bit) == 0) for bit in (1, 2, 4, 8, 16)]
    turned = {}
    for group in GROUPS_OF_THIRD[third]:
        items = []
        for i in range(32):
            p = i // 4
            ah, pair, half = group_tiles(group)[i % 4]
            steps = (4 * i + 4 * station) % 128
            if (ah, pair, i) not in turned:
                tile = block_ref[8 * ah + p, 16 * pair : 16 * pair + 16, :]
                turned[ah, pair, i] = pltpu.roll(tile, steps, 1).astype(f32)
            items.append(turn_rows(turned[ah, pair, i][8 * half : 8 * half + 8], -p))
        for bit, keep in keeps:
            items = [jnp.where(keep, items[j], items[(j + bit) % 32]) for j in range(32)]
        for slot in range(35):
            out_ref[slot, base + 8 * group : base + 8 * group + 8, :] = items[-slot % 32]


def fetch_thirds(block_hbm, block_ref, sems):
    copies = []
    for third in range(3):
        there = (slice(16 * third, 16 * third + 16), slice(None), slice(None))
        copies.append(pltpu.make_async_copy(block_hbm.at[there], block_ref.at[there], sems.at[third]))
    return copies


def join_stations(parts):
    chunk = line_lanes() // 4
    for bit in (1, 2):
        keep = (chunk & bit) == 0
        parts = [jnp.where(keep, parts[j], parts[(j + bit) % 4]) for j in range(4)]
    return [turn_lanes(parts[-x % 4], -4 * x) for x in range(4)]


def unpack_cell(in_ref, base, out_ref, cell):
    for group in range(9):
        at = base + 8 * group
        parts = [in_ref[8 * k + cell, at : at + 8, :] for k in range(4)]
        for x, tile in enumerate(join_stations(parts)):
            at = 8 * (4 * group + x)
            out_ref[cell, at : at + 8, :] = tile


def line_sweep(blocks_ref, const_ref, out_ref, reverse, beside=None):
    order = list(range(8))
    if reverse:
        order = order[::-1]
    state = None
    for turn in range(2):
        for n, cell in enumerate(order):
            if beside is not None:
                beside(turn, n)
            consts = [jnp.broadcast_to(const_ref[t, cell : cell + 1, :], (8, 128)) for t in range(6)]
            if state is None:
                state = consts
                continue
            state = line_step(blocks_ref, cell, state, consts)
            if turn == 1:
                for t in range(6):
                    out_ref[t, cell : cell + 1, :] = state[t][0:1]


def stations_sum(tile):
    station = (line_lanes() // 4) % 4
    before = jnp.where(station > 0, turn_lanes(tile, 4), 0.0)
    after = jnp.where(station < 3, turn_lanes(tile, -4), 0.0)
    return before + after


def first_send_kernel(
    forward_hbm, backward_hbm, inverse_hbm, rhs_hbm, coupling_hbm, out_hbm,
    f_ref, b_ref, i_ref, rhs_ref, coupling_ref, c_ref, vectors_ref, packed_ref, sems, out_sems,
):
    forward = fetch_thirds(forward_hbm, f_ref, sems.at[0])
    inverse = fetch_thirds(inverse_hbm, i_ref, sems.at[1])
    backward = fetch_thirds(backward_hbm, b_ref, sems.at[2])
    vectors = [
        pltpu.make_async_copy(source, target, sems.at[3, n])
        for n, (source, target) in enumerate(((rhs_hbm, rhs_ref), (coupling_hbm, coupling_ref)))
    ]
    for copy in forward + vectors + inverse:
        copy.start()
    leaving = []

    def leave(row, rows, first):
        source = packed_ref.at[pl.ds(first, 32), pl.ds(row, rows), :]
        target = out_hbm.at[:, pl.ds(row, rows), :]
        leaving.append(pltpu.make_async_copy(source, target, out_sems.at[len(leaving)]))
        leaving[-1].start()

    station = lax.axis_index("axial")

    for third in range(3):
        forward[third].wait()
        if third == 0:
            for copy in backward:
                copy.start()
        pack_blocks(f_ref, packed_ref, 0, third)
        leave((0, 16, 48)[third], (16, 32, 24)[third], station)
    for copy in vectors + inverse:
        copy.wait()
    for third in range(3):
        backward[third].wait()
        if third == 0:
            inverse_matvec(i_ref, rhs_ref, c_ref)
            for n, vector_ref in enumerate((c_ref, rhs_ref, coupling_ref)):
                put_cell_vector(vectors_ref, vector_ref, 8, 2 * n)
            for e in range(32):
                packed_ref[e, 144:152, :] = vectors_ref[8 * e : 8 * e + 8, :]
        pack_blocks(b_ref, packed_ref, 72, third)
        if third == 0:
            leave(144, 8, 0)
        leave((72, 88, 120)[third], (16, 32, 24)[third], station)
    for copy in leaving:
        copy.wait()


def first_kernel(slots_ref, *refs):
    own_ref, other_ref, forward_ref, backward_ref, first_ref, middle_ref, coupling_ref, packed_ref, c_ref, y_ref = refs
    for e in range(32):
        packed_ref[8 * e : 8 * e + 8, :] = slots_ref[e, 144:152, :]
    for t, tile in enumerate(get_slots(packed_ref, 8, 0, True)):
        c_ref[t] = to_line(tile)

    def unpack(turn, n):
        if turn == 0:
            unpack_cell(slots_ref, 0, forward_ref, n)
        else:
            unpack_cell(slots_ref, 72, backward_ref, n)

    line_sweep(forward_ref, c_ref, y_ref, False, unpack)
    line_sweep(backward_ref, y_ref, first_ref, True)
    rhs = [to_line(tile) for tile in get_slots(packed_ref, 8, 2, True)]
    coupling = [to_line(tile) for tile in get_slots(packed_ref, 8, 4, True)]
    half, _ = half_position()
    low = row_index() < 4
    own, other = [], []
    for t in range(6):
        first = first_ref[t]
        middle = rhs[t] - first + coupling[t] * stations_sum(first)
        turned = turn_rows(middle, 4)
        other.append(jnp.where(half == 0, turned, middle))
        own.append(jnp.where(half == 0, middle, turned))
        middle_ref[t] = middle
        coupling_ref[t] = coupling[t]
    for u in range(3):
        other_ref[u] = jnp.where(low, other[2 * u], turn_rows(other[2 * u + 1], 4))
        own_ref[u] = jnp.where(low, own[2 * u], turn_rows(own[2 * u + 1], 4))


def half_position():
    cell = lax.axis_index("azim")
    return cell // 4, (cell % 4) * 4 + lax.axis_index("axial")


def inverse_send_kernel(inverse_hbm, *refs):
    outs, (i_ref, packed_ref, fetch_sems, sems) = refs[:16], refs[16:]
    fetches = fetch_thirds(inverse_hbm, i_ref, fetch_sems)
    for copy in fetches:
        copy.start()
    for third, copy in enumerate(fetches):
        copy.wait()
        pack_blocks(i_ref, packed_ref, 0, third)
    half, place = half_position()
    station = place % 4
    copies = []
    for d in range(16):
        target = place ^ d
        for n in range(2):
            cell = 4 * (half if n == 0 else 1 - half) + target // 4
            source = 8 * (target % 4) + cell
            copies.append(
                pltpu.make_async_copy(packed_ref.at[source + station], outs[d].at[pl.ds(72 * n, 72), :], sems.at[2 * d + n])
            )
            copies[-1].start()
    for copy in copies:
        copy.wait()


def inverse_get_kernel(*refs):
    ins, out_ref = refs[:4], refs[4]
    station = lax.axis_index("axial")
    for lines in range(2):
        for group in range(9):
            at = 72 * lines + 8 * group
            parts = [part[at : at + 8, :] for part in ins]
            for bit in (1, 2):
                parts = [jnp.where((station & bit) == 0, parts[k], parts[k ^ bit]) for k in range(4)]
            for x, tile in enumerate(join_stations(parts)):
                at = 8 * (4 * group + x)
                out_ref[lines, at : at + 8, :] = tile


def line_step(blocks_ref, cell, state, consts):
    following = []
    for bh in range(6):
        terms = []
        for ah in range(6):
            at = 8 * TILE_AT[ah, bh]
            terms.append(blocks_ref[cell, at : at + 8, :] * state[ah])
        total = (terms[0] + terms[1]) + (terms[2] + terms[3]) + (terms[4] + terms[5])
        total = pltpu.roll(total, 0, 1, stride=16, stride_axis=0)
        for span in (4, 2):
            total = total + turn_rows(total, span)
        following.append((consts[bh] - total) - turn_rows(total, 1))
    return following


def half_inverse_kernel(lines, vector_ref, *refs):
    blocks, out_ref = refs[:4], refs[4]
    _, place = half_position()
    cell = place // 4
    rows = row_index()
    zero = jnp.zeros((8, 128), f32)
    totals = [zero] * 3
    for n in range(4):
        state = [
            jnp.broadcast_to(vector_ref[t // 2, pl.ds(4 * (t % 2) + (cell ^ n), 1), :], (8, 128)) for t in range(6)
        ]
        for t, product in enumerate(line_step(blocks[n], lines, state, [zero] * 6)):
            totals[t // 2] = jnp.where(rows == 4 * (t % 2) + (cell ^ n), product, totals[t // 2])
    for u in range(3):
        out_ref[u] = -totals[u]


def second_kernel(
    own_ref, other_ref, forward_ref, backward_ref, first_ref, middle_ref, coupling_ref, out_ref, c_ref, y_ref, second_ref
):
    half, _ = half_position()
    low = row_index() < 4
    for t in range(6):
        own, other = own_ref[t // 2], other_ref[t // 2]
        if t % 2:
            own = turn_rows(own, 4)
        else:
            other = turn_rows(other, 4)
        tile = jnp.where(low, own, other)
        c_ref[t] = jnp.where(half == 0, tile, turn_rows(tile, 4))
    line_sweep(forward_ref, c_ref, y_ref, False)
    line_sweep(backward_ref, y_ref, second_ref, True)
    correction, remaining = [], []
    for t in range(6):
        second = second_ref[t]
        correction.append(from_line(first_ref[t] + second))
        remaining.append(from_line(middle_ref[t] - second + coupling_ref[t] * stations_sum(second)))
    put_slots(out_ref, correction, 4, 0, True)
    put_slots(out_ref, remaining, 4, 2, True)


def last_kernel(slots_ref, correction_ref, remaining_ref):
    for out_ref, base in ((correction_ref, 0), (remaining_ref, 2)):
        for t, tile in enumerate(get_slots(slots_ref, 4, base)):
            out_ref[8 * t : 8 * t + 8, :] = swap_rows(tile)


def shaped(*sizes):
    return jax.ShapeDtypeStruct(sizes, f32)


def call(kernel, outs, scratch=()):
    return pl.pallas_call(
        kernel,
        out_shape=outs,
        scratch_shapes=[pltpu.VMEM(sizes, f32) for sizes in scratch],
        compiler_params=pltpu.CompilerParams(vmem_limit_bytes=VMEM_LIMIT),
    )


def exchange(slots, rows):
    moved = lax.all_to_all(slots.reshape(32, rows, 128), SLOTS, 0, 0, tiled=True)
    return moved.reshape(32 * rows, 128)


def line_plan(rhs, coupling, fwd_coupling, bwd_coupling, block_inverse):
    source, coupling_field = rhs.reshape(48, 128), coupling.reshape(48, 128)
    forward_blocks = fwd_coupling.reshape(48, 48, 128)
    backward_blocks = bwd_coupling.reshape(48, 48, 128)
    inverse_blocks = block_inverse.reshape(48, 48, 128)
    tiles, pairs, held = shaped(6, 8, 128), shaped(3, 8, 128), shaped(8, 288, 128)
    blocks = pltpu.VMEM((48, 48, 128), jnp.bfloat16)
    vector = pltpu.VMEM((48, 128), f32)

    slots = pl.pallas_call(
        first_send_kernel,
        out_shape=pltpu.HBM((32, 152, 128), f32),
        in_specs=[pl.BlockSpec(memory_space=pltpu.HBM)] * 5,
        out_specs=pl.BlockSpec(memory_space=pltpu.HBM),
        scratch_shapes=[blocks, blocks, blocks, vector, vector, vector]
        + [
            pltpu.VMEM((256, 128), f32),
            pltpu.VMEM((35, 152, 128), f32),
            pltpu.SemaphoreType.DMA((4, 3)),
            pltpu.SemaphoreType.DMA((7,)),
        ],
        compiler_params=pltpu.CompilerParams(vmem_limit_bytes=VMEM_LIMIT),
    )(*[
        pltpu.with_memory_space_constraint(array, pltpu.HBM)
        for array in (forward_blocks, backward_blocks, inverse_blocks, source, coupling_field)
    ])
    slots, inverse_blocks = lax.optimization_barrier((slots, inverse_blocks))
    slots = lax.all_to_all(slots, SLOTS, 0, 0, tiled=True)

    parts = pl.pallas_call(
        inverse_send_kernel,
        out_shape=[shaped(144, 128)] * 16,
        in_specs=[pl.BlockSpec(memory_space=pltpu.HBM)],
        out_specs=[pl.BlockSpec(memory_space=pltpu.HBM)] * 16,
        scratch_shapes=[
            blocks, pltpu.VMEM((35, 72, 128), f32), pltpu.SemaphoreType.DMA((3,)), pltpu.SemaphoreType.DMA((32,))
        ],
        compiler_params=pltpu.CompilerParams(vmem_limit_bytes=VMEM_LIMIT),
    )(pltpu.with_memory_space_constraint(inverse_blocks, pltpu.HBM))
    parts = [parts[0]] + [lax.ppermute(parts[d], BOTH, [(e, e ^ d) for e in range(32)]) for d in range(1, 16)]
    inverse = [
        call(inverse_get_kernel, pltpu.VMEM((2, 288, 128), f32))(*parts[4 * n : 4 * n + 4]) for n in range(4)
    ]

    own, other, forward, backward, first, middle, coupling_lines = call(
        first_kernel, (pairs, pairs, held, held, tiles, tiles, tiles), [(256, 128), (6, 8, 128), (6, 8, 128)]
    )(slots)

    def with_partner(vector):
        return lax.ppermute(vector, BOTH, [(e, e ^ 16) for e in range(32)])

    other = with_partner(other)
    own = call(functools.partial(half_inverse_kernel, 0), pairs)(own, *inverse)
    other = call(functools.partial(half_inverse_kernel, 1), pairs)(other, *inverse)
    other = with_partner(other)
    slots = call(second_kernel, shaped(128, 128), [(6, 8, 128)] * 3)(
        own, other, forward, backward, first, middle, coupling_lines
    )
    slots = exchange(slots, 4)
    correction, remaining = call(last_kernel, (shaped(48, 128), shaped(48, 128)))(slots)
    return correction.reshape(rhs.shape), remaining.reshape(rhs.shape)


def from_behind(value, axis, steps):
    count = lax.axis_size(axis)
    initial, last = (max(0, -steps), min(count, count - steps))
    return lax.ppermute(value, axis, [(source, source + steps) for source in range(initial, last)])


def from_root(shard, axis, root):
    mine = lax.axis_index(axis) == root
    return lax.psum(jnp.where(mine, shard, jnp.zeros_like(shard)), axis)


def extended(block, sides, width):
    for axis, dim in sides:
        count = lax.axis_size(axis)
        forward = [(i, i + 1) for i in range(count - 1)]
        backward = [(target, source) for source, target in forward]
        low = lax.ppermute(
            lax.slice_in_dim(block, block.shape[dim] - width, None, axis=dim), axis, forward
        )
        high = lax.ppermute(lax.slice_in_dim(block, 0, width, axis=dim), axis, backward)
        block = jnp.concatenate([low, block, high], axis=dim)
    return block


def cell_stride(one_block, carried, const_term):
    return const_term - jnp.einsum(
        "abl,al->bl", one_block.astype(jnp.float32), carried, precision=highest
    )


def compose_cells(blocks, sequence):
    running = None
    for position in sequence:
        one_block = blocks[position].astype(jnp.float32)
        running = -jnp.swapaxes(one_block, 0, 1)
    return running


def doubling_maps(local_map, reverse):
    size = lax.axis_size("azim")
    index = lax.axis_index("azim")
    levels = []
    current = local_map
    distance = 1
    while distance < size:
        if reverse:
            moved = from_behind(current, "azim", -distance)
            exists = index + distance < size
        else:
            moved = from_behind(current, "azim", distance)
            exists = index >= distance
        levels.append((current, distance))
        current = jnp.where(
            exists, jnp.einsum("bcl,cal->bal", current, moved, precision=highest), current
        )
        distance = distance * 2
    return (levels, current)


def doubling_entries(map_levels, local_offset, reverse):
    levels, final_map = map_levels
    size = lax.axis_size("azim")
    index = lax.axis_index("azim")
    running = local_offset
    for current, distance in levels:
        if reverse:
            moved = from_behind(running, "azim", -distance)
        else:
            moved = from_behind(running, "azim", distance)
        running = jnp.einsum("bcl,cl->bl", current, moved, precision=highest) + running
    if reverse:
        wrapped = from_root(running, "azim", 0)
    else:
        wrapped = from_root(running, "azim", size - 1)
    leaving = jnp.einsum("bcl,cl->bl", final_map, wrapped, precision=highest) + running
    if reverse:
        shifted = from_behind(leaving, "azim", -1)
        first_device = index == size - 1
    else:
        shifted = from_behind(leaving, "azim", 1)
        first_device = index == 0
    return jnp.where(first_device, wrapped, shifted)


def sweep(blocks, consts, map_levels, reverse):
    cell_count = blocks.shape[0]
    sequence = list(range(cell_count))
    if reverse:
        sequence = sequence[::-1]
    carried = jnp.zeros(consts.shape[1:], jnp.float32)
    for position in sequence:
        carried = cell_stride(blocks[position], carried, consts[position])
    local_offset = carried
    incoming_maps = doubling_entries(map_levels, local_offset, reverse)
    outputs = [None] * cell_count
    carried = incoming_maps
    for position in sequence:
        carried = cell_stride(blocks[position], carried, consts[position])
        outputs[position] = carried
    return jnp.stack(outputs)


def on_device(rhs, coupling, fwd_coupling, bwd_coupling, block_inverse):
    cell_count, block_width, _, position_total, radial_count = fwd_coupling.shape
    line_count = position_total * radial_count
    forward_blocks = fwd_coupling.reshape(cell_count, block_width, block_width, line_count)
    backward_blocks = bwd_coupling.reshape(cell_count, block_width, block_width, line_count)
    inverse_blocks = block_inverse.reshape(cell_count, block_width, block_width, line_count)
    source = rhs.reshape(cell_count, block_width, line_count)
    coupling_field = coupling.reshape(cell_count, block_width, line_count)
    forward_map = compose_cells(forward_blocks, list(range(cell_count)))
    backward_map = compose_cells(backward_blocks, list(range(cell_count))[::-1])
    forward_levels = None
    backward_levels = None
    forward_levels = doubling_maps(forward_map, False)
    backward_levels = doubling_maps(backward_map, True)

    def precondition(vector):
        consts = jnp.stack(
            [
                jnp.einsum(
                    "abl,al->bl",
                    inverse_blocks[0].astype(jnp.float32),
                    vector[0],
                    precision=highest,
                )
            ]
        )
        forward = sweep(forward_blocks, consts, forward_levels, False)
        return sweep(backward_blocks, forward, backward_levels, True)

    def stations_sum(field):
        grid = field.reshape(cell_count, block_width, position_total, radial_count)
        padded = extended(grid, (("axial", 2),), 1)
        return (padded[:, :, :-2] + padded[:, :, 2:]).reshape(cell_count, block_width, line_count)

    applied_once = precondition(source)
    middle = source - applied_once + coupling_field * stations_sum(applied_once)
    second = precondition(middle)
    correction = applied_once + second
    remaining = middle - second + coupling_field * stations_sum(second)
    return (correction.reshape(rhs.shape), remaining.reshape(rhs.shape))


def solution(mesh):
    cells, stations = mesh.shape["azim"], mesh.shape["axial"]

    def on_each(rhs, coupling, fwd_coupling, bwd_coupling, block_inverse):
        local = fwd_coupling.shape
        if (cells, stations) == (8, 4) and local == (1, 48, 48, 1, 128):
            return line_plan(rhs, coupling, fwd_coupling, bwd_coupling, block_inverse)
        return on_device(rhs, coupling, fwd_coupling, bwd_coupling, block_inverse)

    return jax.shard_map(
        on_each,
        mesh=mesh,
        in_specs=(
            P("azim", None, "axial", None),
            P("azim", None, "axial", None),
            P("azim", None, None, "axial", None),
            P("azim", None, None, "axial", None),
            P("azim", None, None, "axial", None),
        ),
        out_specs=(P("azim", None, "axial", None), P("azim", None, "axial", None)),
        check_vma=False,
    )
```

```python
import functools

import jax
import jax.numpy as jnp
from jax import lax
from jax.experimental import pallas as pl
from jax.experimental.pallas import tpu as pltpu
from jax.sharding import PartitionSpec as P

highest = lax.Precision.HIGHEST
f32 = jnp.float32
BOTH = ("azim", "axial")


def chunk_of(cell, station):
    return 16 * (cell % 2) + 4 * station + cell // 2


ORDER = [[e for chunk in range(32) for e in range(32) if chunk_of(e // 4, e % 4) == chunk]]
VMEM_LIMIT = 16 * 1024 * 1024


def lane_index():
    return lax.broadcasted_iota(jnp.int32, (8, 128), 1)


def row_index():
    return lax.broadcasted_iota(jnp.int32, (8, 128), 0)


def turn_lanes(tile, steps):
    steps = steps % 128
    return pltpu.roll(tile, steps, 1) if steps else tile


def turn_rows(tile, steps):
    steps = steps % 8
    return pltpu.roll(tile, steps, 0) if steps else tile


def line_lanes(other_half=0):
    return lane_index() + 16 - 4 * ((lax.axis_index("azim") // 2) ^ (2 * other_half))


def own_chunk():
    return chunk_of(lax.axis_index("azim"), lax.axis_index("axial"))


def to_line(tile):
    return pltpu.roll(tile, 4 * own_chunk(), 1)


def from_line(tile):
    return pltpu.roll(tile, (128 - 4 * own_chunk()) % 128, 1)


def swap_quads(tiles, lanes=None):
    lanes = lane_index() if lanes is None else lanes
    tiles = list(tiles)
    for bit, width in ((1, 4), (2, 8)):
        low = (lanes // width) % 2 == 0
        for first in range(4):
            if first & bit:
                continue
            one, two = tiles[first], tiles[first | bit]
            tiles[first] = jnp.where(low, one, turn_lanes(two, width))
            tiles[first | bit] = jnp.where(low, turn_lanes(one, -width), two)
    return tiles


def swap_rows(tile):
    lanes, rows = lane_index() // 16, row_index()
    for bit in (1, 2, 4):
        row_bit, lane_bit = (rows // bit) % 2, (lanes // bit) % 2
        up = turn_rows(turn_lanes(tile, 16 * bit), -bit)
        down = turn_rows(turn_lanes(tile, -16 * bit), bit)
        tile = jnp.where(row_bit == lane_bit, tile, jnp.where(row_bit == 0, up, down))
    return tile


def put_slots(out_ref, tiles, rows, base):
    zero = jnp.zeros((8, 128), f32)
    for half in range(2):
        group = [tiles[4 * half + x] if 4 * half + x < 6 else zero for x in range(4)]
        for quad, tile in enumerate(swap_quads(group)):
            out_ref[pl.ds(rows * quad + base + half, 8, stride=4 * rows), :] = tile


def get_slots(in_ref, rows, base):
    tiles = []
    for half in range(2):
        group = [in_ref[pl.ds(rows * quad + base + half, 8, stride=4 * rows), :] for quad in range(4)]
        tiles += swap_quads(group)
    return tiles[:6]


def put_cell_vector(out_ref, vector_ref, rows, base):
    put_slots(out_ref, [swap_rows(vector_ref[8 * t : 8 * t + 8, :]) for t in range(6)], rows, base)


def inverse_matvec(inverse_ref, vector_ref, out_ref):
    totals = None
    for a in range(48):
        term = inverse_ref[a].astype(f32) * vector_ref[a : a + 1, :]
        totals = term if totals is None else totals + term
    out_ref[...] = totals


COMBINATIONS = [(ah, pair) for ah in range(6) for pair in range(3)]
GROUPS_OF_THIRD = ((0, 1), (2, 3, 4, 5), (6, 7, 8))


def group_tiles(group):
    if group == 8:
        return [COMBINATIONS[16 + x // 2] + (x % 2,) for x in range(4)]
    return [COMBINATIONS[4 * (group // 2) + x] + (group % 2,) for x in range(4)]


TILE_AT = {
    (ah, 2 * pair + half): 4 * group + x
    for group in range(9)
    for x, (ah, pair, half) in enumerate(group_tiles(group))
}


def pack_blocks(block_ref, out_ref, base, third):
    station = lax.axis_index("axial")
    quads = lane_index() // 4
    keeps = [(bit, (quads & bit) == 0) for bit in (1, 2, 4, 8, 16)]
    turned = {}
    for group in GROUPS_OF_THIRD[third]:
        items = []
        for i in range(32):
            p = i // 4
            ah, pair, half = group_tiles(group)[i % 4]
            steps = (4 * i + 4 * station) % 128
            if (ah, pair, i) not in turned:
                tile = block_ref[8 * ah + p, 16 * pair : 16 * pair + 16, :]
                turned[ah, pair, i] = pltpu.roll(tile, steps, 1).astype(f32)
            items.append(turn_rows(turned[ah, pair, i][8 * half : 8 * half + 8], -p))
        for bit, keep in keeps:
            items = [jnp.where(keep, items[j], items[(j + bit) % 32]) for j in range(32)]
        for slot in range(35):
            out_ref[slot, base + 8 * group : base + 8 * group + 8, :] = items[-slot % 32]


def fetch_thirds(block_hbm, block_ref, sems):
    copies = []
    for third in range(3):
        there = (slice(16 * third, 16 * third + 16), slice(None), slice(None))
        copies.append(pltpu.make_async_copy(block_hbm.at[there], block_ref.at[there], sems.at[third]))
    return copies


def join_stations(parts, other_half=0):
    chunk = line_lanes(other_half) // 4
    for bit in (1, 2):
        keep = (chunk & bit) == 0
        parts = [jnp.where(keep, parts[j], parts[(j + bit) % 4]) for j in range(4)]
    return [turn_lanes(parts[-x % 4], -4 * x) for x in range(4)]


def unpack_cell(in_ref, base, out_ref, cell):
    for group in range(9):
        at = base + 8 * group
        parts = [in_ref[chunk_of(cell, k), at : at + 8, :] for k in range(4)]
        for x, tile in enumerate(join_stations(parts)):
            at = 8 * (4 * group + x)
            out_ref[cell, at : at + 8, :] = tile


def line_sweep(blocks_ref, const_ref, out_ref, reverse, beside=None):
    order = list(range(8))
    if reverse:
        order = order[::-1]
    state = None
    for turn in range(2):
        for n, cell in enumerate(order):
            if beside is not None:
                beside(turn, n)
            consts = [jnp.broadcast_to(const_ref[t, cell : cell + 1, :], (8, 128)) for t in range(6)]
            if state is None:
                state = consts
                continue
            state = line_step(blocks_ref, cell, state, consts)
            if turn == 1:
                for t in range(6):
                    out_ref[t, cell : cell + 1, :] = state[t][0:1]


def stations_sum(tile):
    station = (line_lanes() // 4) % 4
    before = jnp.where(station > 0, turn_lanes(tile, 4), 0.0)
    after = jnp.where(station < 3, turn_lanes(tile, -4), 0.0)
    return before + after


def first_send_kernel(
    forward_hbm, backward_hbm, inverse_hbm, rhs_hbm, coupling_hbm, out_hbm,
    f_ref, b_ref, i_ref, rhs_ref, coupling_ref, c_ref, vectors_ref, packed_ref, sems, out_sems,
):
    forward = fetch_thirds(forward_hbm, f_ref, sems.at[0])
    inverse = fetch_thirds(inverse_hbm, i_ref, sems.at[1])
    backward = fetch_thirds(backward_hbm, b_ref, sems.at[2])
    vectors = [
        pltpu.make_async_copy(source, target, sems.at[3, n])
        for n, (source, target) in enumerate(((rhs_hbm, rhs_ref), (coupling_hbm, coupling_ref)))
    ]
    for copy in forward + vectors + inverse:
        copy.start()
    leaving = []

    def leave(row, rows, first):
        source = packed_ref.at[pl.ds(first, 32), pl.ds(row, rows), :]
        target = out_hbm.at[:, pl.ds(row, rows), :]
        leaving.append(pltpu.make_async_copy(source, target, out_sems.at[len(leaving)]))
        leaving[-1].start()

    station = lax.axis_index("axial")

    for third in range(3):
        forward[third].wait()
        if third == 0:
            for copy in backward:
                copy.start()
        pack_blocks(f_ref, packed_ref, 0, third)
        leave((0, 16, 48)[third], (16, 32, 24)[third], station)
    for copy in vectors + inverse:
        copy.wait()
    for third in range(3):
        backward[third].wait()
        if third == 0:
            inverse_matvec(i_ref, rhs_ref, c_ref)
            for n, vector_ref in enumerate((c_ref, rhs_ref, coupling_ref)):
                put_cell_vector(vectors_ref, vector_ref, 8, 2 * n)
            for e in range(32):
                packed_ref[e, 144:152, :] = vectors_ref[8 * e : 8 * e + 8, :]
        pack_blocks(b_ref, packed_ref, 72, third)
        if third == 0:
            leave(144, 8, 0)
        leave((72, 88, 120)[third], (16, 32, 24)[third], station)
    for copy in leaving:
        copy.wait()


def first_kernel(slots_ref, *refs):
    own_ref, other_ref, forward_ref, backward_ref, first_ref, middle_ref, coupling_ref, packed_ref, c_ref, y_ref = refs
    for e in range(32):
        packed_ref[8 * e : 8 * e + 8, :] = slots_ref[chunk_of(e // 4, e % 4), 144:152, :]
    for t, tile in enumerate(get_slots(packed_ref, 8, 0)):
        c_ref[t] = to_line(tile)

    def unpack(turn, n):
        if turn == 0:
            unpack_cell(slots_ref, 0, forward_ref, n)
        else:
            unpack_cell(slots_ref, 72, backward_ref, n)

    line_sweep(forward_ref, c_ref, y_ref, False, unpack)
    line_sweep(backward_ref, y_ref, first_ref, True)
    rhs = [to_line(tile) for tile in get_slots(packed_ref, 8, 2)]
    coupling = [to_line(tile) for tile in get_slots(packed_ref, 8, 4)]
    half, _ = half_position()
    low = row_index() < 4
    own, other = [], []
    for t in range(6):
        first = first_ref[t]
        middle = rhs[t] - first + coupling[t] * stations_sum(first)
        turned = turn_rows(middle, 4)
        other.append(jnp.where(half == 0, turned, middle))
        own.append(jnp.where(half == 0, middle, turned))
        middle_ref[t] = middle
        coupling_ref[t] = coupling[t]
    for u in range(3):
        other_ref[u] = jnp.where(low, other[2 * u], turn_rows(other[2 * u + 1], 4))
        own_ref[u] = jnp.where(low, own[2 * u], turn_rows(own[2 * u + 1], 4))


def half_position():
    cell = lax.axis_index("azim")
    return cell // 4, (cell % 4) * 4 + lax.axis_index("axial")


def inverse_send_kernel(inverse_hbm, *refs):
    outs, (i_ref, packed_ref, fetch_sems, sems) = refs[:16], refs[16:]
    fetches = fetch_thirds(inverse_hbm, i_ref, fetch_sems)
    for copy in fetches:
        copy.start()
    for third, copy in enumerate(fetches):
        copy.wait()
        pack_blocks(i_ref, packed_ref, 0, third)
    half, place = half_position()
    station = place % 4
    copies = []
    for d in range(16):
        target = place ^ d
        for n in range(2):
            cell = 4 * (half if n == 0 else 1 - half) + target // 4
            source = chunk_of(cell, target % 4)
            copies.append(
                pltpu.make_async_copy(packed_ref.at[source + station], outs[d].at[pl.ds(72 * n, 72), :], sems.at[2 * d + n])
            )
            copies[-1].start()
    for copy in copies:
        copy.wait()


def inverse_get_kernel(*refs):
    ins, out_ref = refs[:4], refs[4]
    station = lax.axis_index("axial")
    for lines in range(2):
        for group in range(9):
            at = 72 * lines + 8 * group
            parts = [part[at : at + 8, :] for part in ins]
            for bit in (1, 2):
                parts = [jnp.where((station & bit) == 0, parts[k], parts[k ^ bit]) for k in range(4)]
            for x, tile in enumerate(join_stations(parts, lines)):
                at = 8 * (4 * group + x)
                out_ref[lines, at : at + 8, :] = tile


def line_step(blocks_ref, cell, state, consts):
    following = []
    for bh in range(6):
        terms = []
        for ah in range(6):
            at = 8 * TILE_AT[ah, bh]
            terms.append(blocks_ref[cell, at : at + 8, :] * state[ah])
        total = (terms[0] + terms[1]) + (terms[2] + terms[3]) + (terms[4] + terms[5])
        total = pltpu.roll(total, 0, 1, stride=16, stride_axis=0)
        for span in (4, 2):
            total = total + turn_rows(total, span)
        following.append((consts[bh] - total) - turn_rows(total, 1))
    return following


def half_inverse_kernel(lines, vector_ref, *refs):
    blocks, out_ref = refs[:4], refs[4]
    _, place = half_position()
    cell = place // 4
    rows = row_index()
    zero = jnp.zeros((8, 128), f32)
    totals = [zero] * 3
    for n in range(4):
        state = [
            jnp.broadcast_to(vector_ref[t // 2, pl.ds(4 * (t % 2) + (cell ^ n), 1), :], (8, 128)) for t in range(6)
        ]
        for t, product in enumerate(line_step(blocks[n], lines, state, [zero] * 6)):
            totals[t // 2] = jnp.where(rows == 4 * (t % 2) + (cell ^ n), product, totals[t // 2])
    for u in range(3):
        out_ref[u] = -totals[u]


def second_kernel(
    own_ref, other_ref, forward_ref, backward_ref, first_ref, middle_ref, coupling_ref, out_ref, c_ref, y_ref, second_ref,
    slots_ref,
):
    half, _ = half_position()
    low = row_index() < 4
    for t in range(6):
        own, other = own_ref[t // 2], other_ref[t // 2]
        if t % 2:
            own = turn_rows(own, 4)
        else:
            other = turn_rows(other, 4)
        tile = jnp.where(low, own, other)
        c_ref[t] = jnp.where(half == 0, tile, turn_rows(tile, 4))
    line_sweep(forward_ref, c_ref, y_ref, False)
    line_sweep(backward_ref, y_ref, second_ref, True)
    correction, remaining = [], []
    for t in range(6):
        second = second_ref[t]
        correction.append(from_line(first_ref[t] + second))
        remaining.append(from_line(middle_ref[t] - second + coupling_ref[t] * stations_sum(second)))
    put_slots(slots_ref, correction, 4, 0)
    put_slots(slots_ref, remaining, 4, 2)
    for e in range(32):
        at = 4 * chunk_of(e // 4, e % 4)
        out_ref[at : at + 4, :] = slots_ref[4 * e : 4 * e + 4, :]


def last_kernel(slots_ref, correction_ref, remaining_ref):
    for out_ref, base in ((correction_ref, 0), (remaining_ref, 2)):
        for t, tile in enumerate(get_slots(slots_ref, 4, base)):
            out_ref[8 * t : 8 * t + 8, :] = swap_rows(tile)


def shaped(*sizes):
    return jax.ShapeDtypeStruct(sizes, f32)


def call(kernel, outs, scratch=()):
    return pl.pallas_call(
        kernel,
        out_shape=outs,
        scratch_shapes=[pltpu.VMEM(sizes, f32) for sizes in scratch],
        compiler_params=pltpu.CompilerParams(vmem_limit_bytes=VMEM_LIMIT),
    )


def exchange(slots, rows):
    moved = lax.all_to_all(slots.reshape(32, rows, 128), BOTH, 0, 0, axis_index_groups=ORDER, tiled=True)
    return moved.reshape(32 * rows, 128)


def line_plan(rhs, coupling, fwd_coupling, bwd_coupling, block_inverse):
    source, coupling_field = rhs.reshape(48, 128), coupling.reshape(48, 128)
    forward_blocks = fwd_coupling.reshape(48, 48, 128)
    backward_blocks = bwd_coupling.reshape(48, 48, 128)
    inverse_blocks = block_inverse.reshape(48, 48, 128)
    tiles, pairs, held = shaped(6, 8, 128), shaped(3, 8, 128), shaped(8, 288, 128)
    blocks = pltpu.VMEM((48, 48, 128), jnp.bfloat16)
    vector = pltpu.VMEM((48, 128), f32)

    slots = pl.pallas_call(
        first_send_kernel,
        out_shape=pltpu.HBM((32, 152, 128), f32),
        in_specs=[pl.BlockSpec(memory_space=pltpu.HBM)] * 5,
        out_specs=pl.BlockSpec(memory_space=pltpu.HBM),
        scratch_shapes=[blocks, blocks, blocks, vector, vector, vector]
        + [
            pltpu.VMEM((256, 128), f32),
            pltpu.VMEM((35, 152, 128), f32),
            pltpu.SemaphoreType.DMA((4, 3)),
            pltpu.SemaphoreType.DMA((7,)),
        ],
        compiler_params=pltpu.CompilerParams(vmem_limit_bytes=VMEM_LIMIT),
    )(*[
        pltpu.with_memory_space_constraint(array, pltpu.HBM)
        for array in (forward_blocks, backward_blocks, inverse_blocks, source, coupling_field)
    ])
    slots, inverse_blocks = lax.optimization_barrier((slots, inverse_blocks))
    slots = lax.all_to_all(slots, BOTH, 0, 0, axis_index_groups=ORDER, tiled=True)

    parts = pl.pallas_call(
        inverse_send_kernel,
        out_shape=[shaped(144, 128)] * 16,
        in_specs=[pl.BlockSpec(memory_space=pltpu.HBM)],
        out_specs=[pl.BlockSpec(memory_space=pltpu.HBM)] * 16,
        scratch_shapes=[
            blocks, pltpu.VMEM((35, 72, 128), f32), pltpu.SemaphoreType.DMA((3,)), pltpu.SemaphoreType.DMA((32,))
        ],
        compiler_params=pltpu.CompilerParams(vmem_limit_bytes=VMEM_LIMIT),
    )(pltpu.with_memory_space_constraint(inverse_blocks, pltpu.HBM))
    parts = [parts[0]] + [lax.ppermute(parts[d], BOTH, [(e, e ^ d) for e in range(32)]) for d in range(1, 16)]
    inverse = [
        call(inverse_get_kernel, pltpu.VMEM((2, 288, 128), f32))(*parts[4 * n : 4 * n + 4]) for n in range(4)
    ]

    own, other, forward, backward, first, middle, coupling_lines = call(
        first_kernel, (pairs, pairs, held, held, tiles, tiles, tiles), [(256, 128), (6, 8, 128), (6, 8, 128)]
    )(slots)

    def with_partner(vector):
        return lax.ppermute(vector, BOTH, [(e, e ^ 16) for e in range(32)])

    other = with_partner(other)
    own = call(functools.partial(half_inverse_kernel, 0), pairs)(own, *inverse)
    other = call(functools.partial(half_inverse_kernel, 1), pairs)(other, *inverse)
    other = with_partner(other)
    slots = call(second_kernel, shaped(128, 128), [(6, 8, 128)] * 3 + [(128, 128)])(
        own, other, forward, backward, first, middle, coupling_lines
    )
    slots = exchange(slots, 4)
    correction, remaining = call(last_kernel, (shaped(48, 128), shaped(48, 128)))(slots)
    return correction.reshape(rhs.shape), remaining.reshape(rhs.shape)


def from_behind(value, axis, steps):
    count = lax.axis_size(axis)
    initial, last = (max(0, -steps), min(count, count - steps))
    return lax.ppermute(value, axis, [(source, source + steps) for source in range(initial, last)])


def from_root(shard, axis, root):
    mine = lax.axis_index(axis) == root
    return lax.psum(jnp.where(mine, shard, jnp.zeros_like(shard)), axis)


def extended(block, sides, width):
    for axis, dim in sides:
        count = lax.axis_size(axis)
        forward = [(i, i + 1) for i in range(count - 1)]
        backward = [(target, source) for source, target in forward]
        low = lax.ppermute(
            lax.slice_in_dim(block, block.shape[dim] - width, None, axis=dim), axis, forward
        )
        high = lax.ppermute(lax.slice_in_dim(block, 0, width, axis=dim), axis, backward)
        block = jnp.concatenate([low, block, high], axis=dim)
    return block


def cell_stride(one_block, carried, const_term):
    return const_term - jnp.einsum(
        "abl,al->bl", one_block.astype(jnp.float32), carried, precision=highest
    )


def compose_cells(blocks, sequence):
    running = None
    for position in sequence:
        one_block = blocks[position].astype(jnp.float32)
        running = -jnp.swapaxes(one_block, 0, 1)
    return running


def doubling_maps(local_map, reverse):
    size = lax.axis_size("azim")
    index = lax.axis_index("azim")
    levels = []
    current = local_map
    distance = 1
    while distance < size:
        if reverse:
            moved = from_behind(current, "azim", -distance)
            exists = index + distance < size
        else:
            moved = from_behind(current, "azim", distance)
            exists = index >= distance
        levels.append((current, distance))
        current = jnp.where(
            exists, jnp.einsum("bcl,cal->bal", current, moved, precision=highest), current
        )
        distance = distance * 2
    return (levels, current)


def doubling_entries(map_levels, local_offset, reverse):
    levels, final_map = map_levels
    size = lax.axis_size("azim")
    index = lax.axis_index("azim")
    running = local_offset
    for current, distance in levels:
        if reverse:
            moved = from_behind(running, "azim", -distance)
        else:
            moved = from_behind(running, "azim", distance)
        running = jnp.einsum("bcl,cl->bl", current, moved, precision=highest) + running
    if reverse:
        wrapped = from_root(running, "azim", 0)
    else:
        wrapped = from_root(running, "azim", size - 1)
    leaving = jnp.einsum("bcl,cl->bl", final_map, wrapped, precision=highest) + running
    if reverse:
        shifted = from_behind(leaving, "azim", -1)
        first_device = index == size - 1
    else:
        shifted = from_behind(leaving, "azim", 1)
        first_device = index == 0
    return jnp.where(first_device, wrapped, shifted)


def sweep(blocks, consts, map_levels, reverse):
    cell_count = blocks.shape[0]
    sequence = list(range(cell_count))
    if reverse:
        sequence = sequence[::-1]
    carried = jnp.zeros(consts.shape[1:], jnp.float32)
    for position in sequence:
        carried = cell_stride(blocks[position], carried, consts[position])
    local_offset = carried
    incoming_maps = doubling_entries(map_levels, local_offset, reverse)
    outputs = [None] * cell_count
    carried = incoming_maps
    for position in sequence:
        carried = cell_stride(blocks[position], carried, consts[position])
        outputs[position] = carried
    return jnp.stack(outputs)


def on_device(rhs, coupling, fwd_coupling, bwd_coupling, block_inverse):
    cell_count, block_width, _, position_total, radial_count = fwd_coupling.shape
    line_count = position_total * radial_count
    forward_blocks = fwd_coupling.reshape(cell_count, block_width, block_width, line_count)
    backward_blocks = bwd_coupling.reshape(cell_count, block_width, block_width, line_count)
    inverse_blocks = block_inverse.reshape(cell_count, block_width, block_width, line_count)
    source = rhs.reshape(cell_count, block_width, line_count)
    coupling_field = coupling.reshape(cell_count, block_width, line_count)
    forward_map = compose_cells(forward_blocks, list(range(cell_count)))
    backward_map = compose_cells(backward_blocks, list(range(cell_count))[::-1])
    forward_levels = None
    backward_levels = None
    forward_levels = doubling_maps(forward_map, False)
    backward_levels = doubling_maps(backward_map, True)

    def precondition(vector):
        consts = jnp.stack(
            [
                jnp.einsum(
                    "abl,al->bl",
                    inverse_blocks[0].astype(jnp.float32),
                    vector[0],
                    precision=highest,
                )
            ]
        )
        forward = sweep(forward_blocks, consts, forward_levels, False)
        return sweep(backward_blocks, forward, backward_levels, True)

    def stations_sum(field):
        grid = field.reshape(cell_count, block_width, position_total, radial_count)
        padded = extended(grid, (("axial", 2),), 1)
        return (padded[:, :, :-2] + padded[:, :, 2:]).reshape(cell_count, block_width, line_count)

    applied_once = precondition(source)
    middle = source - applied_once + coupling_field * stations_sum(applied_once)
    second = precondition(middle)
    correction = applied_once + second
    remaining = middle - second + coupling_field * stations_sum(second)
    return (correction.reshape(rhs.shape), remaining.reshape(rhs.shape))


def solution(mesh):
    cells, stations = mesh.shape["azim"], mesh.shape["axial"]

    def on_each(rhs, coupling, fwd_coupling, bwd_coupling, block_inverse):
        local = fwd_coupling.shape
        if (cells, stations) == (8, 4) and local == (1, 48, 48, 1, 128):
            return line_plan(rhs, coupling, fwd_coupling, bwd_coupling, block_inverse)
        return on_device(rhs, coupling, fwd_coupling, bwd_coupling, block_inverse)

    return jax.shard_map(
        on_each,
        mesh=mesh,
        in_specs=(
            P("azim", None, "axial", None),
            P("azim", None, "axial", None),
            P("azim", None, None, "axial", None),
            P("azim", None, None, "axial", None),
            P("azim", None, None, "axial", None),
        ),
        out_specs=(P("azim", None, "axial", None), P("azim", None, "axial", None)),
        check_vma=False,
    )
```

```python
import functools

import jax
import jax.numpy as jnp
from jax import lax
from jax.experimental import pallas as pl
from jax.experimental.pallas import tpu as pltpu
from jax.sharding import PartitionSpec as P

highest = lax.Precision.HIGHEST
f32 = jnp.float32
BOTH = ("azim", "axial")


def chunk_of(cell, station):
    return 16 * (station % 2) + 8 * (station // 2) + 4 * (cell % 2) + cell // 2


ORDER = [[e for chunk in range(32) for e in range(32) if chunk_of(e // 4, e % 4) == chunk]]
VMEM_LIMIT = 16 * 1024 * 1024


def lane_index():
    return lax.broadcasted_iota(jnp.int32, (8, 128), 1)


def row_index():
    return lax.broadcasted_iota(jnp.int32, (8, 128), 0)


def turn_lanes(tile, steps):
    steps = steps % 128
    return pltpu.roll(tile, steps, 1) if steps else tile


def turn_rows(tile, steps):
    steps = steps % 8
    return pltpu.roll(tile, steps, 0) if steps else tile


def line_lanes(other_half=0):
    return lane_index() + 16 - 4 * ((lax.axis_index("azim") // 2) ^ (2 * other_half))


def own_chunk():
    return chunk_of(lax.axis_index("azim"), lax.axis_index("axial"))


def to_line(tile):
    return pltpu.roll(tile, 4 * own_chunk(), 1)


def from_line(tile):
    return pltpu.roll(tile, (128 - 4 * own_chunk()) % 128, 1)


def swap_quads(tiles, lanes=None):
    lanes = lane_index() if lanes is None else lanes
    tiles = list(tiles)
    for bit, width in ((1, 4), (2, 8)):
        low = (lanes // width) % 2 == 0
        for first in range(4):
            if first & bit:
                continue
            one, two = tiles[first], tiles[first | bit]
            tiles[first] = jnp.where(low, one, turn_lanes(two, width))
            tiles[first | bit] = jnp.where(low, turn_lanes(one, -width), two)
    return tiles


def swap_rows(tile):
    lanes, rows = lane_index() // 16, row_index()
    for bit in (1, 2, 4):
        row_bit, lane_bit = (rows // bit) % 2, (lanes // bit) % 2
        up = turn_rows(turn_lanes(tile, 16 * bit), -bit)
        down = turn_rows(turn_lanes(tile, -16 * bit), bit)
        tile = jnp.where(row_bit == lane_bit, tile, jnp.where(row_bit == 0, up, down))
    return tile


def put_slots(out_ref, tiles, rows, base):
    zero = jnp.zeros((8, 128), f32)
    for half in range(2):
        group = [tiles[4 * half + x] if 4 * half + x < 6 else zero for x in range(4)]
        for quad, tile in enumerate(swap_quads(group)):
            out_ref[pl.ds(rows * quad + base + half, 8, stride=4 * rows), :] = tile


def get_slots(in_ref, rows, base):
    tiles = []
    for half in range(2):
        group = [in_ref[pl.ds(rows * quad + base + half, 8, stride=4 * rows), :] for quad in range(4)]
        tiles += swap_quads(group)
    return tiles[:6]


def put_cell_vector(out_ref, vector_ref, rows, base):
    put_slots(out_ref, [swap_rows(vector_ref[8 * t : 8 * t + 8, :]) for t in range(6)], rows, base)


def inverse_matvec(inverse_ref, vector_ref, out_ref):
    totals = None
    for a in range(48):
        term = inverse_ref[a].astype(f32) * vector_ref[a : a + 1, :]
        totals = term if totals is None else totals + term
    out_ref[...] = totals


COMBINATIONS = [(ah, pair) for ah in range(6) for pair in range(3)]
GROUPS_OF_THIRD = ((0, 1), (2, 3, 4, 5), (6, 7, 8))


def group_tiles(group):
    if group == 8:
        return [COMBINATIONS[16 + x // 2] + (x % 2,) for x in range(4)]
    return [COMBINATIONS[4 * (group // 2) + x] + (group % 2,) for x in range(4)]


TILE_AT = {
    (ah, 2 * pair + half): 4 * group + x
    for group in range(9)
    for x, (ah, pair, half) in enumerate(group_tiles(group))
}


def pack_blocks(block_ref, out_ref, base, third):
    station = lax.axis_index("axial")
    quads = lane_index() // 4
    keeps = [(bit, (quads & bit) == 0) for bit in (1, 2, 4, 8, 16)]
    turned = {}
    for group in GROUPS_OF_THIRD[third]:
        items = []
        for i in range(32):
            p = i // 4
            ah, pair, half = group_tiles(group)[i % 4]
            steps = (4 * i + 4 * station) % 128
            if (ah, pair, i) not in turned:
                tile = block_ref[8 * ah + p, 16 * pair : 16 * pair + 16, :]
                turned[ah, pair, i] = pltpu.roll(tile, steps, 1).astype(f32)
            items.append(turn_rows(turned[ah, pair, i][8 * half : 8 * half + 8], -p))
        for bit, keep in keeps:
            items = [jnp.where(keep, items[j], items[(j + bit) % 32]) for j in range(32)]
        for slot in range(35):
            out_ref[slot, base + 8 * group : base + 8 * group + 8, :] = items[-slot % 32]


def fetch_thirds(block_hbm, block_ref, sems):
    copies = []
    for third in range(3):
        there = (slice(16 * third, 16 * third + 16), slice(None), slice(None))
        copies.append(pltpu.make_async_copy(block_hbm.at[there], block_ref.at[there], sems.at[third]))
    return copies


def join_stations(parts, other_half=0):
    chunk = line_lanes(other_half) // 4
    for bit in (1, 2):
        keep = (chunk & bit) == 0
        parts = [jnp.where(keep, parts[j], parts[(j + bit) % 4]) for j in range(4)]
    return [turn_lanes(parts[-x % 4], -4 * x) for x in range(4)]


def unpack_cell(in_ref, base, out_ref, cell):
    for group in range(9):
        at = base + 8 * group
        parts = [in_ref[chunk_of(cell, k), at : at + 8, :] for k in range(4)]
        for x, tile in enumerate(join_stations(parts)):
            at = 8 * (4 * group + x)
            out_ref[cell, at : at + 8, :] = tile


def line_sweep(blocks_ref, const_ref, out_ref, reverse, beside=None):
    order = list(range(8))
    if reverse:
        order = order[::-1]
    state = None
    for turn in range(2):
        for n, cell in enumerate(order):
            if beside is not None:
                beside(turn, n)
            consts = [jnp.broadcast_to(const_ref[t, cell : cell + 1, :], (8, 128)) for t in range(6)]
            if state is None:
                state = consts
                continue
            state = line_step(blocks_ref, cell, state, consts)
            if turn == 1:
                for t in range(6):
                    out_ref[t, cell : cell + 1, :] = state[t][0:1]


def stations_sum(tile):
    station = (line_lanes() // 4) % 4
    before = jnp.where(station > 0, turn_lanes(tile, 4), 0.0)
    after = jnp.where(station < 3, turn_lanes(tile, -4), 0.0)
    return before + after


def first_send_kernel(
    forward_hbm, backward_hbm, inverse_hbm, rhs_hbm, coupling_hbm, out_hbm,
    f_ref, b_ref, i_ref, rhs_ref, coupling_ref, c_ref, vectors_ref, packed_ref, sems, out_sems,
):
    forward = fetch_thirds(forward_hbm, f_ref, sems.at[0])
    inverse = fetch_thirds(inverse_hbm, i_ref, sems.at[1])
    backward = fetch_thirds(backward_hbm, b_ref, sems.at[2])
    vectors = [
        pltpu.make_async_copy(source, target, sems.at[3, n])
        for n, (source, target) in enumerate(((rhs_hbm, rhs_ref), (coupling_hbm, coupling_ref)))
    ]
    for copy in forward + vectors + inverse:
        copy.start()
    leaving = []

    def leave(row, rows, first):
        source = packed_ref.at[pl.ds(first, 32), pl.ds(row, rows), :]
        target = out_hbm.at[:, pl.ds(row, rows), :]
        leaving.append(pltpu.make_async_copy(source, target, out_sems.at[len(leaving)]))
        leaving[-1].start()

    station = lax.axis_index("axial")

    for third in range(3):
        forward[third].wait()
        if third == 0:
            for copy in backward:
                copy.start()
        pack_blocks(f_ref, packed_ref, 0, third)
        leave((0, 16, 48)[third], (16, 32, 24)[third], station)
    for copy in vectors + inverse:
        copy.wait()
    for third in range(3):
        backward[third].wait()
        if third == 0:
            inverse_matvec(i_ref, rhs_ref, c_ref)
            for n, vector_ref in enumerate((c_ref, rhs_ref, coupling_ref)):
                put_cell_vector(vectors_ref, vector_ref, 8, 2 * n)
            for e in range(32):
                packed_ref[e, 144:152, :] = vectors_ref[8 * e : 8 * e + 8, :]
        pack_blocks(b_ref, packed_ref, 72, third)
        if third == 0:
            leave(144, 8, 0)
        leave((72, 88, 120)[third], (16, 32, 24)[third], station)
    for copy in leaving:
        copy.wait()


def first_kernel(slots_ref, *refs):
    own_ref, other_ref, forward_ref, backward_ref, first_ref, middle_ref, coupling_ref, packed_ref, c_ref, y_ref = refs
    for e in range(32):
        packed_ref[8 * e : 8 * e + 8, :] = slots_ref[chunk_of(e // 4, e % 4), 144:152, :]
    for t, tile in enumerate(get_slots(packed_ref, 8, 0)):
        c_ref[t] = to_line(tile)

    def unpack(turn, n):
        if turn == 0:
            unpack_cell(slots_ref, 0, forward_ref, n)
        else:
            unpack_cell(slots_ref, 72, backward_ref, n)

    line_sweep(forward_ref, c_ref, y_ref, False, unpack)
    line_sweep(backward_ref, y_ref, first_ref, True)
    rhs = [to_line(tile) for tile in get_slots(packed_ref, 8, 2)]
    coupling = [to_line(tile) for tile in get_slots(packed_ref, 8, 4)]
    half, _ = half_position()
    low = row_index() < 4
    own, other = [], []
    for t in range(6):
        first = first_ref[t]
        middle = rhs[t] - first + coupling[t] * stations_sum(first)
        turned = turn_rows(middle, 4)
        other.append(jnp.where(half == 0, turned, middle))
        own.append(jnp.where(half == 0, middle, turned))
        middle_ref[t] = middle
        coupling_ref[t] = coupling[t]
    for u in range(3):
        other_ref[u] = jnp.where(low, other[2 * u], turn_rows(other[2 * u + 1], 4))
        own_ref[u] = jnp.where(low, own[2 * u], turn_rows(own[2 * u + 1], 4))


def half_position():
    cell = lax.axis_index("azim")
    return cell // 4, (cell % 4) * 4 + lax.axis_index("axial")


def inverse_send_kernel(inverse_hbm, *refs):
    outs, (i_ref, packed_ref, fetch_sems, sems) = refs[:16], refs[16:]
    fetches = fetch_thirds(inverse_hbm, i_ref, fetch_sems)
    for copy in fetches:
        copy.start()
    for third, copy in enumerate(fetches):
        copy.wait()
        pack_blocks(i_ref, packed_ref, 0, third)
    half, place = half_position()
    station = place % 4
    copies = []
    for d in range(16):
        target = place ^ d
        for n in range(2):
            cell = 4 * (half if n == 0 else 1 - half) + target // 4
            source = chunk_of(cell, target % 4)
            copies.append(
                pltpu.make_async_copy(packed_ref.at[source + station], outs[d].at[pl.ds(72 * n, 72), :], sems.at[2 * d + n])
            )
            copies[-1].start()
    for copy in copies:
        copy.wait()


def inverse_get_kernel(*refs):
    ins, out_ref = refs[:4], refs[4]
    station = lax.axis_index("axial")
    for lines in range(2):
        for group in range(9):
            at = 72 * lines + 8 * group
            parts = [part[at : at + 8, :] for part in ins]
            for bit in (1, 2):
                parts = [jnp.where((station & bit) == 0, parts[k], parts[k ^ bit]) for k in range(4)]
            for x, tile in enumerate(join_stations(parts, lines)):
                at = 8 * (4 * group + x)
                out_ref[lines, at : at + 8, :] = tile


def line_step(blocks_ref, cell, state, consts):
    following = []
    for bh in range(6):
        terms = []
        for ah in range(6):
            at = 8 * TILE_AT[ah, bh]
            terms.append(blocks_ref[cell, at : at + 8, :] * state[ah])
        total = (terms[0] + terms[1]) + (terms[2] + terms[3]) + (terms[4] + terms[5])
        total = pltpu.roll(total, 0, 1, stride=16, stride_axis=0)
        for span in (4, 2):
            total = total + turn_rows(total, span)
        following.append((consts[bh] - total) - turn_rows(total, 1))
    return following


def half_inverse_kernel(lines, vector_ref, *refs):
    blocks, out_ref = refs[:4], refs[4]
    _, place = half_position()
    cell = place // 4
    rows = row_index()
    zero = jnp.zeros((8, 128), f32)
    totals = [zero] * 3
    for n in range(4):
        state = [
            jnp.broadcast_to(vector_ref[t // 2, pl.ds(4 * (t % 2) + (cell ^ n), 1), :], (8, 128)) for t in range(6)
        ]
        for t, product in enumerate(line_step(blocks[n], lines, state, [zero] * 6)):
            totals[t // 2] = jnp.where(rows == 4 * (t % 2) + (cell ^ n), product, totals[t // 2])
    for u in range(3):
        out_ref[u] = -totals[u]


def second_kernel(
    own_ref, other_ref, forward_ref, backward_ref, first_ref, middle_ref, coupling_ref, out_ref, c_ref, y_ref, second_ref,
    slots_ref,
):
    half, _ = half_position()
    low = row_index() < 4
    for t in range(6):
        own, other = own_ref[t // 2], other_ref[t // 2]
        if t % 2:
            own = turn_rows(own, 4)
        else:
            other = turn_rows(other, 4)
        tile = jnp.where(low, own, other)
        c_ref[t] = jnp.where(half == 0, tile, turn_rows(tile, 4))
    line_sweep(forward_ref, c_ref, y_ref, False)
    line_sweep(backward_ref, y_ref, second_ref, True)
    correction, remaining = [], []
    for t in range(6):
        second = second_ref[t]
        correction.append(from_line(first_ref[t] + second))
        remaining.append(from_line(middle_ref[t] - second + coupling_ref[t] * stations_sum(second)))
    put_slots(slots_ref, correction, 4, 0)
    put_slots(slots_ref, remaining, 4, 2)
    for e in range(32):
        at = 4 * chunk_of(e // 4, e % 4)
        out_ref[at : at + 4, :] = slots_ref[4 * e : 4 * e + 4, :]


def last_kernel(slots_ref, correction_ref, remaining_ref):
    for out_ref, base in ((correction_ref, 0), (remaining_ref, 2)):
        for t, tile in enumerate(get_slots(slots_ref, 4, base)):
            out_ref[8 * t : 8 * t + 8, :] = swap_rows(tile)


def shaped(*sizes):
    return jax.ShapeDtypeStruct(sizes, f32)


def call(kernel, outs, scratch=()):
    return pl.pallas_call(
        kernel,
        out_shape=outs,
        scratch_shapes=[pltpu.VMEM(sizes, f32) for sizes in scratch],
        compiler_params=pltpu.CompilerParams(vmem_limit_bytes=VMEM_LIMIT),
    )


def exchange(slots, rows):
    moved = lax.all_to_all(slots.reshape(32, rows, 128), BOTH, 0, 0, axis_index_groups=ORDER, tiled=True)
    return moved.reshape(32 * rows, 128)


def line_plan(rhs, coupling, fwd_coupling, bwd_coupling, block_inverse):
    source, coupling_field = rhs.reshape(48, 128), coupling.reshape(48, 128)
    forward_blocks = fwd_coupling.reshape(48, 48, 128)
    backward_blocks = bwd_coupling.reshape(48, 48, 128)
    inverse_blocks = block_inverse.reshape(48, 48, 128)
    tiles, pairs, held = shaped(6, 8, 128), shaped(3, 8, 128), shaped(8, 288, 128)
    blocks = pltpu.VMEM((48, 48, 128), jnp.bfloat16)
    vector = pltpu.VMEM((48, 128), f32)

    slots = pl.pallas_call(
        first_send_kernel,
        out_shape=pltpu.HBM((32, 152, 128), f32),
        in_specs=[pl.BlockSpec(memory_space=pltpu.HBM)] * 5,
        out_specs=pl.BlockSpec(memory_space=pltpu.HBM),
        scratch_shapes=[blocks, blocks, blocks, vector, vector, vector]
        + [
            pltpu.VMEM((256, 128), f32),
            pltpu.VMEM((35, 152, 128), f32),
            pltpu.SemaphoreType.DMA((4, 3)),
            pltpu.SemaphoreType.DMA((7,)),
        ],
        compiler_params=pltpu.CompilerParams(vmem_limit_bytes=VMEM_LIMIT),
    )(*[
        pltpu.with_memory_space_constraint(array, pltpu.HBM)
        for array in (forward_blocks, backward_blocks, inverse_blocks, source, coupling_field)
    ])
    slots, inverse_blocks = lax.optimization_barrier((slots, inverse_blocks))
    slots = lax.all_to_all(slots, BOTH, 0, 0, axis_index_groups=ORDER, tiled=True)

    parts = pl.pallas_call(
        inverse_send_kernel,
        out_shape=[shaped(144, 128)] * 16,
        in_specs=[pl.BlockSpec(memory_space=pltpu.HBM)],
        out_specs=[pl.BlockSpec(memory_space=pltpu.HBM)] * 16,
        scratch_shapes=[
            blocks, pltpu.VMEM((35, 72, 128), f32), pltpu.SemaphoreType.DMA((3,)), pltpu.SemaphoreType.DMA((32,))
        ],
        compiler_params=pltpu.CompilerParams(vmem_limit_bytes=VMEM_LIMIT),
    )(pltpu.with_memory_space_constraint(inverse_blocks, pltpu.HBM))
    parts = [parts[0]] + [lax.ppermute(parts[d], BOTH, [(e, e ^ d) for e in range(32)]) for d in range(1, 16)]
    inverse = [
        call(inverse_get_kernel, pltpu.VMEM((2, 288, 128), f32))(*parts[4 * n : 4 * n + 4]) for n in range(4)
    ]

    own, other, forward, backward, first, middle, coupling_lines = call(
        first_kernel, (pairs, pairs, held, held, tiles, tiles, tiles), [(256, 128), (6, 8, 128), (6, 8, 128)]
    )(slots)

    def with_partner(vector):
        return lax.ppermute(vector, BOTH, [(e, e ^ 16) for e in range(32)])

    other = with_partner(other)
    own = call(functools.partial(half_inverse_kernel, 0), pairs)(own, *inverse)
    other = call(functools.partial(half_inverse_kernel, 1), pairs)(other, *inverse)
    other = with_partner(other)
    slots = call(second_kernel, shaped(128, 128), [(6, 8, 128)] * 3 + [(128, 128)])(
        own, other, forward, backward, first, middle, coupling_lines
    )
    slots = exchange(slots, 4)
    correction, remaining = call(last_kernel, (shaped(48, 128), shaped(48, 128)))(slots)
    return correction.reshape(rhs.shape), remaining.reshape(rhs.shape)


def from_behind(value, axis, steps):
    count = lax.axis_size(axis)
    initial, last = (max(0, -steps), min(count, count - steps))
    return lax.ppermute(value, axis, [(source, source + steps) for source in range(initial, last)])


def from_root(shard, axis, root):
    mine = lax.axis_index(axis) == root
    return lax.psum(jnp.where(mine, shard, jnp.zeros_like(shard)), axis)


def extended(block, sides, width):
    for axis, dim in sides:
        count = lax.axis_size(axis)
        forward = [(i, i + 1) for i in range(count - 1)]
        backward = [(target, source) for source, target in forward]
        low = lax.ppermute(
            lax.slice_in_dim(block, block.shape[dim] - width, None, axis=dim), axis, forward
        )
        high = lax.ppermute(lax.slice_in_dim(block, 0, width, axis=dim), axis, backward)
        block = jnp.concatenate([low, block, high], axis=dim)
    return block


def cell_stride(one_block, carried, const_term):
    return const_term - jnp.einsum(
        "abl,al->bl", one_block.astype(jnp.float32), carried, precision=highest
    )


def compose_cells(blocks, sequence):
    running = None
    for position in sequence:
        one_block = blocks[position].astype(jnp.float32)
        running = -jnp.swapaxes(one_block, 0, 1)
    return running


def doubling_maps(local_map, reverse):
    size = lax.axis_size("azim")
    index = lax.axis_index("azim")
    levels = []
    current = local_map
    distance = 1
    while distance < size:
        if reverse:
            moved = from_behind(current, "azim", -distance)
            exists = index + distance < size
        else:
            moved = from_behind(current, "azim", distance)
            exists = index >= distance
        levels.append((current, distance))
        current = jnp.where(
            exists, jnp.einsum("bcl,cal->bal", current, moved, precision=highest), current
        )
        distance = distance * 2
    return (levels, current)


def doubling_entries(map_levels, local_offset, reverse):
    levels, final_map = map_levels
    size = lax.axis_size("azim")
    index = lax.axis_index("azim")
    running = local_offset
    for current, distance in levels:
        if reverse:
            moved = from_behind(running, "azim", -distance)
        else:
            moved = from_behind(running, "azim", distance)
        running = jnp.einsum("bcl,cl->bl", current, moved, precision=highest) + running
    if reverse:
        wrapped = from_root(running, "azim", 0)
    else:
        wrapped = from_root(running, "azim", size - 1)
    leaving = jnp.einsum("bcl,cl->bl", final_map, wrapped, precision=highest) + running
    if reverse:
        shifted = from_behind(leaving, "azim", -1)
        first_device = index == size - 1
    else:
        shifted = from_behind(leaving, "azim", 1)
        first_device = index == 0
    return jnp.where(first_device, wrapped, shifted)


def sweep(blocks, consts, map_levels, reverse):
    cell_count = blocks.shape[0]
    sequence = list(range(cell_count))
    if reverse:
        sequence = sequence[::-1]
    carried = jnp.zeros(consts.shape[1:], jnp.float32)
    for position in sequence:
        carried = cell_stride(blocks[position], carried, consts[position])
    local_offset = carried
    incoming_maps = doubling_entries(map_levels, local_offset, reverse)
    outputs = [None] * cell_count
    carried = incoming_maps
    for position in sequence:
        carried = cell_stride(blocks[position], carried, consts[position])
        outputs[position] = carried
    return jnp.stack(outputs)


def on_device(rhs, coupling, fwd_coupling, bwd_coupling, block_inverse):
    cell_count, block_width, _, position_total, radial_count = fwd_coupling.shape
    line_count = position_total * radial_count
    forward_blocks = fwd_coupling.reshape(cell_count, block_width, block_width, line_count)
    backward_blocks = bwd_coupling.reshape(cell_count, block_width, block_width, line_count)
    inverse_blocks = block_inverse.reshape(cell_count, block_width, block_width, line_count)
    source = rhs.reshape(cell_count, block_width, line_count)
    coupling_field = coupling.reshape(cell_count, block_width, line_count)
    forward_map = compose_cells(forward_blocks, list(range(cell_count)))
    backward_map = compose_cells(backward_blocks, list(range(cell_count))[::-1])
    forward_levels = None
    backward_levels = None
    forward_levels = doubling_maps(forward_map, False)
    backward_levels = doubling_maps(backward_map, True)

    def precondition(vector):
        consts = jnp.stack(
            [
                jnp.einsum(
                    "abl,al->bl",
                    inverse_blocks[0].astype(jnp.float32),
                    vector[0],
                    precision=highest,
                )
            ]
        )
        forward = sweep(forward_blocks, consts, forward_levels, False)
        return sweep(backward_blocks, forward, backward_levels, True)

    def stations_sum(field):
        grid = field.reshape(cell_count, block_width, position_total, radial_count)
        padded = extended(grid, (("axial", 2),), 1)
        return (padded[:, :, :-2] + padded[:, :, 2:]).reshape(cell_count, block_width, line_count)

    applied_once = precondition(source)
    middle = source - applied_once + coupling_field * stations_sum(applied_once)
    second = precondition(middle)
    correction = applied_once + second
    remaining = middle - second + coupling_field * stations_sum(second)
    return (correction.reshape(rhs.shape), remaining.reshape(rhs.shape))


def solution(mesh):
    cells, stations = mesh.shape["azim"], mesh.shape["axial"]

    def on_each(rhs, coupling, fwd_coupling, bwd_coupling, block_inverse):
        local = fwd_coupling.shape
        if (cells, stations) == (8, 4) and local == (1, 48, 48, 1, 128):
            return line_plan(rhs, coupling, fwd_coupling, bwd_coupling, block_inverse)
        return on_device(rhs, coupling, fwd_coupling, bwd_coupling, block_inverse)

    return jax.shard_map(
        on_each,
        mesh=mesh,
        in_specs=(
            P("azim", None, "axial", None),
            P("azim", None, "axial", None),
            P("azim", None, None, "axial", None),
            P("azim", None, None, "axial", None),
            P("azim", None, None, "axial", None),
        ),
        out_specs=(P("azim", None, "axial", None), P("azim", None, "axial", None)),
        check_vma=False,
    )
```

```python
import functools

import jax
import jax.numpy as jnp
from jax import lax
from jax.experimental import pallas as pl
from jax.experimental.pallas import tpu as pltpu
from jax.sharding import PartitionSpec as P

highest = lax.Precision.HIGHEST
f32 = jnp.float32
BOTH = ("azim", "axial")


def chunk_of(cell, station):
    return 16 * (station // 2) + 8 * (cell % 2) + 4 * (station % 2) + cell // 2


ORDER = [[e for chunk in range(32) for e in range(32) if chunk_of(e // 4, e % 4) == chunk]]
VMEM_LIMIT = 16 * 1024 * 1024


def lane_index():
    return lax.broadcasted_iota(jnp.int32, (8, 128), 1)


def row_index():
    return lax.broadcasted_iota(jnp.int32, (8, 128), 0)


def turn_lanes(tile, steps):
    steps = steps % 128
    return pltpu.roll(tile, steps, 1) if steps else tile


def turn_rows(tile, steps):
    steps = steps % 8
    return pltpu.roll(tile, steps, 0) if steps else tile


def line_lanes(other_half=0):
    return lane_index() + 16 - 4 * ((lax.axis_index("azim") // 2) ^ (2 * other_half))


def own_chunk():
    return chunk_of(lax.axis_index("azim"), lax.axis_index("axial"))


def to_line(tile):
    return pltpu.roll(tile, 4 * own_chunk(), 1)


def from_line(tile):
    return pltpu.roll(tile, (128 - 4 * own_chunk()) % 128, 1)


def swap_quads(tiles, lanes=None):
    lanes = lane_index() if lanes is None else lanes
    tiles = list(tiles)
    for bit, width in ((1, 4), (2, 8)):
        low = (lanes // width) % 2 == 0
        for first in range(4):
            if first & bit:
                continue
            one, two = tiles[first], tiles[first | bit]
            tiles[first] = jnp.where(low, one, turn_lanes(two, width))
            tiles[first | bit] = jnp.where(low, turn_lanes(one, -width), two)
    return tiles


def swap_rows(tile):
    lanes, rows = lane_index() // 16, row_index()
    for bit in (1, 2, 4):
        row_bit, lane_bit = (rows // bit) % 2, (lanes // bit) % 2
        up = turn_rows(turn_lanes(tile, 16 * bit), -bit)
        down = turn_rows(turn_lanes(tile, -16 * bit), bit)
        tile = jnp.where(row_bit == lane_bit, tile, jnp.where(row_bit == 0, up, down))
    return tile


def put_slots(out_ref, tiles, rows, base):
    zero = jnp.zeros((8, 128), f32)
    for half in range(2):
        group = [tiles[4 * half + x] if 4 * half + x < 6 else zero for x in range(4)]
        for quad, tile in enumerate(swap_quads(group)):
            out_ref[pl.ds(rows * quad + base + half, 8, stride=4 * rows), :] = tile


def get_slots(in_ref, rows, base):
    tiles = []
    for half in range(2):
        group = [in_ref[pl.ds(rows * quad + base + half, 8, stride=4 * rows), :] for quad in range(4)]
        tiles += swap_quads(group)
    return tiles[:6]


def put_cell_vector(out_ref, vector_ref, rows, base):
    put_slots(out_ref, [swap_rows(vector_ref[8 * t : 8 * t + 8, :]) for t in range(6)], rows, base)


def inverse_matvec(inverse_ref, vector_ref, out_ref):
    totals = None
    for a in range(48):
        term = inverse_ref[a].astype(f32) * vector_ref[a : a + 1, :]
        totals = term if totals is None else totals + term
    out_ref[...] = totals


COMBINATIONS = [(ah, pair) for ah in range(6) for pair in range(3)]
GROUPS_OF_THIRD = ((0, 1), (2, 3, 4, 5), (6, 7, 8))


def group_tiles(group):
    if group == 8:
        return [COMBINATIONS[16 + x // 2] + (x % 2,) for x in range(4)]
    return [COMBINATIONS[4 * (group // 2) + x] + (group % 2,) for x in range(4)]


TILE_AT = {
    (ah, 2 * pair + half): 4 * group + x
    for group in range(9)
    for x, (ah, pair, half) in enumerate(group_tiles(group))
}


def pack_blocks(block_ref, out_ref, base, third):
    station = lax.axis_index("axial")
    quads = lane_index() // 4
    keeps = [(bit, (quads & bit) == 0) for bit in (1, 2, 4, 8, 16)]
    turned = {}
    for group in GROUPS_OF_THIRD[third]:
        items = []
        for i in range(32):
            p = i // 4
            ah, pair, half = group_tiles(group)[i % 4]
            steps = (4 * i + 4 * station) % 128
            if (ah, pair, i) not in turned:
                tile = block_ref[8 * ah + p, 16 * pair : 16 * pair + 16, :]
                turned[ah, pair, i] = pltpu.roll(tile, steps, 1).astype(f32)
            items.append(turn_rows(turned[ah, pair, i][8 * half : 8 * half + 8], -p))
        for bit, keep in keeps:
            items = [jnp.where(keep, items[j], items[(j + bit) % 32]) for j in range(32)]
        for slot in range(35):
            out_ref[slot, base + 8 * group : base + 8 * group + 8, :] = items[-slot % 32]


def fetch_thirds(block_hbm, block_ref, sems):
    copies = []
    for third in range(3):
        there = (slice(16 * third, 16 * third + 16), slice(None), slice(None))
        copies.append(pltpu.make_async_copy(block_hbm.at[there], block_ref.at[there], sems.at[third]))
    return copies


def join_stations(parts, other_half=0):
    chunk = line_lanes(other_half) // 4
    for bit in (1, 2):
        keep = (chunk & bit) == 0
        parts = [jnp.where(keep, parts[j], parts[(j + bit) % 4]) for j in range(4)]
    return [turn_lanes(parts[-x % 4], -4 * x) for x in range(4)]


def unpack_cell(in_ref, base, out_ref, cell):
    for group in range(9):
        at = base + 8 * group
        parts = [in_ref[chunk_of(cell, k), at : at + 8, :] for k in range(4)]
        for x, tile in enumerate(join_stations(parts)):
            at = 8 * (4 * group + x)
            out_ref[cell, at : at + 8, :] = tile


def line_sweep(blocks_ref, const_ref, out_ref, reverse, beside=None):
    order = list(range(8))
    if reverse:
        order = order[::-1]
    state = None
    for turn in range(2):
        for n, cell in enumerate(order):
            if beside is not None:
                beside(turn, n)
            consts = [jnp.broadcast_to(const_ref[t, cell : cell + 1, :], (8, 128)) for t in range(6)]
            if state is None:
                state = consts
                continue
            state = line_step(blocks_ref, cell, state, consts)
            if turn == 1:
                for t in range(6):
                    out_ref[t, cell : cell + 1, :] = state[t][0:1]


def stations_sum(tile):
    station = (line_lanes() // 4) % 4
    before = jnp.where(station > 0, turn_lanes(tile, 4), 0.0)
    after = jnp.where(station < 3, turn_lanes(tile, -4), 0.0)
    return before + after


def first_send_kernel(
    forward_hbm, backward_hbm, inverse_hbm, rhs_hbm, coupling_hbm, out_hbm,
    f_ref, b_ref, i_ref, rhs_ref, coupling_ref, c_ref, vectors_ref, packed_ref, sems, out_sems,
):
    forward = fetch_thirds(forward_hbm, f_ref, sems.at[0])
    inverse = fetch_thirds(inverse_hbm, i_ref, sems.at[1])
    backward = fetch_thirds(backward_hbm, b_ref, sems.at[2])
    vectors = [
        pltpu.make_async_copy(source, target, sems.at[3, n])
        for n, (source, target) in enumerate(((rhs_hbm, rhs_ref), (coupling_hbm, coupling_ref)))
    ]
    for copy in forward + vectors + inverse:
        copy.start()
    leaving = []

    def leave(row, rows, first):
        source = packed_ref.at[pl.ds(first, 32), pl.ds(row, rows), :]
        target = out_hbm.at[:, pl.ds(row, rows), :]
        leaving.append(pltpu.make_async_copy(source, target, out_sems.at[len(leaving)]))
        leaving[-1].start()

    station = lax.axis_index("axial")

    for third in range(3):
        forward[third].wait()
        if third == 0:
            for copy in backward:
                copy.start()
        pack_blocks(f_ref, packed_ref, 0, third)
        leave((0, 16, 48)[third], (16, 32, 24)[third], station)
    for copy in vectors + inverse:
        copy.wait()
    for third in range(3):
        backward[third].wait()
        if third == 0:
            inverse_matvec(i_ref, rhs_ref, c_ref)
            for n, vector_ref in enumerate((c_ref, rhs_ref, coupling_ref)):
                put_cell_vector(vectors_ref, vector_ref, 8, 2 * n)
            for e in range(32):
                packed_ref[e, 144:152, :] = vectors_ref[8 * e : 8 * e + 8, :]
        pack_blocks(b_ref, packed_ref, 72, third)
        if third == 0:
            leave(144, 8, 0)
        leave((72, 88, 120)[third], (16, 32, 24)[third], station)
    for copy in leaving:
        copy.wait()


def first_kernel(slots_ref, *refs):
    own_ref, other_ref, forward_ref, backward_ref, first_ref, middle_ref, coupling_ref, packed_ref, c_ref, y_ref = refs
    for e in range(32):
        packed_ref[8 * e : 8 * e + 8, :] = slots_ref[chunk_of(e // 4, e % 4), 144:152, :]
    for t, tile in enumerate(get_slots(packed_ref, 8, 0)):
        c_ref[t] = to_line(tile)

    def unpack(turn, n):
        if turn == 0:
            unpack_cell(slots_ref, 0, forward_ref, n)
        else:
            unpack_cell(slots_ref, 72, backward_ref, n)

    line_sweep(forward_ref, c_ref, y_ref, False, unpack)
    line_sweep(backward_ref, y_ref, first_ref, True)
    rhs = [to_line(tile) for tile in get_slots(packed_ref, 8, 2)]
    coupling = [to_line(tile) for tile in get_slots(packed_ref, 8, 4)]
    half, _ = half_position()
    low = row_index() < 4
    own, other = [], []
    for t in range(6):
        first = first_ref[t]
        middle = rhs[t] - first + coupling[t] * stations_sum(first)
        turned = turn_rows(middle, 4)
        other.append(jnp.where(half == 0, turned, middle))
        own.append(jnp.where(half == 0, middle, turned))
        middle_ref[t] = middle
        coupling_ref[t] = coupling[t]
    for u in range(3):
        other_ref[u] = jnp.where(low, other[2 * u], turn_rows(other[2 * u + 1], 4))
        own_ref[u] = jnp.where(low, own[2 * u], turn_rows(own[2 * u + 1], 4))


def half_position():
    cell = lax.axis_index("azim")
    return cell // 4, (cell % 4) * 4 + lax.axis_index("axial")


def inverse_send_kernel(inverse_hbm, *refs):
    outs, (i_ref, packed_ref, fetch_sems, sems) = refs[:16], refs[16:]
    fetches = fetch_thirds(inverse_hbm, i_ref, fetch_sems)
    for copy in fetches:
        copy.start()
    for third, copy in enumerate(fetches):
        copy.wait()
        pack_blocks(i_ref, packed_ref, 0, third)
    half, place = half_position()
    station = place % 4
    copies = []
    for d in range(16):
        target = place ^ d
        for n in range(2):
            cell = 4 * (half if n == 0 else 1 - half) + target // 4
            source = chunk_of(cell, target % 4)
            copies.append(
                pltpu.make_async_copy(packed_ref.at[source + station], outs[d].at[pl.ds(72 * n, 72), :], sems.at[2 * d + n])
            )
            copies[-1].start()
    for copy in copies:
        copy.wait()


def inverse_get_kernel(*refs):
    ins, out_ref = refs[:4], refs[4]
    station = lax.axis_index("axial")
    for lines in range(2):
        for group in range(9):
            at = 72 * lines + 8 * group
            parts = [part[at : at + 8, :] for part in ins]
            for bit in (1, 2):
                parts = [jnp.where((station & bit) == 0, parts[k], parts[k ^ bit]) for k in range(4)]
            for x, tile in enumerate(join_stations(parts, lines)):
                at = 8 * (4 * group + x)
                out_ref[lines, at : at + 8, :] = tile


def line_step(blocks_ref, cell, state, consts):
    following = []
    for bh in range(6):
        terms = []
        for ah in range(6):
            at = 8 * TILE_AT[ah, bh]
            terms.append(blocks_ref[cell, at : at + 8, :] * state[ah])
        total = (terms[0] + terms[1]) + (terms[2] + terms[3]) + (terms[4] + terms[5])
        total = pltpu.roll(total, 0, 1, stride=16, stride_axis=0)
        for span in (4, 2):
            total = total + turn_rows(total, span)
        following.append((consts[bh] - total) - turn_rows(total, 1))
    return following


def half_inverse_kernel(lines, vector_ref, *refs):
    blocks, out_ref = refs[:4], refs[4]
    _, place = half_position()
    cell = place // 4
    rows = row_index()
    zero = jnp.zeros((8, 128), f32)
    totals = [zero] * 3
    for n in range(4):
        state = [
            jnp.broadcast_to(vector_ref[t // 2, pl.ds(4 * (t % 2) + (cell ^ n), 1), :], (8, 128)) for t in range(6)
        ]
        for t, product in enumerate(line_step(blocks[n], lines, state, [zero] * 6)):
            totals[t // 2] = jnp.where(rows == 4 * (t % 2) + (cell ^ n), product, totals[t // 2])
    for u in range(3):
        out_ref[u] = -totals[u]


def second_kernel(
    own_ref, other_ref, forward_ref, backward_ref, first_ref, middle_ref, coupling_ref, out_ref, c_ref, y_ref, second_ref,
    slots_ref,
):
    half, _ = half_position()
    low = row_index() < 4
    for t in range(6):
        own, other = own_ref[t // 2], other_ref[t // 2]
        if t % 2:
            own = turn_rows(own, 4)
        else:
            other = turn_rows(other, 4)
        tile = jnp.where(low, own, other)
        c_ref[t] = jnp.where(half == 0, tile, turn_rows(tile, 4))
    line_sweep(forward_ref, c_ref, y_ref, False)
    line_sweep(backward_ref, y_ref, second_ref, True)
    correction, remaining = [], []
    for t in range(6):
        second = second_ref[t]
        correction.append(from_line(first_ref[t] + second))
        remaining.append(from_line(middle_ref[t] - second + coupling_ref[t] * stations_sum(second)))
    put_slots(slots_ref, correction, 4, 0)
    put_slots(slots_ref, remaining, 4, 2)
    for e in range(32):
        at = 4 * chunk_of(e // 4, e % 4)
        out_ref[at : at + 4, :] = slots_ref[4 * e : 4 * e + 4, :]


def last_kernel(slots_ref, correction_ref, remaining_ref):
    for out_ref, base in ((correction_ref, 0), (remaining_ref, 2)):
        for t, tile in enumerate(get_slots(slots_ref, 4, base)):
            out_ref[8 * t : 8 * t + 8, :] = swap_rows(tile)


def shaped(*sizes):
    return jax.ShapeDtypeStruct(sizes, f32)


def call(kernel, outs, scratch=()):
    return pl.pallas_call(
        kernel,
        out_shape=outs,
        scratch_shapes=[pltpu.VMEM(sizes, f32) for sizes in scratch],
        compiler_params=pltpu.CompilerParams(vmem_limit_bytes=VMEM_LIMIT),
    )


def exchange(slots, rows):
    moved = lax.all_to_all(slots.reshape(32, rows, 128), BOTH, 0, 0, axis_index_groups=ORDER, tiled=True)
    return moved.reshape(32 * rows, 128)


def line_plan(rhs, coupling, fwd_coupling, bwd_coupling, block_inverse):
    source, coupling_field = rhs.reshape(48, 128), coupling.reshape(48, 128)
    forward_blocks = fwd_coupling.reshape(48, 48, 128)
    backward_blocks = bwd_coupling.reshape(48, 48, 128)
    inverse_blocks = block_inverse.reshape(48, 48, 128)
    tiles, pairs, held = shaped(6, 8, 128), shaped(3, 8, 128), shaped(8, 288, 128)
    blocks = pltpu.VMEM((48, 48, 128), jnp.bfloat16)
    vector = pltpu.VMEM((48, 128), f32)

    slots = pl.pallas_call(
        first_send_kernel,
        out_shape=pltpu.HBM((32, 152, 128), f32),
        in_specs=[pl.BlockSpec(memory_space=pltpu.HBM)] * 5,
        out_specs=pl.BlockSpec(memory_space=pltpu.HBM),
        scratch_shapes=[blocks, blocks, blocks, vector, vector, vector]
        + [
            pltpu.VMEM((256, 128), f32),
            pltpu.VMEM((35, 152, 128), f32),
            pltpu.SemaphoreType.DMA((4, 3)),
            pltpu.SemaphoreType.DMA((7,)),
        ],
        compiler_params=pltpu.CompilerParams(vmem_limit_bytes=VMEM_LIMIT),
    )(*[
        pltpu.with_memory_space_constraint(array, pltpu.HBM)
        for array in (forward_blocks, backward_blocks, inverse_blocks, source, coupling_field)
    ])
    slots, inverse_blocks = lax.optimization_barrier((slots, inverse_blocks))
    slots = lax.all_to_all(slots, BOTH, 0, 0, axis_index_groups=ORDER, tiled=True)

    parts = pl.pallas_call(
        inverse_send_kernel,
        out_shape=[shaped(144, 128)] * 16,
        in_specs=[pl.BlockSpec(memory_space=pltpu.HBM)],
        out_specs=[pl.BlockSpec(memory_space=pltpu.HBM)] * 16,
        scratch_shapes=[
            blocks, pltpu.VMEM((35, 72, 128), f32), pltpu.SemaphoreType.DMA((3,)), pltpu.SemaphoreType.DMA((32,))
        ],
        compiler_params=pltpu.CompilerParams(vmem_limit_bytes=VMEM_LIMIT),
    )(pltpu.with_memory_space_constraint(inverse_blocks, pltpu.HBM))
    parts = [parts[0]] + [lax.ppermute(parts[d], BOTH, [(e, e ^ d) for e in range(32)]) for d in range(1, 16)]
    inverse = [
        call(inverse_get_kernel, pltpu.VMEM((2, 288, 128), f32))(*parts[4 * n : 4 * n + 4]) for n in range(4)
    ]

    own, other, forward, backward, first, middle, coupling_lines = call(
        first_kernel, (pairs, pairs, held, held, tiles, tiles, tiles), [(256, 128), (6, 8, 128), (6, 8, 128)]
    )(slots)

    def with_partner(vector):
        return lax.ppermute(vector, BOTH, [(e, e ^ 16) for e in range(32)])

    other = with_partner(other)
    own = call(functools.partial(half_inverse_kernel, 0), pairs)(own, *inverse)
    other = call(functools.partial(half_inverse_kernel, 1), pairs)(other, *inverse)
    other = with_partner(other)
    slots = call(second_kernel, shaped(128, 128), [(6, 8, 128)] * 3 + [(128, 128)])(
        own, other, forward, backward, first, middle, coupling_lines
    )
    slots = exchange(slots, 4)
    correction, remaining = call(last_kernel, (shaped(48, 128), shaped(48, 128)))(slots)
    return correction.reshape(rhs.shape), remaining.reshape(rhs.shape)


def from_behind(value, axis, steps):
    count = lax.axis_size(axis)
    initial, last = (max(0, -steps), min(count, count - steps))
    return lax.ppermute(value, axis, [(source, source + steps) for source in range(initial, last)])


def from_root(shard, axis, root):
    mine = lax.axis_index(axis) == root
    return lax.psum(jnp.where(mine, shard, jnp.zeros_like(shard)), axis)


def extended(block, sides, width):
    for axis, dim in sides:
        count = lax.axis_size(axis)
        forward = [(i, i + 1) for i in range(count - 1)]
        backward = [(target, source) for source, target in forward]
        low = lax.ppermute(
            lax.slice_in_dim(block, block.shape[dim] - width, None, axis=dim), axis, forward
        )
        high = lax.ppermute(lax.slice_in_dim(block, 0, width, axis=dim), axis, backward)
        block = jnp.concatenate([low, block, high], axis=dim)
    return block


def cell_stride(one_block, carried, const_term):
    return const_term - jnp.einsum(
        "abl,al->bl", one_block.astype(jnp.float32), carried, precision=highest
    )


def compose_cells(blocks, sequence):
    running = None
    for position in sequence:
        one_block = blocks[position].astype(jnp.float32)
        running = -jnp.swapaxes(one_block, 0, 1)
    return running


def doubling_maps(local_map, reverse):
    size = lax.axis_size("azim")
    index = lax.axis_index("azim")
    levels = []
    current = local_map
    distance = 1
    while distance < size:
        if reverse:
            moved = from_behind(current, "azim", -distance)
            exists = index + distance < size
        else:
            moved = from_behind(current, "azim", distance)
            exists = index >= distance
        levels.append((current, distance))
        current = jnp.where(
            exists, jnp.einsum("bcl,cal->bal", current, moved, precision=highest), current
        )
        distance = distance * 2
    return (levels, current)


def doubling_entries(map_levels, local_offset, reverse):
    levels, final_map = map_levels
    size = lax.axis_size("azim")
    index = lax.axis_index("azim")
    running = local_offset
    for current, distance in levels:
        if reverse:
            moved = from_behind(running, "azim", -distance)
        else:
            moved = from_behind(running, "azim", distance)
        running = jnp.einsum("bcl,cl->bl", current, moved, precision=highest) + running
    if reverse:
        wrapped = from_root(running, "azim", 0)
    else:
        wrapped = from_root(running, "azim", size - 1)
    leaving = jnp.einsum("bcl,cl->bl", final_map, wrapped, precision=highest) + running
    if reverse:
        shifted = from_behind(leaving, "azim", -1)
        first_device = index == size - 1
    else:
        shifted = from_behind(leaving, "azim", 1)
        first_device = index == 0
    return jnp.where(first_device, wrapped, shifted)


def sweep(blocks, consts, map_levels, reverse):
    cell_count = blocks.shape[0]
    sequence = list(range(cell_count))
    if reverse:
        sequence = sequence[::-1]
    carried = jnp.zeros(consts.shape[1:], jnp.float32)
    for position in sequence:
        carried = cell_stride(blocks[position], carried, consts[position])
    local_offset = carried
    incoming_maps = doubling_entries(map_levels, local_offset, reverse)
    outputs = [None] * cell_count
    carried = incoming_maps
    for position in sequence:
        carried = cell_stride(blocks[position], carried, consts[position])
        outputs[position] = carried
    return jnp.stack(outputs)


def on_device(rhs, coupling, fwd_coupling, bwd_coupling, block_inverse):
    cell_count, block_width, _, position_total, radial_count = fwd_coupling.shape
    line_count = position_total * radial_count
    forward_blocks = fwd_coupling.reshape(cell_count, block_width, block_width, line_count)
    backward_blocks = bwd_coupling.reshape(cell_count, block_width, block_width, line_count)
    inverse_blocks = block_inverse.reshape(cell_count, block_width, block_width, line_count)
    source = rhs.reshape(cell_count, block_width, line_count)
    coupling_field = coupling.reshape(cell_count, block_width, line_count)
    forward_map = compose_cells(forward_blocks, list(range(cell_count)))
    backward_map = compose_cells(backward_blocks, list(range(cell_count))[::-1])
    forward_levels = None
    backward_levels = None
    forward_levels = doubling_maps(forward_map, False)
    backward_levels = doubling_maps(backward_map, True)

    def precondition(vector):
        consts = jnp.stack(
            [
                jnp.einsum(
                    "abl,al->bl",
                    inverse_blocks[0].astype(jnp.float32),
                    vector[0],
                    precision=highest,
                )
            ]
        )
        forward = sweep(forward_blocks, consts, forward_levels, False)
        return sweep(backward_blocks, forward, backward_levels, True)

    def stations_sum(field):
        grid = field.reshape(cell_count, block_width, position_total, radial_count)
        padded = extended(grid, (("axial", 2),), 1)
        return (padded[:, :, :-2] + padded[:, :, 2:]).reshape(cell_count, block_width, line_count)

    applied_once = precondition(source)
    middle = source - applied_once + coupling_field * stations_sum(applied_once)
    second = precondition(middle)
    correction = applied_once + second
    remaining = middle - second + coupling_field * stations_sum(second)
    return (correction.reshape(rhs.shape), remaining.reshape(rhs.shape))


def solution(mesh):
    cells, stations = mesh.shape["azim"], mesh.shape["axial"]

    def on_each(rhs, coupling, fwd_coupling, bwd_coupling, block_inverse):
        local = fwd_coupling.shape
        if (cells, stations) == (8, 4) and local == (1, 48, 48, 1, 128):
            return line_plan(rhs, coupling, fwd_coupling, bwd_coupling, block_inverse)
        return on_device(rhs, coupling, fwd_coupling, bwd_coupling, block_inverse)

    return jax.shard_map(
        on_each,
        mesh=mesh,
        in_specs=(
            P("azim", None, "axial", None),
            P("azim", None, "axial", None),
            P("azim", None, None, "axial", None),
            P("azim", None, None, "axial", None),
            P("azim", None, None, "axial", None),
        ),
        out_specs=(P("azim", None, "axial", None), P("azim", None, "axial", None)),
        check_vma=False,
    )
```

```python
import functools

import jax
import jax.numpy as jnp
from jax import lax
from jax.experimental import pallas as pl
from jax.experimental.pallas import tpu as pltpu
from jax.sharding import PartitionSpec as P

highest = lax.Precision.HIGHEST
f32 = jnp.float32
BOTH = ("azim", "axial")


def chunk_of(cell, station):
    return 16 * (cell % 2) + 8 * (station % 2) + 4 * (station // 2) + cell // 2


ORDER = [[e for chunk in range(32) for e in range(32) if chunk_of(e // 4, e % 4) == chunk]]
VMEM_LIMIT = 16 * 1024 * 1024


def lane_index():
    return lax.broadcasted_iota(jnp.int32, (8, 128), 1)


def row_index():
    return lax.broadcasted_iota(jnp.int32, (8, 128), 0)


def turn_lanes(tile, steps):
    steps = steps % 128
    return pltpu.roll(tile, steps, 1) if steps else tile


def turn_rows(tile, steps):
    steps = steps % 8
    return pltpu.roll(tile, steps, 0) if steps else tile


def line_lanes(other_half=0):
    return lane_index() + 16 - 4 * ((lax.axis_index("azim") // 2) ^ (2 * other_half))


def own_chunk():
    return chunk_of(lax.axis_index("azim"), lax.axis_index("axial"))


def to_line(tile):
    return pltpu.roll(tile, 4 * own_chunk(), 1)


def from_line(tile):
    return pltpu.roll(tile, (128 - 4 * own_chunk()) % 128, 1)


def swap_quads(tiles, lanes=None):
    lanes = lane_index() if lanes is None else lanes
    tiles = list(tiles)
    for bit, width in ((1, 4), (2, 8)):
        low = (lanes // width) % 2 == 0
        for first in range(4):
            if first & bit:
                continue
            one, two = tiles[first], tiles[first | bit]
            tiles[first] = jnp.where(low, one, turn_lanes(two, width))
            tiles[first | bit] = jnp.where(low, turn_lanes(one, -width), two)
    return tiles


def swap_rows(tile):
    lanes, rows = lane_index() // 16, row_index()
    for bit in (1, 2, 4):
        row_bit, lane_bit = (rows // bit) % 2, (lanes // bit) % 2
        up = turn_rows(turn_lanes(tile, 16 * bit), -bit)
        down = turn_rows(turn_lanes(tile, -16 * bit), bit)
        tile = jnp.where(row_bit == lane_bit, tile, jnp.where(row_bit == 0, up, down))
    return tile


def put_slots(out_ref, tiles, rows, base):
    zero = jnp.zeros((8, 128), f32)
    for half in range(2):
        group = [tiles[4 * half + x] if 4 * half + x < 6 else zero for x in range(4)]
        for quad, tile in enumerate(swap_quads(group)):
            out_ref[pl.ds(rows * quad + base + half, 8, stride=4 * rows), :] = tile


def get_slots(in_ref, rows, base):
    tiles = []
    for half in range(2):
        group = [in_ref[pl.ds(rows * quad + base + half, 8, stride=4 * rows), :] for quad in range(4)]
        tiles += swap_quads(group)
    return tiles[:6]


def put_cell_vector(out_ref, vector_ref, rows, base):
    put_slots(out_ref, [swap_rows(vector_ref[8 * t : 8 * t + 8, :]) for t in range(6)], rows, base)


def inverse_matvec(inverse_ref, vector_ref, out_ref):
    totals = None
    for a in range(48):
        term = inverse_ref[a].astype(f32) * vector_ref[a : a + 1, :]
        totals = term if totals is None else totals + term
    out_ref[...] = totals


COMBINATIONS = [(ah, pair) for ah in range(6) for pair in range(3)]
GROUPS_OF_THIRD = ((0, 1), (2, 3, 4, 5), (6, 7, 8))


def group_tiles(group):
    if group == 8:
        return [COMBINATIONS[16 + x // 2] + (x % 2,) for x in range(4)]
    return [COMBINATIONS[4 * (group // 2) + x] + (group % 2,) for x in range(4)]


TILE_AT = {
    (ah, 2 * pair + half): 4 * group + x
    for group in range(9)
    for x, (ah, pair, half) in enumerate(group_tiles(group))
}


def pack_blocks(block_ref, out_ref, base, third):
    station = lax.axis_index("axial")
    quads = lane_index() // 4
    keeps = [(bit, (quads & bit) == 0) for bit in (1, 2, 4, 8, 16)]
    turned = {}
    for group in GROUPS_OF_THIRD[third]:
        items = []
        for i in range(32):
            p = i // 4
            ah, pair, half = group_tiles(group)[i % 4]
            steps = (4 * i + 4 * station) % 128
            if (ah, pair, i) not in turned:
                tile = block_ref[8 * ah + p, 16 * pair : 16 * pair + 16, :]
                turned[ah, pair, i] = pltpu.roll(tile, steps, 1).astype(f32)
            items.append(turn_rows(turned[ah, pair, i][8 * half : 8 * half + 8], -p))
        for bit, keep in keeps:
            items = [jnp.where(keep, items[j], items[(j + bit) % 32]) for j in range(32)]
        for slot in range(35):
            out_ref[slot, base + 8 * group : base + 8 * group + 8, :] = items[-slot % 32]


def fetch_thirds(block_hbm, block_ref, sems):
    copies = []
    for third in range(3):
        there = (slice(16 * third, 16 * third + 16), slice(None), slice(None))
        copies.append(pltpu.make_async_copy(block_hbm.at[there], block_ref.at[there], sems.at[third]))
    return copies


def join_stations(parts, other_half=0):
    chunk = line_lanes(other_half) // 4
    for bit in (1, 2):
        keep = (chunk & bit) == 0
        parts = [jnp.where(keep, parts[j], parts[(j + bit) % 4]) for j in range(4)]
    return [turn_lanes(parts[-x % 4], -4 * x) for x in range(4)]


def unpack_cell(in_ref, base, out_ref, cell):
    for group in range(9):
        at = base + 8 * group
        parts = [in_ref[chunk_of(cell, k), at : at + 8, :] for k in range(4)]
        for x, tile in enumerate(join_stations(parts)):
            at = 8 * (4 * group + x)
            out_ref[cell, at : at + 8, :] = tile


def line_sweep(blocks_ref, const_ref, out_ref, reverse, beside=None):
    order = list(range(8))
    if reverse:
        order = order[::-1]
    state = None
    for turn in range(2):
        for n, cell in enumerate(order):
            if beside is not None:
                beside(turn, n)
            consts = [jnp.broadcast_to(const_ref[t, cell : cell + 1, :], (8, 128)) for t in range(6)]
            if state is None:
                state = consts
                continue
            state = line_step(blocks_ref, cell, state, consts)
            if turn == 1:
                for t in range(6):
                    out_ref[t, cell : cell + 1, :] = state[t][0:1]


def stations_sum(tile):
    station = (line_lanes() // 4) % 4
    before = jnp.where(station > 0, turn_lanes(tile, 4), 0.0)
    after = jnp.where(station < 3, turn_lanes(tile, -4), 0.0)
    return before + after


def first_send_kernel(
    forward_hbm, backward_hbm, inverse_hbm, rhs_hbm, coupling_hbm, out_hbm,
    f_ref, b_ref, i_ref, rhs_ref, coupling_ref, c_ref, vectors_ref, packed_ref, sems, out_sems,
):
    forward = fetch_thirds(forward_hbm, f_ref, sems.at[0])
    inverse = fetch_thirds(inverse_hbm, i_ref, sems.at[1])
    backward = fetch_thirds(backward_hbm, b_ref, sems.at[2])
    vectors = [
        pltpu.make_async_copy(source, target, sems.at[3, n])
        for n, (source, target) in enumerate(((rhs_hbm, rhs_ref), (coupling_hbm, coupling_ref)))
    ]
    for copy in forward + vectors + inverse:
        copy.start()
    leaving = []

    def leave(row, rows, first):
        source = packed_ref.at[pl.ds(first, 32), pl.ds(row, rows), :]
        target = out_hbm.at[:, pl.ds(row, rows), :]
        leaving.append(pltpu.make_async_copy(source, target, out_sems.at[len(leaving)]))
        leaving[-1].start()

    station = lax.axis_index("axial")

    for third in range(3):
        forward[third].wait()
        if third == 0:
            for copy in backward:
                copy.start()
        pack_blocks(f_ref, packed_ref, 0, third)
        leave((0, 16, 48)[third], (16, 32, 24)[third], station)
    for copy in vectors + inverse:
        copy.wait()
    for third in range(3):
        backward[third].wait()
        if third == 0:
            inverse_matvec(i_ref, rhs_ref, c_ref)
            for n, vector_ref in enumerate((c_ref, rhs_ref, coupling_ref)):
                put_cell_vector(vectors_ref, vector_ref, 8, 2 * n)
            for e in range(32):
                packed_ref[e, 144:152, :] = vectors_ref[8 * e : 8 * e + 8, :]
        pack_blocks(b_ref, packed_ref, 72, third)
        if third == 0:
            leave(144, 8, 0)
        leave((72, 88, 120)[third], (16, 32, 24)[third], station)
    for copy in leaving:
        copy.wait()


def first_kernel(slots_ref, *refs):
    own_ref, other_ref, forward_ref, backward_ref, first_ref, middle_ref, coupling_ref, packed_ref, c_ref, y_ref = refs
    for e in range(32):
        packed_ref[8 * e : 8 * e + 8, :] = slots_ref[chunk_of(e // 4, e % 4), 144:152, :]
    for t, tile in enumerate(get_slots(packed_ref, 8, 0)):
        c_ref[t] = to_line(tile)

    def unpack(turn, n):
        if turn == 0:
            unpack_cell(slots_ref, 0, forward_ref, n)
        else:
            unpack_cell(slots_ref, 72, backward_ref, n)

    line_sweep(forward_ref, c_ref, y_ref, False, unpack)
    line_sweep(backward_ref, y_ref, first_ref, True)
    rhs = [to_line(tile) for tile in get_slots(packed_ref, 8, 2)]
    coupling = [to_line(tile) for tile in get_slots(packed_ref, 8, 4)]
    half, _ = half_position()
    low = row_index() < 4
    own, other = [], []
    for t in range(6):
        first = first_ref[t]
        middle = rhs[t] - first + coupling[t] * stations_sum(first)
        turned = turn_rows(middle, 4)
        other.append(jnp.where(half == 0, turned, middle))
        own.append(jnp.where(half == 0, middle, turned))
        middle_ref[t] = middle
        coupling_ref[t] = coupling[t]
    for u in range(3):
        other_ref[u] = jnp.where(low, other[2 * u], turn_rows(other[2 * u + 1], 4))
        own_ref[u] = jnp.where(low, own[2 * u], turn_rows(own[2 * u + 1], 4))


def half_position():
    cell = lax.axis_index("azim")
    return cell // 4, (cell % 4) * 4 + lax.axis_index("axial")


def inverse_send_kernel(inverse_hbm, *refs):
    outs, (i_ref, packed_ref, fetch_sems, sems) = refs[:16], refs[16:]
    fetches = fetch_thirds(inverse_hbm, i_ref, fetch_sems)
    for copy in fetches:
        copy.start()
    for third, copy in enumerate(fetches):
        copy.wait()
        pack_blocks(i_ref, packed_ref, 0, third)
    half, place = half_position()
    station = place % 4
    copies = []
    for d in range(16):
        target = place ^ d
        for n in range(2):
            cell = 4 * (half if n == 0 else 1 - half) + target // 4
            source = chunk_of(cell, target % 4)
            copies.append(
                pltpu.make_async_copy(packed_ref.at[source + station], outs[d].at[pl.ds(72 * n, 72), :], sems.at[2 * d + n])
            )
            copies[-1].start()
    for copy in copies:
        copy.wait()


def inverse_get_kernel(*refs):
    ins, out_ref = refs[:4], refs[4]
    station = lax.axis_index("axial")
    for lines in range(2):
        for group in range(9):
            at = 72 * lines + 8 * group
            parts = [part[at : at + 8, :] for part in ins]
            for bit in (1, 2):
                parts = [jnp.where((station & bit) == 0, parts[k], parts[k ^ bit]) for k in range(4)]
            for x, tile in enumerate(join_stations(parts, lines)):
                at = 8 * (4 * group + x)
                out_ref[lines, at : at + 8, :] = tile


def line_step(blocks_ref, cell, state, consts):
    following = []
    for bh in range(6):
        terms = []
        for ah in range(6):
            at = 8 * TILE_AT[ah, bh]
            terms.append(blocks_ref[cell, at : at + 8, :] * state[ah])
        total = (terms[0] + terms[1]) + (terms[2] + terms[3]) + (terms[4] + terms[5])
        total = pltpu.roll(total, 0, 1, stride=16, stride_axis=0)
        for span in (4, 2):
            total = total + turn_rows(total, span)
        following.append((consts[bh] - total) - turn_rows(total, 1))
    return following


def half_inverse_kernel(lines, vector_ref, *refs):
    blocks, out_ref = refs[:4], refs[4]
    _, place = half_position()
    cell = place // 4
    rows = row_index()
    zero = jnp.zeros((8, 128), f32)
    totals = [zero] * 3
    for n in range(4):
        state = [
            jnp.broadcast_to(vector_ref[t // 2, pl.ds(4 * (t % 2) + (cell ^ n), 1), :], (8, 128)) for t in range(6)
        ]
        for t, product in enumerate(line_step(blocks[n], lines, state, [zero] * 6)):
            totals[t // 2] = jnp.where(rows == 4 * (t % 2) + (cell ^ n), product, totals[t // 2])
    for u in range(3):
        out_ref[u] = -totals[u]


def second_kernel(
    own_ref, other_ref, forward_ref, backward_ref, first_ref, middle_ref, coupling_ref, out_ref, c_ref, y_ref, second_ref,
    slots_ref,
):
    half, _ = half_position()
    low = row_index() < 4
    for t in range(6):
        own, other = own_ref[t // 2], other_ref[t // 2]
        if t % 2:
            own = turn_rows(own, 4)
        else:
            other = turn_rows(other, 4)
        tile = jnp.where(low, own, other)
        c_ref[t] = jnp.where(half == 0, tile, turn_rows(tile, 4))
    line_sweep(forward_ref, c_ref, y_ref, False)
    line_sweep(backward_ref, y_ref, second_ref, True)
    correction, remaining = [], []
    for t in range(6):
        second = second_ref[t]
        correction.append(from_line(first_ref[t] + second))
        remaining.append(from_line(middle_ref[t] - second + coupling_ref[t] * stations_sum(second)))
    put_slots(slots_ref, correction, 4, 0)
    put_slots(slots_ref, remaining, 4, 2)
    for e in range(32):
        at = 4 * chunk_of(e // 4, e % 4)
        out_ref[at : at + 4, :] = slots_ref[4 * e : 4 * e + 4, :]


def last_kernel(slots_ref, correction_ref, remaining_ref):
    for out_ref, base in ((correction_ref, 0), (remaining_ref, 2)):
        for t, tile in enumerate(get_slots(slots_ref, 4, base)):
            out_ref[8 * t : 8 * t + 8, :] = swap_rows(tile)


def shaped(*sizes):
    return jax.ShapeDtypeStruct(sizes, f32)


def call(kernel, outs, scratch=()):
    return pl.pallas_call(
        kernel,
        out_shape=outs,
        scratch_shapes=[pltpu.VMEM(sizes, f32) for sizes in scratch],
        compiler_params=pltpu.CompilerParams(vmem_limit_bytes=VMEM_LIMIT),
    )


def exchange(slots, rows):
    moved = lax.all_to_all(slots.reshape(32, rows, 128), BOTH, 0, 0, axis_index_groups=ORDER, tiled=True)
    return moved.reshape(32 * rows, 128)


def line_plan(rhs, coupling, fwd_coupling, bwd_coupling, block_inverse):
    source, coupling_field = rhs.reshape(48, 128), coupling.reshape(48, 128)
    forward_blocks = fwd_coupling.reshape(48, 48, 128)
    backward_blocks = bwd_coupling.reshape(48, 48, 128)
    inverse_blocks = block_inverse.reshape(48, 48, 128)
    tiles, pairs, held = shaped(6, 8, 128), shaped(3, 8, 128), shaped(8, 288, 128)
    blocks = pltpu.VMEM((48, 48, 128), jnp.bfloat16)
    vector = pltpu.VMEM((48, 128), f32)

    slots = pl.pallas_call(
        first_send_kernel,
        out_shape=pltpu.HBM((32, 152, 128), f32),
        in_specs=[pl.BlockSpec(memory_space=pltpu.HBM)] * 5,
        out_specs=pl.BlockSpec(memory_space=pltpu.HBM),
        scratch_shapes=[blocks, blocks, blocks, vector, vector, vector]
        + [
            pltpu.VMEM((256, 128), f32),
            pltpu.VMEM((35, 152, 128), f32),
            pltpu.SemaphoreType.DMA((4, 3)),
            pltpu.SemaphoreType.DMA((7,)),
        ],
        compiler_params=pltpu.CompilerParams(vmem_limit_bytes=VMEM_LIMIT),
    )(*[
        pltpu.with_memory_space_constraint(array, pltpu.HBM)
        for array in (forward_blocks, backward_blocks, inverse_blocks, source, coupling_field)
    ])
    slots, inverse_blocks = lax.optimization_barrier((slots, inverse_blocks))
    slots = lax.all_to_all(slots, BOTH, 0, 0, axis_index_groups=ORDER, tiled=True)

    parts = pl.pallas_call(
        inverse_send_kernel,
        out_shape=[shaped(144, 128)] * 16,
        in_specs=[pl.BlockSpec(memory_space=pltpu.HBM)],
        out_specs=[pl.BlockSpec(memory_space=pltpu.HBM)] * 16,
        scratch_shapes=[
            blocks, pltpu.VMEM((35, 72, 128), f32), pltpu.SemaphoreType.DMA((3,)), pltpu.SemaphoreType.DMA((32,))
        ],
        compiler_params=pltpu.CompilerParams(vmem_limit_bytes=VMEM_LIMIT),
    )(pltpu.with_memory_space_constraint(inverse_blocks, pltpu.HBM))
    parts = [parts[0]] + [lax.ppermute(parts[d], BOTH, [(e, e ^ d) for e in range(32)]) for d in range(1, 16)]
    inverse = [
        call(inverse_get_kernel, pltpu.VMEM((2, 288, 128), f32))(*parts[4 * n : 4 * n + 4]) for n in range(4)
    ]

    own, other, forward, backward, first, middle, coupling_lines = call(
        first_kernel, (pairs, pairs, held, held, tiles, tiles, tiles), [(256, 128), (6, 8, 128), (6, 8, 128)]
    )(slots)

    def with_partner(vector):
        return lax.ppermute(vector, BOTH, [(e, e ^ 16) for e in range(32)])

    other = with_partner(other)
    own = call(functools.partial(half_inverse_kernel, 0), pairs)(own, *inverse)
    other = call(functools.partial(half_inverse_kernel, 1), pairs)(other, *inverse)
    other = with_partner(other)
    slots = call(second_kernel, shaped(128, 128), [(6, 8, 128)] * 3 + [(128, 128)])(
        own, other, forward, backward, first, middle, coupling_lines
    )
    slots = exchange(slots, 4)
    correction, remaining = call(last_kernel, (shaped(48, 128), shaped(48, 128)))(slots)
    return correction.reshape(rhs.shape), remaining.reshape(rhs.shape)


def from_behind(value, axis, steps):
    count = lax.axis_size(axis)
    initial, last = (max(0, -steps), min(count, count - steps))
    return lax.ppermute(value, axis, [(source, source + steps) for source in range(initial, last)])


def from_root(shard, axis, root):
    mine = lax.axis_index(axis) == root
    return lax.psum(jnp.where(mine, shard, jnp.zeros_like(shard)), axis)


def extended(block, sides, width):
    for axis, dim in sides:
        count = lax.axis_size(axis)
        forward = [(i, i + 1) for i in range(count - 1)]
        backward = [(target, source) for source, target in forward]
        low = lax.ppermute(
            lax.slice_in_dim(block, block.shape[dim] - width, None, axis=dim), axis, forward
        )
        high = lax.ppermute(lax.slice_in_dim(block, 0, width, axis=dim), axis, backward)
        block = jnp.concatenate([low, block, high], axis=dim)
    return block


def cell_stride(one_block, carried, const_term):
    return const_term - jnp.einsum(
        "abl,al->bl", one_block.astype(jnp.float32), carried, precision=highest
    )


def compose_cells(blocks, sequence):
    running = None
    for position in sequence:
        one_block = blocks[position].astype(jnp.float32)
        running = -jnp.swapaxes(one_block, 0, 1)
    return running


def doubling_maps(local_map, reverse):
    size = lax.axis_size("azim")
    index = lax.axis_index("azim")
    levels = []
    current = local_map
    distance = 1
    while distance < size:
        if reverse:
            moved = from_behind(current, "azim", -distance)
            exists = index + distance < size
        else:
            moved = from_behind(current, "azim", distance)
            exists = index >= distance
        levels.append((current, distance))
        current = jnp.where(
            exists, jnp.einsum("bcl,cal->bal", current, moved, precision=highest), current
        )
        distance = distance * 2
    return (levels, current)


def doubling_entries(map_levels, local_offset, reverse):
    levels, final_map = map_levels
    size = lax.axis_size("azim")
    index = lax.axis_index("azim")
    running = local_offset
    for current, distance in levels:
        if reverse:
            moved = from_behind(running, "azim", -distance)
        else:
            moved = from_behind(running, "azim", distance)
        running = jnp.einsum("bcl,cl->bl", current, moved, precision=highest) + running
    if reverse:
        wrapped = from_root(running, "azim", 0)
    else:
        wrapped = from_root(running, "azim", size - 1)
    leaving = jnp.einsum("bcl,cl->bl", final_map, wrapped, precision=highest) + running
    if reverse:
        shifted = from_behind(leaving, "azim", -1)
        first_device = index == size - 1
    else:
        shifted = from_behind(leaving, "azim", 1)
        first_device = index == 0
    return jnp.where(first_device, wrapped, shifted)


def sweep(blocks, consts, map_levels, reverse):
    cell_count = blocks.shape[0]
    sequence = list(range(cell_count))
    if reverse:
        sequence = sequence[::-1]
    carried = jnp.zeros(consts.shape[1:], jnp.float32)
    for position in sequence:
        carried = cell_stride(blocks[position], carried, consts[position])
    local_offset = carried
    incoming_maps = doubling_entries(map_levels, local_offset, reverse)
    outputs = [None] * cell_count
    carried = incoming_maps
    for position in sequence:
        carried = cell_stride(blocks[position], carried, consts[position])
        outputs[position] = carried
    return jnp.stack(outputs)


def on_device(rhs, coupling, fwd_coupling, bwd_coupling, block_inverse):
    cell_count, block_width, _, position_total, radial_count = fwd_coupling.shape
    line_count = position_total * radial_count
    forward_blocks = fwd_coupling.reshape(cell_count, block_width, block_width, line_count)
    backward_blocks = bwd_coupling.reshape(cell_count, block_width, block_width, line_count)
    inverse_blocks = block_inverse.reshape(cell_count, block_width, block_width, line_count)
    source = rhs.reshape(cell_count, block_width, line_count)
    coupling_field = coupling.reshape(cell_count, block_width, line_count)
    forward_map = compose_cells(forward_blocks, list(range(cell_count)))
    backward_map = compose_cells(backward_blocks, list(range(cell_count))[::-1])
    forward_levels = None
    backward_levels = None
    forward_levels = doubling_maps(forward_map, False)
    backward_levels = doubling_maps(backward_map, True)

    def precondition(vector):
        consts = jnp.stack(
            [
                jnp.einsum(
                    "abl,al->bl",
                    inverse_blocks[0].astype(jnp.float32),
                    vector[0],
                    precision=highest,
                )
            ]
        )
        forward = sweep(forward_blocks, consts, forward_levels, False)
        return sweep(backward_blocks, forward, backward_levels, True)

    def stations_sum(field):
        grid = field.reshape(cell_count, block_width, position_total, radial_count)
        padded = extended(grid, (("axial", 2),), 1)
        return (padded[:, :, :-2] + padded[:, :, 2:]).reshape(cell_count, block_width, line_count)

    applied_once = precondition(source)
    middle = source - applied_once + coupling_field * stations_sum(applied_once)
    second = precondition(middle)
    correction = applied_once + second
    remaining = middle - second + coupling_field * stations_sum(second)
    return (correction.reshape(rhs.shape), remaining.reshape(rhs.shape))


def solution(mesh):
    cells, stations = mesh.shape["azim"], mesh.shape["axial"]

    def on_each(rhs, coupling, fwd_coupling, bwd_coupling, block_inverse):
        local = fwd_coupling.shape
        if (cells, stations) == (8, 4) and local == (1, 48, 48, 1, 128):
            return line_plan(rhs, coupling, fwd_coupling, bwd_coupling, block_inverse)
        return on_device(rhs, coupling, fwd_coupling, bwd_coupling, block_inverse)

    return jax.shard_map(
        on_each,
        mesh=mesh,
        in_specs=(
            P("azim", None, "axial", None),
            P("azim", None, "axial", None),
            P("azim", None, None, "axial", None),
            P("azim", None, None, "axial", None),
            P("azim", None, None, "axial", None),
        ),
        out_specs=(P("azim", None, "axial", None), P("azim", None, "axial", None)),
        check_vma=False,
    )
```

```python
import functools

import jax
import jax.numpy as jnp
from jax import lax
from jax.experimental import pallas as pl
from jax.experimental.pallas import tpu as pltpu
from jax.sharding import PartitionSpec as P

highest = lax.Precision.HIGHEST
f32 = jnp.float32
BOTH = ("azim", "axial")


def chunk_of(cell, station):
    return 16 * (cell % 2) + 4 * station + 3 - cell // 2


ORDER = [[e for chunk in range(32) for e in range(32) if chunk_of(e // 4, e % 4) == chunk]]
VMEM_LIMIT = 16 * 1024 * 1024


def lane_index():
    return lax.broadcasted_iota(jnp.int32, (8, 128), 1)


def row_index():
    return lax.broadcasted_iota(jnp.int32, (8, 128), 0)


def turn_lanes(tile, steps):
    steps = steps % 128
    return pltpu.roll(tile, steps, 1) if steps else tile


def turn_rows(tile, steps):
    steps = steps % 8
    return pltpu.roll(tile, steps, 0) if steps else tile


def line_lanes(other_half=0):
    return lane_index() + 16 - 4 * ((3 - lax.axis_index("azim") // 2) ^ (2 * other_half))


def own_chunk():
    return chunk_of(lax.axis_index("azim"), lax.axis_index("axial"))


def to_line(tile):
    return pltpu.roll(tile, 4 * own_chunk(), 1)


def from_line(tile):
    return pltpu.roll(tile, (128 - 4 * own_chunk()) % 128, 1)


def swap_quads(tiles, lanes=None):
    lanes = lane_index() if lanes is None else lanes
    tiles = list(tiles)
    for bit, width in ((1, 4), (2, 8)):
        low = (lanes // width) % 2 == 0
        for first in range(4):
            if first & bit:
                continue
            one, two = tiles[first], tiles[first | bit]
            tiles[first] = jnp.where(low, one, turn_lanes(two, width))
            tiles[first | bit] = jnp.where(low, turn_lanes(one, -width), two)
    return tiles


def swap_rows(tile):
    lanes, rows = lane_index() // 16, row_index()
    for bit in (1, 2, 4):
        row_bit, lane_bit = (rows // bit) % 2, (lanes // bit) % 2
        up = turn_rows(turn_lanes(tile, 16 * bit), -bit)
        down = turn_rows(turn_lanes(tile, -16 * bit), bit)
        tile = jnp.where(row_bit == lane_bit, tile, jnp.where(row_bit == 0, up, down))
    return tile


def put_slots(out_ref, tiles, rows, base):
    zero = jnp.zeros((8, 128), f32)
    for half in range(2):
        group = [tiles[4 * half + x] if 4 * half + x < 6 else zero for x in range(4)]
        for quad, tile in enumerate(swap_quads(group)):
            out_ref[pl.ds(rows * quad + base + half, 8, stride=4 * rows), :] = tile


def get_slots(in_ref, rows, base):
    tiles = []
    for half in range(2):
        group = [in_ref[pl.ds(rows * quad + base + half, 8, stride=4 * rows), :] for quad in range(4)]
        tiles += swap_quads(group)
    return tiles[:6]


def put_cell_vector(out_ref, vector_ref, rows, base):
    put_slots(out_ref, [swap_rows(vector_ref[8 * t : 8 * t + 8, :]) for t in range(6)], rows, base)


def inverse_matvec(inverse_ref, vector_ref, out_ref):
    totals = None
    for a in range(48):
        term = inverse_ref[a].astype(f32) * vector_ref[a : a + 1, :]
        totals = term if totals is None else totals + term
    out_ref[...] = totals


COMBINATIONS = [(ah, pair) for ah in range(6) for pair in range(3)]
GROUPS_OF_THIRD = ((0, 1), (2, 3, 4, 5), (6, 7, 8))


def group_tiles(group):
    if group == 8:
        return [COMBINATIONS[16 + x // 2] + (x % 2,) for x in range(4)]
    return [COMBINATIONS[4 * (group // 2) + x] + (group % 2,) for x in range(4)]


TILE_AT = {
    (ah, 2 * pair + half): 4 * group + x
    for group in range(9)
    for x, (ah, pair, half) in enumerate(group_tiles(group))
}


def pack_blocks(block_ref, out_ref, base, third):
    station = lax.axis_index("axial")
    quads = lane_index() // 4
    keeps = [(bit, (quads & bit) == 0) for bit in (1, 2, 4, 8, 16)]
    turned = {}
    for group in GROUPS_OF_THIRD[third]:
        items = []
        for i in range(32):
            p = i // 4
            ah, pair, half = group_tiles(group)[i % 4]
            steps = (4 * i + 4 * station) % 128
            if (ah, pair, i) not in turned:
                tile = block_ref[8 * ah + p, 16 * pair : 16 * pair + 16, :]
                turned[ah, pair, i] = pltpu.roll(tile, steps, 1).astype(f32)
            items.append(turn_rows(turned[ah, pair, i][8 * half : 8 * half + 8], -p))
        for bit, keep in keeps:
            items = [jnp.where(keep, items[j], items[(j + bit) % 32]) for j in range(32)]
        for slot in range(35):
            out_ref[slot, base + 8 * group : base + 8 * group + 8, :] = items[-slot % 32]


def fetch_thirds(block_hbm, block_ref, sems):
    copies = []
    for third in range(3):
        there = (slice(16 * third, 16 * third + 16), slice(None), slice(None))
        copies.append(pltpu.make_async_copy(block_hbm.at[there], block_ref.at[there], sems.at[third]))
    return copies


def join_stations(parts, other_half=0):
    chunk = line_lanes(other_half) // 4
    for bit in (1, 2):
        keep = (chunk & bit) == 0
        parts = [jnp.where(keep, parts[j], parts[(j + bit) % 4]) for j in range(4)]
    return [turn_lanes(parts[-x % 4], -4 * x) for x in range(4)]


def unpack_cell(in_ref, base, out_ref, cell):
    for group in range(9):
        at = base + 8 * group
        parts = [in_ref[chunk_of(cell, k), at : at + 8, :] for k in range(4)]
        for x, tile in enumerate(join_stations(parts)):
            at = 8 * (4 * group + x)
            out_ref[cell, at : at + 8, :] = tile


def line_sweep(blocks_ref, const_ref, out_ref, reverse, beside=None):
    order = list(range(8))
    if reverse:
        order = order[::-1]
    state = None
    for turn in range(2):
        for n, cell in enumerate(order):
            if beside is not None:
                beside(turn, n)
            consts = [jnp.broadcast_to(const_ref[t, cell : cell + 1, :], (8, 128)) for t in range(6)]
            if state is None:
                state = consts
                continue
            state = line_step(blocks_ref, cell, state, consts)
            if turn == 1:
                for t in range(6):
                    out_ref[t, cell : cell + 1, :] = state[t][0:1]


def stations_sum(tile):
    station = (line_lanes() // 4) % 4
    before = jnp.where(station > 0, turn_lanes(tile, 4), 0.0)
    after = jnp.where(station < 3, turn_lanes(tile, -4), 0.0)
    return before + after


def first_send_kernel(
    forward_hbm, backward_hbm, inverse_hbm, rhs_hbm, coupling_hbm, out_hbm,
    f_ref, b_ref, i_ref, rhs_ref, coupling_ref, c_ref, vectors_ref, packed_ref, sems, out_sems,
):
    forward = fetch_thirds(forward_hbm, f_ref, sems.at[0])
    inverse = fetch_thirds(inverse_hbm, i_ref, sems.at[1])
    backward = fetch_thirds(backward_hbm, b_ref, sems.at[2])
    vectors = [
        pltpu.make_async_copy(source, target, sems.at[3, n])
        for n, (source, target) in enumerate(((rhs_hbm, rhs_ref), (coupling_hbm, coupling_ref)))
    ]
    for copy in forward + vectors + inverse:
        copy.start()
    leaving = []

    def leave(row, rows, first):
        source = packed_ref.at[pl.ds(first, 32), pl.ds(row, rows), :]
        target = out_hbm.at[:, pl.ds(row, rows), :]
        leaving.append(pltpu.make_async_copy(source, target, out_sems.at[len(leaving)]))
        leaving[-1].start()

    station = lax.axis_index("axial")

    for third in range(3):
        forward[third].wait()
        if third == 0:
            for copy in backward:
                copy.start()
        pack_blocks(f_ref, packed_ref, 0, third)
        leave((0, 16, 48)[third], (16, 32, 24)[third], station)
    for copy in vectors + inverse:
        copy.wait()
    for third in range(3):
        backward[third].wait()
        if third == 0:
            inverse_matvec(i_ref, rhs_ref, c_ref)
            for n, vector_ref in enumerate((c_ref, rhs_ref, coupling_ref)):
                put_cell_vector(vectors_ref, vector_ref, 8, 2 * n)
            for e in range(32):
                packed_ref[e, 144:152, :] = vectors_ref[8 * e : 8 * e + 8, :]
        pack_blocks(b_ref, packed_ref, 72, third)
        if third == 0:
            leave(144, 8, 0)
        leave((72, 88, 120)[third], (16, 32, 24)[third], station)
    for copy in leaving:
        copy.wait()


def first_kernel(slots_ref, *refs):
    own_ref, other_ref, forward_ref, backward_ref, first_ref, middle_ref, coupling_ref, packed_ref, c_ref, y_ref = refs
    for e in range(32):
        packed_ref[8 * e : 8 * e + 8, :] = slots_ref[chunk_of(e // 4, e % 4), 144:152, :]
    for t, tile in enumerate(get_slots(packed_ref, 8, 0)):
        c_ref[t] = to_line(tile)

    def unpack(turn, n):
        if turn == 0:
            unpack_cell(slots_ref, 0, forward_ref, n)
        else:
            unpack_cell(slots_ref, 72, backward_ref, n)

    line_sweep(forward_ref, c_ref, y_ref, False, unpack)
    line_sweep(backward_ref, y_ref, first_ref, True)
    rhs = [to_line(tile) for tile in get_slots(packed_ref, 8, 2)]
    coupling = [to_line(tile) for tile in get_slots(packed_ref, 8, 4)]
    half, _ = half_position()
    low = row_index() < 4
    own, other = [], []
    for t in range(6):
        first = first_ref[t]
        middle = rhs[t] - first + coupling[t] * stations_sum(first)
        turned = turn_rows(middle, 4)
        other.append(jnp.where(half == 0, turned, middle))
        own.append(jnp.where(half == 0, middle, turned))
        middle_ref[t] = middle
        coupling_ref[t] = coupling[t]
    for u in range(3):
        other_ref[u] = jnp.where(low, other[2 * u], turn_rows(other[2 * u + 1], 4))
        own_ref[u] = jnp.where(low, own[2 * u], turn_rows(own[2 * u + 1], 4))


def half_position():
    cell = lax.axis_index("azim")
    return cell // 4, (cell % 4) * 4 + lax.axis_index("axial")


def inverse_send_kernel(inverse_hbm, *refs):
    outs, (i_ref, packed_ref, fetch_sems, sems) = refs[:16], refs[16:]
    fetches = fetch_thirds(inverse_hbm, i_ref, fetch_sems)
    for copy in fetches:
        copy.start()
    for third, copy in enumerate(fetches):
        copy.wait()
        pack_blocks(i_ref, packed_ref, 0, third)
    half, place = half_position()
    station = place % 4
    copies = []
    for d in range(16):
        target = place ^ d
        for n in range(2):
            cell = 4 * (half if n == 0 else 1 - half) + target // 4
            source = chunk_of(cell, target % 4)
            copies.append(
                pltpu.make_async_copy(packed_ref.at[source + station], outs[d].at[pl.ds(72 * n, 72), :], sems.at[2 * d + n])
            )
            copies[-1].start()
    for copy in copies:
        copy.wait()


def inverse_get_kernel(*refs):
    ins, out_ref = refs[:4], refs[4]
    station = lax.axis_index("axial")
    for lines in range(2):
        for group in range(9):
            at = 72 * lines + 8 * group
            parts = [part[at : at + 8, :] for part in ins]
            for bit in (1, 2):
                parts = [jnp.where((station & bit) == 0, parts[k], parts[k ^ bit]) for k in range(4)]
            for x, tile in enumerate(join_stations(parts, lines)):
                at = 8 * (4 * group + x)
                out_ref[lines, at : at + 8, :] = tile


def line_step(blocks_ref, cell, state, consts):
    following = []
    for bh in range(6):
        terms = []
        for ah in range(6):
            at = 8 * TILE_AT[ah, bh]
            terms.append(blocks_ref[cell, at : at + 8, :] * state[ah])
        total = (terms[0] + terms[1]) + (terms[2] + terms[3]) + (terms[4] + terms[5])
        total = pltpu.roll(total, 0, 1, stride=16, stride_axis=0)
        for span in (4, 2):
            total = total + turn_rows(total, span)
        following.append((consts[bh] - total) - turn_rows(total, 1))
    return following


def half_inverse_kernel(lines, vector_ref, *refs):
    blocks, out_ref = refs[:4], refs[4]
    _, place = half_position()
    cell = place // 4
    rows = row_index()
    zero = jnp.zeros((8, 128), f32)
    totals = [zero] * 3
    for n in range(4):
        state = [
            jnp.broadcast_to(vector_ref[t // 2, pl.ds(4 * (t % 2) + (cell ^ n), 1), :], (8, 128)) for t in range(6)
        ]
        for t, product in enumerate(line_step(blocks[n], lines, state, [zero] * 6)):
            totals[t // 2] = jnp.where(rows == 4 * (t % 2) + (cell ^ n), product, totals[t // 2])
    for u in range(3):
        out_ref[u] = -totals[u]


def second_kernel(
    own_ref, other_ref, forward_ref, backward_ref, first_ref, middle_ref, coupling_ref, out_ref, c_ref, y_ref, second_ref,
    slots_ref,
):
    half, _ = half_position()
    low = row_index() < 4
    for t in range(6):
        own, other = own_ref[t // 2], other_ref[t // 2]
        if t % 2:
            own = turn_rows(own, 4)
        else:
            other = turn_rows(other, 4)
        tile = jnp.where(low, own, other)
        c_ref[t] = jnp.where(half == 0, tile, turn_rows(tile, 4))
    line_sweep(forward_ref, c_ref, y_ref, False)
    line_sweep(backward_ref, y_ref, second_ref, True)
    correction, remaining = [], []
    for t in range(6):
        second = second_ref[t]
        correction.append(from_line(first_ref[t] + second))
        remaining.append(from_line(middle_ref[t] - second + coupling_ref[t] * stations_sum(second)))
    put_slots(slots_ref, correction, 4, 0)
    put_slots(slots_ref, remaining, 4, 2)
    for e in range(32):
        at = 4 * chunk_of(e // 4, e % 4)
        out_ref[at : at + 4, :] = slots_ref[4 * e : 4 * e + 4, :]


def last_kernel(slots_ref, correction_ref, remaining_ref):
    for out_ref, base in ((correction_ref, 0), (remaining_ref, 2)):
        for t, tile in enumerate(get_slots(slots_ref, 4, base)):
            out_ref[8 * t : 8 * t + 8, :] = swap_rows(tile)


def shaped(*sizes):
    return jax.ShapeDtypeStruct(sizes, f32)


def call(kernel, outs, scratch=()):
    return pl.pallas_call(
        kernel,
        out_shape=outs,
        scratch_shapes=[pltpu.VMEM(sizes, f32) for sizes in scratch],
        compiler_params=pltpu.CompilerParams(vmem_limit_bytes=VMEM_LIMIT),
    )


def exchange(slots, rows):
    moved = lax.all_to_all(slots.reshape(32, rows, 128), BOTH, 0, 0, axis_index_groups=ORDER, tiled=True)
    return moved.reshape(32 * rows, 128)


def line_plan(rhs, coupling, fwd_coupling, bwd_coupling, block_inverse):
    source, coupling_field = rhs.reshape(48, 128), coupling.reshape(48, 128)
    forward_blocks = fwd_coupling.reshape(48, 48, 128)
    backward_blocks = bwd_coupling.reshape(48, 48, 128)
    inverse_blocks = block_inverse.reshape(48, 48, 128)
    tiles, pairs, held = shaped(6, 8, 128), shaped(3, 8, 128), shaped(8, 288, 128)
    blocks = pltpu.VMEM((48, 48, 128), jnp.bfloat16)
    vector = pltpu.VMEM((48, 128), f32)

    slots = pl.pallas_call(
        first_send_kernel,
        out_shape=pltpu.HBM((32, 152, 128), f32),
        in_specs=[pl.BlockSpec(memory_space=pltpu.HBM)] * 5,
        out_specs=pl.BlockSpec(memory_space=pltpu.HBM),
        scratch_shapes=[blocks, blocks, blocks, vector, vector, vector]
        + [
            pltpu.VMEM((256, 128), f32),
            pltpu.VMEM((35, 152, 128), f32),
            pltpu.SemaphoreType.DMA((4, 3)),
            pltpu.SemaphoreType.DMA((7,)),
        ],
        compiler_params=pltpu.CompilerParams(vmem_limit_bytes=VMEM_LIMIT),
    )(*[
        pltpu.with_memory_space_constraint(array, pltpu.HBM)
        for array in (forward_blocks, backward_blocks, inverse_blocks, source, coupling_field)
    ])
    slots, inverse_blocks = lax.optimization_barrier((slots, inverse_blocks))
    slots = lax.all_to_all(slots, BOTH, 0, 0, axis_index_groups=ORDER, tiled=True)

    parts = pl.pallas_call(
        inverse_send_kernel,
        out_shape=[shaped(144, 128)] * 16,
        in_specs=[pl.BlockSpec(memory_space=pltpu.HBM)],
        out_specs=[pl.BlockSpec(memory_space=pltpu.HBM)] * 16,
        scratch_shapes=[
            blocks, pltpu.VMEM((35, 72, 128), f32), pltpu.SemaphoreType.DMA((3,)), pltpu.SemaphoreType.DMA((32,))
        ],
        compiler_params=pltpu.CompilerParams(vmem_limit_bytes=VMEM_LIMIT),
    )(pltpu.with_memory_space_constraint(inverse_blocks, pltpu.HBM))
    parts = [parts[0]] + [lax.ppermute(parts[d], BOTH, [(e, e ^ d) for e in range(32)]) for d in range(1, 16)]
    inverse = [
        call(inverse_get_kernel, pltpu.VMEM((2, 288, 128), f32))(*parts[4 * n : 4 * n + 4]) for n in range(4)
    ]

    own, other, forward, backward, first, middle, coupling_lines = call(
        first_kernel, (pairs, pairs, held, held, tiles, tiles, tiles), [(256, 128), (6, 8, 128), (6, 8, 128)]
    )(slots)

    def with_partner(vector):
        return lax.ppermute(vector, BOTH, [(e, e ^ 16) for e in range(32)])

    other = with_partner(other)
    own = call(functools.partial(half_inverse_kernel, 0), pairs)(own, *inverse)
    other = call(functools.partial(half_inverse_kernel, 1), pairs)(other, *inverse)
    other = with_partner(other)
    slots = call(second_kernel, shaped(128, 128), [(6, 8, 128)] * 3 + [(128, 128)])(
        own, other, forward, backward, first, middle, coupling_lines
    )
    slots = exchange(slots, 4)
    correction, remaining = call(last_kernel, (shaped(48, 128), shaped(48, 128)))(slots)
    return correction.reshape(rhs.shape), remaining.reshape(rhs.shape)


def from_behind(value, axis, steps):
    count = lax.axis_size(axis)
    initial, last = (max(0, -steps), min(count, count - steps))
    return lax.ppermute(value, axis, [(source, source + steps) for source in range(initial, last)])


def from_root(shard, axis, root):
    mine = lax.axis_index(axis) == root
    return lax.psum(jnp.where(mine, shard, jnp.zeros_like(shard)), axis)


def extended(block, sides, width):
    for axis, dim in sides:
        count = lax.axis_size(axis)
        forward = [(i, i + 1) for i in range(count - 1)]
        backward = [(target, source) for source, target in forward]
        low = lax.ppermute(
            lax.slice_in_dim(block, block.shape[dim] - width, None, axis=dim), axis, forward
        )
        high = lax.ppermute(lax.slice_in_dim(block, 0, width, axis=dim), axis, backward)
        block = jnp.concatenate([low, block, high], axis=dim)
    return block


def cell_stride(one_block, carried, const_term):
    return const_term - jnp.einsum(
        "abl,al->bl", one_block.astype(jnp.float32), carried, precision=highest
    )


def compose_cells(blocks, sequence):
    running = None
    for position in sequence:
        one_block = blocks[position].astype(jnp.float32)
        running = -jnp.swapaxes(one_block, 0, 1)
    return running


def doubling_maps(local_map, reverse):
    size = lax.axis_size("azim")
    index = lax.axis_index("azim")
    levels = []
    current = local_map
    distance = 1
    while distance < size:
        if reverse:
            moved = from_behind(current, "azim", -distance)
            exists = index + distance < size
        else:
            moved = from_behind(current, "azim", distance)
            exists = index >= distance
        levels.append((current, distance))
        current = jnp.where(
            exists, jnp.einsum("bcl,cal->bal", current, moved, precision=highest), current
        )
        distance = distance * 2
    return (levels, current)


def doubling_entries(map_levels, local_offset, reverse):
    levels, final_map = map_levels
    size = lax.axis_size("azim")
    index = lax.axis_index("azim")
    running = local_offset
    for current, distance in levels:
        if reverse:
            moved = from_behind(running, "azim", -distance)
        else:
            moved = from_behind(running, "azim", distance)
        running = jnp.einsum("bcl,cl->bl", current, moved, precision=highest) + running
    if reverse:
        wrapped = from_root(running, "azim", 0)
    else:
        wrapped = from_root(running, "azim", size - 1)
    leaving = jnp.einsum("bcl,cl->bl", final_map, wrapped, precision=highest) + running
    if reverse:
        shifted = from_behind(leaving, "azim", -1)
        first_device = index == size - 1
    else:
        shifted = from_behind(leaving, "azim", 1)
        first_device = index == 0
    return jnp.where(first_device, wrapped, shifted)


def sweep(blocks, consts, map_levels, reverse):
    cell_count = blocks.shape[0]
    sequence = list(range(cell_count))
    if reverse:
        sequence = sequence[::-1]
    carried = jnp.zeros(consts.shape[1:], jnp.float32)
    for position in sequence:
        carried = cell_stride(blocks[position], carried, consts[position])
    local_offset = carried
    incoming_maps = doubling_entries(map_levels, local_offset, reverse)
    outputs = [None] * cell_count
    carried = incoming_maps
    for position in sequence:
        carried = cell_stride(blocks[position], carried, consts[position])
        outputs[position] = carried
    return jnp.stack(outputs)


def on_device(rhs, coupling, fwd_coupling, bwd_coupling, block_inverse):
    cell_count, block_width, _, position_total, radial_count = fwd_coupling.shape
    line_count = position_total * radial_count
    forward_blocks = fwd_coupling.reshape(cell_count, block_width, block_width, line_count)
    backward_blocks = bwd_coupling.reshape(cell_count, block_width, block_width, line_count)
    inverse_blocks = block_inverse.reshape(cell_count, block_width, block_width, line_count)
    source = rhs.reshape(cell_count, block_width, line_count)
    coupling_field = coupling.reshape(cell_count, block_width, line_count)
    forward_map = compose_cells(forward_blocks, list(range(cell_count)))
    backward_map = compose_cells(backward_blocks, list(range(cell_count))[::-1])
    forward_levels = None
    backward_levels = None
    forward_levels = doubling_maps(forward_map, False)
    backward_levels = doubling_maps(backward_map, True)

    def precondition(vector):
        consts = jnp.stack(
            [
                jnp.einsum(
                    "abl,al->bl",
                    inverse_blocks[0].astype(jnp.float32),
                    vector[0],
                    precision=highest,
                )
            ]
        )
        forward = sweep(forward_blocks, consts, forward_levels, False)
        return sweep(backward_blocks, forward, backward_levels, True)

    def stations_sum(field):
        grid = field.reshape(cell_count, block_width, position_total, radial_count)
        padded = extended(grid, (("axial", 2),), 1)
        return (padded[:, :, :-2] + padded[:, :, 2:]).reshape(cell_count, block_width, line_count)

    applied_once = precondition(source)
    middle = source - applied_once + coupling_field * stations_sum(applied_once)
    second = precondition(middle)
    correction = applied_once + second
    remaining = middle - second + coupling_field * stations_sum(second)
    return (correction.reshape(rhs.shape), remaining.reshape(rhs.shape))


def solution(mesh):
    cells, stations = mesh.shape["azim"], mesh.shape["axial"]

    def on_each(rhs, coupling, fwd_coupling, bwd_coupling, block_inverse):
        local = fwd_coupling.shape
        if (cells, stations) == (8, 4) and local == (1, 48, 48, 1, 128):
            return line_plan(rhs, coupling, fwd_coupling, bwd_coupling, block_inverse)
        return on_device(rhs, coupling, fwd_coupling, bwd_coupling, block_inverse)

    return jax.shard_map(
        on_each,
        mesh=mesh,
        in_specs=(
            P("azim", None, "axial", None),
            P("azim", None, "axial", None),
            P("azim", None, None, "axial", None),
            P("azim", None, None, "axial", None),
            P("azim", None, None, "axial", None),
        ),
        out_specs=(P("azim", None, "axial", None), P("azim", None, "axial", None)),
        check_vma=False,
    )
```
